32 devices in a mesh: dp: 8 (over y, x, core), tensor: 4 (over z).
Axes of the slice: x: 2, y: 2, z: 4, core: 2. Of those that a mesh axis runs over, the one named last changes fastest.
Arguments:
- inputs: bfloat16 [8, 1024, 1536], P('dp', 'tensor'), may hold values from -6 to 6
- context: bfloat16 [8, 130, 1536], P('dp', None, 'tensor'), may hold values from -6 to 6
- positions: int32 [8, 1024], P('dp'), may hold values from 0 to 3069, as said below
- adapter_index: int32 [8], P('dp'), may hold values from 0 to 7
- self_in_weight: bfloat16 [1536, 3, 1536], P('dp', None, 'tensor'), may hold values from -0.15625 to 0.15625
- self_out_weight: bfloat16 [1536, 1536], P('tensor', 'dp'), may hold values from -3 to 3
- cross_query_weight: bfloat16 [1536, 1536], P('dp', 'tensor'), may hold values from -0.15625 to 0.15625
- cross_keyval_weight: bfloat16 [1536, 2, 1536], P('dp', None, 'tensor'), may hold values from -0.15625 to 0.15625
- cross_out_weight: bfloat16 [1536, 1536], P('tensor', 'dp'), may hold values from -1 to 1
- feed_in_weight: bfloat16 [1536, 2, 6144], P('dp', None, 'tensor'), may hold values from -0.15625 to 0.15625
- feed_out_weight: bfloat16 [6144, 1536], P('tensor', 'dp'), may hold values from -0.078125 to 0.078125
- norm_gains: float32 [3, 1536], replicated, may hold values from 0.25 to 1.75
- norm_biases: float32 [3, 1536], replicated, may hold values from -1.75 to 1.75
- adapter_down: bfloat16 [8, 6, 1536, 16], replicated, may hold values from -0.15625 to 0.15625
- adapter_down_hidden: bfloat16 [8, 6144, 16], replicated, may hold values from -0.078125 to 0.078125
- adapter_up: bfloat16 [8, 16, 9, 1536], replicated, may hold values from -1.5 to 1.5
- adapter_up_hidden: bfloat16 [8, 16, 2, 6144], replicated, may hold values from -1.5 to 1.5
- out_cotangent: bfloat16 [8, 1024, 1536], P('dp', 'tensor'), may hold values from -6 to 6
Outputs:
- block_output: bfloat16 [8, 1024, 1536], P('dp', 'tensor')
- grad_inputs: float32 [8, 1024, 1536], P('dp', 'tensor')
- grad_context: float32 [8, 130, 1536], P('dp', None, 'tensor')
- grad_adapter_down: float32 [8, 6, 1536, 16], P(None, None, 'tensor')
- grad_adapter_down_hidden: float32 [8, 6144, 16], P(None, 'tensor')
- grad_adapter_up: float32 [8, 16, 9, 1536], P(None, None, None, 'tensor')
- grad_adapter_up_hidden: float32 [8, 16, 2, 6144], P(None, None, None, 'tensor')
The draws below stay inside these ranges and needn't reach their ends.
Inputs may be any that keep to these rules, and one draw needn't show every extreme that they name: Within each sequence the positions start at 0 and rise by 1 to 3 from one token to the next.
All inputs are finite; a program needn't handle non-finite values.
Results may differ from the reference program's by a relative error of at most 0.03.
Values may be sent and summed in bfloat16 or wider, within the bound.
No kernel may reach another device: no remote copies, remote signals or barrier semaphores. Data moves between devices by JAX's collectives and lax.ppermute only.
A program may use at most 256 MiB of HBM per device.

```python
import jax
import jax.numpy as jnp
from jax import lax

D = 1536
HEADS = 24
HEAD_DIM = 64
FF = 6144
ROT = 32
RANK = 16
ADAPTERS = 8
COND = 130
SEQ_LEN = 1024
SEQS = 8


def draw_positions(key, part):
    key = jax.random.fold_in(key, 7)
    stride_key, row_key = jax.random.split(key)
    strides = jax.random.randint(stride_key, (SEQS, SEQ_LEN), 1, 4)
    widest = jax.random.randint(row_key, (), 0, SEQS)
    strides = jnp.where(jnp.arange(SEQS, dtype=jnp.int32)[:, None] == widest, 3, strides)
    return (jnp.cumsum(strides, axis=1) - strides[:, :1]).astype(jnp.int32)


def set_ends(drawn, stream_key, least, top_value):
    longest = drawn.shape.index(max(drawn.shape))
    spots = []
    for shift in (0, 1):
        where = [jax.random.randint(jax.random.fold_in(stream_key, axis), (), 0, length) for axis, length in enumerate(drawn.shape)]
        where[longest] = (where[longest] + shift) % drawn.shape[longest]
        spots.append(tuple(where))
    return drawn.at[spots[0]].set(least).at[spots[1]].set(top_value)


def shard_levels(key, shape, pieces, low, top_value):
    factor_of, own = 1.0, jax.random.fold_in(key, 6)
    for axis_at, parts in pieces:
        steps = jnp.exp(jax.random.uniform(jax.random.fold_in(own, axis_at), (parts,), jnp.float32, low / len(pieces), top_value / len(pieces)))
        factor_of = factor_of * jnp.repeat(steps, shape[axis_at] // parts).reshape([-1 if axis == axis_at else 1 for axis in range(len(shape))])
    return factor_of


def noise(key, shape, spread, reach, cuts=(), held_as=jnp.bfloat16):
    array = spread * jax.random.normal(key, shape, jnp.float32)
    if cuts:
        array = array * shard_levels(key, shape, cuts, -0.22, 0.18)
    return jnp.clip(array, -reach, reach).astype(held_as)


def setup_inputs(seed: int = 0) -> dict:
    splits = jax.random.split(jax.random.key(seed), 19)
    inputs = noise(splits[0], (SEQS, SEQ_LEN, D), 1.0, 6.0, ((0, 8), (1, 4)))
    context = noise(splits[1], (SEQS, COND, D), 1.0, 6.0, ((0, 8), (2, 4)))
    positions = draw_positions(jax.random.fold_in(splits[18], 71), 0)
    adapter_index = set_ends(jax.random.randint(splits[3], (SEQS,), 0, ADAPTERS), jax.random.fold_in(splits[3], 1), 0, ADAPTERS - 1).astype(jnp.int32)
    self_in_weight = noise(splits[4], (D, 3, D), D ** -0.5, 0.15625, ((0, 8), (2, 4)))
    self_out_weight = noise(splits[5], (D, D), (max(3 * D // SEQ_LEN, 1)) ** -0.5, 3.0, ((0, 4), (1, 8)))
    cross_query_weight = noise(splits[6], (D, D), D ** -0.5, 0.15625, ((0, 8), (1, 4)))
    cross_keyval_weight = noise(splits[7], (D, 2, D), D ** -0.5, 0.15625, ((0, 8), (2, 4)))
    cross_out_weight = noise(splits[8], (D, D), (max(3 * D // COND, 1)) ** -0.5, 1.0, ((0, 4), (1, 8)))
    feed_in_weight = noise(splits[9], (D, 2, FF), D ** -0.5, 0.15625, ((0, 8), (2, 4)))
    feed_out_weight = noise(splits[10], (FF, D), FF ** -0.5, 0.078125, ((0, 4), (1, 8)))
    norm_gains = jnp.clip(1.0 + 0.15 * jax.random.normal(splits[11], (3, D), jnp.float32), 0.25, 1.75)
    norm_biases = noise(splits[12], (3, D), 0.3, 1.75, (), jnp.float32)
    adapter_down = noise(splits[13], (ADAPTERS, 6, D, RANK), D ** -0.5, 0.15625)
    adapter_down_hidden = noise(splits[14], (ADAPTERS, FF, RANK), FF ** -0.5, 0.078125)
    adapter_up = noise(splits[15], (ADAPTERS, RANK, 9, D), 0.25, 1.5)
    adapter_up_hidden = noise(splits[16], (ADAPTERS, RANK, 2, FF), 0.25, 1.5)
    out_cotangent = noise(splits[17], (SEQS, SEQ_LEN, D), 1.0, 6.0, ((0, 8), (1, 4)))
    return {"inputs": inputs, "context": context, "positions": positions, "adapter_index": adapter_index, "self_in_weight": self_in_weight, "self_out_weight": self_out_weight, "cross_query_weight": cross_query_weight, "cross_keyval_weight": cross_keyval_weight, "cross_out_weight": cross_out_weight, "feed_in_weight": feed_in_weight, "feed_out_weight": feed_out_weight, "norm_gains": norm_gains, "norm_biases": norm_biases, "adapter_down": adapter_down, "adapter_down_hidden": adapter_down_hidden, "adapter_up": adapter_up, "adapter_up_hidden": adapter_up_hidden, "out_cotangent": out_cotangent}


EPSILON = 1e-05
HIGHEST = lax.Precision.HIGHEST

@jax.custom_vjp
def low(v):
    return lax.optimization_barrier(v.astype(jnp.bfloat16)).astype(jnp.float32)

@jax.custom_vjp
def low_back(v):
    return v

def low_keep(v):
    return (low(v), None)

def low_pass(kept, grad):
    return (grad,)

def back_keep(v):
    return (v, None)

def back_low(kept, grad):
    return (low(grad),)
low.defvjp(low_keep, low_pass)
low_back.defvjp(back_keep, back_low)

def layer_norm(stream, norm_gain, norm_bias):
    average = lax.optimization_barrier(jnp.mean(stream, axis=-1, keepdims=True))
    centred = stream - average
    variance = lax.optimization_barrier(jnp.mean(centred * centred, axis=-1, keepdims=True))
    return centred * lax.rsqrt(variance + EPSILON) * norm_gain + norm_bias

def rotate(values, cosines, sines):
    half_rot = cosines.shape[-1]
    leading = values[..., :half_rot]
    second = values[..., half_rot:2 * half_rot]
    return jnp.concatenate([leading * cosines - second * sines, second * cosines + leading * sines, values[..., 2 * half_rot:]], axis=-1)

def matmul(left, right):
    return jnp.dot(left, right, precision=HIGHEST)

def attend(query, keys, values):
    scaling = query.shape[-1] ** (-0.5)
    scores = low_back(jnp.einsum('lhe,mhe->hlm', query, keys, precision=HIGHEST) * scaling)
    row_max = lax.optimization_barrier(jnp.max(scores, axis=-1, keepdims=True))
    exponentials = jnp.exp(scores - row_max)
    probabilities = low(exponentials / lax.optimization_barrier(jnp.sum(exponentials, axis=-1, keepdims=True)))
    result = jnp.einsum('hlm,mhe->lhe', probabilities, values, precision=HIGHEST)
    return low(low_back(result))

def reference(inputs, context, positions, adapter_index, self_in_weight, self_out_weight, cross_query_weight, cross_keyval_weight, cross_out_weight, feed_in_weight, feed_out_weight, norm_gains, norm_biases, adapter_down, adapter_down_hidden, adapter_up, adapter_up_hidden, out_cotangent):
    self_in = self_in_weight.astype(jnp.float32).reshape(D, 3 * D)
    self_out = self_out_weight.astype(jnp.float32)
    cross_query = cross_query_weight.astype(jnp.float32)
    cross_keyval = cross_keyval_weight.astype(jnp.float32).reshape(D, 2 * D)
    cross_out = cross_out_weight.astype(jnp.float32)
    feed_in = feed_in_weight.astype(jnp.float32).reshape(D, 2 * FF)
    feed_out = feed_out_weight.astype(jnp.float32)
    onehot = (adapter_index[:, None] == jnp.arange(ADAPTERS, dtype=jnp.int32)[None, :]).astype(jnp.float32)
    half_rot = ROT // 2
    inverse = 10000.0 ** (-jnp.arange(half_rot, dtype=jnp.float32) / half_rot)
    angles = positions.astype(jnp.float32)[:, :, None, None] * inverse
    cosines = jnp.cos(angles)
    sines = jnp.sin(angles)

    def forward(stream_all, context_all, down_table, down_hidden, up_table, up_hidden):

        def one_sequence(packed):
            stream, context_rows, cosine_rows, sine_rows, selector = packed
            chosen_down = jnp.einsum('a,akdr->kdr', selector, down_table, precision=HIGHEST)
            chosen_down_hidden = jnp.einsum('a,afr->fr', selector, down_hidden, precision=HIGHEST)
            chosen_up = jnp.einsum('a,arkd->rkd', selector, up_table, precision=HIGHEST)
            chosen_up_hidden = jnp.einsum('a,arkf->rkf', selector, up_hidden, precision=HIGHEST)
            row_count = stream.shape[0]
            normed = low(layer_norm(stream, norm_gains[0], norm_biases[0]))
            lowrank = low(matmul(normed, chosen_down[0]))
            mixed = low_back(matmul(normed, self_in) + matmul(lowrank, chosen_up[:, 0:3].reshape(RANK, 3 * D)))
            mixed = mixed.reshape(row_count, 3, HEADS, HEAD_DIM)
            query = low(rotate(mixed[:, 0], cosine_rows, sine_rows))
            keys = low(rotate(mixed[:, 1], cosine_rows, sine_rows))
            values = low(mixed[:, 2])
            heads = attend(query, keys, values).reshape(row_count, D)
            lowrank = low(low_back(matmul(heads, chosen_down[1])))
            stream = stream + low_back(matmul(heads, self_out) + matmul(lowrank, chosen_up[:, 3]))
            normed = low(layer_norm(stream, norm_gains[1], norm_biases[1]))
            lowrank = low(matmul(normed, chosen_down[2]))
            query = low(low_back(matmul(normed, cross_query) + matmul(lowrank, chosen_up[:, 4])))
            query = query.reshape(row_count, HEADS, HEAD_DIM)
            lowrank = low(matmul(context_rows, chosen_down[3]))
            keyval = low_back(matmul(context_rows, cross_keyval) + matmul(lowrank, chosen_up[:, 5:7].reshape(RANK, 2 * D)))
            keyval = keyval.reshape(context_rows.shape[0], 2, HEADS, HEAD_DIM)
            heads = attend(query, low(keyval[:, 0]), low(keyval[:, 1])).reshape(row_count, D)
            lowrank = low(low_back(matmul(heads, chosen_down[4])))
            stream = stream + low_back(matmul(heads, cross_out) + matmul(lowrank, chosen_up[:, 7]))
            normed = low(layer_norm(stream, norm_gains[2], norm_biases[2]))
            lowrank = low(matmul(normed, chosen_down[5]))
            gate_up = low_back(matmul(normed, feed_in) + matmul(lowrank, chosen_up_hidden.reshape(RANK, 2 * FF)))
            gate_up = gate_up.reshape(row_count, 2, FF)
            hidden = low(jax.nn.silu(gate_up[:, 0]) * gate_up[:, 1])
            lowrank = low(low_back(matmul(hidden, chosen_down_hidden)))
            return stream + low_back(matmul(hidden, feed_out) + matmul(lowrank, chosen_up[:, 8]))
        return lax.map(jax.checkpoint(one_sequence), (stream_all, context_all, cosines, sines, onehot))
    result, pullback = jax.vjp(forward, inputs.astype(jnp.float32), context.astype(jnp.float32), adapter_down.astype(jnp.float32), adapter_down_hidden.astype(jnp.float32), adapter_up.astype(jnp.float32), adapter_up_hidden.astype(jnp.float32))
    gradients = pullback(out_cotangent.astype(jnp.float32))
    return (result.astype(jnp.bfloat16), gradients[0], gradients[1], gradients[2], gradients[3], gradients[4], gradients[5])
```

```python
import jax
import jax.numpy as jnp
from jax import lax
from jax.sharding import Mesh, PartitionSpec as P

HEAD_DIM = 64
ROT = 32
EPSILON = 1e-05
EXT = 128
CHUNKS = 3
F32 = jnp.float32
BF = jnp.bfloat16
SWAP = ((0, 1), (1, 0))


def dot(left, right):
    return jnp.dot(left, right, preferred_element_type=F32)


def dot_nt(left, right):
    return lax.dot_general(left, right, (((1,), (1,)), ((), ())), preferred_element_type=F32)


def dot_tn(left, right):
    return lax.dot_general(left, right, (((0,), (0,)), ((), ())), preferred_element_type=F32)


def core_swap(x):
    return lax.ppermute(x, "core", SWAP)


def xor_move(x, axis, size, k):
    return lax.ppermute(x, axis, [(i, i ^ k) for i in range(size)])


def home_swap(x):
    return lax.ppermute(x, ("core", "zhi"), [(0, 0), (1, 2), (2, 1), (3, 3)])


class Group:
    def __init__(self, pairs, chips):
        self.pairs, self.chips = pairs, chips
        self.core, self.zhi, self.p = (lax.axis_index(n) for n in ("core", "zhi", "p"))
        self.chip = lax.axis_index("chip")
        self.home = self.core == self.zhi
        self.pieces = [
            (self.core ^ kc) * pairs + (self.p ^ kp) for kp in range(pairs) for kc in (0, 1)
        ]

    def gather(self, own):
        blocks = [own, core_swap(own)]
        for k in range(1, self.pairs):
            far = xor_move(own, "p", self.pairs, k)
            blocks += [far, core_swap(far)]
        return blocks

    def scatter(self, partials):
        sums = [
            partials[2 * k].astype(F32) + core_swap(partials[2 * k + 1].astype(BF)).astype(F32)
            for k in range(self.pairs)
        ]
        total = sums[0]
        for k in range(1, self.pairs):
            total = total + xor_move(sums[k].astype(BF), "p", self.pairs, k).astype(F32)
        return total

    def spread_chips(self, block):
        got = {0: block}
        if self.chips == 4:
            got[1] = xor_move(block, "chip", 4, 1)
            got[2] = xor_move(block, "chip", 4, 2)
            half = block.shape[0] // 2
            got[3] = jnp.concatenate(
                [
                    xor_move(got[2][:half], "chip", 4, 1),
                    xor_move(got[1][half:], "chip", 4, 2),
                ],
                axis=0,
            )
        else:
            for k in range(1, self.chips):
                got[k] = xor_move(block, "chip", self.chips, k)
        return [got[k] for k in range(self.chips)]

    def gather_weights(self, shard):
        rows, columns = shard.shape
        other = core_swap(shard)
        both = jnp.zeros((2 * rows, columns), shard.dtype)
        both = lax.dynamic_update_slice(both, shard, (self.core * rows, 0))
        both = lax.dynamic_update_slice(both, other, ((1 - self.core) * rows, 0))
        far = lax.ppermute(both, ("core", "zhi"), [(0, 1), (3, 2)])
        both = jnp.where(self.home, both, far)
        blocks = self.spread_chips(both)
        whole = jnp.zeros((2 * rows * self.chips + EXT, columns), shard.dtype)
        for k, block in enumerate(blocks):
            whole = lax.dynamic_update_slice(whole, block, ((self.chip ^ k) * 2 * rows, 0))
        return whole


def stats(stream):
    average = jnp.mean(stream, axis=-1, keepdims=True)
    centred = stream - average
    variance = jnp.mean(centred * centred, axis=-1, keepdims=True)
    scale = lax.rsqrt(variance + EPSILON)
    return centred * scale, scale


def layer_norm(stream, gain, bias):
    return (stats(stream)[0] * gain + bias).astype(BF)


def norm_backward(stream, gain, grad):
    unit, scale = stats(stream)
    grad = grad * gain
    return scale * (
        grad
        - jnp.mean(grad, axis=-1, keepdims=True)
        - unit * jnp.mean(grad * unit, axis=-1, keepdims=True)
    )


def widen(rows, low):
    pad = jnp.zeros((rows.shape[0], EXT - low.shape[1]), rows.dtype)
    return jnp.concatenate([rows, low.astype(rows.dtype), pad], axis=1)


def rotate(values, cosines, sines):
    half = ROT // 2
    rows, width = values.shape
    values = values.reshape(rows, width // HEAD_DIM, HEAD_DIM)
    leading, second = values[..., :half], values[..., half:ROT]
    cosines, sines = cosines[:, None], sines[:, None]
    return jnp.concatenate(
        [
            leading * cosines - second * sines,
            second * cosines + leading * sines,
            values[..., ROT:],
        ],
        axis=-1,
    ).reshape(rows, width)


def split_heads(x):
    return x.reshape(x.shape[0], -1, HEAD_DIM)


def attend(query, keys, values):
    query, keys, values = split_heads(query), split_heads(keys), split_heads(values)
    scores = jnp.einsum("qhe,khe->hqk", query, keys, preferred_element_type=F32) * 0.125
    top = jnp.max(scores, axis=-1, keepdims=True)
    powers = jnp.exp(scores - top)
    total = jnp.sum(powers, axis=-1, keepdims=True)
    out = jnp.einsum(
        "hqk,khe->qhe", (powers / total).astype(BF), values, preferred_element_type=F32
    )
    return out.reshape(out.shape[0], -1).astype(BF), top + jnp.log(total)


def attend_backward(query, keys, values, logsum, grad):
    query, keys, values = split_heads(query), split_heads(keys), split_heads(values)
    grad = split_heads(grad)
    scores = jnp.einsum("qhe,khe->hqk", query, keys, preferred_element_type=F32) * 0.125
    probs = jnp.exp(scores - logsum)
    grad_probs = jnp.einsum("qhe,khe->hqk", grad, values, preferred_element_type=F32)
    delta = jnp.sum(probs * grad_probs, axis=-1, keepdims=True)
    grad_scores = (probs * (grad_probs - delta)).astype(BF)
    grad_query = jnp.einsum("hqk,khe->qhe", grad_scores, keys, preferred_element_type=F32) * 0.125
    grad_keys = jnp.einsum("hqk,qhe->khe", grad_scores, query, preferred_element_type=F32) * 0.125
    grad_values = jnp.einsum("hqk,qhe->khe", probs.astype(BF), grad, preferred_element_type=F32)
    return tuple(g.reshape(g.shape[0], -1) for g in (grad_query, grad_keys, grad_values))


def body(
    inputs,
    context,
    positions,
    adapter_index,
    self_in_weight,
    self_out_weight,
    cross_query_weight,
    cross_keyval_weight,
    cross_out_weight,
    feed_in_weight,
    feed_out_weight,
    norm_gains,
    norm_biases,
    adapter_down,
    adapter_down_hidden,
    adapter_up,
    adapter_up_hidden,
    out_cotangent,
    *,
    pairs,
    chips,
):
    group = Group(pairs, chips)
    members = 2 * pairs
    rows, width = inputs.shape[1], inputs.shape[2]
    local = self_in_weight.shape[2]
    hidden = feed_in_weight.shape[2]
    slots, rank = adapter_down.shape[0], adapter_down.shape[3]
    part = hidden // CHUNKS
    pieces = group.pieces
    gains, biases = norm_gains, norm_biases

    index = jnp.where(group.home, adapter_index, core_swap(adapter_index))[0]
    positions = jnp.where(group.home, positions, core_swap(positions))[0]
    stream = group.gather(home_swap(inputs[0]))
    cotangent = group.gather(home_swap(out_cotangent[0]))
    context_blocks = group.gather(home_swap(context[0]))

    down = lax.dynamic_index_in_dim(adapter_down.transpose(0, 1, 3, 2), index, 0, keepdims=False)
    down_hidden = lax.dynamic_index_in_dim(
        adapter_down_hidden.transpose(0, 2, 1), index, 0, keepdims=False
    )
    up = lax.dynamic_index_in_dim(adapter_up.transpose(0, 2, 1, 3), index, 0, keepdims=False)
    up_hidden = lax.dynamic_index_in_dim(
        adapter_up_hidden.transpose(0, 2, 1, 3), index, 0, keepdims=False
    )

    def piece(array, k, size):
        return lax.dynamic_slice_in_dim(array, pieces[k] * size, size, array.ndim - 1)

    def relative(array, size):
        return jnp.concatenate([piece(array, k, size) for k in range(members)], axis=-1)

    def own(array):
        return piece(array, 0, local)

    def weights(shards, low):
        whole = group.gather_weights(jnp.concatenate(shards, axis=1))
        return lax.dynamic_update_slice(whole, jnp.concatenate(low, axis=1), (width, 0))

    self_in = weights(
        [self_in_weight[:, i] for i in range(3)], [own(up[i]) for i in range(3)]
    )
    rest = weights(
        [
            self_out_weight.T,
            cross_query_weight,
            cross_out_weight.T,
            cross_keyval_weight[:, 0],
            cross_keyval_weight[:, 1],
        ],
        [own(down[1]), own(up[4]), own(down[4]), own(up[5]), own(up[6])],
    )
    self_out = rest[:, :local]
    cross_keyval = rest[:, 3 * local :]
    cross_blocks = group.gather(rest[:, local : 3 * local])
    cross_query = jnp.concatenate([b[:, :local] for b in cross_blocks], axis=1)
    cross_out = jnp.concatenate([b[:, local:] for b in cross_blocks], axis=1)
    feed_down = piece(down_hidden, 0, hidden)
    feed_up = piece(up_hidden, 0, hidden)
    feed = []
    for i in range(CHUNKS):
        at = slice(i * part, (i + 1) * part)
        feed.append(
            weights(
                [feed_in_weight[:, 0, at], feed_in_weight[:, 1, at], feed_out_weight.T[:, at]],
                [feed_up[0, :, at], feed_up[1, :, at], feed_down[:, at]],
            )
        )

    blocks_at = [
        lax.dynamic_slice_in_dim(positions, pieces[k] * rows, rows, 0) for k in range(members)
    ]
    half = ROT // 2
    inverse = 10000.0 ** (-jnp.arange(half, dtype=F32) / half)
    angles = jnp.concatenate(blocks_at).astype(F32)[:, None] * inverse
    cosines, sines = jnp.cos(angles), jnp.sin(angles)

    def project(normed, down_rows, weight):
        low = dot_nt(normed, down_rows).astype(BF)
        return dot(widen(normed, low), weight), low

    stream_zero = stream[0].astype(F32)
    normed_one = layer_norm(jnp.concatenate(stream, axis=0).astype(F32), gains[0], biases[0])
    mixed, low_one = project(normed_one, down[0], self_in)
    query = rotate(mixed[:, :local], cosines, sines).astype(BF)
    keys = rotate(mixed[:, local : 2 * local], cosines, sines).astype(BF)
    values = mixed[:, 2 * local :].astype(BF)
    heads, logsum = attend(query, keys, values)

    def split_rows(x):
        return [x[k * rows : (k + 1) * rows] for k in range(members)]

    def tail(partial, up_rows):
        total = group.scatter(partial)
        low = total[:, width : width + rank].astype(BF)
        return total[:, :width] + dot(low, up_rows), low

    branch, low_two = tail(split_rows(dot_nt(heads, self_out)), up[3])
    stream_one = stream_zero + branch

    normed_two = layer_norm(stream_one, gains[1], biases[1])
    query_cross, low_three = project(normed_two, down[2], cross_query)
    query_cross = query_cross.astype(BF)
    context_count = context_blocks[0].shape[0]
    context_all = jnp.zeros((members,) + context_blocks[0].shape, BF)
    for k in range(members):
        context_all = lax.dynamic_update_slice(
            context_all, context_blocks[k][None], (pieces[k], 0, 0)
        )
    context_all = context_all.transpose(1, 0, 2).reshape(context_count, width)
    keyval, low_context = project(context_all, down[3], cross_keyval)
    keyval_blocks = group.gather(keyval.astype(BF))
    keys_cross = jnp.concatenate([b[:, :local] for b in keyval_blocks], axis=1)
    values_cross = jnp.concatenate([b[:, local:] for b in keyval_blocks], axis=1)
    heads_cross, logsum_cross = attend(query_cross, keys_cross, values_cross)
    total = dot_nt(heads_cross, cross_out)
    low_four = total[:, width : width + rank].astype(BF)
    stream_two = stream_one + total[:, :width] + dot(low_four, up[7])

    normed_three = layer_norm(stream_two, gains[2], biases[2])
    low_own_five = dot_nt(normed_three, down[5]).astype(BF)
    normed_all = jnp.concatenate(group.gather(normed_three), axis=0)
    low_five = dot_nt(normed_all, down[5]).astype(BF)
    wide = widen(normed_all, low_five)
    cotangent_all = jnp.concatenate(cotangent, axis=0)
    grad_low = dot_nt(cotangent_all, up[8]).astype(BF)
    wide_grad = widen(cotangent_all, grad_low)
    feed_sum, grad_sum = 0.0, 0.0
    grad_feed_down, grad_gate_up, grad_upper_up = [], [], []
    for weight in feed:
        gate = dot(wide, weight[:, :part])
        upper = dot(wide, weight[:, part : 2 * part])
        sigmoid = 1.0 / (1.0 + jnp.exp(-gate))
        acted = gate * sigmoid
        unit = (acted * upper).astype(BF)
        feed_sum = feed_sum + dot_nt(unit, weight[:, 2 * part :])
        grad_unit = dot(wide_grad, weight[:, 2 * part :])
        grad_gate = (grad_unit * upper * (sigmoid + acted * (1.0 - sigmoid))).astype(BF)
        grad_upper = (grad_unit * acted).astype(BF)
        grad_sum = grad_sum + dot_nt(grad_gate, weight[:, :part])
        grad_sum = grad_sum + dot_nt(grad_upper, weight[:, part : 2 * part])
        grad_feed_down.append(dot_tn(grad_low, unit))
        grad_gate_up.append(dot_tn(low_five, grad_gate))
        grad_upper_up.append(dot_tn(low_five, grad_upper))

    def head(partial, down_rows):
        total = group.scatter(partial)
        grad_low = total[:, width : width + rank].astype(BF)
        return total[:, :width] + dot(grad_low, down_rows), grad_low

    grad_normed, grad_low_five = head(split_rows(grad_sum), down[5])
    grad_down_five = dot_tn(grad_low_five, normed_three)
    branch, low_six = tail(split_rows(feed_sum), up[8])
    block_output = home_swap((stream_two + branch).astype(BF))
    grad_up_eight = dot_tn(low_six, cotangent[0])
    grad_stream = cotangent[0].astype(F32) + norm_backward(stream_two, gains[2], grad_normed)

    branch_grad = grad_stream.astype(BF)
    grad_low_four = dot_nt(branch_grad, up[7]).astype(BF)
    grad_up_seven = dot_tn(low_four, branch_grad)
    grad_down_four = dot_tn(grad_low_four, heads_cross)
    grad_heads = dot(widen(branch_grad, grad_low_four), cross_out).astype(BF)
    grad_query, grad_keys, grad_values = attend_backward(
        query_cross, keys_cross, values_cross, logsum_cross, grad_heads
    )
    grad_query = grad_query.astype(BF)
    total = dot_nt(grad_query, cross_query)
    grad_low_two = total[:, width : width + rank].astype(BF)
    grad_up_four = dot_tn(low_three, grad_query)
    grad_down_two = dot_tn(grad_low_two, normed_two)
    grad_normed = total[:, :width] + dot(grad_low_two, down[2])
    grad_stream = grad_stream + norm_backward(stream_one, gains[1], grad_normed)
    grad_keyval = group.scatter(
        [
            jnp.concatenate([g[:, k * local : (k + 1) * local] for g in (grad_keys, grad_values)], axis=1)
            for k in range(members)
        ]
    ).astype(BF)
    total = dot_nt(grad_keyval, cross_keyval)
    grad_low_three = total[:, width : width + rank].astype(BF)
    grad_up_keyval = dot_tn(low_context, grad_keyval)
    grad_down_three = dot_tn(grad_low_three, context_all)
    context_partial = total[:, :width] + dot(grad_low_three, down[3])
    grad_context = home_swap(
        group.scatter([piece(context_partial, k, local) for k in range(members)]).astype(BF)
    ).astype(F32)

    branch_grad = jnp.concatenate(group.gather(grad_stream.astype(BF)), axis=0)
    grad_low_one = dot_nt(branch_grad, up[3]).astype(BF)
    grad_up_three = dot_tn(low_two, branch_grad[:rows])
    grad_down_one = dot_tn(grad_low_one, heads)
    grad_heads = dot(widen(branch_grad, grad_low_one), self_out).astype(BF)
    grad_query, grad_keys, grad_values = attend_backward(query, keys, values, logsum, grad_heads)
    grad_mixed = jnp.concatenate(
        [rotate(grad_query, cosines, -sines), rotate(grad_keys, cosines, -sines), grad_values],
        axis=1,
    ).astype(BF)
    grad_up_self = dot_tn(low_one, grad_mixed)
    grad_normed, grad_low_zero = head(split_rows(dot_nt(grad_mixed, self_in)), down[0])
    grad_down_zero = dot_tn(grad_low_zero, normed_one[:rows])
    grad_inputs = grad_stream + norm_backward(stream_zero, gains[0], grad_normed)
    grad_inputs = home_swap(grad_inputs.astype(BF)).astype(F32)

    summed = group.scatter(
        [
            jnp.concatenate(
                [
                    piece(g, k, local)
                    for g in (
                        grad_down_zero,
                        grad_down_two,
                        grad_down_three,
                        grad_down_five,
                        grad_up_three,
                        grad_up_seven,
                        grad_up_eight,
                    )
                ]
                + [g[:, k * local : (k + 1) * local] for g in (grad_down_four, grad_up_four)],
                axis=0,
            )
            for k in range(members)
        ]
    ).reshape(9, rank, local)
    fold = hidden // local

    def columns(array):
        return array.reshape(rank, -1, local).transpose(1, 0, 2)

    grads = jnp.concatenate(
        [
            summed[0:1],
            grad_down_one[None],
            summed[1:3],
            summed[7:8],
            summed[3:4],
            columns(grad_up_self),
            summed[4:5],
            summed[8:9],
            columns(grad_up_keyval),
            summed[5:7],
            columns(jnp.concatenate(grad_feed_down, axis=1)),
            columns(jnp.concatenate(grad_gate_up, axis=1)),
            columns(jnp.concatenate(grad_upper_up, axis=1)),
            jnp.full((1, rank, local), index, F32),
        ],
        axis=0,
    ).astype(BF)
    across = xor_move(grads, "zhi", 2, 1)
    both = jnp.stack([grads, across])
    both = jnp.where(group.home, both, core_swap(both))
    every = jnp.concatenate(group.spread_chips(both), axis=0)
    labels = every[:, -1, 0, 0]

    def settle(array):
        return jnp.stack(
            [
                sum(
                    jnp.where(labels[s] == slot, array[s], 0).astype(F32)
                    for s in range(array.shape[0])
                )
                for slot in range(slots)
            ]
        )

    grad_down = settle(every[:, 0:6]).transpose(0, 1, 3, 2)
    grad_up = settle(every[:, 6:15]).transpose(0, 2, 1, 3)
    grad_hidden = settle(every[:, 15 : 15 + fold]).transpose(0, 1, 3, 2)
    grad_hidden = grad_hidden.reshape(slots, hidden, rank)
    grad_gate = settle(every[:, 15 + fold : 15 + 3 * fold])
    grad_gate = grad_gate.reshape(slots, 2, fold, rank, local).transpose(0, 3, 1, 2, 4)
    return (
        block_output[None],
        grad_inputs[None],
        grad_context[None],
        grad_down,
        grad_hidden,
        grad_up,
        grad_gate.reshape(slots, rank, 2, hidden),
    )


def solution(mesh):
    members = mesh.shape["tensor"]
    chips = mesh.shape["dp"] // 2
    mesh = Mesh(
        mesh.devices.reshape(chips, 2, 2, members // 2), ("chip", "core", "zhi", "p")
    )
    dp, tensor = ("chip", "core"), ("zhi", "p")
    in_specs = (
        P(dp, tensor, None),
        P(dp, None, tensor),
        P(dp, None),
        P(dp),
        P(dp, None, tensor),
        P(tensor, dp),
        P(dp, tensor),
        P(dp, None, tensor),
        P(tensor, dp),
        P(dp, None, tensor),
        P(tensor, dp),
        P(),
        P(),
        P(),
        P(),
        P(),
        P(),
        P(dp, tensor, None),
    )
    out_specs = (
        P(dp, tensor, None),
        P(dp, tensor, None),
        P(dp, None, tensor),
        P(None, None, tensor, None),
        P(None, tensor, None),
        P(None, None, None, tensor),
        P(None, None, None, tensor),
    )

    def run(*args):
        return body(*args, pairs=members // 2, chips=chips)

    return jax.shard_map(run, mesh=mesh, in_specs=in_specs, out_specs=out_specs, check_vma=False)
```

```python
import functools

import jax
import jax.numpy as jnp
from jax import lax
from jax.experimental import pallas as pl
from jax.experimental.pallas import tpu as pltpu
from jax.sharding import Mesh, PartitionSpec as P

HEAD_DIM = 64
ROT = 32
EPSILON = 1e-05
EXT = 128
CHUNKS = 3
F32 = jnp.float32
BF = jnp.bfloat16
SWAP = ((0, 1), (1, 0))
VMEM_LIMIT = 56 * 1024 * 1024


def dot(left, right):
    return jnp.dot(left, right, preferred_element_type=F32)


def dot_nt(left, right):
    return lax.dot_general(left, right, (((1,), (1,)), ((), ())), preferred_element_type=F32)


def dot_tn(left, right):
    return lax.dot_general(left, right, (((0,), (0,)), ((), ())), preferred_element_type=F32)


def after(x, *earlier):
    return lax.optimization_barrier((x, *earlier))[0]


def core_swap(x):
    return lax.ppermute(x, "core", SWAP)


def xor_move(x, axis, size, k):
    return lax.ppermute(x, axis, [(i, i ^ k) for i in range(size)])


def home_swap(x):
    return lax.ppermute(x, ("core", "zhi"), [(0, 0), (1, 2), (2, 1), (3, 3)])


class Group:
    def __init__(self, pairs, chips):
        self.pairs, self.chips = pairs, chips
        self.core, self.zhi, self.p = (lax.axis_index(n) for n in ("core", "zhi", "p"))
        self.chip = lax.axis_index("chip")
        self.home = self.core == self.zhi
        self.pieces = [
            (self.core ^ kc) * pairs + (self.p ^ kp) for kp in range(pairs) for kc in (0, 1)
        ]

    def gather(self, own):
        blocks = [own, core_swap(own)]
        for k in range(1, self.pairs):
            far = xor_move(own, "p", self.pairs, k)
            blocks += [far, core_swap(far)]
        return blocks

    def scatter(self, partials):
        sums = [
            partials[2 * k].astype(F32) + core_swap(partials[2 * k + 1].astype(BF)).astype(F32)
            for k in reversed(range(self.pairs))
        ][::-1]
        total = sums[0]
        for k in range(1, self.pairs):
            total = total + xor_move(sums[k].astype(BF), "p", self.pairs, k).astype(F32)
        return total

    def spread_chips(self, block):
        got = {0: block}
        if self.chips == 4:
            got[1] = xor_move(block, "chip", 4, 1)
            got[2] = xor_move(block, "chip", 4, 2)
            half = block.shape[0] // 2
            got[3] = jnp.concatenate(
                [
                    xor_move(got[2][:half], "chip", 4, 1),
                    xor_move(got[1][half:], "chip", 4, 2),
                ],
                axis=0,
            )
        else:
            for k in range(1, self.chips):
                got[k] = xor_move(block, "chip", self.chips, k)
        return [got[k] for k in range(self.chips)]

    def pair_shard(self, shard):
        rows, columns = shard.shape
        other = core_swap(shard)
        both = jnp.zeros((2 * rows, columns), shard.dtype)
        both = lax.dynamic_update_slice(both, shard, (self.core * rows, 0))
        return lax.dynamic_update_slice(both, other, ((1 - self.core) * rows, 0))

    def cross_shard(self, both):
        far = lax.ppermute(both, ("core", "zhi"), [(0, 1), (3, 2)])
        return jnp.where(self.home, both, far)

    def assemble(self, blocks, low):
        rows, columns = blocks[0].shape
        whole = jnp.zeros((rows * self.chips + EXT, columns), blocks[0].dtype)
        for k, block in enumerate(blocks):
            whole = lax.dynamic_update_slice(whole, block, ((self.chip ^ k) * rows, 0))
        return lax.dynamic_update_slice(whole, low, (rows * self.chips, 0))


def stats(stream):
    average = jnp.mean(stream, axis=-1, keepdims=True)
    centred = stream - average
    variance = jnp.mean(centred * centred, axis=-1, keepdims=True)
    scale = lax.rsqrt(variance + EPSILON)
    return centred * scale, scale


def layer_norm(stream, gain, bias):
    return (stats(stream)[0] * gain + bias).astype(BF)


def norm_backward(stream, gain, grad):
    unit, scale = stats(stream)
    grad = grad * gain
    return scale * (
        grad
        - jnp.mean(grad, axis=-1, keepdims=True)
        - unit * jnp.mean(grad * unit, axis=-1, keepdims=True)
    )


def turn(x, cosines, left_sines, right_sines):
    breadth = 2 * HEAD_DIM if x.shape[1] % (2 * HEAD_DIM) == 0 else HEAD_DIM
    half = ROT // 2
    for at in range(0, x.shape[1], breadth):
        group = x[:, at : at + breadth]
        if breadth % 128 == 0:
            left, right = pltpu.roll(group, breadth - half, 1), pltpu.roll(group, half, 1)
        else:
            left = jnp.concatenate([group[:, half:], group[:, :half]], axis=1)
            right = jnp.concatenate([group[:, -half:], group[:, :-half]], axis=1)
        yield (
            at,
            breadth,
            group * cosines[:, :breadth]
            + left * left_sines[:, :breadth]
            + right * right_sines[:, :breadth],
        )


def whole_spec(shape):
    return pl.BlockSpec(shape, lambda *_: (0,) * len(shape))


def row_spec(rows, columns):
    return pl.BlockSpec((rows, columns), lambda t: (t, 0))


def params(semantics=1):
    return pltpu.CompilerParams(
        dimension_semantics=("arbitrary",) * semantics, vmem_limit_bytes=VMEM_LIMIT
    )


def cost(flops, moved, exps=0):
    return pl.CostEstimate(flops=int(flops), bytes_accessed=int(moved), transcendentals=int(exps))


def sds(shape, dtype):
    return jax.ShapeDtypeStruct(shape, dtype)


def query_kernel(
    x_ref, gain_ref, bias_ref, down_ref, w_ref, cos_ref, left_ref, right_ref,
    q_ref, k_ref, v_ref, low_ref,
):
    local, width = q_ref.shape[1], x_ref.shape[1]
    normed = layer_norm(x_ref[...].astype(F32), gain_ref[...], bias_ref[...])
    low = dot_nt(normed, down_ref[...]).astype(BF)
    low_ref[...] = low
    mixed = dot(normed, w_ref[:width, :]) + dot(low, w_ref[width:, :])
    tables = cos_ref[...], left_ref[...], right_ref[...]
    for at, breadth, turned in turn(mixed[:, :local], *tables):
        q_ref[:, at : at + breadth] = (turned * HEAD_DIM**-0.5).astype(BF)
    for at, breadth, turned in turn(mixed[:, local : 2 * local], *tables):
        k_ref[:, at : at + breadth] = turned.astype(BF)
    v_ref[...] = mixed[:, 2 * local :].astype(BF)


def project_self(x, gain, bias, down, weight, tables, rows):
    tokens, width = x.shape
    local = weight.shape[1] // 3
    return pl.pallas_call(
        query_kernel,
        grid=(tokens // rows,),
        in_specs=[
            row_spec(rows, width),
            whole_spec(gain.shape),
            whole_spec(bias.shape),
            whole_spec(down.shape),
            whole_spec(weight.shape),
            *[row_spec(rows, t.shape[1]) for t in tables],
        ],
        out_specs=[row_spec(rows, local)] * 3 + [row_spec(rows, EXT)],
        out_shape=[sds((tokens, local), BF)] * 3 + [sds((tokens, EXT), BF)],
        compiler_params=params(),
        cost_estimate=cost(2 * tokens * weight.size, 2 * (x.size + weight.size)),
    )(x, gain, bias, down, weight, *tables)


def attend_kernel(q_ref, k_ref, v_ref, w_ref, y_ref, o_ref, lse_ref):
    rows, local = q_ref.shape
    lanes = lax.broadcasted_iota(jnp.int32, (rows, EXT), 1)
    logsums = jnp.zeros((rows, EXT), F32)
    for head in range(local // HEAD_DIM):
        at = slice(head * HEAD_DIM, (head + 1) * HEAD_DIM)
        scores = dot_nt(q_ref[:, at], k_ref[:, at])
        top = jnp.max(scores, axis=1, keepdims=True)
        powers = jnp.exp(scores - top)
        total = jnp.sum(powers, axis=1, keepdims=True)
        out = dot(powers.astype(BF), v_ref[:, at]) / total
        o_ref[:, at] = out.astype(BF)
        logsums = jnp.where(lanes == head, top + jnp.log(total), logsums)
    lse_ref[...] = logsums.T[: lse_ref.shape[0]]
    y_ref[...] = dot_nt(o_ref[...], w_ref[...]).astype(BF)


def attend_self(query, keys, values, weight, rows):
    tokens, local = query.shape
    heads = -(-local // HEAD_DIM // 8) * 8
    return pl.pallas_call(
        attend_kernel,
        grid=(tokens // rows,),
        in_specs=[
            row_spec(rows, local),
            whole_spec(keys.shape),
            whole_spec(values.shape),
            whole_spec(weight.shape),
        ],
        out_specs=[
            row_spec(rows, weight.shape[0]),
            row_spec(rows, local),
            pl.BlockSpec((heads, rows), lambda t: (0, t)),
        ],
        out_shape=[
            sds((tokens, weight.shape[0]), BF),
            sds((tokens, local), BF),
            sds((heads, tokens), F32),
        ],
        compiler_params=params(),
        cost_estimate=cost(
            16 * tokens * tokens * local, 10 * query.size, tokens * tokens * local // HEAD_DIM
        ),
    )(query, keys, values, weight)


def attend_back_kernel(
    g_ref, up_ref, w_ref, q_ref, k_ref, v_ref, o_ref, lse_ref, cos_ref, left_ref, right_ref, low_ref,
    m_ref, down_ref, gup_ref, gk_ref, gv_ref,
):
    step, rows = pl.program_id(0), q_ref.shape[0]
    width, local = g_ref.shape[1], q_ref.shape[1]
    at_rows = pl.ds(pl.multiple_of(step * rows, rows), rows)

    @pl.when(step == 0)
    def _():
        gk_ref[...] = jnp.zeros_like(gk_ref)
        gv_ref[...] = jnp.zeros_like(gv_ref)
        down_ref[...] = jnp.zeros_like(down_ref)

    grad = g_ref[...]
    grad_low = dot_nt(grad, up_ref[...]).astype(BF)
    grad_out = (dot(grad, w_ref[:width, :]) + dot(grad_low, w_ref[width:, :])).astype(BF)
    out = o_ref[...]
    down_ref[...] += dot_tn(grad_low, out)[: down_ref.shape[0]]
    product = grad_out.astype(F32) * out.astype(F32)
    ones = jnp.ones((8, HEAD_DIM), F32)
    parts = []
    for head in range(local // HEAD_DIM):
        at = slice(head * HEAD_DIM, (head + 1) * HEAD_DIM)
        q, k, v, g = q_ref[:, at], k_ref[:, at], v_ref[:, at], grad_out[:, at]
        delta = lax.dot_general(
            ones, product[:, at], (((1,), (1,)), ((), ())),
            precision=lax.Precision.HIGHEST, preferred_element_type=F32,
        )[:1]
        probs = jnp.exp(dot_nt(k, q) - lse_ref[head : head + 1, :])
        grad_scores = (probs * (dot_nt(v, g) - delta)).astype(BF)
        gv_ref[:, at] += dot(probs.astype(BF), g)
        gk_ref[:, at] += dot(grad_scores, q)
        parts.append(dot_tn(grad_scores, k) * HEAD_DIM**-0.5)
    tables = cos_ref[at_rows, :], -left_ref[at_rows, :], -right_ref[at_rows, :]
    for at, breadth, turned in turn(jnp.concatenate(parts, axis=1), *tables):
        m_ref[at_rows, at : at + breadth] = turned.astype(BF)

    @pl.when(step == pl.num_programs(0) - 1)
    def _():
        tables = cos_ref[...], -left_ref[...], -right_ref[...]
        for at, breadth, turned in turn(gk_ref[...], *tables):
            m_ref[:, local + at : local + at + breadth] = turned.astype(BF)
        m_ref[:, 2 * local :] = gv_ref[...].astype(BF)
        gup_ref[...] = dot_tn(low_ref[...], m_ref[...])[: gup_ref.shape[0]]


def attend_back(grad, up, weight, query, keys, values, out, lse, tables, low, rank, rows):
    tokens, local = query.shape
    width = grad.shape[1]
    return pl.pallas_call(
        attend_back_kernel,
        grid=(tokens // rows,),
        in_specs=[
            row_spec(rows, width),
            whole_spec(up.shape),
            whole_spec(weight.shape),
            row_spec(rows, local),
            whole_spec(keys.shape),
            whole_spec(values.shape),
            row_spec(rows, local),
            pl.BlockSpec((lse.shape[0], rows), lambda t: (0, t)),
            *[whole_spec(t.shape) for t in tables],
            whole_spec(low.shape),
        ],
        out_specs=[
            whole_spec((tokens, 3 * local)),
            whole_spec((rank, local)),
            whole_spec((rank, 3 * local)),
        ],
        out_shape=[
            sds((tokens, 3 * local), BF),
            sds((rank, local), F32),
            sds((rank, 3 * local), F32),
        ],
        scratch_shapes=[pltpu.VMEM((tokens, local), F32)] * 2,
        compiler_params=params(),
        cost_estimate=cost(
            40 * tokens * tokens * local, 10 * query.size, tokens * tokens * local // HEAD_DIM
        ),
    )(grad, up, weight, query, keys, values, out, lse, *tables, low)


def cross_kernel(members, local, *refs):
    (x_ref, y_ref, up_self_ref, up_cross_ref, down_ref, gain_ref, bias_ref), refs = refs[:7], refs[7:]
    weights, refs = refs[:members], refs[members:]
    keyvals, refs = refs[:members], refs[members:]
    s1_ref, s2_ref, n2_ref, n3_ref, q_ref, o_ref, lse_ref, z2_ref, u_ref, z4_ref = refs
    width = x_ref.shape[1]
    rows = x_ref.shape[0]
    low = y_ref[:, width:].astype(BF)
    z2_ref[...] = low
    stream = x_ref[...].astype(F32) + y_ref[:, :width] + dot(low, up_self_ref[...])
    s1_ref[...] = stream
    normed = layer_norm(stream, gain_ref[1:2, :], bias_ref[1:2, :])
    n2_ref[...] = normed
    low = dot_nt(normed, down_ref[...]).astype(BF)
    u_ref[...] = low
    lanes = lax.broadcasted_iota(jnp.int32, (rows, EXT), 1)
    logsums = jnp.zeros((rows, EXT), F32)
    total = jnp.zeros((rows, width + EXT), F32)
    for k in range(members):
        weight, keyval = weights[k][...], keyvals[k][...]
        query = dot(normed, weight[:width, :local]) + dot(low, weight[width:, :local])
        query = (query * HEAD_DIM**-0.5).astype(BF)
        q_ref[:, k * local : (k + 1) * local] = query
        parts = []
        for head in range(local // HEAD_DIM):
            at = slice(head * HEAD_DIM, (head + 1) * HEAD_DIM)
            scores = dot_nt(query[:, at], keyval[:, at])
            top = jnp.max(scores, axis=1, keepdims=True)
            powers = jnp.exp(scores - top)
            sums = jnp.sum(powers, axis=1, keepdims=True)
            values = keyval[:, local + head * HEAD_DIM : local + (head + 1) * HEAD_DIM]
            parts.append((dot(powers.astype(BF), values) / sums).astype(BF))
            number = k * (local // HEAD_DIM) + head
            logsums = jnp.where(lanes == number, top + jnp.log(sums), logsums)
        out = jnp.concatenate(parts, axis=1)
        o_ref[:, k * local : (k + 1) * local] = out
        total = total + dot_nt(out, weight[:, local:])
    lse_ref[...] = logsums
    low = total[:, width:].astype(BF)
    z4_ref[...] = low
    stream = stream + total[:, :width] + dot(low, up_cross_ref[...])
    s2_ref[...] = stream
    n3_ref[...] = layer_norm(stream, gain_ref[2:3, :], bias_ref[2:3, :])


def cross_forward(x, y, up_self, up_cross, down, gains, biases, weights, keyvals):
    rows, width = x.shape
    members, local = len(weights), weights[0].shape[1] // 2
    plain, wide = sds((rows, width), BF), sds((rows, width), F32)
    low = sds((rows, EXT), BF)
    return pl.pallas_call(
        functools.partial(cross_kernel, members, local),
        out_shape=[wide, wide, plain, plain, plain, plain, sds((rows, EXT), F32), low, low, low],
        compiler_params=pltpu.CompilerParams(vmem_limit_bytes=VMEM_LIMIT),
        cost_estimate=cost(6 * rows * width * width, 8 * width * width),
    )(x, y, up_self, up_cross, down, gains, biases, *weights, *keyvals)


def cross_back_kernel(members, local, *refs):
    (
        g_ref, dn_ref, s1_ref, s2_ref, n2_ref, q_ref, o_ref, lse_ref, u_ref, z4_ref,
        up_ref, down5_ref, down2_ref, gain_ref, bias_ref,
    ), refs = refs[:15], refs[15:]
    weights, refs = refs[:members], refs[members:]
    keyvals, refs = refs[:members], refs[members:]
    r1_ref, r1b_ref, gup7_ref, gdown4_ref, gup4_ref, gdown2_ref, gdown5_ref, *gkv_refs = refs
    width = g_ref.shape[1]
    rank = gup7_ref.shape[0]
    stream = s2_ref[...]
    low = dn_ref[:, width:].astype(BF)
    grad_normed = dn_ref[:, :width] + dot(low, down5_ref[...])
    normed = layer_norm(stream, gain_ref[2:3, :], bias_ref[2:3, :])
    gdown5_ref[...] = dot_tn(low, normed)[:rank]
    grad = g_ref[...].astype(F32) + norm_backward(stream, gain_ref[2:3, :], grad_normed)
    branch = grad.astype(BF)
    low = dot_nt(branch, up_ref[...]).astype(BF)
    gup7_ref[...] = dot_tn(z4_ref[...], branch)[:rank]
    gdown4_ref[...] = dot_tn(low, o_ref[...])[:rank]
    total = jnp.zeros((g_ref.shape[0], width + EXT), F32)
    for k in range(members):
        weight, keyval = weights[k][...], keyvals[k][...]
        columns = slice(k * local, (k + 1) * local)
        grad_out = dot(branch, weight[:width, local:]) + dot(low, weight[width:, local:])
        grad_out = grad_out.astype(BF)
        out, query = o_ref[:, columns], q_ref[:, columns]
        product = grad_out.astype(F32) * out.astype(F32)
        queries, keys, values = [], [], []
        for head in range(local // HEAD_DIM):
            at = slice(head * HEAD_DIM, (head + 1) * HEAD_DIM)
            number = k * (local // HEAD_DIM) + head
            key, q, g = keyval[:, at], query[:, at], grad_out[:, at]
            value = keyval[:, local + head * HEAD_DIM : local + (head + 1) * HEAD_DIM]
            delta = jnp.sum(product[:, at], axis=1, keepdims=True)
            probs = jnp.exp(dot_nt(q, key) - lse_ref[:, number : number + 1])
            grad_scores = (probs * (dot_nt(g, value) - delta)).astype(BF)
            queries.append((dot(grad_scores, key) * HEAD_DIM**-0.5).astype(BF))
            keys.append(dot_tn(grad_scores, q))
            values.append(dot_tn(probs.astype(BF), g))
        grad_query = jnp.concatenate(queries, axis=1)
        gkv_refs[k][...] = jnp.concatenate(keys + values, axis=1).astype(BF)
        gup4_ref[:, columns] = dot_tn(u_ref[...], grad_query)[:rank]
        total = total + dot_nt(grad_query, weight[:, :local])
    low = total[:, width:].astype(BF)
    gdown2_ref[...] = dot_tn(low, n2_ref[...])[:rank]
    grad_normed = total[:, :width] + dot(low, down2_ref[...])
    grad = grad + norm_backward(s1_ref[...], gain_ref[1:2, :], grad_normed)
    r1_ref[...] = grad
    r1b_ref[...] = grad.astype(BF)


def cross_back(rank, g, dn, s1, s2, n2, q, o, lse, u, z4, up, down5, down2, gains, biases, weights, keyvals):
    rows, width = g.shape
    members, local = len(weights), weights[0].shape[1] // 2
    return pl.pallas_call(
        functools.partial(cross_back_kernel, members, local),
        out_shape=[sds((rows, width), F32), sds((rows, width), BF)]
        + [sds((rank, width), F32)] * 5
        + [sds(keyvals[0].shape, BF)] * members,
        compiler_params=pltpu.CompilerParams(vmem_limit_bytes=VMEM_LIMIT),
        cost_estimate=cost(8 * rows * width * width, 8 * width * width),
    )(g, dn, s1, s2, n2, q, o, lse, u, z4, up, down5, down2, gains, biases, *weights, *keyvals)


def feed_kernel(first, last, *refs):
    (n_ref, g_ref, down_ref, up_ref, gate_ref, upper_ref, out_ref), refs = refs[:7], refs[7:]
    if not first:
        (y_in, dn_in), refs = refs[:2], refs[2:]
    (y_ref, dn_ref, gdown_ref, ggate_ref, gupper_ref), refs = refs[:5], refs[5:]
    low_ref, glow_ref, y_sum, dn_sum = refs
    step, width = pl.program_id(0), n_ref.shape[1]
    rank = gdown_ref.shape[0]

    @pl.when(step == 0)
    def _():
        low_ref[...] = dot_nt(n_ref[...], down_ref[...]).astype(BF)
        glow_ref[...] = dot_nt(g_ref[...], up_ref[...]).astype(BF)
        if first:
            y_sum[...] = jnp.zeros_like(y_sum)
            dn_sum[...] = jnp.zeros_like(dn_sum)
        else:
            y_sum[...] = y_in[...]
            dn_sum[...] = dn_in[...]

    normed, low = n_ref[...], low_ref[...]
    grad, grad_low = g_ref[...], glow_ref[...]
    gate = dot(normed, gate_ref[:width, :]) + dot(low, gate_ref[width:, :])
    upper = dot(normed, upper_ref[:width, :]) + dot(low, upper_ref[width:, :])
    grad_unit = dot(grad, out_ref[:width, :]) + dot(grad_low, out_ref[width:, :])
    sigmoid = 1.0 / (1.0 + jnp.exp(-gate))
    acted = gate * sigmoid
    unit = (acted * upper).astype(BF)
    grad_gate = (grad_unit * upper * (sigmoid + acted * (1.0 - sigmoid))).astype(BF)
    grad_upper = (grad_unit * acted).astype(BF)
    y_sum[...] += dot_nt(unit, out_ref[...])
    dn_sum[...] += dot_nt(grad_gate, gate_ref[...]) + dot_nt(grad_upper, upper_ref[...])
    gdown_ref[...] = dot_tn(grad_low, unit)[:rank]
    ggate_ref[...] = dot_tn(low, grad_gate)[:rank]
    gupper_ref[...] = dot_tn(low, grad_upper)[:rank]

    @pl.when(step == pl.num_programs(0) - 1)
    def _():
        y_ref[...] = y_sum[...].astype(y_ref.dtype)
        dn_ref[...] = dn_sum[...].astype(dn_ref.dtype)


def feed(normed, grad, down, up, weight, rank, sums, last):
    tokens, width = normed.shape
    part = weight.shape[1] // 3
    block = min(256, part)
    steps = part // block
    deep = weight.shape[0]
    wide = sds((tokens, deep), BF if last else F32)
    narrow = sds((rank, part), F32)
    first = sums is None
    sums = () if first else sums

    def columns(number):
        return pl.BlockSpec((deep, block), lambda j: (0, number * steps + j))

    return pl.pallas_call(
        functools.partial(feed_kernel, first, last),
        grid=(steps,),
        in_specs=[whole_spec(a.shape) for a in (normed, grad, down, up)]
        + [columns(0), columns(1), columns(2)]
        + [whole_spec(a.shape) for a in sums],
        out_specs=[whole_spec(wide.shape)] * 2
        + [pl.BlockSpec((rank, block), lambda j: (0, j))] * 3,
        out_shape=[wide, wide, narrow, narrow, narrow],
        scratch_shapes=[pltpu.VMEM((tokens, EXT), BF)] * 2 + [pltpu.VMEM((tokens, deep), F32)] * 2,
        compiler_params=params(),
        cost_estimate=cost(4 * tokens * weight.size, 2 * weight.size + 16 * tokens * deep),
    )(normed, grad, down, up, weight, weight, weight, *sums)


def settle_kernel(fold, labels_ref, first_ref, second_ref, down_ref, up_ref, hid_ref, gate_ref):
    slot = pl.program_id(0)
    local = down_ref.shape[-1]
    for ref in (down_ref, up_ref, hid_ref, gate_ref):
        ref[...] = jnp.zeros_like(ref)
    for s in range(first_ref.shape[0]):

        @pl.when(labels_ref[s] == slot)
        def _(s=s):
            down_ref[0, 0:2] += second_ref[s, 0:2].astype(F32)
            down_ref[0, 2:6] += first_ref[s, 0:4].astype(F32)
            up_ref[0, 0:4] += second_ref[s, 2:6].astype(F32)
            up_ref[0, 4:9] += first_ref[s, 4:9].astype(F32)
            for k in range(fold):
                at = slice(k * local, (k + 1) * local)
                hid_ref[0, :, at] += first_ref[s, 9 + k].astype(F32)
                gate_ref[0, 0, :, at] += first_ref[s, 9 + fold + k].astype(F32)
                gate_ref[0, 1, :, at] += first_ref[s, 9 + 2 * fold + k].astype(F32)


def settle(labels, first, second, slots, fold):
    rank, local = first.shape[2:]
    hidden = fold * local
    shapes = [
        (slots, 6, rank, local),
        (slots, 9, rank, local),
        (slots, rank, hidden),
        (slots, 2, rank, hidden),
    ]
    return pl.pallas_call(
        functools.partial(settle_kernel, fold),
        grid_spec=pltpu.PrefetchScalarGridSpec(
            num_scalar_prefetch=1,
            grid=(slots,),
            in_specs=[whole_spec(first.shape), whole_spec(second.shape)],
            out_specs=[
                pl.BlockSpec((1,) + s[1:], lambda i, *_, n=len(s): (i,) + (0,) * (n - 1))
                for s in shapes
            ],
        ),
        out_shape=[sds(s, F32) for s in shapes],
        compiler_params=params(),
    )(labels, first, second)


def body(
    inputs,
    context,
    positions,
    adapter_index,
    self_in_weight,
    self_out_weight,
    cross_query_weight,
    cross_keyval_weight,
    cross_out_weight,
    feed_in_weight,
    feed_out_weight,
    norm_gains,
    norm_biases,
    adapter_down,
    adapter_down_hidden,
    adapter_up,
    adapter_up_hidden,
    out_cotangent,
    *,
    pairs,
    chips,
):
    group = Group(pairs, chips)
    members = 2 * pairs
    rows, width = inputs.shape[1], inputs.shape[2]
    local = self_in_weight.shape[2]
    hidden = feed_in_weight.shape[2]
    slots, rank = adapter_down.shape[0], adapter_down.shape[3]
    part = hidden // CHUNKS
    fold = hidden // local
    pieces = group.pieces
    gains, biases = norm_gains, norm_biases

    shards = [
        [self_in_weight[:, i] for i in range(3)],
        [
            self_out_weight.T,
            cross_query_weight,
            cross_out_weight.T,
            cross_keyval_weight[:, 0],
            cross_keyval_weight[:, 1],
        ],
    ]
    for i in range(CHUNKS):
        at = slice(i * part, (i + 1) * part)
        shards.append(
            [feed_in_weight[:, 0, at], feed_in_weight[:, 1, at], feed_out_weight.T[:, at]]
        )
    shards = [group.pair_shard(jnp.concatenate(s, axis=1)) for s in shards]

    index = jnp.where(group.home, adapter_index, core_swap(adapter_index))[0]
    positions = jnp.where(group.home, positions, core_swap(positions))[0]
    context_own = home_swap(context[0])
    ready = [group.cross_shard(shards[0])]
    stream_own = home_swap(after(inputs[0], ready[0]))
    ready.append(group.cross_shard(after(shards[1], stream_own)))
    cotangent_own = home_swap(after(out_cotangent[0], ready[1]))
    last = cotangent_own
    for shard in shards[2:]:
        ready.append(group.cross_shard(after(shard, last)))
        last = ready[-1]

    stream = group.gather(stream_own)
    context_blocks = group.gather(context_own)

    down = lax.dynamic_index_in_dim(adapter_down.transpose(0, 1, 3, 2), index, 0, keepdims=False)
    down_hidden = lax.dynamic_index_in_dim(
        adapter_down_hidden.transpose(0, 2, 1), index, 0, keepdims=False
    )
    up = lax.dynamic_index_in_dim(adapter_up.transpose(0, 2, 1, 3), index, 0, keepdims=False)
    up_hidden = lax.dynamic_index_in_dim(
        adapter_up_hidden.transpose(0, 2, 1, 3), index, 0, keepdims=False
    )

    def piece(array, k, size):
        return lax.dynamic_slice_in_dim(array, pieces[k] * size, size, array.ndim - 1)

    def own(array):
        return piece(array, 0, local)

    def tall(array):
        return jnp.pad(array, ((0, EXT - rank), (0, 0)))

    down_tall = [tall(down[i]) for i in range(6)]
    up_tall = {i: tall(up[i]) for i in (3, 7, 8)}
    feed_down = piece(down_hidden, 0, hidden)
    feed_up = piece(up_hidden, 0, hidden)
    lows = [
        [own(up[i]) for i in range(3)],
        [own(down[1]), own(up[4]), own(down[4]), own(up[5]), own(up[6])],
    ]
    for i in range(CHUNKS):
        at = slice(i * part, (i + 1) * part)
        lows.append([feed_up[0, :, at], feed_up[1, :, at], feed_down[:, at]])

    whole, last = [], None
    for shard, low in zip(ready, lows):
        blocks = group.spread_chips(shard if last is None else after(shard, last))
        last = blocks[1]
        whole.append(group.assemble(blocks, jnp.concatenate(low, axis=1)))
    self_in, rest, *feeds = whole
    self_out = rest[:, :local]
    cross_keyval = rest[:, 3 * local :]

    blocks_at = [
        lax.dynamic_slice_in_dim(positions, pieces[k] * rows, rows, 0) for k in range(members)
    ]
    half = ROT // 2
    lanes = jnp.arange(2 * HEAD_DIM)
    inverse = 10000.0 ** (-(lanes % half).astype(F32) / half)
    inverse = jnp.where(lanes % HEAD_DIM < ROT, inverse, 0.0)
    angles = jnp.concatenate(blocks_at).astype(F32)[:, None] * inverse
    sines = jnp.sin(angles)
    leading = lanes % HEAD_DIM < half
    tables = (
        jnp.cos(angles),
        jnp.where(leading, -sines, 0.0),
        jnp.where(leading, 0.0, sines),
    )

    tile = min(256, members * rows)
    stream_all = jnp.concatenate(stream, axis=0)
    query, keys, values, low_one = project_self(
        stream_all, gains[0:1], biases[0:1], down_tall[0], self_in, tables, tile
    )
    branch, heads, logsum = attend_self(query, keys, values, self_out, tile)

    def split_rows(x):
        return [x[k * rows : (k + 1) * rows] for k in range(members)]

    branch = group.scatter(split_rows(branch))

    cross_blocks = group.gather(rest[:, local : 3 * local])
    context_count = context_blocks[0].shape[0]
    context_all = jnp.zeros((members,) + context_blocks[0].shape, BF)
    for k in range(members):
        context_all = lax.dynamic_update_slice(
            context_all, context_blocks[k][None], (pieces[k], 0, 0)
        )
    context_all = context_all.transpose(1, 0, 2).reshape(context_count, width)
    low_context = dot_nt(context_all, down_tall[3]).astype(BF)
    keyval = dot(context_all, cross_keyval[:width]) + dot(low_context, cross_keyval[width:])
    keyval_blocks = group.gather(keyval.astype(BF))
    (
        stream_one, stream_two, normed_two, normed_three, query_cross, heads_cross, logsum_cross,
        low_two, low_three, low_four,
    ) = cross_forward(
        stream_own, branch, up_tall[3], up_tall[7], down_tall[2], gains, biases,
        cross_blocks, keyval_blocks,
    )

    def by_chip(blocks):
        return [
            jnp.concatenate(blocks[2 * k : 2 * k + 2], axis=0) for k in range(pairs)
        ]

    normed_parts = by_chip(group.gather(normed_three))
    cotangent_parts = by_chip(group.gather(cotangent_own))
    sums = [None] * pairs
    feed_grads = []
    for i, weight in enumerate(feeds):
        order = range(pairs)
        if i == CHUNKS - 1:
            order = reversed(order)
        found = []
        for k in order:
            y, dn, *grads = feed(
                normed_parts[k], cotangent_parts[k], down_tall[5], up_tall[8], weight, rank,
                sums[k], i == CHUNKS - 1,
            )
            sums[k] = (y, dn)
            found.append(grads)
        feed_grads.append([sum(g[1:], g[0]) for g in zip(*found)])

    def scatter_parts(parts):
        return group.scatter([p[at] for p in parts for at in (slice(0, rows), slice(rows, None))])

    grad_normed = scatter_parts([s[1] for s in sums])
    feed_sum = scatter_parts([s[0] for s in sums])
    low_six = feed_sum[:, width:].astype(BF)
    branch = feed_sum[:, :width] + dot(low_six, up_tall[8])
    block_output = home_swap((stream_two + branch).astype(BF))
    grad_up_eight = dot_tn(low_six, cotangent_own)[:rank]

    (
        grad_stream, branch_grad, grad_up_seven, grad_down_four, grad_up_four, grad_down_two,
        grad_down_five, *grad_keyval,
    ) = cross_back(
        rank, cotangent_own, grad_normed, stream_one, stream_two, normed_two, query_cross,
        heads_cross, logsum_cross, low_three, low_four, up_tall[7], down_tall[5], down_tall[2],
        gains, biases, cross_blocks, keyval_blocks,
    )

    branch_grads = group.gather(branch_grad)
    grad_up_three = dot_tn(low_two, branch_grad)[:rank]
    grad_mixed, grad_down_one, grad_up_self = attend_back(
        jnp.concatenate(branch_grads, axis=0), up_tall[3], self_out, query, keys, values, heads,
        logsum, tables, low_one, rank, tile,
    )
    grad_normed = scatter_parts(
        [
            dot_nt(grad_mixed[2 * k * rows : 2 * (k + 1) * rows], self_in).astype(BF)
            for k in range(pairs)
        ]
    )
    stream_zero = stream_own.astype(F32)
    grad_low = grad_normed[:, width:].astype(BF)
    grad_down_zero = dot_tn(grad_low, layer_norm(stream_zero, gains[0], biases[0]))[:rank]
    grad_normed = grad_normed[:, :width] + dot(grad_low, down_tall[0])
    grad_inputs = grad_stream + norm_backward(stream_zero, gains[0], grad_normed)
    grad_inputs = home_swap(grad_inputs.astype(BF)).astype(F32)

    grad_keyval = group.scatter(grad_keyval).astype(BF)
    total = dot_nt(grad_keyval, cross_keyval)
    grad_low = total[:, width:].astype(BF)
    grad_up_keyval = dot_tn(low_context, grad_keyval)[:rank]
    grad_down_three = dot_tn(grad_low, context_all)[:rank]
    context_partial = total[:, :width] + dot(grad_low, down_tall[3])
    grad_context = home_swap(
        group.scatter([piece(context_partial, k, local) for k in range(members)]).astype(BF)
    ).astype(F32)

    def gathered(partial, relative):
        return group.scatter(
            [
                jnp.concatenate(
                    [piece(g, k, local) for g in partial]
                    + [g[:, k * local : (k + 1) * local] for g in relative],
                    axis=0,
                )
                for k in range(members)
            ]
        ).reshape(-1, rank, local)

    def columns(array):
        return array.reshape(rank, -1, local).transpose(1, 0, 2)

    def every(parts):
        parts.append(jnp.full((1, rank, local), index, F32))
        grads = jnp.concatenate(parts, axis=0).astype(BF)
        both = jnp.stack([grads, xor_move(grads, "zhi", 2, 1)])
        both = jnp.where(group.home, both, core_swap(both))
        return jnp.concatenate(group.spread_chips(both), axis=0)

    summed = gathered(
        [grad_down_two, grad_down_three, grad_down_five, grad_up_seven, grad_up_eight],
        [grad_down_four, grad_up_four],
    )
    first = every(
        [
            summed[0:2],
            summed[5:6],
            summed[2:3],
            summed[6:7],
            columns(grad_up_keyval),
            summed[3:5],
            *[columns(jnp.concatenate(g, axis=1)) for g in zip(*feed_grads)],
        ]
    )
    summed = gathered([grad_down_zero, grad_up_three], [])
    second = every([summed[0:1], grad_down_one[None], columns(grad_up_self), summed[1:2]])
    grad_down, grad_up, grad_hidden, grad_gate = settle(
        first[:, -1, 0, 0].astype(jnp.int32), first, second, slots, fold
    )
    return (
        block_output[None],
        grad_inputs[None],
        grad_context[None],
        grad_down.transpose(0, 1, 3, 2),
        grad_hidden.transpose(0, 2, 1),
        grad_up.transpose(0, 2, 1, 3),
        grad_gate.transpose(0, 2, 1, 3),
    )


def solution(mesh):
    members = mesh.shape["tensor"]
    chips = mesh.shape["dp"] // 2
    mesh = Mesh(
        mesh.devices.reshape(chips, 2, 2, members // 2), ("chip", "core", "zhi", "p")
    )
    dp, tensor = ("chip", "core"), ("zhi", "p")
    in_specs = (
        P(dp, tensor, None),
        P(dp, None, tensor),
        P(dp, None),
        P(dp),
        P(dp, None, tensor),
        P(tensor, dp),
        P(dp, tensor),
        P(dp, None, tensor),
        P(tensor, dp),
        P(dp, None, tensor),
        P(tensor, dp),
        P(),
        P(),
        P(),
        P(),
        P(),
        P(),
        P(dp, tensor, None),
    )
    out_specs = (
        P(dp, tensor, None),
        P(dp, tensor, None),
        P(dp, None, tensor),
        P(None, None, tensor, None),
        P(None, tensor, None),
        P(None, None, None, tensor),
        P(None, None, None, tensor),
    )

    def run(*args):
        return body(*args, pairs=members // 2, chips=chips)

    return jax.shard_map(run, mesh=mesh, in_specs=in_specs, out_specs=out_specs, check_vma=False)
```

```python
import functools

import jax
import jax.numpy as jnp
from jax import lax
from jax.experimental import pallas as pl
from jax.experimental.pallas import tpu as pltpu
from jax.sharding import Mesh, PartitionSpec as P

HEAD_DIM = 64
ROT = 32
EPSILON = 1e-05
F32 = jnp.float32
BF = jnp.bfloat16
SWAP = ((0, 1), (1, 0))
LANES = 128
VMEM_LIMIT = 56 * 1024 * 1024


def dot(left, right):
    return jnp.dot(left, right, preferred_element_type=F32)


def dot_nt(left, right):
    return lax.dot_general(left, right, (((1,), (1,)), ((), ())), preferred_element_type=F32)


def dot_tn(left, right):
    return lax.dot_general(left, right, (((0,), (0,)), ((), ())), preferred_element_type=F32)


class Order:
    def __init__(self, first):
        self.token = first

    def wait(self, *values):
        *values, self.token = lax.optimization_barrier((*values, self.token))
        return values[0] if len(values) == 1 else values

    mark = wait


def core_swap(x):
    return lax.ppermute(x, "core", SWAP)


def xor_move(x, axis, size, k):
    return lax.ppermute(x, axis, [(i, i ^ k) for i in range(size)])


def home_swap(x):
    return lax.ppermute(x, ("core", "zhi"), [(0, 0), (1, 2), (2, 1), (3, 3)])


def turned(x):
    return lax.ppermute(x, ("core", "zhi"), [(0, 1), (1, 3), (2, 0), (3, 2)])


def turned_back(x):
    return lax.ppermute(x, ("core", "zhi"), [(0, 2), (1, 0), (2, 3), (3, 1)])


class Group:
    def __init__(self, pairs, chips):
        self.pairs, self.chips = pairs, chips
        self.core, self.zhi, self.p = (lax.axis_index(n) for n in ("core", "zhi", "p"))
        self.chip = lax.axis_index("chip")
        self.home = self.core == self.zhi
        self.pieces = [
            (self.core ^ kc) * pairs + (self.p ^ kp) for kp in range(pairs) for kc in (0, 1)
        ]

    def far_p(self, own):
        return [xor_move(own, "p", self.pairs, k) for k in range(1, self.pairs)]

    def near_sums(self, own, other):
        return own.astype(F32) + other.astype(F32)

    def cross(self, shard):
        return xor_move(shard, "zhi", 2, 1)

    def spread_one(self, block):
        if self.chips == 4:
            return [xor_move(block, "chip", 4, k) for k in (1, 2)]
        return [xor_move(block, "chip", self.chips, k) for k in range(1, self.chips)]

    def spread_two(self, got):
        if self.chips != 4:
            return []
        half = got[0].shape[0] // 2
        return [xor_move(got[1][:half], "chip", 4, 1), xor_move(got[0][half:], "chip", 4, 2)]

    def places(self, rows):
        if self.chips == 4:
            diagonal = (self.chip ^ 3) * rows
            return [(self.chip ^ 1) * rows, (self.chip ^ 2) * rows, diagonal, diagonal + rows // 2]
        return [(self.chip ^ k) * rows for k in range(1, self.chips)]


def place_kernel(count, moves, olds, places_ref, *refs):
    sources, refs = refs[:count], refs[count + olds :]
    *targets, sems = refs
    copies = []
    for number, (source, row, rows, target, lead, place, offset) in enumerate(moves):
        at = pl.ds(pl.multiple_of(places_ref[place] + offset, 16), rows)
        to = targets[target].at[at] if lead is None else targets[target].at[lead, at]
        copy = pltpu.make_async_copy(
            sources[source].at[pl.ds(row, rows)], to, sems.at[number]
        )
        copy.start()
        copies.append(copy)
    for copy in copies:
        copy.wait()


def place(sources, moves, places, targets, fresh):
    shapes = [sds(t, BF) if fresh else sds(t.shape, BF) for t in targets]
    olds = () if fresh else tuple(targets)
    any_spec = pl.BlockSpec(memory_space=pl.ANY)
    return pl.pallas_call(
        functools.partial(place_kernel, len(sources), moves, len(olds)),
        grid_spec=pltpu.PrefetchScalarGridSpec(
            num_scalar_prefetch=1,
            grid=(1,),
            in_specs=[whole_spec(a.shape) for a in sources] + [any_spec] * len(olds),
            out_specs=[any_spec] * len(shapes),
            scratch_shapes=[pltpu.SemaphoreType.DMA((len(moves),))],
        ),
        out_shape=shapes,
        input_output_aliases={1 + len(sources) + i: i for i in range(len(olds))},
        compiler_params=params(),
        cost_estimate=cost(0, 0),
    )(places, *sources, *olds)


def stats(stream):
    average = jnp.mean(stream, axis=-1, keepdims=True)
    centred = stream - average
    variance = jnp.mean(centred * centred, axis=-1, keepdims=True)
    scale = lax.rsqrt(variance + EPSILON)
    return centred * scale, scale


def layer_norm(stream, gain, bias):
    return (stats(stream)[0] * gain + bias).astype(BF)


def norm_backward(stream, gain, grad):
    unit, scale = stats(stream)
    grad = grad * gain
    return scale * (
        grad
        - jnp.mean(grad, axis=-1, keepdims=True)
        - unit * jnp.mean(grad * unit, axis=-1, keepdims=True)
    )


def turn(x, cosines, left_sines, right_sines):
    breadth = 2 * HEAD_DIM if x.shape[1] % (2 * HEAD_DIM) == 0 else HEAD_DIM
    half = ROT // 2
    for at in range(0, x.shape[1], breadth):
        group = x[:, at : at + breadth]
        if breadth % 128 == 0:
            left, right = pltpu.roll(group, breadth - half, 1), pltpu.roll(group, half, 1)
        else:
            left = jnp.concatenate([group[:, half:], group[:, :half]], axis=1)
            right = jnp.concatenate([group[:, -half:], group[:, :-half]], axis=1)
        yield (
            at,
            breadth,
            group * cosines[:, :breadth]
            + left * left_sines[:, :breadth]
            + right * right_sines[:, :breadth],
        )


def whole_spec(shape):
    return pl.BlockSpec(shape, lambda *_: (0,) * len(shape))


def row_spec(rows, columns):
    return pl.BlockSpec((rows, columns), lambda t: (t, 0))


def take_tile(refs, tile_ref, step):
    rows, tile = refs[0].shape[0], tile_ref.shape[0]
    for i, ref in enumerate(refs):

        @pl.when(step == i * rows // tile)
        def _(i=i, ref=ref):
            tile_ref[i * rows % tile : i * rows % tile + rows, :] = ref[...]


def give_tile(value, refs, step):
    rows, (tile, columns) = refs[0].shape[0], value.shape
    for i, ref in enumerate(refs):

        @pl.when(step == i * rows // tile)
        def _(i=i, ref=ref):
            ref[:, :columns] = value[i * rows % tile : i * rows % tile + rows]
            ref[:, columns:] = jnp.zeros((rows, ref.shape[1] - columns), ref.dtype)


def total_of(refs):
    total = refs[0][...].astype(F32)
    for ref in refs[1:]:
        total = total + ref[...].astype(F32)
    return total


def by_piece(ref, row, value):
    local = ref.shape[2]
    for k in range(ref.shape[0]):
        ref[k, row : row + value.shape[0], :] = value[:, k * local : (k + 1) * local].astype(
            ref.dtype
        )


def columns_of(weight, start, size):
    if size % 128 == 0:
        return pl.BlockSpec((weight.shape[0], size), lambda *_: (0, start // size)), 0
    return whole_spec(weight.shape), start


def params(semantics=1):
    return pltpu.CompilerParams(
        dimension_semantics=("arbitrary",) * semantics, vmem_limit_bytes=VMEM_LIMIT
    )


def cost(flops, moved, exps=0):
    return pl.CostEstimate(flops=int(flops), bytes_accessed=int(moved), transcendentals=int(exps))


def sds(shape, dtype):
    return jax.ShapeDtypeStruct(shape, dtype)


def query_kernel(count, *refs):
    blocks, (gain_ref, bias_ref, down_ref, w_ref, cos_ref, left_ref, right_ref), refs = (
        refs[:count],
        refs[count : count + 7],
        refs[count + 7 :],
    )
    q_ref, k_ref, v_ref, low_ref, n_ref, x_ref = refs
    take_tile(blocks, x_ref, pl.program_id(0))
    local, width = q_ref.shape[1], x_ref.shape[1]
    normed = layer_norm(x_ref[...].astype(F32), gain_ref[...], bias_ref[...])
    n_ref[...] = normed
    low = dot_nt(normed, down_ref[...]).astype(BF)
    low_ref[...] = low
    mixed = dot(normed, w_ref[:width, : 3 * local]) + dot(low, w_ref[width:, : 3 * local])
    tables = cos_ref[...], left_ref[...], right_ref[...]
    for at, breadth, turned in turn(mixed[:, :local], *tables):
        q_ref[:, at : at + breadth] = (turned * HEAD_DIM**-0.5).astype(BF)
    for at, breadth, turned in turn(mixed[:, local : 2 * local], *tables):
        k_ref[:, at : at + breadth] = turned.astype(BF)
    v_ref[...] = mixed[:, 2 * local :].astype(BF)


def project_self(blocks, gain, bias, down, weight, tables, rows):
    width = blocks[0].shape[1]
    tokens = len(blocks) * blocks[0].shape[0]
    local = weight.shape[1] // 4
    spec, _ = columns_of(weight, 0, 3 * local)
    return pl.pallas_call(
        functools.partial(query_kernel, len(blocks)),
        grid=(tokens // rows,),
        in_specs=[whole_spec(b.shape) for b in blocks]
        + [whole_spec(gain.shape), whole_spec(bias.shape), whole_spec(down.shape), spec]
        + [row_spec(rows, t.shape[1]) for t in tables],
        out_specs=[row_spec(rows, local)] * 3
        + [row_spec(rows, down.shape[0]), row_spec(rows, width)],
        out_shape=[sds((tokens, local), BF)] * 3
        + [sds((tokens, down.shape[0]), BF), sds((tokens, width), BF)],
        scratch_shapes=[pltpu.VMEM((rows, width), BF)],
        compiler_params=params(),
        cost_estimate=cost(2 * tokens * weight.size, 2 * weight.size),
    )(*blocks, gain, bias, down, weight, *tables)


def attend_kernel(start, q_ref, k_ref, v_ref, w_ref, o_ref, lse_ref, *y_refs):
    rows, local = q_ref.shape
    lanes = lax.broadcasted_iota(jnp.int32, (rows, 128), 1)
    logsums = jnp.zeros((rows, 128), F32)
    for head in range(local // HEAD_DIM):
        at = slice(head * HEAD_DIM, (head + 1) * HEAD_DIM)
        scores = dot_nt(q_ref[:, at], k_ref[:, at])
        top = jnp.max(scores, axis=1, keepdims=True)
        powers = jnp.exp(scores - top)
        total = jnp.sum(powers, axis=1, keepdims=True)
        out = dot(powers.astype(BF), v_ref[:, at]) / total
        o_ref[:, at] = out.astype(BF)
        logsums = jnp.where(lanes == head, top + jnp.log(total), logsums)
    lse_ref[...] = logsums.T[: lse_ref.shape[0]]
    y = dot_nt(o_ref[...], w_ref[:, start : start + local]).astype(BF)
    give_tile(y, y_refs, pl.program_id(0))


def attend_self(query, keys, values, weight, rows, first, count, block):
    tokens, local = query.shape
    deep = weight.shape[0] // LANES * LANES + LANES
    heads = -(-local // HEAD_DIM // 8) * 8
    spec, start = columns_of(weight, 3 * local, local)
    return pl.pallas_call(
        functools.partial(attend_kernel, start),
        grid=(count,),
        in_specs=[
            pl.BlockSpec((rows, local), lambda t: (first + t, 0)),
            whole_spec(keys.shape),
            whole_spec(values.shape),
            spec,
        ],
        out_specs=[row_spec(rows, local), pl.BlockSpec((heads, rows), lambda t: (0, t))]
        + [whole_spec((block, deep))] * (count * rows // block),
        out_shape=[sds((count * rows, local), BF), sds((heads, count * rows), F32)]
        + [sds((block, deep), BF)] * (count * rows // block),
        compiler_params=params(),
        cost_estimate=cost(
            16 * count * rows * tokens * local, 4 * weight.size, count * rows * tokens
        ),
    )(query, keys, values, weight)


def project_back_kernel(local, m_ref, w_ref, low_ref, *refs):
    width = w_ref.shape[0] - low_ref.shape[1]
    value = dot_nt(m_ref[...], w_ref[:, : 3 * local]).astype(BF)
    low_ref[...] = value[:, width:]
    give_tile(value, refs, pl.program_id(0))


def project_back(mixed, weight, rows, first, count, block, rank):
    local, deep = weight.shape[1] // 4, weight.shape[0] // LANES * LANES + LANES
    spec, _ = columns_of(weight, 0, 3 * local)
    blocks = count * rows // block
    return pl.pallas_call(
        functools.partial(project_back_kernel, local),
        grid=(count,),
        in_specs=[pl.BlockSpec((rows, 3 * local), lambda t: (first + t, 0)), spec],
        out_specs=[row_spec(rows, rank)] + [whole_spec((block, deep))] * blocks,
        out_shape=[sds((count * rows, rank), BF)] + [sds((block, deep), BF)] * blocks,
        compiler_params=params(),
        cost_estimate=cost(40 * count * rows * deep * local, 2 * weight.size),
    )(mixed, weight)


def attend_back_kernel(
    first, last, tiles, column, number, *refs,
):
    grads, refs = refs[:number], refs[number:]
    (
        up_ref, w_ref, q_ref, k_ref, v_ref, o_ref, lse_ref, cos_ref, left_ref, right_ref, low_ref,
    ), refs = refs[:11], refs[11:]
    *refs, g_ref = refs
    take_tile(grads, g_ref, pl.program_id(0))
    if not first:
        (mq_ref, gk_in, gv_in, down_in), refs = refs[:4], refs[4:]
    if last:
        m_ref, down_ref, gup_ref, gk_ref, gv_ref = refs
    else:
        m_ref, gk_ref, gv_ref, down_ref = refs
    step, rows = pl.program_id(0), q_ref.shape[0]
    width, local = g_ref.shape[1], q_ref.shape[1]
    at_rows = pl.ds(pl.multiple_of((step + tiles) * rows, rows), rows)
    at_query = at_rows if last else pl.ds(pl.multiple_of(step * rows, rows), rows)

    @pl.when(step == 0)
    def _():
        if first:
            gk_ref[...] = jnp.zeros_like(gk_ref)
            gv_ref[...] = jnp.zeros_like(gv_ref)
            down_ref[...] = jnp.zeros_like(down_ref)
        else:
            gk_ref[...] = gk_in[...]
            gv_ref[...] = gv_in[...]
            down_ref[...] = down_in[...]
            m_ref[: mq_ref.shape[0], :local] = mq_ref[...]

    grad = g_ref[...]
    grad_low = dot_nt(grad, up_ref[...]).astype(BF)
    weight = w_ref[:, column : column + local]
    grad_out = dot(grad, weight[:width]) + dot(grad_low, weight[width:])
    grad_out = grad_out.astype(BF)
    out = o_ref[...]
    down_ref[...] += dot_tn(grad_low, out)
    product = grad_out.astype(F32) * out.astype(F32)
    ones = jnp.ones((8, HEAD_DIM), F32)
    parts = []
    for head in range(local // HEAD_DIM):
        at = slice(head * HEAD_DIM, (head + 1) * HEAD_DIM)
        q, k, v, g = q_ref[:, at], k_ref[:, at], v_ref[:, at], grad_out[:, at]
        delta = lax.dot_general(
            ones, product[:, at], (((1,), (1,)), ((), ())),
            precision=lax.Precision.HIGHEST, preferred_element_type=F32,
        )[:1]
        probs = jnp.exp(dot_nt(k, q) - lse_ref[head : head + 1, :])
        grad_scores = (probs * (dot_nt(v, g) - delta)).astype(BF)
        gv_ref[:, at] += dot(probs.astype(BF), g)
        gk_ref[:, at] += dot(grad_scores, q)
        parts.append(dot_tn(grad_scores, k) * HEAD_DIM**-0.5)
    tables = cos_ref[at_rows, :], -left_ref[at_rows, :], -right_ref[at_rows, :]
    for at, breadth, turned in turn(jnp.concatenate(parts, axis=1), *tables):
        m_ref[at_query, at : at + breadth] = turned.astype(BF)

    if last:

        @pl.when(step == pl.num_programs(0) - 1)
        def _():
            tables = cos_ref[...], -left_ref[...], -right_ref[...]
            for at, breadth, turned in turn(gk_ref[...], *tables):
                m_ref[:, local + at : local + at + breadth] = turned.astype(BF)
            m_ref[:, 2 * local :] = gv_ref[...].astype(BF)
            gup_ref[...] = dot_tn(low_ref[...], m_ref[...])


def attend_back(grads, up, weight, query, keys, values, out, lse, tables, low, rank, rows, start, before):
    tokens, local = query.shape
    block, width = grads[0].shape
    count = len(grads) * block // rows
    first, last = before is None, (start + count) * rows == tokens
    before = () if first else before
    sums = [sds((tokens, local), F32)] * 2 + [sds((rank, local), F32)]
    if last:
        shapes = [sds((tokens, 3 * local), BF), sums[2], sds((rank, 3 * local), F32)]
        scratch = [pltpu.VMEM((tokens, local), F32)] * 2
    else:
        shapes, scratch = [sds((count * rows, local), BF), *sums], []
    scratch.append(pltpu.VMEM((rows, width), BF))

    def tile(columns):
        return pl.BlockSpec((rows, columns), lambda t: (start + t, 0))

    spec, column = columns_of(weight, 3 * local, local)
    return pl.pallas_call(
        functools.partial(attend_back_kernel, first, last, start, column, len(grads)),
        grid=(count,),
        in_specs=[
            *[whole_spec(g.shape) for g in grads],
            whole_spec(up.shape),
            spec,
            tile(local),
            whole_spec(keys.shape),
            whole_spec(values.shape),
            row_spec(rows, local),
            pl.BlockSpec((lse.shape[0], rows), lambda t: (0, t)),
            *[whole_spec(t.shape) for t in tables],
            whole_spec(low.shape),
            *[whole_spec(b.shape) for b in before],
        ],
        out_specs=[whole_spec(s.shape) for s in shapes],
        out_shape=shapes,
        scratch_shapes=scratch,
        compiler_params=params(),
        cost_estimate=cost(
            40 * count * rows * tokens * local, 10 * query.size, count * rows * tokens
        ),
    )(*grads, up, weight, query, keys, values, out, lse, *tables, low, *before)


def cross_kernel(members, local, *refs):
    (x_ref, up_self_ref, up_cross_ref, down_ref, gain_ref, bias_ref, w_ref), refs = (
        refs[:7],
        refs[7:],
    )
    kv_refs, refs = refs[:members], refs[members:]
    y_refs, refs = refs[:-10], refs[-10:]
    branch = total_of(y_refs)
    s1_ref, s2_ref, n2_ref, n3_ref, q_ref, o_ref, lse_ref, z2_ref, u_ref, z4_ref = refs
    rows, width = x_ref.shape
    rank = down_ref.shape[0]
    deep = slice(width, width + rank)
    low = branch[:, deep].astype(BF)
    z2_ref[...] = low
    stream = x_ref[...].astype(F32) + branch[:, :width] + dot(low, up_self_ref[...])
    s1_ref[...] = stream
    normed = layer_norm(stream, gain_ref[1:2, :], bias_ref[1:2, :])
    n2_ref[...] = normed
    low = dot_nt(normed, down_ref[...]).astype(BF)
    u_ref[...] = low
    lanes = lax.broadcasted_iota(jnp.int32, (rows, 128), 1)
    logsums = jnp.zeros((rows, 128), F32)
    total = jnp.zeros((rows, width + rank), F32)
    for k in range(members):
        weight, keyval = w_ref[k], kv_refs[k][...]
        query = dot(normed, weight[:width, :local]) + dot(low, weight[deep, :local])
        query = (query * HEAD_DIM**-0.5).astype(BF)
        q_ref[:, k * local : (k + 1) * local] = query
        parts = []
        for head in range(local // HEAD_DIM):
            at = slice(head * HEAD_DIM, (head + 1) * HEAD_DIM)
            scores = dot_nt(query[:, at], keyval[:, at])
            top = jnp.max(scores, axis=1, keepdims=True)
            powers = jnp.exp(scores - top)
            sums = jnp.sum(powers, axis=1, keepdims=True)
            values = keyval[:, local + head * HEAD_DIM : local + (head + 1) * HEAD_DIM]
            parts.append((dot(powers.astype(BF), values) / sums).astype(BF))
            number = k * (local // HEAD_DIM) + head
            logsums = jnp.where(lanes == number, top + jnp.log(sums), logsums)
        out = jnp.concatenate(parts, axis=1)
        o_ref[:, k * local : (k + 1) * local] = out
        total = total + dot_nt(out, weight[:, local:])
    lse_ref[...] = logsums
    low = total[:, deep].astype(BF)
    z4_ref[...] = low
    stream = stream + total[:, :width] + dot(low, up_cross_ref[...])
    s2_ref[...] = stream
    n3_ref[...] = layer_norm(stream, gain_ref[2:3, :], bias_ref[2:3, :])


def cross_forward(x, ys, up_self, up_cross, down, gains, biases, weight, keyvals):
    rows, width = x.shape
    members, local = len(keyvals), weight.shape[2] // 2
    plain, wide = sds((rows, width), BF), sds((rows, width), F32)
    low = sds((rows, down.shape[0]), BF)
    return pl.pallas_call(
        functools.partial(cross_kernel, members, local),
        out_shape=[wide, wide, plain, plain, plain, plain, sds((rows, 128), F32), low, low, low],
        compiler_params=pltpu.CompilerParams(vmem_limit_bytes=VMEM_LIMIT),
        cost_estimate=cost(24 * rows * width * width, 8 * width * width),
    )(x, up_self, up_cross, down, gains, biases, weight, *keyvals, *ys)


def cross_back_kernel(members, local, *refs):
    (
        g_ref, s1_ref, s2_ref, n2_ref, q_ref, o_ref, lse_ref, u_ref, z4_ref,
        up_ref, down5_ref, down2_ref, gain_ref, bias_ref, w_ref,
    ), refs = refs[:15], refs[15:]
    kv_refs, refs = refs[:members], refs[members:]
    dn_refs, (r1_ref, r1b_ref, fixed_ref, near_ref, *gkv_refs) = (
        refs[: -4 - members],
        refs[-4 - members :],
    )
    summed = total_of(dn_refs)
    width = g_ref.shape[1]
    rank = up_ref.shape[0]
    deep = slice(width, width + rank)
    stream = s2_ref[...]
    low = summed[:, deep].astype(BF)
    grad_normed = summed[:, :width] + dot(low, down5_ref[...])
    normed = layer_norm(stream, gain_ref[2:3, :], bias_ref[2:3, :])
    by_piece(fixed_ref, rank, dot_tn(low, normed))
    grad = g_ref[...].astype(F32) + norm_backward(stream, gain_ref[2:3, :], grad_normed)
    branch = grad.astype(BF)
    low = dot_nt(branch, up_ref[...]).astype(BF)
    by_piece(fixed_ref, 2 * rank, dot_tn(z4_ref[...], branch))
    by_piece(near_ref, 0, dot_tn(low, o_ref[...]))
    total = jnp.zeros((g_ref.shape[0], width + rank), F32)
    for k in range(members):
        weight, keyval = w_ref[k], kv_refs[k][...]
        columns = slice(k * local, (k + 1) * local)
        grad_out = dot(branch, weight[:width, local:]) + dot(low, weight[deep, local:])
        grad_out = grad_out.astype(BF)
        out, query = o_ref[:, columns], q_ref[:, columns]
        product = grad_out.astype(F32) * out.astype(F32)
        queries, keys, values = [], [], []
        for head in range(local // HEAD_DIM):
            at = slice(head * HEAD_DIM, (head + 1) * HEAD_DIM)
            number = k * (local // HEAD_DIM) + head
            key, q, g = keyval[:, at], query[:, at], grad_out[:, at]
            value = keyval[:, local + head * HEAD_DIM : local + (head + 1) * HEAD_DIM]
            delta = jnp.sum(product[:, at], axis=1, keepdims=True)
            probs = jnp.exp(dot_nt(q, key) - lse_ref[:, number : number + 1])
            grad_scores = (probs * (dot_nt(g, value) - delta)).astype(BF)
            queries.append((dot(grad_scores, key) * HEAD_DIM**-0.5).astype(BF))
            keys.append(dot_tn(grad_scores, q))
            values.append(dot_tn(probs.astype(BF), g))
        grad_query = jnp.concatenate(queries, axis=1)
        gkv_refs[k][...] = jnp.concatenate(keys + values, axis=1).astype(BF)
        near_ref[k, rank:, :] = dot_tn(u_ref[...], grad_query).astype(BF)
        total = total + dot_nt(grad_query, weight[:, :local])
    low = total[:, deep].astype(BF)
    by_piece(fixed_ref, 0, dot_tn(low, n2_ref[...]))
    grad_normed = total[:, :width] + dot(low, down2_ref[...])
    grad = grad + norm_backward(s1_ref[...], gain_ref[1:2, :], grad_normed)
    r1_ref[...] = grad
    r1b_ref[...] = grad.astype(BF)


def cross_back(
    g, dns, s1, s2, n2, q, o, lse, u, z4, up, down5, down2, gains, biases, weight, keyvals
):
    rows, width = g.shape
    rank = up.shape[0]
    members, local = len(keyvals), weight.shape[2] // 2
    return pl.pallas_call(
        functools.partial(cross_back_kernel, members, local),
        out_shape=[sds((rows, width), F32), sds((rows, width), BF)]
        + [sds((members, n * rank, local), BF) for n in (3, 2)]
        + [sds(keyvals[0].shape, BF)] * members,
        compiler_params=pltpu.CompilerParams(vmem_limit_bytes=VMEM_LIMIT),
        cost_estimate=cost(32 * rows * width * width, 8 * width * width),
    )(g, s1, s2, n2, q, o, lse, u, z4, up, down5, down2, gains, biases, weight, *keyvals, *dns)


def output_kernel(s2_ref, up_ref, g_ref, *refs):
    *y_refs, out_ref, gup_ref = refs
    width, rank = out_ref.shape[1], up_ref.shape[0]
    total = total_of(y_refs)
    low = total[:, width : width + rank].astype(BF)
    out_ref[...] = (s2_ref[...] + total[:, :width] + dot(low, up_ref[...])).astype(BF)
    by_piece(gup_ref, 0, dot_tn(low, g_ref[...]))


def output_end(s2, ys, up, g, members):
    rank, width = up.shape
    return pl.pallas_call(
        output_kernel,
        out_shape=[sds(g.shape, BF), sds((members, rank, width // members), BF)],
        compiler_params=pltpu.CompilerParams(vmem_limit_bytes=VMEM_LIMIT),
        cost_estimate=cost(0, 0),
    )(s2, up, g, *ys)


def input_kernel(x_ref, r_ref, down_ref, gain_ref, *refs):
    *dn_refs, out_ref = refs
    width, rank = out_ref.shape[1], down_ref.shape[0]
    total = total_of(dn_refs)
    low = total[:, width : width + rank].astype(BF)
    grad = total[:, :width] + dot(low, down_ref[...])
    back = norm_backward(x_ref[...].astype(F32), gain_ref[...], grad)
    out_ref[...] = (r_ref[...] + back).astype(BF)


def input_end(x, r1, dns, down, gain):
    return pl.pallas_call(
        input_kernel,
        out_shape=sds(x.shape, BF),
        compiler_params=pltpu.CompilerParams(vmem_limit_bytes=VMEM_LIMIT),
        cost_estimate=cost(0, 0),
    )(x, r1, down, gain, *dns)


def rows_kernel(near_ref, far_ref, n_ref, z_ref, r_ref, out_ref):
    rows, rank = near_ref.shape
    down = dot_tn(near_ref[...], n_ref[:rows, :]) + dot_tn(far_ref[...], n_ref[rows:, :])
    by_piece(out_ref, 0, down)
    by_piece(out_ref, rank, dot_tn(z_ref[...], r_ref[...]))


def self_rows(low_near, low_far, normed, low_two, branch, members):
    rank, width = low_near.shape[1], normed.shape[1]
    return pl.pallas_call(
        rows_kernel,
        out_shape=sds((members, 2 * rank, width // members), BF),
        compiler_params=pltpu.CompilerParams(vmem_limit_bytes=VMEM_LIMIT),
        cost_estimate=cost(0, 0),
    )(low_near, low_far, normed, low_two, branch)


def context_kernel(members, places_ref, *refs):
    blocks, (w_ref, down_ref, kv_ref, low_ref) = refs[:members], refs[members:]
    rank, local = down_ref.shape[1], blocks[0].shape[1]
    width = members * local
    low, keyval = 0.0, 0.0
    for k in range(members):
        at = pl.ds(pl.multiple_of(places_ref[k], local), local)
        low = low + dot(blocks[k][...], down_ref[at, :])
        keyval = keyval + dot(blocks[k][...], w_ref[at, :])
    low = low.astype(BF)
    low_ref[...] = low
    kv_ref[...] = (keyval + dot(low, w_ref[width : width + rank, :])).astype(BF)


def context_forward(places, blocks, weight, down):
    count = blocks[0].shape[0]
    arrays = (*blocks, weight, down)
    shapes = [sds((count, weight.shape[1]), BF), sds((count, down.shape[1]), BF)]
    return pl.pallas_call(
        functools.partial(context_kernel, len(blocks)),
        grid_spec=pltpu.PrefetchScalarGridSpec(
            num_scalar_prefetch=1,
            grid=(1,),
            in_specs=[whole_spec(a.shape) for a in arrays],
            out_specs=[whole_spec(s.shape) for s in shapes],
        ),
        out_shape=shapes,
        compiler_params=params(),
        cost_estimate=cost(0, 0),
    )(places, *arrays)


def context_back_kernel(members, places_ref, *refs):
    blocks, (w_ref, down_ref, low_ref, g_ref), refs = (
        refs[:members],
        refs[members : members + 4],
        refs[members + 4 :],
    )
    gup_ref, *refs = refs
    rank, local = down_ref.shape[1], blocks[0].shape[1]
    width = members * local
    grad = g_ref[...]
    low = dot_nt(grad, w_ref[width : width + rank, :]).astype(BF)
    gup_ref[...] = dot_tn(low_ref[...], grad)
    for k in range(members):
        at = pl.ds(pl.multiple_of(places_ref[k], local), local)
        out = dot_nt(grad, w_ref[at, :]) + dot_nt(low, down_ref[at, :])
        refs[k][...] = out.astype(BF)
        refs[members + k][...] = dot_tn(low, blocks[k][...]).astype(BF)


def context_back(places, blocks, weight, down, low, grad):
    count, local = blocks[0].shape
    rank, members = down.shape[1], len(blocks)
    arrays = (*blocks, weight, down, low, grad)
    shapes = (
        [sds((rank, weight.shape[1]), F32)]
        + [sds((count, local), BF)] * members
        + [sds((rank, local), BF)] * members
    )
    return pl.pallas_call(
        functools.partial(context_back_kernel, members),
        grid_spec=pltpu.PrefetchScalarGridSpec(
            num_scalar_prefetch=1,
            grid=(1,),
            in_specs=[whole_spec(a.shape) for a in arrays],
            out_specs=[whole_spec(s.shape) for s in shapes],
        ),
        out_shape=shapes,
        compiler_params=params(),
        cost_estimate=cost(0, 0),
    )(places, *arrays)


def table_kernel(cos_ref, sin_ref, out_cos_ref, out_left_ref, out_right_ref):
    half, breadth = ROT // 2, 2 * HEAD_DIM
    lane = lax.broadcasted_iota(jnp.int32, (half, breadth), 1)
    row = lax.broadcasted_iota(jnp.int32, (half, breadth), 0)
    within = lane % HEAD_DIM
    first = jnp.where(within == row, 1.0, 0.0)
    second = jnp.where(within == row + half, 1.0, 0.0)

    def spread(ref, pattern):
        return lax.dot_general(
            ref[...], pattern, (((0,), (0,)), ((), ())),
            precision=lax.Precision.HIGHEST, preferred_element_type=F32,
        )

    lanes = lax.broadcasted_iota(jnp.int32, out_cos_ref.shape, 1) % HEAD_DIM
    out_cos_ref[...] = jnp.where(lanes < ROT, spread(cos_ref, first + second), 1.0)
    out_left_ref[...] = -spread(sin_ref, first)
    out_right_ref[...] = spread(sin_ref, second)


def rotary_tables(cosines, sines):
    tokens = cosines.shape[1]
    return pl.pallas_call(
        table_kernel,
        out_shape=[sds((tokens, 2 * HEAD_DIM), F32)] * 3,
        compiler_params=pltpu.CompilerParams(vmem_limit_bytes=VMEM_LIMIT),
        cost_estimate=cost(0, 0),
    )(cosines, sines)


def feed_kernel(first, last, number, *refs):
    n_refs, g_refs, (down_ref, up_ref, w_ref), refs = (
        refs[:number],
        refs[number : 2 * number],
        refs[2 * number : 2 * number + 3],
        refs[2 * number + 3 :],
    )
    if not first:
        (y_in, dn_in), refs = refs[:2], refs[2:]
    *refs, gdown_ref, ggate_ref, gupper_ref, n_ref, g_ref = refs
    step, width = pl.program_id(0), n_ref.shape[1]
    rank, part = gdown_ref.shape
    take_tile(n_refs, n_ref, step)
    take_tile(g_refs, g_ref, step)

    @pl.when(step == 0)
    def _():
        for ref in (gdown_ref, ggate_ref, gupper_ref):
            ref[...] = jnp.zeros_like(ref)

    normed, grad = n_ref[...], g_ref[...]
    low = dot_nt(normed, down_ref[...]).astype(BF)
    grad_low = dot_nt(grad, up_ref[...]).astype(BF)
    deep = slice(width, width + rank)
    both = dot(normed, w_ref[:width, : 2 * part]) + dot(low, w_ref[deep, : 2 * part])
    gate, upper = both[:, :part], both[:, part:]
    grad_unit = dot(grad, w_ref[:width, 2 * part :]) + dot(grad_low, w_ref[deep, 2 * part :])
    sigmoid = 1.0 / (1.0 + jnp.exp(-gate))
    acted = gate * sigmoid
    unit = (acted * upper).astype(BF)
    grad_gate = (grad_unit * upper * (sigmoid + acted * (1.0 - sigmoid))).astype(BF)
    grad_upper = (grad_unit * acted).astype(BF)
    y = dot_nt(unit, w_ref[:, 2 * part :])
    dn = dot_nt(grad_gate, w_ref[:, :part]) + dot_nt(grad_upper, w_ref[:, part : 2 * part])
    if not first:
        y, dn = y + y_in[...].astype(F32), dn + dn_in[...].astype(F32)
    if last:
        give_tile(y.astype(BF), refs[:number], step)
        give_tile(dn.astype(BF), refs[number:], step)
    else:
        refs[0][...] = y.astype(BF)
        refs[1][...] = dn.astype(BF)
    gdown_ref[...] += dot_tn(grad_low, unit)
    ggate_ref[...] += dot_tn(low, grad_gate)
    gupper_ref[...] += dot_tn(low, grad_upper)


def feed(normed, grads, down, up, weight, sums, rows, start, last):
    block, width = normed[0].shape
    rank, number = down.shape[0], len(normed)
    deep, part = weight.shape[0], weight.shape[1] // 3
    narrow = sds((rank, part), F32)
    tokens = number * block
    if last:
        wide = sds((block, deep // LANES * LANES + LANES), BF)
        shapes, specs = [wide] * (2 * number), [whole_spec(wide.shape)] * (2 * number)
    else:
        shapes, specs = [sds((tokens, deep), BF)] * 2, [row_spec(rows, deep)] * 2
    first = not sums
    arrays = (*normed, *grads, down, up, weight)
    return pl.pallas_call(
        functools.partial(feed_kernel, first, last, number),
        grid=(tokens // rows,),
        in_specs=[whole_spec(a.shape) for a in arrays]
        + [pl.BlockSpec((rows, deep), lambda t: (start + t, 0)) for _ in sums],
        out_specs=specs + [whole_spec(narrow.shape)] * 3,
        out_shape=shapes + [narrow] * 3,
        scratch_shapes=[pltpu.VMEM((rows, width), BF)] * 2,
        compiler_params=params(),
        cost_estimate=cost(8 * tokens * weight.size, 2 * weight.size),
    )(*arrays, *sums)


def settle_first_kernel(fold, labels_ref, in_ref, down_ref, up_ref, hid_ref, gate_ref):
    slot = pl.program_id(0)
    local = down_ref.shape[-1]
    for ref in (down_ref, up_ref, hid_ref, gate_ref):
        ref[...] = jnp.zeros_like(ref)
    for s in range(in_ref.shape[0]):

        @pl.when(labels_ref[s] == slot)
        def _(s=s):
            for n, k in enumerate(DOWN_FIRST):
                down_ref[0, k] += in_ref[s, n].astype(F32)
            for n, k in enumerate(UP_FIRST):
                up_ref[0, k] += in_ref[s, len(DOWN_FIRST) + n].astype(F32)
            for k in range(fold):
                at, n = slice(k * local, (k + 1) * local), 6 + k
                hid_ref[0, :, at] += in_ref[s, n].astype(F32)
                gate_ref[0, 0, :, at] += in_ref[s, n + fold].astype(F32)
                gate_ref[0, 1, :, at] += in_ref[s, n + 2 * fold].astype(F32)


def settle_second_kernel(labels_ref, in_ref, down_in, up_in, down_ref, up_ref):
    slot = pl.program_id(0)
    down_ref[...] = down_in[...]
    up_ref[...] = up_in[...]
    for s in range(in_ref.shape[0]):

        @pl.when(labels_ref[s] == slot)
        def _(s=s):
            for n, k in enumerate(DOWN_SECOND):
                down_ref[0, k] += in_ref[s, n].astype(F32)
            for n, k in enumerate(UP_SECOND):
                up_ref[0, k] += in_ref[s, len(DOWN_SECOND) + n].astype(F32)


DOWN_FIRST, UP_FIRST = (2, 4, 5), (4, 7, 8)
DOWN_SECOND, UP_SECOND = (0, 1, 3), (0, 1, 2, 3, 5, 6)


def slot_spec(shape):
    return pl.BlockSpec((1,) + shape[1:], lambda i, *_, n=len(shape): (i,) + (0,) * (n - 1))


def settle_first(labels, grads, slots, fold):
    rank, local = grads.shape[2:]
    hidden = fold * local
    shapes = [
        (slots, 6, rank, local),
        (slots, 9, rank, local),
        (slots, rank, hidden),
        (slots, 2, rank, hidden),
    ]
    return pl.pallas_call(
        functools.partial(settle_first_kernel, fold),
        grid_spec=pltpu.PrefetchScalarGridSpec(
            num_scalar_prefetch=1,
            grid=(slots,),
            in_specs=[whole_spec(grads.shape)],
            out_specs=[slot_spec(s) for s in shapes],
        ),
        out_shape=[sds(s, F32) for s in shapes],
        compiler_params=params(),
        cost_estimate=cost(0, 0),
    )(labels, grads)


def settle_second(labels, grads, down, up):
    return pl.pallas_call(
        settle_second_kernel,
        grid_spec=pltpu.PrefetchScalarGridSpec(
            num_scalar_prefetch=1,
            grid=(down.shape[0],),
            in_specs=[whole_spec(grads.shape), slot_spec(down.shape), slot_spec(up.shape)],
            out_specs=[slot_spec(down.shape), slot_spec(up.shape)],
        ),
        out_shape=[sds(down.shape, F32), sds(up.shape, F32)],
        compiler_params=params(),
        cost_estimate=cost(0, 0),
    )(labels, grads, down, up)


def chunks(hidden):
    return (hidden // 3,) * 3


def body(
    inputs,
    context,
    positions,
    adapter_index,
    self_in_weight,
    self_out_weight,
    cross_query_weight,
    cross_keyval_weight,
    cross_out_weight,
    feed_in_weight,
    feed_out_weight,
    norm_gains,
    norm_biases,
    adapter_down,
    adapter_down_hidden,
    adapter_up,
    adapter_up_hidden,
    out_cotangent,
    *,
    pairs,
    chips,
):
    group = Group(pairs, chips)
    members = 2 * pairs
    rows, width = inputs.shape[1], inputs.shape[2]
    block = self_in_weight.shape[0]
    local = self_in_weight.shape[2]
    hidden = feed_in_weight.shape[2]
    slots, rank = adapter_down.shape[0], adapter_down.shape[3]
    deep = width + rank
    parts = chunks(hidden)
    fold = hidden // local
    pieces = group.pieces
    gains, biases = norm_gains, norm_biases
    tile = min(256, members * rows)
    tiles = members * rows // tile
    near_tiles = tiles // pairs

    def packed(*parts):
        return jnp.concatenate(parts, axis=1)

    def stacked(*parts):
        return jnp.concatenate(parts, axis=0)

    def listed(values):
        return list(values) if isinstance(values, (list, tuple)) else [values]

    def piece(array, k, size):
        return lax.dynamic_slice_in_dim(array, pieces[k] * size, size, array.ndim - 1)

    def own(array):
        return piece(array, 0, local)

    near_chips = [1, 2] if chips == 4 else list(range(1, chips))
    chip_rows = [(group.chip ^ k) * 2 * block for k in range(chips)]
    mine_rows = [c + group.core * block for c in chip_rows]
    other_rows = [c + (1 - group.core) * block for c in chip_rows]
    first_rows = [c + group.zhi * block for c in chip_rows]
    second_rows = [c + (1 - group.zhi) * block for c in chip_rows]
    fixed = [jnp.zeros_like(group.core), group.core * block, (1 - group.core) * block]
    row_places = jnp.stack(
        chip_rows + mine_rows + other_rows + first_rows + second_rows + fixed
    ).astype(jnp.int32)
    zero, mine_at, other_at = 5 * chips, 5 * chips + 1, 5 * chips + 2

    def put_all(own_entry, near, rest, low, columns, by_core=True):
        entries, moves = [own_entry, *near, *rest], []
        for i, k in enumerate([0, *near_chips] + [3] * len(rest)):
            row = entries[i][1]
            if len(rest) == 2 and i > len(near):
                moves.append((i, row, block, 0, None, (2 + i - len(near)) * chips + k, 0))
            elif by_core:
                moves.append((i, row, 2 * block, 0, None, k, 0))
            else:
                moves.append((i, row, block, 0, None, 3 * chips + k, 0))
                moves.append((i, row + block, block, 0, None, 4 * chips + k, 0))
        moves.append((len(entries), 0, rank, 0, None, zero, width))
        sources = [e[0] for e in entries]
        return place([*sources, low], moves, row_places, [(deep, columns)], True)[0]

    def spread(prev, own_block):
        if prev and chips == 4:
            half = prev[0][1]
            turns = [
                prev[1][0][prev[1][2] : prev[1][2] + half],
                prev[0][0][prev[0][2] + half : prev[0][2] + 2 * half],
            ]
            if own_block is not None:
                turns = listed(step.mark(*[stacked(turn, own_block) for turn in turns]))
            return [xor_move(turn, "chip", 4, k) for turn, k in zip(turns, near_chips)]
        if own_block is None:
            return []
        return [xor_move(own_block, "chip", chips, k) for k in near_chips]

    def flat(*groups):
        return [x for g in groups for x in listed(g)]

    def wait_all(*groups):
        groups = [listed(g) for g in groups]
        values = iter(listed(step.wait(*flat(*groups))))
        return [[next(values) for _ in g] for g in groups]

    def swap_all(blocks):
        if not blocks:
            return []
        blocks = listed(step.wait(*blocks))
        return listed(step.wait(*[core_swap(b) for b in blocks]))

    shard_self = packed(*[self_in_weight[:, i] for i in range(3)], self_out_weight.T)
    step = Order(shard_self[:8, :128])
    self_from = [home_swap(shard_self), turned(shard_self)]
    stream_own, context_own = home_swap(inputs[0]), home_swap(context[0])
    index, positions = step.wait(adapter_index, positions)
    index_other, positions_other = step.wait(core_swap(index), core_swap(positions))
    index = jnp.where(group.home, index, index_other)[0]
    positions = jnp.where(group.home, positions, positions_other)[0]
    down = lax.dynamic_index_in_dim(adapter_down.transpose(0, 1, 3, 2), index, 0, keepdims=False)
    up = lax.dynamic_index_in_dim(adapter_up.transpose(0, 2, 1, 3), index, 0, keepdims=False)
    down, up = step.mark(down, up)
    low_self = packed(*[own(up[i]) for i in range(3)], own(down[1]))
    low_keyval = packed(own(up[5]), own(up[6]))
    low_cross = stacked(
        *[packed(piece(up[4], k, local), piece(down[4], k, local)) for k in range(members)]
    )
    low_self, low_keyval, low_cross = step.mark(low_self, low_keyval, low_cross)
    keyval_parts = step.wait(cross_keyval_weight)
    keyval_parts = step.mark(keyval_parts[:, 0], keyval_parts[:, 1])
    shard_cross = step.mark(packed(cross_query_weight, cross_out_weight.T, *keyval_parts))
    stream_own, context_own, *self_from = step.wait(stream_own, context_own, *self_from)
    ready_self = step.mark(stacked(*self_from))

    near_self, far_cross = spread([], ready_self), group.cross(shard_cross)
    stream_other, stream_far = core_swap(stream_own), group.far_p(stream_own)
    blocks_at = [
        lax.dynamic_slice_in_dim(positions, pieces[k] * rows, rows, 0) for k in range(members)
    ]
    half = ROT // 2
    inverse = 10000.0 ** (-jnp.arange(half, dtype=F32) / half)
    angles = inverse[:, None] * step.wait(jnp.concatenate(blocks_at)).astype(F32)[None]
    tables = step.mark(*rotary_tables(*step.mark(jnp.cos(angles), jnp.sin(angles))))
    feed_in, feed_out = step.wait(feed_in_weight, feed_out_weight)
    gate_rows, upper_rows = step.mark(feed_in[:, 0], feed_in[:, 1])
    at = [sum(parts[:i]) for i in range(len(parts))]

    def feed_shard(i):
        to = slice(at[i], at[i] + parts[i])
        gate, upper, out = step.wait(gate_rows, upper_rows, feed_out)
        return step.mark(packed(gate[:, to], upper[:, to], out.T[:, to]))

    shard_feed = [feed_shard(i) for i in range(len(parts))]
    near_self, stream_far, (far_cross, stream_other) = wait_all(
        near_self, stream_far, [far_cross, stream_other]
    )
    mine = jnp.where(group.home, shard_cross, far_cross)
    given = jnp.where(group.home, far_cross, shard_cross)
    keyval_mine, keyval_give = mine[:, 2 * local :], given[:, 2 * local :]
    pair = stacked(mine[:, : 2 * local], given[:, : 2 * local])
    keyval_mine, keyval_give, pair = step.mark(keyval_mine, keyval_give, pair)
    keyval_other, *stream_far_other = swap_all([keyval_give, *stream_far])

    rest_self = spread([(g, block, 0) for g in near_self], None)
    pair_far = group.far_p(pair)
    feed_from = [[home_swap(shard_feed[0]), turned(shard_feed[0])]]
    moves = [
        (0, 0, block, 0, None, mine_at, 0),
        (1, 0, block, 0, None, other_at, 0),
        (2, 0, 2 * block, 0, None, zero, 2 * block),
    ]
    ready_keyval = step.mark(
        place(
            [keyval_mine, keyval_other, pair], moves, row_places, [(4 * block, 2 * local)], True
        )[0]
    )
    stream = [stream_own, stream_other]
    for far, far_other in zip(stream_far, stream_far_other):
        stream += [far, far_other]
    rest_self, pair_far, feed_from[0] = wait_all(rest_self, pair_far, feed_from[0])
    self_weight = step.mark(
        put_all(
            (ready_self, 0), [(g, 0) for g in near_self], [(g, 0) for g in rest_self], low_self,
            4 * local, by_core=False,
        )
    )

    near_keyval = spread([], ready_keyval)
    cotangent_own = home_swap(step.wait(out_cotangent[0]))
    context_far = group.far_p(context_own)
    query, keys, values, low_one, normed_one = project_self(
        listed(step.wait(*stream)), gains[0:1], biases[0:1], down[0], self_weight, tables, tile
    )
    query, keys, values = step.mark(query, keys, values)
    heads_far, logsum_far, *y_far = attend_self(
        query, keys, values, self_weight, tile, near_tiles, tiles - near_tiles, rows
    )
    y_far = listed(step.mark(*y_far))

    def far_sums(*groups):
        others = iter(swap_all([g[2 * k + 1] for g in groups for k in range(pairs - 1)]))
        sums = [
            [group.near_sums(g[2 * k], next(others)).astype(BF) for k in range(pairs - 1)]
            for g in groups
        ]
        values = iter(listed(step.mark(*flat(*sums))))
        return [[next(values) for _ in s] for s in sums]

    def move_p(sums):
        return [xor_move(s, "p", pairs, k + 1) for k, s in enumerate(sums)]

    def sum_up(blocks, other, far):
        total = group.near_sums(blocks[0], other)
        for f in far:
            total = total + f.astype(F32)
        return step.mark(total)

    near_keyval, context_far, (cotangent_own,) = wait_all(
        near_keyval, context_far, [cotangent_own]
    )
    (y_sums,) = far_sums(y_far)

    far = move_p(y_sums)
    if chips == 4:
        both_far = [spread([(g, 2 * block, 0) for g in near_keyval], pair_far[0])]
    else:
        both_far = [spread([], p) for p in pair_far]
    heads_near, logsum_near, *y_rows = attend_self(
        step.wait(query), keys, values, self_weight, tile, 0, near_tiles, rows
    )
    y_rows = listed(step.mark(*y_rows))
    far, *both_far = wait_all(far, *both_far)
    y_other, context_other, *swapped = swap_all([y_rows[1], context_own, *context_far])
    branch = [y_rows[0], y_other, *far]
    context_blocks = [context_own, context_other]
    for far, far_other in zip(context_far, swapped):
        context_blocks += [far, far_other]

    if chips == 4:
        (x_got, y_got), (x_first, y_first) = both_far[0], near_keyval
        at_rest = 2 * block
        keyval_from = [(ready_keyval, 0), (x_first, 0), (y_first, 0)], [(x_got, 0)]
        pair_from = [[(ready_keyval, at_rest), (x_first, at_rest), (y_first, at_rest), (y_got, 0)]]
        pair_from.append([(pair_far[0], 0), (x_got, at_rest), (y_got, at_rest)])
    else:
        at_rest = 0
        keyval_from = [(b, 0) for b in [ready_keyval, *near_keyval]], []
        pair_from = [[(b, 2 * block) for b in [ready_keyval, *near_keyval]]]
        pair_from += [[(b, 0) for b in [p, *n]] for p, n in zip(pair_far, both_far)]
    keyval_weight = step.mark(
        put_all(keyval_from[0][0], keyval_from[0][1:], keyval_from[1], low_keyval, 2 * local)
    )
    context_places = (jnp.stack(pieces) * local).astype(jnp.int32)
    down_context = step.mark(down[3].T)
    keyval, low_context = context_forward(
        context_places, context_blocks, keyval_weight, down_context
    )
    keyval = step.mark(keyval)

    if chips == 4:
        rest_far = spread([(x_got, block, at_rest), (y_got, block, at_rest)], None)
    else:
        rest_far = []
    keyval_far = group.far_p(keyval)
    ready_feed = [step.mark(stacked(*feed_from[0]))]
    keyval_far, rest_far = wait_all(keyval_far, rest_far)
    near_feed = [spread([], ready_feed[0])]
    cotangent_far = group.far_p(cotangent_own)
    distances = [0, *near_chips]
    by_chip = [(n, i, e) for n, found in enumerate(pair_from) for i, e in enumerate(found)]
    swapped = swap_all(
        [
            keyval, *keyval_far, *rest_far, cotangent_own,
            *[e[0][e[1] : e[1] + 2 * block] for _, _, e in by_chip],
        ]
    )
    keyvals = [keyval, swapped[0]]
    for far, far_other in zip(keyval_far, swapped[1:]):
        keyvals += [far, far_other]
    swapped = swapped[1 + len(keyval_far) :]
    rest_other, swapped = swapped[: len(rest_far)], swapped[len(rest_far) :]
    cotangent_blocks = [cotangent_own, swapped[0]]
    swapped = swapped[1:]
    sources, moves = [], []
    for (n, i, (array, row)), other in zip(by_chip, swapped):
        chip = distances[i] if i < len(distances) else 3
        for r in (0, 1):
            at_source = len(sources)
            moves.append((at_source, row + r * block, block, 0, 2 * n + r, chips + chip, 0))
            moves.append((at_source + 1, r * block, block, 0, 2 * n + 1 - r, 2 * chips + chip, 0))
        sources += [array, other]
    for r, (mine, other) in enumerate(zip(rest_far, rest_other)):
        at_source = len(sources)
        moves.append((at_source, 0, block, 0, 2 + r, chips + 3, 0))
        moves.append((at_source + 1, 0, block, 0, 3 - r, 2 * chips + 3, 0))
        sources += [mine, other]
    moves += [(len(sources), r * rank, rank, 0, r, zero, width) for r in range(members)]
    cross_weight = step.mark(
        place([*sources, low_cross], moves, row_places, [(members, deep, 2 * local)], True)[0]
    )

    near_feed[0], cotangent_far = wait_all(near_feed[0], cotangent_far)

    rest_feed = [spread([(g, block, 0) for g in near_feed[0]], None)]
    feed_from.append([home_swap(shard_feed[1]), turned(shard_feed[1])])
    stream_own, *branch = step.wait(stream_own, *branch)

    (
        stream_one, stream_two, normed_two, normed_three, query_cross, heads_cross, logsum_cross,
        low_two, low_three, low_four,
    ) = cross_forward(
        stream_own, branch, up[3], up[7], down[2], gains, biases, cross_weight, keyvals,
    )
    normed_own = step.mark(normed_three)
    rest_feed[0], feed_from[1] = wait_all(rest_feed[0], feed_from[1])
    ready_feed.append(step.mark(stacked(*feed_from[1])))

    normed_far = group.far_p(normed_own)
    near_feed.append(spread([], ready_feed[1]))
    feed_from.append([home_swap(shard_feed[2]), turned(shard_feed[2])])
    down_hidden = lax.dynamic_index_in_dim(
        adapter_down_hidden.transpose(0, 2, 1), index, 0, keepdims=False
    )
    up_hidden = lax.dynamic_index_in_dim(
        adapter_up_hidden.transpose(0, 2, 1, 3), index, 0, keepdims=False
    )
    feed_down, feed_up = piece(down_hidden, 0, hidden), piece(up_hidden, 0, hidden)
    feed_down, feed_gate, feed_upper = step.mark(feed_down, feed_up[0], feed_up[1])
    low_feed = [
        packed(feed_gate[:, to], feed_upper[:, to], feed_down[:, to])
        for to in [slice(a, a + p) for a, p in zip(at, parts)]
    ]
    low_feed = step.mark(*low_feed)
    near_feed[1], normed_far, feed_from[2] = wait_all(near_feed[1], normed_far, feed_from[2])
    normed_other, *swapped = swap_all([normed_own, *normed_far, *cotangent_far])
    normed_blocks = [normed_own, normed_other]
    for far, far_other in zip(normed_far, swapped):
        normed_blocks += [far, far_other]
    for far, far_other in zip(cotangent_far, swapped[len(normed_far) :]):
        cotangent_blocks += [far, far_other]
    ready_feed.append(step.mark(stacked(*feed_from[2])))

    def feed_weight(i, skip, rest):
        return step.mark(
            put_all(
                (ready_feed[i], 0), [(g, skip) for g in near_feed[i]], [(g, 0) for g in rest],
                low_feed[i], 3 * parts[i], by_core=False,
            )
        )

    weight = feed_weight(0, 0, rest_feed[0])
    skip = block if chips == 4 else 0

    near_feed.append(spread([(g, block, 0) for g in near_feed[1]], ready_feed[2]))

    def feed_pass(weight, sums, picked, start, last):
        normed, cotangent = wait_all(normed_blocks[picked], cotangent_blocks[picked])
        found = feed(normed, cotangent, down[5], up[8], weight, sums, tile, start, last)
        *values, gdown, ggate, gupper = found
        values = step.mark(*values)
        half = len(values) // 2
        return values[:half], values[half:], [gdown, ggate, gupper]

    everything, far_only, near_only = slice(0, None), slice(2, None), slice(0, 2)
    y, dn, *feed_grads = feed_pass(weight, (), everything, 0, False)
    (near_feed[2],) = wait_all(near_feed[2])
    weight = feed_weight(1, 0, near_feed[2] if chips == 4 else [])
    rest_feed.append(spread([(g, block, skip) for g in near_feed[2]], None))
    y, dn, grads = feed_pass(weight, (*y, *dn), everything, 0, False)
    feed_grads.append(grads)
    (rest_feed[1],) = wait_all(rest_feed[1]) if rest_feed[1] else ([],)
    weight = feed_weight(2, skip, rest_feed[1])
    y_far, dn_far, grads = feed_pass(weight, (*y, *dn), far_only, near_tiles, True)

    dn_sums, y_sums = far_sums(dn_far, y_far)
    far = move_p(dn_sums)
    y_rows, dn_rows, more = feed_pass(weight, (*y, *dn), near_only, 0, True)
    feed_grads.append([a + b for a, b in zip(grads, more)])
    (far,) = wait_all(far)
    dn_other, y_other = swap_all([dn_rows[1], y_rows[1]])
    grad_normed = [dn_rows[0], dn_other, *far]

    far = move_p(step.mark(*y_sums) if len(y_sums) > 1 else [step.mark(*y_sums)])
    grad_stream, branch_grad, fixed_rows, near_rows, *keyval_rows = cross_back(
        cotangent_own, listed(step.wait(*grad_normed)), stream_one, stream_two, normed_two,
        query_cross, heads_cross, logsum_cross, low_three, low_four, up[7], down[5], down[2],
        gains, biases, cross_weight, keyvals,
    )
    branch_grad, *keyval_rows = step.mark(branch_grad, *keyval_rows)
    (far,) = wait_all(far)

    branch_far = group.far_p(branch_grad)
    (branch_other,) = swap_all([branch_grad])

    def back(grad, heads, logsum, first, before):
        return attend_back(
            grad, up[3], self_weight, query, keys, values, heads, logsum, tables, low_one, rank,
            tile, first, before,
        )

    near_back = step.mark(
        *back([branch_grad, branch_other], heads_near, logsum_near, 0, None)
    )
    (branch_far,) = wait_all(branch_far)
    keyval_other, *branch_swapped = swap_all([keyval_rows[1], *branch_far])
    branch_blocks = []
    for f, o in zip(branch_far, branch_swapped):
        branch_blocks += [f, o]

    output, grad_up_eight = step.mark(
        *output_end(stream_two, [y_rows[0], y_other, *far], up[8], cotangent_own, members)
    )

    def taken(by_piece, k):
        return lax.dynamic_index_in_dim(by_piece, pieces[k], 0, keepdims=False)

    first_rows = listed(
        step.mark(
            *[
                stacked(taken(fixed_rows, k), taken(grad_up_eight, k), near_rows[k])
                for k in range(members)
            ]
        )
    )
    first_sums, keyval_sums = far_sums(first_rows[2:], keyval_rows[2:])
    (first_other,) = swap_all([first_rows[1]])

    def columns(array):
        return array.reshape(rank, -1, local).transpose(1, 0, 2)

    def sent(parts):
        parts.append(jnp.full((1, rank, local), index, F32))
        grads = step.mark(jnp.concatenate(parts, axis=0).astype(BF))
        return [home_swap(grads), turned_back(grads)]

    def to_chips(blocks):
        both = step.mark(stacked(*blocks))
        return [both] + [xor_move(both, "chip", chips, k) for k in range(1, chips)]

    def every(blocks):
        grads = stacked(*blocks)
        grads = grads.reshape(-1, grads.shape[0] // (2 * chips), rank, local)
        return grads, grads[:, -1, 0, 0].astype(jnp.int32)

    first_far, keyval_far, block_output = move_p(first_sums), move_p(keyval_sums), home_swap(output)
    branch_blocks = listed(step.wait(*branch_blocks))
    grad_mixed, grad_down_one, grad_up_self = back(
        branch_blocks, heads_far, logsum_far, near_tiles, near_back
    )
    grad_mixed = step.mark(grad_mixed)
    first_far, keyval_far, (block_output,) = wait_all(first_far, keyval_far, [block_output])
    low_far, *dn_far = step.mark(
        *project_back(grad_mixed, self_weight, tile, near_tiles, tiles - near_tiles, rows, rank)
    )
    (dn_sums,) = far_sums(dn_far)

    summed = sum_up(first_rows, first_other, first_far).reshape(-1, rank, local)
    grad_keyval = step.mark(sum_up(keyval_rows, keyval_other, keyval_far).astype(BF))
    far = move_p(step.mark(*dn_sums) if len(dn_sums) > 1 else [step.mark(*dn_sums)])
    low_near, *dn_rows = step.mark(
        *project_back(step.wait(grad_mixed), self_weight, tile, 0, near_tiles, rows, rank)
    )
    grad_up_keyval, *found = step.mark(
        *context_back(
            context_places, context_blocks, keyval_weight, down_context, low_context,
            step.wait(grad_keyval),
        )
    )
    context_rows, grad_down_three = found[:members], found[members:]
    own_rows = step.mark(
        self_rows(low_near, low_far, normed_one, low_two, branch_grad, members)
    )
    (far,) = wait_all(far)

    first = sent(
        [
            summed[0:1],
            summed[4:5],
            summed[1:2],
            summed[5:6],
            summed[2:4],
            *[columns(jnp.concatenate(g, axis=1)) for g in zip(*feed_grads)],
        ]
    )
    second_rows = listed(
        step.mark(
            *[stacked(taken(own_rows, k), grad_down_three[k]) for k in range(members)]
        )
    )
    dn_other, second_other, context_other, *others = swap_all(
        [dn_rows[1], second_rows[1], context_rows[1], *second_rows[3::2], *context_rows[3::2]]
    )
    grad_inputs = step.mark(
        input_end(stream_own, grad_stream, [dn_rows[0], dn_other, *far], down[0], gains[0:1])
    )
    sums = [
        group.near_sums(b, o).astype(BF)
        for b, o in zip([*second_rows[2::2], *context_rows[2::2]], others)
    ]
    sums = listed(step.mark(*sums))
    second_far, context_far = move_p(sums[: pairs - 1]), move_p(sums[pairs - 1 :])
    second_far, context_far, first = wait_all(second_far, context_far, first)
    grad_inputs = home_swap(grad_inputs)
    summed = sum_up(second_rows, second_other, second_far).reshape(-1, rank, local)
    second = sent(
        [
            summed[0:1],
            grad_down_one[None],
            summed[2:3],
            columns(grad_up_self),
            summed[1:2],
            columns(grad_up_keyval),
        ]
    )
    grad_context = home_swap(step.mark(sum_up(context_rows, context_other, context_far).astype(BF)))
    first = to_chips(first)
    (first,) = wait_all(first)
    first, labels = every(first)
    grad_down, grad_up, grad_hidden, grad_gate = settle_first(labels, first, slots, fold)
    grad_down, grad_up = step.mark(grad_down, grad_up)
    (second,) = wait_all(second)
    (second,) = wait_all(to_chips(second))
    second, labels = every(second)
    grad_down, grad_up = settle_second(labels, second, grad_down, grad_up)
    return (
        block_output[None],
        grad_inputs.astype(F32)[None],
        grad_context.astype(F32)[None],
        grad_down.transpose(0, 1, 3, 2),
        grad_hidden.transpose(0, 2, 1),
        grad_up.transpose(0, 2, 1, 3),
        grad_gate.transpose(0, 2, 1, 3),
    )


def solution(mesh):
    members = mesh.shape["tensor"]
    chips = mesh.shape["dp"] // 2
    mesh = Mesh(
        mesh.devices.reshape(chips, 2, 2, members // 2), ("chip", "core", "zhi", "p")
    )
    dp, tensor = ("chip", "core"), ("zhi", "p")
    in_specs = (
        P(dp, tensor, None),
        P(dp, None, tensor),
        P(dp, None),
        P(dp),
        P(dp, None, tensor),
        P(tensor, dp),
        P(dp, tensor),
        P(dp, None, tensor),
        P(tensor, dp),
        P(dp, None, tensor),
        P(tensor, dp),
        P(),
        P(),
        P(),
        P(),
        P(),
        P(),
        P(dp, tensor, None),
    )
    out_specs = (
        P(dp, tensor, None),
        P(dp, tensor, None),
        P(dp, None, tensor),
        P(None, None, tensor, None),
        P(None, tensor, None),
        P(None, None, None, tensor),
        P(None, None, None, tensor),
    )

    def run(*args):
        return body(*args, pairs=members // 2, chips=chips)

    return jax.shard_map(run, mesh=mesh, in_specs=in_specs, out_specs=out_specs, check_vma=False)
```

```python
import functools

import jax
import jax.numpy as jnp
from jax import lax
from jax.experimental import pallas as pl
from jax.experimental.pallas import tpu as pltpu
from jax.sharding import Mesh, PartitionSpec as P

HEAD_DIM = 64
ROT = 32
EPSILON = 1e-05
F32 = jnp.float32
BF = jnp.bfloat16
SWAP = ((0, 1), (1, 0))
LANES = 128
VMEM_LIMIT = 56 * 1024 * 1024


def dot(left, right):
    return jnp.dot(left, right, preferred_element_type=F32)


def dot_nt(left, right):
    return lax.dot_general(left, right, (((1,), (1,)), ((), ())), preferred_element_type=F32)


def dot_tn(left, right):
    return lax.dot_general(left, right, (((0,), (0,)), ((), ())), preferred_element_type=F32)


class Order:
    def __init__(self, first):
        self.token = first

    def wait(self, *values):
        *values, self.token = lax.optimization_barrier((*values, self.token))
        return values[0] if len(values) == 1 else values

    mark = wait


def core_swap(x):
    return lax.ppermute(x, "core", SWAP)


def xor_move(x, axis, size, k):
    return lax.ppermute(x, axis, [(i, i ^ k) for i in range(size)])


def home_swap(x):
    return lax.ppermute(x, ("core", "zhi"), [(0, 0), (1, 2), (2, 1), (3, 3)])


def turned(x):
    return lax.ppermute(x, ("core", "zhi"), [(0, 1), (1, 3), (2, 0), (3, 2)])


def turned_back(x):
    return lax.ppermute(x, ("core", "zhi"), [(0, 2), (1, 0), (2, 3), (3, 1)])


class Group:
    def __init__(self, pairs, chips):
        self.pairs, self.chips = pairs, chips
        self.core, self.zhi, self.p = (lax.axis_index(n) for n in ("core", "zhi", "p"))
        self.chip = lax.axis_index("chip")
        self.home = self.core == self.zhi
        self.pieces = [
            (self.core ^ kc) * pairs + (self.p ^ kp) for kp in range(pairs) for kc in (0, 1)
        ]

    def far_p(self, own):
        return [xor_move(own, "p", self.pairs, k) for k in range(1, self.pairs)]

    def near_sums(self, own, other):
        return own.astype(F32) + other.astype(F32)

    def cross(self, shard):
        return xor_move(shard, "zhi", 2, 1)

    def spread_one(self, block):
        if self.chips == 4:
            return [xor_move(block, "chip", 4, k) for k in (1, 2)]
        return [xor_move(block, "chip", self.chips, k) for k in range(1, self.chips)]

    def spread_two(self, got):
        if self.chips != 4:
            return []
        half = got[0].shape[0] // 2
        return [xor_move(got[1][:half], "chip", 4, 1), xor_move(got[0][half:], "chip", 4, 2)]

    def places(self, rows):
        if self.chips == 4:
            diagonal = (self.chip ^ 3) * rows
            return [(self.chip ^ 1) * rows, (self.chip ^ 2) * rows, diagonal, diagonal + rows // 2]
        return [(self.chip ^ k) * rows for k in range(1, self.chips)]


class Weight:
    def __init__(self, shape, places):
        self.shape, self.places, self.arrays, self.moves = shape, places, [], []

    def add(self, array, *parts):
        self.moves += [(len(self.arrays), *part) for part in parts]
        self.arrays.append(array)

    @property
    def count(self):
        return len(self.arrays)

    def specs(self):
        return [pl.BlockSpec(memory_space=pl.ANY)] * self.count

    def columns(self, start, size):
        if size % 128 or start % 128:
            return 0, self.shape[-1], start
        return start, size, 0

    def scratch(self, size=None):
        shape = self.shape if size is None else self.shape[:-1] + (size,)
        return [pltpu.VMEM(shape, BF), pltpu.SemaphoreType.DMA((len(self.moves),))]

    def at_first(self, step, refs, places_ref, target, sems, start=0, size=None):
        def begin():
            @pl.when(step == 0)
            def _():
                self.bring(refs, places_ref, target, sems, start, size)

        def end():
            @pl.when(step == 0)
            def _():
                wait_for(self.bring(refs, places_ref, target, sems, start, size, go=False))

        return begin, end

    def bring(self, refs, places_ref, target, sems, start=0, size=None, go=True):
        copies = []
        for number, (source, row, rows, column, columns, lead, place, offset) in enumerate(self.moves):
            at = pl.ds(pl.multiple_of(places_ref[place] + offset, 16), rows)
            to = target.at[at] if lead is None else target.at[lead, at]
            if size is not None:
                column, columns = column + start, size
            found = refs[source].at[pl.ds(row, rows), pl.ds(column, columns)]
            copies.append(pltpu.make_async_copy(found, to, sems.at[number]))
        if go:
            for copy in copies:
                copy.start()
        return copies


def wait_for(copies):
    for copy in copies:
        copy.wait()


def weight_call(kernel, weight, grid, in_specs, out_specs, out_shape, scratch, estimate, arrays):
    return pl.pallas_call(
        kernel,
        grid_spec=pltpu.PrefetchScalarGridSpec(
            num_scalar_prefetch=1,
            grid=grid,
            in_specs=weight.specs() + in_specs,
            out_specs=out_specs,
            scratch_shapes=scratch,
        ),
        out_shape=out_shape,
        compiler_params=params(),
        cost_estimate=estimate,
    )(weight.places, *weight.arrays, *arrays)


def stats(stream):
    average = jnp.mean(stream, axis=-1, keepdims=True)
    centred = stream - average
    variance = jnp.mean(centred * centred, axis=-1, keepdims=True)
    scale = lax.rsqrt(variance + EPSILON)
    return centred * scale, scale


def layer_norm(stream, gain, bias):
    return (stats(stream)[0] * gain + bias).astype(BF)


def norm_backward(stream, gain, grad):
    unit, scale = stats(stream)
    grad = grad * gain
    return scale * (
        grad
        - jnp.mean(grad, axis=-1, keepdims=True)
        - unit * jnp.mean(grad * unit, axis=-1, keepdims=True)
    )


def turn(x, cosines, left_sines, right_sines):
    breadth = 2 * HEAD_DIM if x.shape[1] % (2 * HEAD_DIM) == 0 else HEAD_DIM
    half = ROT // 2
    for at in range(0, x.shape[1], breadth):
        group = x[:, at : at + breadth]
        if breadth % 128 == 0:
            left, right = pltpu.roll(group, breadth - half, 1), pltpu.roll(group, half, 1)
        else:
            left = jnp.concatenate([group[:, half:], group[:, :half]], axis=1)
            right = jnp.concatenate([group[:, -half:], group[:, :-half]], axis=1)
        yield (
            at,
            breadth,
            group * cosines[:, :breadth]
            + left * left_sines[:, :breadth]
            + right * right_sines[:, :breadth],
        )


def head_sums(product):
    columns = product.shape[1]
    rows = -(-columns // HEAD_DIM // 8) * 8
    head = lax.broadcasted_iota(jnp.int32, (rows, columns), 0)
    lane = lax.broadcasted_iota(jnp.int32, (rows, columns), 1)
    picked = jnp.where(lane // HEAD_DIM == head, 1.0, 0.0).astype(F32)
    return lax.dot_general(
        picked, product, (((1,), (1,)), ((), ())),
        precision=lax.Precision.HIGHEST, preferred_element_type=F32,
    )


def whole_spec(shape):
    return pl.BlockSpec(shape, lambda *_: (0,) * len(shape))


def row_spec(rows, columns):
    return pl.BlockSpec((rows, columns), lambda t, *_: (t, 0))


def take_tile(refs, tile_ref, step):
    rows, tile = refs[0].shape[0], tile_ref.shape[0]
    for i, ref in enumerate(refs):

        @pl.when(step == i * rows // tile)
        def _(i=i, ref=ref):
            tile_ref[i * rows % tile : i * rows % tile + rows, :] = ref[...]


def give_tile(value, refs, step):
    rows, (tile, columns) = refs[0].shape[0], value.shape
    for i, ref in enumerate(refs):

        @pl.when(step == i * rows // tile)
        def _(i=i, ref=ref):
            ref[:, :columns] = value[i * rows % tile : i * rows % tile + rows]
            ref[:, columns:] = jnp.zeros((rows, ref.shape[1] - columns), ref.dtype)


def total_of(refs):
    total = refs[0][...].astype(F32)
    for ref in refs[1:]:
        total = total + ref[...].astype(F32)
    return total


def by_piece(ref, row, value):
    local = ref.shape[2]
    for k in range(ref.shape[0]):
        ref[k, row : row + value.shape[0], :] = value[:, k * local : (k + 1) * local].astype(
            ref.dtype
        )


def params(semantics=1):
    return pltpu.CompilerParams(
        dimension_semantics=("arbitrary",) * semantics, vmem_limit_bytes=VMEM_LIMIT
    )


def cost(flops, moved, exps=0):
    return pl.CostEstimate(
        flops=int(flops) or 1000, bytes_accessed=int(moved) or 1000, transcendentals=int(exps)
    )


def sds(shape, dtype):
    return jax.ShapeDtypeStruct(shape, dtype)


def query_kernel(weight, part, count, places_ref, *refs):
    w_refs, refs = refs[: weight.count], refs[weight.count :]
    blocks, (gain_ref, bias_ref, down_ref, cos_ref, left_ref, right_ref), refs = (
        refs[:count],
        refs[count : count + 6],
        refs[count + 6 :],
    )
    q_ref, k_ref, v_ref, low_ref, n_ref, x_ref, w_ref, sems = refs
    step = pl.program_id(0)

    begin, end = weight.at_first(step, w_refs, places_ref, w_ref, sems, *part[:2])
    begin()
    take_tile(blocks, x_ref, step)
    local, width = q_ref.shape[1], x_ref.shape[1]
    normed = layer_norm(x_ref[...].astype(F32), gain_ref[...], bias_ref[...])
    n_ref[...] = normed
    low = dot_nt(normed, down_ref[...]).astype(BF)
    low_ref[...] = low
    end()
    at = slice(part[2], part[2] + 3 * local)
    mixed = dot(normed, w_ref[:width, at]) + dot(low, w_ref[width:, at])
    tables = cos_ref[...], left_ref[...], right_ref[...]
    for at, breadth, turned in turn(mixed[:, :local], *tables):
        q_ref[:, at : at + breadth] = (turned * HEAD_DIM**-0.5).astype(BF)
    for at, breadth, turned in turn(mixed[:, local : 2 * local], *tables):
        k_ref[:, at : at + breadth] = turned.astype(BF)
    v_ref[...] = mixed[:, 2 * local :].astype(BF)


def project_self(blocks, gain, bias, down, weight, tables, rows):
    width = blocks[0].shape[1]
    tokens = len(blocks) * blocks[0].shape[0]
    local = weight.shape[1] // 4
    part = weight.columns(0, 3 * local)
    return weight_call(
        functools.partial(query_kernel, weight, part, len(blocks)),
        weight,
        (tokens // rows,),
        [whole_spec(b.shape) for b in blocks]
        + [whole_spec(gain.shape), whole_spec(bias.shape), whole_spec(down.shape)]
        + [row_spec(rows, t.shape[1]) for t in tables],
        [row_spec(rows, local)] * 3 + [row_spec(rows, down.shape[0]), row_spec(rows, width)],
        [sds((tokens, local), BF)] * 3
        + [sds((tokens, down.shape[0]), BF), sds((tokens, width), BF)],
        [pltpu.VMEM((rows, width), BF), *weight.scratch(part[1])],
        cost(8 * tokens * width * local, 8 * width * local),
        [*blocks, gain, bias, down, *tables],
    )


def attend_kernel(weight, part, places_ref, *refs):
    w_refs, refs = refs[: weight.count], refs[weight.count :]
    q_ref, k_ref, v_ref, o_ref, lse_ref, *y_refs, w_ref, sems = refs
    rows, local = q_ref.shape
    step = pl.program_id(0)

    begin, end = weight.at_first(step, w_refs, places_ref, w_ref, sems, *part[:2])
    begin()
    lanes = lax.broadcasted_iota(jnp.int32, (rows, 128), 1)
    logsums = jnp.zeros((rows, 128), F32)
    for head in range(local // HEAD_DIM):
        at = slice(head * HEAD_DIM, (head + 1) * HEAD_DIM)
        scores = dot_nt(q_ref[:, at], k_ref[:, at])
        top = jnp.max(scores, axis=1, keepdims=True)
        powers = jnp.exp(scores - top)
        total = jnp.sum(powers, axis=1, keepdims=True)
        out = dot(powers.astype(BF), v_ref[:, at]) / total
        o_ref[:, at] = out.astype(BF)
        logsums = jnp.where(lanes == head, top + jnp.log(total), logsums)
    lse_ref[...] = logsums.T[: lse_ref.shape[0]]
    end()
    y = dot_nt(o_ref[...], w_ref[:, part[2] : part[2] + local]).astype(BF)
    give_tile(y, y_refs, step)


def wide_of(weight):
    return weight.shape[-2] // LANES * LANES + LANES


def attend_self(query, keys, values, weight, rows, first, count, block):
    tokens, local = query.shape
    heads = -(-local // HEAD_DIM // 8) * 8
    part = weight.columns(3 * local, local)
    blocks = count * rows // block
    return weight_call(
        functools.partial(attend_kernel, weight, part),
        weight,
        (count,),
        [
            pl.BlockSpec((rows, local), lambda t, *_: (first + t, 0)),
            whole_spec(keys.shape),
            whole_spec(values.shape),
        ],
        [row_spec(rows, local), pl.BlockSpec((heads, rows), lambda t, *_: (0, t))]
        + [whole_spec((block, wide_of(weight)))] * blocks,
        [sds((count * rows, local), BF), sds((heads, count * rows), F32)]
        + [sds((block, wide_of(weight)), BF)] * blocks,
        weight.scratch(part[1]),
        cost(16 * count * rows * tokens * local, 8 * query.size, count * rows * tokens),
        [query, keys, values],
    )


def project_back_kernel(weight, part, local, places_ref, *refs):
    w_refs, refs = refs[: weight.count], refs[weight.count :]
    m_ref, low_ref, *refs, w_ref, sems = refs
    step = pl.program_id(0)

    @pl.when(step == 0)
    def _():
        wait_for(weight.bring(w_refs, places_ref, w_ref, sems, *part[:2]))

    width = w_ref.shape[0] - low_ref.shape[1]
    value = dot_nt(m_ref[...], w_ref[:, part[2] : part[2] + 3 * local]).astype(BF)
    low_ref[...] = value[:, width:]
    give_tile(value, refs, step)


def project_back(mixed, weight, rows, first, count, block, rank):
    local, wide = weight.shape[1] // 4, wide_of(weight)
    part = weight.columns(0, 3 * local)
    blocks = count * rows // block
    return weight_call(
        functools.partial(project_back_kernel, weight, part, local),
        weight,
        (count,),
        [pl.BlockSpec((rows, 3 * local), lambda t, *_: (first + t, 0))],
        [row_spec(rows, rank)] + [whole_spec((block, wide))] * blocks,
        [sds((count * rows, rank), BF)] + [sds((block, wide), BF)] * blocks,
        weight.scratch(part[1]),
        cost(40 * count * rows * wide * local, 8 * wide * local),
        [mixed],
    )


def attend_back_kernel(weight, part, first, last, tiles, number, places_ref, *refs):
    w_refs, refs = refs[: weight.count], refs[weight.count :]
    grads, refs = refs[:number], refs[number:]
    (
        up_ref, q_ref, k_ref, v_ref, o_ref, lse_ref, cos_ref, left_ref, right_ref, low_ref,
    ), refs = refs[:10], refs[10:]
    *refs, g_ref, w_ref, sems = refs

    @pl.when(pl.program_id(0) == 0)
    def _():
        wait_for(weight.bring(w_refs, places_ref, w_ref, sems, *part[:2]))

    take_tile(grads, g_ref, pl.program_id(0))
    if not first:
        (mq_ref, gk_in, gv_in, down_in), refs = refs[:4], refs[4:]
    if last:
        m_ref, down_ref, gup_ref, gk_ref, gv_ref = refs
    else:
        m_ref, gk_ref, gv_ref, down_ref = refs
    step, rows = pl.program_id(0), q_ref.shape[0]
    width, local = g_ref.shape[1], q_ref.shape[1]
    at_rows = pl.ds(pl.multiple_of((step + tiles) * rows, rows), rows)
    at_query = at_rows if last else pl.ds(pl.multiple_of(step * rows, rows), rows)

    @pl.when(step == 0)
    def _():
        if first:
            gk_ref[...] = jnp.zeros_like(gk_ref)
            gv_ref[...] = jnp.zeros_like(gv_ref)
            down_ref[...] = jnp.zeros_like(down_ref)
        else:
            gk_ref[...] = gk_in[...]
            gv_ref[...] = gv_in[...]
            down_ref[...] = down_in[...]
            m_ref[: mq_ref.shape[0], :local] = mq_ref[...]

    grad = g_ref[...]
    grad_low = dot_nt(grad, up_ref[...]).astype(BF)
    at = slice(part[2], part[2] + local)
    grad_out = dot(grad, w_ref[:width, at]) + dot(grad_low, w_ref[width:, at])
    grad_out = grad_out.astype(BF)
    out = o_ref[...]
    down_ref[...] += dot_tn(grad_low, out)
    product = grad_out.astype(F32) * out.astype(F32)
    deltas = head_sums(product)
    parts = []
    for head in range(local // HEAD_DIM):
        at = slice(head * HEAD_DIM, (head + 1) * HEAD_DIM)
        q, k, v, g = q_ref[:, at], k_ref[:, at], v_ref[:, at], grad_out[:, at]
        delta = deltas[head : head + 1]
        probs = jnp.exp(dot_nt(k, q) - lse_ref[head : head + 1, :])
        grad_scores = (probs * (dot_nt(v, g) - delta)).astype(BF)
        gv_ref[:, at] += dot(probs.astype(BF), g)
        gk_ref[:, at] += dot(grad_scores, q)
        parts.append(dot_tn(grad_scores, k) * HEAD_DIM**-0.5)
    tables = cos_ref[at_rows, :], -left_ref[at_rows, :], -right_ref[at_rows, :]
    for at, breadth, turned in turn(jnp.concatenate(parts, axis=1), *tables):
        m_ref[at_query, at : at + breadth] = turned.astype(BF)

    if last:

        @pl.when(step == pl.num_programs(0) - 1)
        def _():
            tables = cos_ref[...], -left_ref[...], -right_ref[...]
            for at, breadth, turned in turn(gk_ref[...], *tables):
                m_ref[:, local + at : local + at + breadth] = turned.astype(BF)
            m_ref[:, 2 * local :] = gv_ref[...].astype(BF)
            gup_ref[...] = dot_tn(low_ref[...], m_ref[...])


def attend_back(grads, up, weight, query, keys, values, out, lse, tables, low, rank, rows, start, before):
    tokens, local = query.shape
    block, width = grads[0].shape
    count = len(grads) * block // rows
    first, last = before is None, (start + count) * rows == tokens
    before = () if first else before
    sums = [sds((tokens, local), F32)] * 2 + [sds((rank, local), F32)]
    if last:
        shapes = [sds((tokens, 3 * local), BF), sums[2], sds((rank, 3 * local), F32)]
        scratch = [pltpu.VMEM((tokens, local), F32)] * 2
    else:
        shapes, scratch = [sds((count * rows, local), BF), *sums], []
    scratch.append(pltpu.VMEM((rows, width), BF))

    def tile(columns):
        return pl.BlockSpec((rows, columns), lambda t, *_: (start + t, 0))

    part = weight.columns(3 * local, local)
    return weight_call(
        functools.partial(attend_back_kernel, weight, part, first, last, start, len(grads)),
        weight,
        (count,),
        [
            *[whole_spec(g.shape) for g in grads],
            whole_spec(up.shape),
            tile(local),
            whole_spec(keys.shape),
            whole_spec(values.shape),
            row_spec(rows, local),
            pl.BlockSpec((lse.shape[0], rows), lambda t, *_: (0, t)),
            *[whole_spec(t.shape) for t in tables],
            whole_spec(low.shape),
            *[whole_spec(b.shape) for b in before],
        ],
        [whole_spec(s.shape) for s in shapes],
        shapes,
        scratch + weight.scratch(part[1]),
        cost(40 * count * rows * tokens * local, 10 * query.size, count * rows * tokens),
        [*grads, up, query, keys, values, out, lse, *tables, low, *before],
    )


def in_order(swap, first, second):
    keep = swap == 0
    return jnp.where(keep, first, second), jnp.where(keep, second, first)


def cross_kernel(weight, members, local, core_at, places_ref, *refs):
    w_refs, refs = refs[: weight.count], refs[weight.count :]
    *refs, w_ref, sems = refs
    copies = weight.bring(w_refs, places_ref, w_ref, sems)
    (x_ref, up_self_ref, up_cross_ref, down_ref, gain_ref, bias_ref), refs = refs[:6], refs[6:]
    kv_refs, refs = refs[:members], refs[members:]
    y_refs, refs = refs[:-10], refs[-10:]
    branch = total_of(y_refs)
    s1_ref, s2_ref, n2_ref, n3_ref, q_ref, o_ref, lse_ref, z2_ref, u_ref, z4_ref = refs
    rows, width = x_ref.shape
    rank = down_ref.shape[0]
    deep = slice(width, width + rank)
    low = branch[:, deep].astype(BF)
    z2_ref[...] = low
    stream = x_ref[...].astype(F32) + branch[:, :width] + dot(low, up_self_ref[...])
    s1_ref[...] = stream
    normed = layer_norm(stream, gain_ref[1:2, :], bias_ref[1:2, :])
    n2_ref[...] = normed
    low = dot_nt(normed, down_ref[...]).astype(BF)
    u_ref[...] = low
    total = jnp.zeros((rows, width + rank), F32)
    wait_for(copies)
    both = 2 * local
    for n in range(members // 2):
        query = dot(normed, w_ref[n, :width, :both]) + dot(low, w_ref[n, deep, :both])
        query = (query * HEAD_DIM**-0.5).astype(BF)
        q_ref[:, n * both : (n + 1) * both] = query
        found = in_order(places_ref[core_at], kv_refs[2 * n][...], kv_refs[2 * n + 1][...])
        parts, logsums = [], []
        for head in range(both // HEAD_DIM):
            keyval, own = found[head * HEAD_DIM // local], head * HEAD_DIM % local
            keys = keyval[:, own : own + HEAD_DIM]
            values = keyval[:, local + own : local + own + HEAD_DIM]
            scores = dot_nt(keys, query[:, head * HEAD_DIM : (head + 1) * HEAD_DIM])
            top = jnp.max(scores, axis=0, keepdims=True)
            powers = jnp.exp(scores - top)
            sums = jnp.sum(powers, axis=0, keepdims=True)
            parts.append(dot_tn(values, powers.astype(BF)) / sums)
            logsums.append(top + jnp.log(sums))
        out = jnp.concatenate(parts, axis=0).T.astype(BF)
        o_ref[:, n * both : (n + 1) * both] = out
        lse_ref[n] = jnp.concatenate(logsums, axis=0)
        total = total + dot_nt(out, w_ref[n, :, both:])
    low = total[:, deep].astype(BF)
    z4_ref[...] = low
    stream = stream + total[:, :width] + dot(low, up_cross_ref[...])
    s2_ref[...] = stream
    n3_ref[...] = layer_norm(stream, gain_ref[2:3, :], bias_ref[2:3, :])


def cross_forward(x, ys, up_self, up_cross, down, gains, biases, weight, keyvals, core_at):
    rows, width = x.shape
    members, local = len(keyvals), weight.shape[2] // 4
    plain, wide = sds((rows, width), BF), sds((rows, width), F32)
    low = sds((rows, down.shape[0]), BF)
    logsums = sds((members // 2, 2 * local // HEAD_DIM, rows), F32)
    shapes = [wide, wide, plain, plain, plain, plain, logsums, low, low, low]
    arrays = [x, up_self, up_cross, down, gains, biases, *keyvals, *ys]
    return weight_call(
        functools.partial(cross_kernel, weight, members, local, core_at),
        weight,
        (1,),
        [whole_spec(a.shape) for a in arrays],
        [whole_spec(o.shape) for o in shapes],
        shapes,
        weight.scratch(),
        cost(24 * rows * width * width, 8 * width * width),
        arrays,
    )


def cross_back_kernel(weight, members, local, core_at, places_ref, *refs):
    w_refs, refs = refs[: weight.count], refs[weight.count :]
    *refs, w_ref, sems = refs
    copies = weight.bring(w_refs, places_ref, w_ref, sems)
    (
        g_ref, s1_ref, s2_ref, n2_ref, q_ref, o_ref, lse_ref, u_ref, z4_ref,
        up_ref, down5_ref, down2_ref, gain_ref, bias_ref,
    ), refs = refs[:14], refs[14:]
    kv_refs, refs = refs[:members], refs[members:]
    dn_refs, (r1_ref, r1b_ref, fixed_ref, near_ref, *gkv_refs) = (
        refs[: -4 - members],
        refs[-4 - members :],
    )
    summed = total_of(dn_refs)
    width = g_ref.shape[1]
    rank = up_ref.shape[0]
    deep = slice(width, width + rank)
    stream = s2_ref[...]
    low = summed[:, deep].astype(BF)
    grad_normed = summed[:, :width] + dot(low, down5_ref[...])
    normed = layer_norm(stream, gain_ref[2:3, :], bias_ref[2:3, :])
    by_piece(fixed_ref, rank, dot_tn(low, normed))
    grad = g_ref[...].astype(F32) + norm_backward(stream, gain_ref[2:3, :], grad_normed)
    branch = grad.astype(BF)
    low = dot_nt(branch, up_ref[...]).astype(BF)
    by_piece(fixed_ref, 2 * rank, dot_tn(z4_ref[...], branch))
    by_piece(near_ref, 0, dot_tn(low, o_ref[...]))
    total = jnp.zeros((g_ref.shape[0], width + rank), F32)
    wait_for(copies)
    both, swap = 2 * local, places_ref[core_at]
    for n in range(members // 2):
        columns = slice(n * both, (n + 1) * both)
        grad_out = dot(branch, w_ref[n, :width, both:]) + dot(low, w_ref[n, deep, both:])
        grad_out = grad_out.astype(BF)
        query = q_ref[:, columns]
        deltas = head_sums(grad_out.astype(F32) * o_ref[:, columns].astype(F32))
        found = in_order(swap, kv_refs[2 * n][...], kv_refs[2 * n + 1][...])
        queries, keys, values = [], [], []
        for head in range(both // HEAD_DIM):
            keyval, own = found[head * HEAD_DIM // local], head * HEAD_DIM % local
            key = keyval[:, own : own + HEAD_DIM]
            value = keyval[:, local + own : local + own + HEAD_DIM]
            at = slice(head * HEAD_DIM, (head + 1) * HEAD_DIM)
            q, g = query[:, at], grad_out[:, at]
            probs = jnp.exp(dot_nt(key, q) - lse_ref[n, head : head + 1, :])
            grad_scores = (probs * (dot_nt(value, g) - deltas[head : head + 1])).astype(BF)
            queries.append(dot_tn(key, grad_scores))
            keys.append(dot(grad_scores, q))
            values.append(dot(probs.astype(BF), g))
        grad_query = (jnp.concatenate(queries, axis=0).T * HEAD_DIM**-0.5).astype(BF)
        half = len(keys) // 2
        first = jnp.concatenate(keys[:half] + values[:half], axis=1).astype(BF)
        second = jnp.concatenate(keys[half:] + values[half:], axis=1).astype(BF)
        gkv_refs[2 * n][...], gkv_refs[2 * n + 1][...] = in_order(swap, first, second)
        ups = dot_tn(u_ref[...], grad_query).astype(BF)
        near_ref[2 * n, rank:, :] = ups[:, :local]
        near_ref[2 * n + 1, rank:, :] = ups[:, local:]
        total = total + dot_nt(grad_query, w_ref[n, :, :both])
    low = total[:, deep].astype(BF)
    by_piece(fixed_ref, 0, dot_tn(low, n2_ref[...]))
    grad_normed = total[:, :width] + dot(low, down2_ref[...])
    grad = grad + norm_backward(s1_ref[...], gain_ref[1:2, :], grad_normed)
    r1_ref[...] = grad
    r1b_ref[...] = grad.astype(BF)


def cross_back(
    g, dns, s1, s2, n2, q, o, lse, u, z4, up, down5, down2, gains, biases, weight, keyvals, core_at
):
    rows, width = g.shape
    rank = up.shape[0]
    members, local = len(keyvals), weight.shape[2] // 4
    shapes = [sds((rows, width), F32), sds((rows, width), BF)]
    shapes += [sds((members, n * rank, local), BF) for n in (3, 2)]
    shapes += [sds(keyvals[0].shape, BF)] * members
    arrays = [g, s1, s2, n2, q, o, lse, u, z4, up, down5, down2, gains, biases, *keyvals, *dns]
    return weight_call(
        functools.partial(cross_back_kernel, weight, members, local, core_at),
        weight,
        (1,),
        [whole_spec(a.shape) for a in arrays],
        [whole_spec(o.shape) for o in shapes],
        shapes,
        weight.scratch(),
        cost(32 * rows * width * width, 8 * width * width),
        arrays,
    )


def output_kernel(s2_ref, up_ref, g_ref, *refs):
    *y_refs, out_ref, gup_ref = refs
    width, rank = out_ref.shape[1], up_ref.shape[0]
    total = total_of(y_refs)
    low = total[:, width : width + rank].astype(BF)
    out_ref[...] = (s2_ref[...] + total[:, :width] + dot(low, up_ref[...])).astype(BF)
    by_piece(gup_ref, 0, dot_tn(low, g_ref[...]))


def output_end(s2, ys, up, g, members):
    rank, width = up.shape
    return pl.pallas_call(
        output_kernel,
        out_shape=[sds(g.shape, BF), sds((members, rank, width // members), BF)],
        compiler_params=pltpu.CompilerParams(vmem_limit_bytes=VMEM_LIMIT),
        cost_estimate=cost(0, 0),
    )(s2, up, g, *ys)


def input_kernel(x_ref, r_ref, down_ref, gain_ref, *refs):
    *dn_refs, out_ref = refs
    width, rank = out_ref.shape[1], down_ref.shape[0]
    total = total_of(dn_refs)
    low = total[:, width : width + rank].astype(BF)
    grad = total[:, :width] + dot(low, down_ref[...])
    back = norm_backward(x_ref[...].astype(F32), gain_ref[...], grad)
    out_ref[...] = (r_ref[...] + back).astype(BF)


def input_end(x, r1, dns, down, gain):
    return pl.pallas_call(
        input_kernel,
        out_shape=sds(x.shape, BF),
        compiler_params=pltpu.CompilerParams(vmem_limit_bytes=VMEM_LIMIT),
        cost_estimate=cost(0, 0),
    )(x, r1, down, gain, *dns)


def rows_kernel(near_ref, far_ref, n_ref, z_ref, r_ref, out_ref):
    rows, rank = near_ref.shape
    down = dot_tn(near_ref[...], n_ref[:rows, :]) + dot_tn(far_ref[...], n_ref[rows:, :])
    by_piece(out_ref, 0, down)
    by_piece(out_ref, rank, dot_tn(z_ref[...], r_ref[...]))


def self_rows(low_near, low_far, normed, low_two, branch, members):
    rank, width = low_near.shape[1], normed.shape[1]
    return pl.pallas_call(
        rows_kernel,
        out_shape=sds((members, 2 * rank, width // members), BF),
        compiler_params=pltpu.CompilerParams(vmem_limit_bytes=VMEM_LIMIT),
        cost_estimate=cost(0, 0),
    )(low_near, low_far, normed, low_two, branch)


def context_kernel(weight, members, at_pieces, places_ref, *refs):
    w_refs, refs = refs[: weight.count], refs[weight.count :]
    blocks, (down_ref, kv_ref, low_ref, w_ref, sems) = refs[:members], refs[members:]
    wait_for(weight.bring(w_refs, places_ref, w_ref, sems))
    rank, local = down_ref.shape[1], blocks[0].shape[1]
    width = members * local
    low, keyval = 0.0, 0.0
    for k in range(members):
        at = pl.ds(pl.multiple_of(places_ref[at_pieces + k], local), local)
        low = low + dot(blocks[k][...], down_ref[at, :])
        keyval = keyval + dot(blocks[k][...], w_ref[at, :])
    low = low.astype(BF)
    low_ref[...] = low
    kv_ref[...] = (keyval + dot(low, w_ref[width : width + rank, :])).astype(BF)


def context_forward(at_pieces, blocks, weight, down):
    count = blocks[0].shape[0]
    arrays = (*blocks, down)
    shapes = [sds((count, weight.shape[1]), BF), sds((count, down.shape[1]), BF)]
    return weight_call(
        functools.partial(context_kernel, weight, len(blocks), at_pieces),
        weight,
        (1,),
        [whole_spec(a.shape) for a in arrays],
        [whole_spec(s.shape) for s in shapes],
        shapes,
        weight.scratch(),
        cost(0, 0),
        arrays,
    )


def context_back_kernel(weight, members, at_pieces, places_ref, *refs):
    w_refs, refs = refs[: weight.count], refs[weight.count :]
    blocks, (down_ref, low_ref, g_ref), refs = (
        refs[:members],
        refs[members : members + 3],
        refs[members + 3 :],
    )
    gup_ref, *refs, w_ref, sems = refs
    wait_for(weight.bring(w_refs, places_ref, w_ref, sems))
    rank, local = down_ref.shape[1], blocks[0].shape[1]
    width = members * local
    grad = g_ref[...]
    low = dot_nt(grad, w_ref[width : width + rank, :]).astype(BF)
    gup_ref[...] = dot_tn(low_ref[...], grad)
    for k in range(members):
        at = pl.ds(pl.multiple_of(places_ref[at_pieces + k], local), local)
        out = dot_nt(grad, w_ref[at, :]) + dot_nt(low, down_ref[at, :])
        refs[k][...] = out.astype(BF)
        refs[members + k][...] = dot_tn(low, blocks[k][...]).astype(BF)


def context_back(at_pieces, blocks, weight, down, low, grad):
    count, local = blocks[0].shape
    rank, members = down.shape[1], len(blocks)
    arrays = (*blocks, down, low, grad)
    shapes = (
        [sds((rank, weight.shape[1]), F32)]
        + [sds((count, local), BF)] * members
        + [sds((rank, local), BF)] * members
    )
    return weight_call(
        functools.partial(context_back_kernel, weight, members, at_pieces),
        weight,
        (1,),
        [whole_spec(a.shape) for a in arrays],
        [whole_spec(s.shape) for s in shapes],
        shapes,
        weight.scratch(),
        cost(0, 0),
        arrays,
    )


def table_kernel(cos_ref, sin_ref, out_cos_ref, out_left_ref, out_right_ref):
    half, breadth = ROT // 2, 2 * HEAD_DIM
    lane = lax.broadcasted_iota(jnp.int32, (half, breadth), 1)
    row = lax.broadcasted_iota(jnp.int32, (half, breadth), 0)
    within = lane % HEAD_DIM
    first = jnp.where(within == row, 1.0, 0.0)
    second = jnp.where(within == row + half, 1.0, 0.0)

    def spread(ref, pattern):
        return lax.dot_general(
            ref[...], pattern, (((0,), (0,)), ((), ())),
            precision=lax.Precision.HIGHEST, preferred_element_type=F32,
        )

    lanes = lax.broadcasted_iota(jnp.int32, out_cos_ref.shape, 1) % HEAD_DIM
    out_cos_ref[...] = jnp.where(lanes < ROT, spread(cos_ref, first + second), 1.0)
    out_left_ref[...] = -spread(sin_ref, first)
    out_right_ref[...] = spread(sin_ref, second)


def rotary_tables(cosines, sines):
    tokens = cosines.shape[1]
    return pl.pallas_call(
        table_kernel,
        out_shape=[sds((tokens, 2 * HEAD_DIM), F32)] * 3,
        compiler_params=pltpu.CompilerParams(vmem_limit_bytes=VMEM_LIMIT),
        cost_estimate=cost(0, 0),
    )(cosines, sines)


def feed_kernel(weight, first, last, number, places_ref, *refs):
    w_refs, refs = refs[: weight.count], refs[weight.count :]
    n_refs, g_refs, (down_ref, up_ref), refs = (
        refs[:number],
        refs[number : 2 * number],
        refs[2 * number : 2 * number + 2],
        refs[2 * number + 2 :],
    )
    if not first:
        (low_in, glow_in, y_in, dn_in), refs = refs[:4], refs[4:]
    *refs, gdown_ref, ggate_ref, gupper_ref, n_ref, g_ref, w_ref, sems = refs
    step, width = pl.program_id(0), n_ref.shape[1]
    rank, part = gdown_ref.shape
    take_tile(n_refs, n_ref, step)
    take_tile(g_refs, g_ref, step)

    @pl.when(step == 0)
    def _():
        wait_for(weight.bring(w_refs, places_ref, w_ref, sems))
        for ref in (gdown_ref, ggate_ref, gupper_ref):
            ref[...] = jnp.zeros_like(ref)

    normed, grad = n_ref[...], g_ref[...]
    if first:
        low = dot_nt(normed, down_ref[...]).astype(BF)
        grad_low = dot_nt(grad, up_ref[...]).astype(BF)
        refs[2][...] = low
        refs[3][...] = grad_low
    else:
        low, grad_low = low_in[...], glow_in[...]
    deep = slice(width, width + rank)
    both = dot(normed, w_ref[:width, : 2 * part]) + dot(low, w_ref[deep, : 2 * part])
    gate, upper = both[:, :part], both[:, part:]
    grad_unit = dot(grad, w_ref[:width, 2 * part :]) + dot(grad_low, w_ref[deep, 2 * part :])
    sigmoid = 1.0 / (1.0 + jnp.exp(-gate))
    acted = gate * sigmoid
    unit = (acted * upper).astype(BF)
    grad_gate = (grad_unit * upper * (sigmoid + acted * (1.0 - sigmoid))).astype(BF)
    grad_upper = (grad_unit * acted).astype(BF)
    y = dot_nt(unit, w_ref[:, 2 * part :])
    dn = dot_nt(grad_gate, w_ref[:, :part]) + dot_nt(grad_upper, w_ref[:, part : 2 * part])
    if not first:
        y, dn = y + y_in[...].astype(F32), dn + dn_in[...].astype(F32)
    if last:
        give_tile(y.astype(BF), refs[:number], step)
        give_tile(dn.astype(BF), refs[number:], step)
    else:
        refs[0][...] = y.astype(BF)
        refs[1][...] = dn.astype(BF)
    gdown_ref[...] += dot_tn(grad_low, unit)
    ggate_ref[...] += dot_tn(low, grad_gate)
    gupper_ref[...] += dot_tn(low, grad_upper)


def feed(normed, grads, down, up, weight, sums, rows, start, last):
    block, width = normed[0].shape
    rank, number = down.shape[0], len(normed)
    deep, part = weight.shape[0], weight.shape[1] // 3
    narrow = sds((rank, part), F32)
    tokens = number * block
    if last:
        wide = sds((block, deep // LANES * LANES + LANES), BF)
        shapes, specs = [wide] * (2 * number), [whole_spec(wide.shape)] * (2 * number)
    else:
        shapes, specs = [sds((tokens, deep), BF)] * 2, [row_spec(rows, deep)] * 2
    first = not sums
    if first:
        shapes, specs = shapes + [sds((tokens, rank), BF)] * 2, specs + [row_spec(rows, rank)] * 2
    arrays = (*normed, *grads, down, up)
    size = weight.shape[0] * weight.shape[1]
    return weight_call(
        functools.partial(feed_kernel, weight, first, last, number),
        weight,
        (tokens // rows,),
        [whole_spec(a.shape) for a in arrays]
        + [pl.BlockSpec((rows, a.shape[1]), lambda t, *_: (start + t, 0)) for a in sums],
        specs + [whole_spec(narrow.shape)] * 3,
        shapes + [narrow] * 3,
        [pltpu.VMEM((rows, width), BF)] * 2 + weight.scratch(),
        cost(8 * tokens * size, 2 * size),
        [*arrays, *sums],
    )


def settle_first_kernel(fold, labels_ref, in_ref, down_ref, up_ref, hid_ref, gate_ref):
    slot = pl.program_id(0)
    local = down_ref.shape[-1]
    for ref in (down_ref, up_ref, hid_ref, gate_ref):
        ref[...] = jnp.zeros_like(ref)
    for s in range(in_ref.shape[0]):

        @pl.when(labels_ref[s] == slot)
        def _(s=s):
            for n, k in enumerate(DOWN_FIRST):
                down_ref[0, k] += in_ref[s, n].astype(F32)
            for n, k in enumerate(UP_FIRST):
                up_ref[0, k] += in_ref[s, len(DOWN_FIRST) + n].astype(F32)
            for k in range(fold):
                at, n = slice(k * local, (k + 1) * local), 4 + k
                hid_ref[0, :, at] += in_ref[s, n].astype(F32)
                gate_ref[0, 0, :, at] += in_ref[s, n + fold].astype(F32)
                gate_ref[0, 1, :, at] += in_ref[s, n + 2 * fold].astype(F32)


def settle_second_kernel(labels_ref, in_ref, down_in, up_in, down_ref, up_ref):
    del down_in, up_in
    slot = pl.program_id(0)
    downs, ups = down_ref.shape[1], up_ref.shape[1]
    for ref in (down_ref, up_ref):
        ref[...] = jnp.zeros_like(ref)
    for s in range(in_ref.shape[0]):

        @pl.when(labels_ref[s] == slot)
        def _(s=s):
            down_ref[0] += in_ref[s, :downs].astype(F32)
            up_ref[0] += in_ref[s, downs : downs + ups].astype(F32)


DOWN_FIRST, UP_FIRST = (4, 5), (7, 8)


def slot_spec(shape):
    return pl.BlockSpec((1,) + shape[1:], lambda i, *_, n=len(shape): (i,) + (0,) * (n - 1))


def settle_first(labels, grads, slots, fold):
    rank, local = grads.shape[2:]
    hidden = fold * local
    shapes = [
        (slots, 6, rank, local),
        (slots, 9, rank, local),
        (slots, rank, hidden),
        (slots, 2, rank, hidden),
    ]
    return pl.pallas_call(
        functools.partial(settle_first_kernel, fold),
        grid_spec=pltpu.PrefetchScalarGridSpec(
            num_scalar_prefetch=1,
            grid=(slots,),
            in_specs=[whole_spec(grads.shape)],
            out_specs=[slot_spec(s) for s in shapes],
        ),
        out_shape=[sds(s, F32) for s in shapes],
        compiler_params=params(),
        cost_estimate=cost(0, 0),
    )(labels, grads)


def settle_second(labels, grads, down, up):
    downs, ups = DOWN_FIRST[0], UP_FIRST[0]
    return pl.pallas_call(
        settle_second_kernel,
        grid_spec=pltpu.PrefetchScalarGridSpec(
            num_scalar_prefetch=1,
            grid=(down.shape[0],),
            in_specs=[whole_spec(grads.shape)] + [pl.BlockSpec(memory_space=pl.ANY)] * 2,
            out_specs=[
                slot_spec((1, downs) + down.shape[2:]),
                slot_spec((1, ups) + up.shape[2:]),
            ],
        ),
        out_shape=[sds(down.shape, F32), sds(up.shape, F32)],
        input_output_aliases={2: 0, 3: 1},
        compiler_params=params(),
        cost_estimate=cost(0, 0),
    )(labels, grads, down, up)


def chunks(hidden):
    return (hidden // 3,) * 3


def body(
    inputs,
    context,
    positions,
    adapter_index,
    self_in_weight,
    self_out_weight,
    cross_query_weight,
    cross_keyval_weight,
    cross_out_weight,
    feed_in_weight,
    feed_out_weight,
    norm_gains,
    norm_biases,
    adapter_down,
    adapter_down_hidden,
    adapter_up,
    adapter_up_hidden,
    out_cotangent,
    *,
    pairs,
    chips,
):
    group = Group(pairs, chips)
    members = 2 * pairs
    rows, width = inputs.shape[1], inputs.shape[2]
    block = self_in_weight.shape[0]
    local = self_in_weight.shape[2]
    hidden = feed_in_weight.shape[2]
    slots, rank = adapter_down.shape[0], adapter_down.shape[3]
    deep = width + rank
    parts = chunks(hidden)
    fold = hidden // local
    pieces = group.pieces
    gains, biases = norm_gains, norm_biases
    tile = min(256, members * rows)
    tiles = members * rows // tile
    near_tiles = tiles // pairs

    def packed(*parts):
        return jnp.concatenate(parts, axis=1)

    def stacked(*parts):
        return jnp.concatenate(parts, axis=0)

    def listed(values):
        return list(values) if isinstance(values, (list, tuple)) else [values]

    def piece(array, k, size):
        return lax.dynamic_slice_in_dim(array, pieces[k] * size, size, array.ndim - 1)

    def own(array):
        return piece(array, 0, local)

    near_chips = [1, 2] if chips == 4 else list(range(1, chips))
    chip_rows = [(group.chip ^ k) * 2 * block for k in range(chips)]
    one = [[c + o * block for c in chip_rows] for o in (group.core, 1 - group.core)]
    one += [[c + o * block for c in chip_rows] for o in (group.zhi, 1 - group.zhi)]
    row_places = jnp.stack(
        [r for found in one for r in found] + [jnp.zeros_like(group.core)]
        + [p * local for p in pieces] + [group.core]
    ).astype(jnp.int32)
    mine_at, other_at, first_at, second_at, zero = (n * chips for n in range(5))
    at_pieces = zero + 1
    core_at = at_pieces + members

    def chip_weight(own_entry, near, rest, low, columns, halves):
        weight = Weight((deep, columns), row_places)
        entries = [own_entry, *near]
        for k, (array, row) in zip([0, *near_chips], entries):
            weight.add(
                array,
                *[(row + r, block, c, columns, None, at + k, 0) for r, c, at in halves],
            )
        if rest:
            side_by_side = halves[1][0] == 0
            for n, (array, row) in enumerate(rest):
                size = block // 2 if side_by_side else block
                picked = halves if side_by_side else halves[n : n + 1]
                weight.add(
                    array,
                    *[
                        (row, size, c, columns, None, at + 3, n * size if side_by_side else 0)
                        for _, c, at in picked
                    ],
                )
        weight.add(low, (0, rank, 0, columns, None, zero, width))
        return weight

    stacked_halves = [(0, 0, first_at), (block, 0, second_at)]
    packed_halves = [(0, 0, mine_at), (0, 2 * local, other_at)]

    def spread(got, half_at, half, own_block):
        if got and chips == 4:
            turns = [
                got[1][half_at : half_at + half],
                got[0][half_at + half : half_at + 2 * half],
            ]
            if own_block is not None:
                turns = listed(step.mark(*[stacked(turn, own_block) for turn in turns]))
            return [xor_move(turn, "chip", 4, k) for turn, k in zip(turns, near_chips)]
        if own_block is None:
            return []
        return [xor_move(own_block, "chip", chips, k) for k in near_chips]

    def skip(half):
        return half if chips == 4 else 0

    def flat(*groups):
        return [x for g in groups for x in listed(g)]

    def wait_all(*groups):
        groups = [listed(g) for g in groups]
        values = iter(listed(step.wait(*flat(*groups))))
        return [[next(values) for _ in g] for g in groups]

    def swap_all(blocks):
        if not blocks:
            return []
        blocks = listed(step.wait(*blocks))
        return listed(step.wait(*[core_swap(b) for b in blocks]))

    shard_self = packed(*[self_in_weight[:, i] for i in range(3)], self_out_weight.T)
    step = Order(shard_self[:8, :128])
    self_from = [home_swap(shard_self), turned(shard_self)]
    stream_own, context_own = home_swap(inputs[0]), home_swap(context[0])
    index, positions = step.wait(adapter_index, positions)
    index_other, positions_other = step.wait(core_swap(index), core_swap(positions))
    index = jnp.where(group.home, index, index_other)[0]
    positions = jnp.where(group.home, positions, positions_other)[0]
    down = lax.dynamic_index_in_dim(adapter_down.transpose(0, 1, 3, 2), index, 0, keepdims=False)
    up = lax.dynamic_index_in_dim(adapter_up.transpose(0, 2, 1, 3), index, 0, keepdims=False)
    down, up = step.mark(down, up)
    low_self = packed(*[own(up[i]) for i in range(3)], own(down[1]))
    low_keyval = packed(own(up[5]), own(up[6]))
    low_cross = []
    for k in range(pairs):
        two = [
            (group.p ^ k) * local + core * pairs * local for core in (0, 1)
        ]
        low_cross.append(
            packed(
                *[
                    lax.dynamic_slice_in_dim(table[4], where, local, 1)
                    for table in (up, down)
                    for where in two
                ]
            )
        )
    low_cross = stacked(*low_cross)
    low_self, low_keyval, low_cross = step.mark(low_self, low_keyval, low_cross)
    keyval_parts = step.wait(cross_keyval_weight)
    keyval_parts = step.mark(keyval_parts[:, 0], keyval_parts[:, 1])
    shard_cross = step.mark(packed(cross_query_weight, cross_out_weight.T, *keyval_parts))
    far_cross = group.cross(shard_cross)
    blocks_at = [
        lax.dynamic_slice_in_dim(positions, pieces[k] * rows, rows, 0) for k in range(members)
    ]
    half = ROT // 2
    inverse = 10000.0 ** (-jnp.arange(half, dtype=F32) / half)
    angles = inverse[:, None] * step.wait(jnp.concatenate(blocks_at)).astype(F32)[None]
    tables = step.mark(*rotary_tables(*step.mark(jnp.cos(angles), jnp.sin(angles))))
    feed_in, feed_out = step.wait(feed_in_weight, feed_out_weight)
    gate_rows, upper_rows = step.mark(feed_in[:, 0], feed_in[:, 1])
    at = [sum(parts[:i]) for i in range(len(parts))]

    def feed_shard(i):
        to = slice(at[i], at[i] + parts[i])
        gate, upper, out = step.wait(gate_rows, upper_rows, feed_out)
        return step.mark(packed(gate[:, to], upper[:, to], out.T[:, to]))

    shard_feed = [feed_shard(i) for i in range(len(parts))]

    self_from = step.wait(*self_from)
    ready_self = step.mark(stacked(*self_from))
    near_self = spread([], 0, 0, ready_self)
    stream_own, context_own = step.wait(stream_own, context_own)
    stream_far, context_far = group.far_p(stream_own), group.far_p(context_own)
    (near_self,) = wait_all(near_self)
    rest_self = spread(near_self, 0, block, None)
    rest_self, stream_far, context_far, (far_cross,) = wait_all(
        rest_self, stream_far, context_far, [far_cross]
    )
    stream_other, *stream_far_other = swap_all([stream_own, *stream_far])
    stream = [stream_own, stream_other]
    for far, far_other in zip(stream_far, stream_far_other):
        stream += [far, far_other]
    self_weight = chip_weight(
        (ready_self, 0), [(g, 0) for g in near_self], [(g, 0) for g in rest_self], low_self,
        4 * local, stacked_halves,
    )

    mine = jnp.where(group.home, shard_cross, far_cross)
    given = jnp.where(group.home, far_cross, shard_cross)
    keyval_mine, keyval_give = mine[:, 2 * local :], given[:, 2 * local :]
    low_zhi = jnp.where(group.zhi == 0, shard_cross, far_cross)
    high_zhi = jnp.where(group.zhi == 0, far_cross, shard_cross)
    pair = packed(
        *[two[:, n * local : (n + 1) * local] for n in (0, 1) for two in (low_zhi, high_zhi)]
    )
    keyval_mine, keyval_give, pair = step.mark(keyval_mine, keyval_give, pair)
    (keyval_other,) = swap_all([keyval_give])
    ready_keyval = step.mark(stacked(packed(keyval_mine, keyval_other), pair))

    got_one = spread([], 0, 0, ready_keyval)
    pair_far = group.far_p(pair)
    feed_from = [[home_swap(step.wait(shard_feed[0])), turned(step.wait(shard_feed[0]))]]
    query, keys, values, low_one, normed_one = project_self(
        listed(step.wait(*stream)), gains[0:1], biases[0:1], down[0], self_weight, tables, tile
    )
    query, keys, values = step.mark(query, keys, values)
    heads_far, logsum_far, *y_far = attend_self(
        query, keys, values, self_weight, tile, near_tiles, tiles - near_tiles, rows
    )
    y_far = listed(step.mark(*y_far))

    def far_sums(*groups):
        others = iter(swap_all([g[2 * k + 1] for g in groups for k in range(pairs - 1)]))
        sums = [
            [group.near_sums(g[2 * k], next(others)).astype(BF) for k in range(pairs - 1)]
            for g in groups
        ]
        values = iter(listed(step.mark(*flat(*sums))))
        return [[next(values) for _ in s] for s in sums]

    def move_p(sums):
        return [xor_move(s, "p", pairs, k + 1) for k, s in enumerate(sums)]

    def sum_up(blocks, other, far):
        total = group.near_sums(blocks[0], other)
        for f in far:
            total = total + f.astype(F32)
        return step.mark(total)

    got_one, pair_far, feed_from[0] = wait_all(got_one, pair_far, feed_from[0])
    (y_sums,) = far_sums(y_far)

    far = move_p(y_sums)
    quarter = block // 2
    if chips == 4:
        turns = [
            stacked(got[start : start + quarter], got[start + block : start + block + quarter], pair_far[0])
            for got, start in ((got_one[1], 0), (got_one[0], quarter))
        ]
        turns = step.mark(*turns)
        got_two = [xor_move(turn, "chip", 4, k) for turn, k in zip(turns, near_chips)]
    else:
        got_two = flat(*[spread([], 0, 0, p) for p in pair_far])
    early = [ready_keyval, *got_one]
    early_swapped = [core_swap(b) for b in early]
    heads_near, logsum_near, *y_rows = attend_self(
        step.wait(query), keys, values, self_weight, tile, 0, near_tiles, rows
    )
    y_rows = listed(step.mark(*y_rows))
    far, got_two, early_swapped = wait_all(far, got_two, early_swapped)
    y_other, context_other, *swapped = swap_all([y_rows[1], context_own, *context_far])
    branch = [y_rows[0], y_other, *far]
    context_blocks = [context_own, context_other]
    for far, far_other in zip(context_far, swapped):
        context_blocks += [far, far_other]
    keyval_weight = chip_weight(
        (ready_keyval, 0), [(g, 0) for g in got_one],
        [(g, 0) for g in got_two] if chips == 4 else [], low_keyval, 2 * local, packed_halves,
    )
    down_context = step.mark(down[3].T)
    keyval, low_context = context_forward(at_pieces, context_blocks, keyval_weight, down_context)
    keyval = step.mark(keyval)

    keyval_far = group.far_p(keyval)
    cotangent_own = home_swap(step.wait(out_cotangent[0]))
    ready_feed = [step.mark(stacked(*feed_from[0]))]
    found = [(ready_keyval, block, block, 0, 0, 0)]
    found += [(g, block, block, k, 0, 0) for g, k in zip(got_one, near_chips)]
    if chips == 4:
        turns = [got_two[1][block : block + quarter], got_two[0][block + quarter :]]
        got_three = [xor_move(turn, "chip", 4, k) for turn, k in zip(turns, near_chips)]
        keyval_far, got_three = wait_all(keyval_far, got_three)
        found += [(g, 0, quarter, 3, n * quarter, 1) for n, g in enumerate(got_three)]
        found.append((pair_far[0], 0, block, 0, 0, 1))
        for n, (g, k) in enumerate(zip(got_two, near_chips)):
            found += [(g, block, block, k, 0, 1), (g, quarter, quarter, 3, n * quarter, 0)]
    else:
        (keyval_far,) = wait_all(keyval_far)
        count = len(near_chips)
        for n, p in enumerate(pair_far):
            found.append((p, 0, block, 0, 0, n + 1))
            found += [
                (g, 0, block, k, 0, n + 1)
                for g, k in zip(got_two[n * count : (n + 1) * count], near_chips)
            ]
    arrays = []
    for entry in found:
        if not any(entry[0] is a for a in arrays):
            arrays.append(entry[0])
    swapped = swap_all([keyval, *keyval_far, *arrays[len(early) :]])
    keyvals = [keyval, swapped[0]]
    for far, far_other in zip(keyval_far, swapped[1:]):
        keyvals += [far, far_other]
    others = early_swapped + swapped[1 + len(keyval_far) :]
    cotangent_own = step.wait(cotangent_own)
    cross_weight = Weight((pairs, deep, 4 * local), row_places)
    for array, other in zip(arrays, others):
        entries = [e[1:] for e in found if e[0] is array]
        for source, places in ((array, mine_at), (other, other_at)):
            cross_weight.add(
                source,
                *[
                    (row, size, 0, 4 * local, n, places + k, offset)
                    for row, size, k, offset, n in entries
                ],
            )
    cross_weight.add(
        low_cross, *[(n * rank, rank, 0, 4 * local, n, zero, width) for n in range(pairs)]
    )

    near_feed = [spread([], 0, 0, ready_feed[0])]
    feed_from.append([home_swap(step.wait(shard_feed[1])), turned(step.wait(shard_feed[1]))])
    cotangent_far = group.far_p(step.wait(cotangent_own))
    stream_own, *branch = step.wait(stream_own, *branch)

    (
        stream_one, stream_two, normed_two, normed_three, query_cross, heads_cross, logsum_cross,
        low_two, low_three, low_four,
    ) = cross_forward(
        stream_own, branch, up[3], up[7], down[2], gains, biases, cross_weight, keyvals, core_at,
    )
    normed_own = step.mark(normed_three)
    near_feed[0], cotangent_far, feed_from[1] = wait_all(
        near_feed[0], cotangent_far, feed_from[1]
    )
    ready_feed.append(step.mark(stacked(*feed_from[1])))

    normed_far = group.far_p(normed_own)
    near_feed.append(spread(near_feed[0], 0, block, ready_feed[1]))
    down_hidden = lax.dynamic_index_in_dim(
        adapter_down_hidden.transpose(0, 2, 1), index, 0, keepdims=False
    )
    up_hidden = lax.dynamic_index_in_dim(
        adapter_up_hidden.transpose(0, 2, 1, 3), index, 0, keepdims=False
    )
    feed_down, feed_up = piece(down_hidden, 0, hidden), piece(up_hidden, 0, hidden)
    feed_down, feed_gate, feed_upper = step.mark(feed_down, feed_up[0], feed_up[1])
    low_feed = [
        packed(feed_gate[:, to], feed_upper[:, to], feed_down[:, to])
        for to in [slice(a, a + p) for a, p in zip(at, parts)]
    ]
    low_feed = step.mark(*low_feed)
    near_feed[1], normed_far = wait_all(near_feed[1], normed_far)
    normed_other, cotangent_other, *swapped = swap_all(
        [normed_own, cotangent_own, *normed_far, *cotangent_far]
    )
    normed_blocks, cotangent_blocks = [normed_own, normed_other], [cotangent_own, cotangent_other]
    for far, far_other in zip(normed_far, swapped):
        normed_blocks += [far, far_other]
    for far, far_other in zip(cotangent_far, swapped[len(normed_far) :]):
        cotangent_blocks += [far, far_other]

    def feed_weight(i, first, rest):
        return chip_weight(
            (ready_feed[i], 0), [(g, first) for g in near_feed[i]], [(g, 0) for g in rest],
            low_feed[i], 3 * parts[i], stacked_halves,
        )

    def feed_pass(weight, sums, picked, start, last):
        normed, cotangent = wait_all(normed_blocks[picked], cotangent_blocks[picked])
        found = feed(normed, cotangent, down[5], up[8], weight, sums, tile, start, last)
        *values, gdown, ggate, gupper = found
        return listed(step.mark(*values)), [gdown, ggate, gupper]

    everything, far_only, near_only = slice(0, None), slice(2, None), slice(0, 2)

    feed_from.append([home_swap(step.wait(shard_feed[2])), turned(step.wait(shard_feed[2]))])
    rests = near_feed[1] if chips == 4 else []
    weight = feed_weight(0, 0, rests)
    rest_feed = spread(near_feed[1], skip(block), block, None)
    (y, dn, *lows), *feed_grads = feed_pass(weight, (), everything, 0, False)
    rest_feed, feed_from[2] = wait_all(rest_feed, feed_from[2])
    ready_feed.append(step.mark(stacked(*feed_from[2])))

    weight = feed_weight(1, skip(block), rest_feed)
    near_feed.append(spread([], 0, 0, ready_feed[2]))
    (y, dn), grads = feed_pass(weight, (*lows, y, dn), everything, 0, False)
    feed_grads.append(grads)
    (near_feed[2],) = wait_all(near_feed[2])
    (rest_feed,) = wait_all(spread(near_feed[2], 0, block, None)) if chips == 4 else ([],)
    weight = feed_weight(2, 0, rest_feed)
    found, grads = feed_pass(weight, (*lows, y, dn), far_only, near_tiles, True)
    y_far, dn_far = found[: len(found) // 2], found[len(found) // 2 :]

    dn_sums, y_sums = far_sums(dn_far, y_far)
    far = move_p(dn_sums)
    found, more = feed_pass(weight, (*lows, y, dn), near_only, 0, True)
    y_rows, dn_rows = found[:2], found[2:]
    feed_grads.append([a + b for a, b in zip(grads, more)])
    (far,) = wait_all(far)
    dn_other, y_other = swap_all([dn_rows[1], y_rows[1]])
    grad_normed = [dn_rows[0], dn_other, *far]

    far = move_p(step.mark(*y_sums) if len(y_sums) > 1 else [step.mark(*y_sums)])
    grad_stream, branch_grad, fixed_rows, near_rows, *keyval_rows = cross_back(
        cotangent_own, listed(step.wait(*grad_normed)), stream_one, stream_two, normed_two,
        query_cross, heads_cross, logsum_cross, low_three, low_four, up[7], down[5], down[2],
        gains, biases, cross_weight, keyvals, core_at,
    )
    branch_grad, *keyval_rows = step.mark(branch_grad, *keyval_rows)
    (far,) = wait_all(far)

    branch_far = group.far_p(branch_grad)
    (branch_other,) = swap_all([branch_grad])

    def back(grad, heads, logsum, first, before):
        return attend_back(
            grad, up[3], self_weight, query, keys, values, heads, logsum, tables, low_one, rank,
            tile, first, before,
        )

    grads = listed(step.wait(branch_grad, branch_other))
    near_back = step.mark(*back(grads, heads_near, logsum_near, 0, None))
    (branch_far,) = wait_all(branch_far)

    output, grad_up_eight = step.mark(
        *output_end(
            stream_two, [step.wait(y_rows[0]), y_other, *far], up[8], cotangent_own, members
        )
    )

    def taken(by_piece, k):
        return lax.dynamic_index_in_dim(by_piece, pieces[k], 0, keepdims=False)

    def taken_near(by_member, k):
        member = k // 2 * 2 + (group.core ^ (k % 2))
        return lax.dynamic_index_in_dim(by_member, member, 0, keepdims=False)

    first_rows = listed(
        step.mark(
            *[
                stacked(
                    taken(fixed_rows, k)[rank:], taken(grad_up_eight, k),
                    taken_near(near_rows, k)[:rank],
                )
                for k in range(members)
            ]
        )
    )
    swapped = swap_all([*branch_far, *first_rows[1::2], *keyval_rows[1::2]])
    branch_blocks = []
    for f, o in zip(branch_far, swapped):
        branch_blocks += [f, o]
    others = swapped[len(branch_far) :]
    first_sums, keyval_sums = (
        [group.near_sums(a, b) for a, b in zip(even[::2], other)]
        for even, other in ((first_rows, others[:pairs]), (keyval_rows, others[pairs:]))
    )
    moving = listed(step.mark(*[x.astype(BF) for x in first_sums[1:] + keyval_sums[1:]]))

    def columns(array):
        return array.reshape(rank, -1, local).transpose(1, 0, 2)

    def sent(parts):
        parts.append(jnp.full((1, rank, local), index, F32))
        grads = step.mark(jnp.concatenate(parts, axis=0).astype(BF))
        return [home_swap(grads), turned_back(grads)]

    def to_chips(blocks):
        both = step.mark(stacked(*blocks))
        return [both] + [xor_move(both, "chip", chips, k) for k in range(1, chips)]

    def every(blocks):
        grads = stacked(*blocks)
        grads = grads.reshape(-1, grads.shape[0] // (2 * chips), rank, local)
        return grads, grads[:, -1, 0, 0].astype(jnp.int32)

    def total(own, far):
        for f in far:
            own = own + f.astype(F32)
        return own

    first_far, keyval_far = move_p(moving[: pairs - 1]), move_p(moving[pairs - 1 :])
    block_output = home_swap(step.wait(output))
    branch_blocks = listed(step.wait(*branch_blocks))
    grad_mixed, grad_down_one, grad_up_self = back(
        branch_blocks, heads_far, logsum_far, near_tiles, near_back
    )
    grad_mixed = step.mark(grad_mixed)
    first_far, keyval_far, (block_output,) = wait_all(first_far, keyval_far, [block_output])
    summed = total(first_sums[0], first_far).reshape(-1, rank, local)
    first = sent(
        [
            summed[3:4],
            summed[0:1],
            summed[1:3],
            *[columns(jnp.concatenate(g, axis=1)) for g in zip(*feed_grads)],
        ]
    )
    low_far, *dn_far = step.mark(
        *project_back(
            step.wait(grad_mixed), self_weight, tile, near_tiles, tiles - near_tiles, rows, rank
        )
    )
    (first,) = wait_all(first)
    (dn_sums,) = far_sums(dn_far)

    far = move_p(dn_sums)
    low_near, *dn_rows = step.mark(
        *project_back(step.wait(grad_mixed), self_weight, tile, 0, near_tiles, rows, rank)
    )
    (far,) = wait_all(far)
    first = to_chips(first)
    grad_keyval = step.mark(total(keyval_sums[0], keyval_far).astype(BF))
    grad_up_keyval, *found = step.mark(
        *context_back(
            at_pieces, context_blocks, keyval_weight, down_context, low_context, grad_keyval
        )
    )
    context_rows, grad_down_three = found[:members], found[members:]
    own_rows = step.mark(
        self_rows(step.wait(low_near), low_far, normed_one, low_two, branch_grad, members)
    )
    second_rows = listed(
        step.mark(
            *[
                stacked(
                    taken(own_rows, k), taken(fixed_rows, k)[:rank], grad_down_three[k],
                    taken_near(near_rows, k)[rank:],
                )
                for k in range(members)
            ]
        )
    )
    dn_other, *others = swap_all([dn_rows[1], *second_rows[1::2], *context_rows[1::2]])
    second_sums, context_sums = (
        [group.near_sums(a, b) for a, b in zip(even[::2], other)]
        for even, other in ((second_rows, others[:pairs]), (context_rows, others[pairs:]))
    )
    moving = listed(step.mark(*[x.astype(BF) for x in second_sums[1:] + context_sums[1:]]))

    second_far, context_far = move_p(moving[: pairs - 1]), move_p(moving[pairs - 1 :])
    grad_inputs = step.mark(
        input_end(stream_own, grad_stream, [dn_rows[0], dn_other, *far], down[0], gains[0:1])
    )
    second_far, context_far, first = wait_all(second_far, context_far, first)
    summed = total(second_sums[0], second_far).reshape(-1, rank, local)
    second = sent(
        [
            summed[0:1],
            grad_down_one[None],
            summed[2:4],
            columns(grad_up_self),
            summed[1:2],
            summed[4:5],
            columns(grad_up_keyval),
        ]
    )
    grad_inputs = home_swap(step.wait(grad_inputs))
    grad_context = home_swap(step.mark(total(context_sums[0], context_far).astype(BF)))
    first, labels = every(first)
    grad_down, grad_up, grad_hidden, grad_gate = settle_first(labels, first, slots, fold)
    grad_down, grad_up = step.mark(grad_down, grad_up)
    (second,) = wait_all(second)
    (second,) = wait_all(to_chips(second))
    second, labels = every(second)
    labels = labels + (step.token[0, 0].astype(F32) * 0.0).astype(jnp.int32)
    grad_down, grad_up = settle_second(labels, second, grad_down, grad_up)
    return (
        block_output[None],
        grad_inputs.astype(F32)[None],
        grad_context.astype(F32)[None],
        grad_down.transpose(0, 1, 3, 2),
        grad_hidden.transpose(0, 2, 1),
        grad_up.transpose(0, 2, 1, 3),
        grad_gate.transpose(0, 2, 1, 3),
    )


def solution(mesh):
    members = mesh.shape["tensor"]
    chips = mesh.shape["dp"] // 2
    mesh = Mesh(
        mesh.devices.reshape(chips, 2, 2, members // 2), ("chip", "core", "zhi", "p")
    )
    dp, tensor = ("chip", "core"), ("zhi", "p")
    in_specs = (
        P(dp, tensor, None),
        P(dp, None, tensor),
        P(dp, None),
        P(dp),
        P(dp, None, tensor),
        P(tensor, dp),
        P(dp, tensor),
        P(dp, None, tensor),
        P(tensor, dp),
        P(dp, None, tensor),
        P(tensor, dp),
        P(),
        P(),
        P(),
        P(),
        P(),
        P(),
        P(dp, tensor, None),
    )
    out_specs = (
        P(dp, tensor, None),
        P(dp, tensor, None),
        P(dp, None, tensor),
        P(None, None, tensor, None),
        P(None, tensor, None),
        P(None, None, None, tensor),
        P(None, None, None, tensor),
    )

    def run(*args):
        return body(*args, pairs=members // 2, chips=chips)

    return jax.shard_map(run, mesh=mesh, in_specs=in_specs, out_specs=out_specs, check_vma=False)
```

```python
import functools

import jax
import jax.numpy as jnp
from jax import lax
from jax.experimental import pallas as pl
from jax.experimental.pallas import tpu as pltpu
from jax.sharding import Mesh, PartitionSpec as P

HEAD_DIM = 64
ROT = 32
EPSILON = 1e-05
F32 = jnp.float32
BF = jnp.bfloat16
SWAP = ((0, 1), (1, 0))
LANES = 128
VMEM_LIMIT = 56 * 1024 * 1024


def dot(left, right):
    return jnp.dot(left, right, preferred_element_type=F32)


def dot_nt(left, right):
    return lax.dot_general(left, right, (((1,), (1,)), ((), ())), preferred_element_type=F32)


def dot_tn(left, right):
    return lax.dot_general(left, right, (((0,), (0,)), ((), ())), preferred_element_type=F32)


class Order:
    def __init__(self, first):
        self.token = first

    def wait(self, *values):
        *values, self.token = lax.optimization_barrier((*values, self.token))
        return values[0] if len(values) == 1 else values

    mark = wait


def core_swap(x):
    return lax.ppermute(x, "core", SWAP)


def xor_move(x, axis, size, k):
    return lax.ppermute(x, axis, [(i, i ^ k) for i in range(size)])


def home_swap(x):
    return lax.ppermute(x, ("core", "zhi"), [(0, 0), (1, 2), (2, 1), (3, 3)])


def turned(x):
    return lax.ppermute(x, ("core", "zhi"), [(0, 1), (1, 3), (2, 0), (3, 2)])


def turned_back(x):
    return lax.ppermute(x, ("core", "zhi"), [(0, 2), (1, 0), (2, 3), (3, 1)])


class Group:
    def __init__(self, pairs, chips):
        self.pairs, self.chips = pairs, chips
        self.core, self.zhi, self.p = (lax.axis_index(n) for n in ("core", "zhi", "p"))
        self.chip = lax.axis_index("chip")
        self.home = self.core == self.zhi
        self.pieces = [
            (self.core ^ kc) * pairs + (self.p ^ kp) for kp in range(pairs) for kc in (0, 1)
        ]

    def far_p(self, own):
        return [xor_move(own, "p", self.pairs, k) for k in range(1, self.pairs)]

    def near_sums(self, own, other):
        return own.astype(F32) + other.astype(F32)

    def cross(self, shard):
        return xor_move(shard, "zhi", 2, 1)

    def spread_one(self, block):
        if self.chips == 4:
            return [xor_move(block, "chip", 4, k) for k in (1, 2)]
        return [xor_move(block, "chip", self.chips, k) for k in range(1, self.chips)]

    def spread_two(self, got):
        if self.chips != 4:
            return []
        half = got[0].shape[0] // 2
        return [xor_move(got[1][:half], "chip", 4, 1), xor_move(got[0][half:], "chip", 4, 2)]

    def places(self, rows):
        if self.chips == 4:
            diagonal = (self.chip ^ 3) * rows
            return [(self.chip ^ 1) * rows, (self.chip ^ 2) * rows, diagonal, diagonal + rows // 2]
        return [(self.chip ^ k) * rows for k in range(1, self.chips)]


class Weight:
    def __init__(self, shape, places):
        self.shape, self.places, self.arrays, self.moves = shape, places, [], []

    def add(self, array, *parts):
        self.moves += [(len(self.arrays), *part) for part in parts]
        self.arrays.append(array)

    @property
    def count(self):
        return len(self.arrays)

    def specs(self):
        return [pl.BlockSpec(memory_space=pl.ANY)] * self.count

    def columns(self, start, size):
        if size % 128 or start % 128:
            return 0, self.shape[-1], start
        return start, size, 0

    def scratch(self, size=None):
        shape = self.shape if size is None else self.shape[:-1] + (size,)
        return [pltpu.VMEM(shape, BF), pltpu.SemaphoreType.DMA((len(self.moves),))]

    def at_first(self, step, refs, places_ref, target, sems, start=0, size=None):
        def begin():
            @pl.when(step == 0)
            def _():
                self.bring(refs, places_ref, target, sems, start, size)

        def end():
            @pl.when(step == 0)
            def _():
                wait_for(self.bring(refs, places_ref, target, sems, start, size, go=False))

        return begin, end

    def bring(self, refs, places_ref, target, sems, start=0, size=None, go=True):
        copies = []
        for number, (source, row, rows, column, columns, lead, place, offset) in enumerate(self.moves):
            at = pl.ds(pl.multiple_of(places_ref[place] + offset, 16), rows)
            to = target.at[at] if lead is None else target.at[lead, at]
            if size is not None:
                column, columns = column + start, size
            found = refs[source].at[pl.ds(row, rows), pl.ds(column, columns)]
            copies.append(pltpu.make_async_copy(found, to, sems.at[number]))
        if go:
            for copy in copies:
                copy.start()
        return copies


def wait_for(copies):
    for copy in copies:
        copy.wait()


def weight_call(kernel, weight, grid, in_specs, out_specs, out_shape, scratch, estimate, arrays):
    return pl.pallas_call(
        kernel,
        grid_spec=pltpu.PrefetchScalarGridSpec(
            num_scalar_prefetch=1,
            grid=grid,
            in_specs=weight.specs() + in_specs,
            out_specs=out_specs,
            scratch_shapes=scratch,
        ),
        out_shape=out_shape,
        compiler_params=params(),
        cost_estimate=estimate,
    )(weight.places, *weight.arrays, *arrays)


def stats(stream):
    average = jnp.mean(stream, axis=-1, keepdims=True)
    centred = stream - average
    variance = jnp.mean(centred * centred, axis=-1, keepdims=True)
    scale = lax.rsqrt(variance + EPSILON)
    return centred * scale, scale


def layer_norm(stream, gain, bias):
    return (stats(stream)[0] * gain + bias).astype(BF)


def norm_backward(stream, gain, grad):
    unit, scale = stats(stream)
    grad = grad * gain
    return scale * (
        grad
        - jnp.mean(grad, axis=-1, keepdims=True)
        - unit * jnp.mean(grad * unit, axis=-1, keepdims=True)
    )


def turn(x, cosines, left_sines, right_sines):
    breadth = 2 * HEAD_DIM if x.shape[1] % (2 * HEAD_DIM) == 0 else HEAD_DIM
    half = ROT // 2
    for at in range(0, x.shape[1], breadth):
        group = x[:, at : at + breadth]
        if breadth % 128 == 0:
            left, right = pltpu.roll(group, breadth - half, 1), pltpu.roll(group, half, 1)
        else:
            left = jnp.concatenate([group[:, half:], group[:, :half]], axis=1)
            right = jnp.concatenate([group[:, -half:], group[:, :-half]], axis=1)
        yield (
            at,
            breadth,
            group * cosines[:, :breadth]
            + left * left_sines[:, :breadth]
            + right * right_sines[:, :breadth],
        )


def head_sums(product):
    columns = product.shape[1]
    rows = -(-columns // HEAD_DIM // 8) * 8
    head = lax.broadcasted_iota(jnp.int32, (rows, columns), 0)
    lane = lax.broadcasted_iota(jnp.int32, (rows, columns), 1)
    picked = jnp.where(lane // HEAD_DIM == head, 1.0, 0.0).astype(F32)
    return lax.dot_general(
        picked, product, (((1,), (1,)), ((), ())),
        precision=lax.Precision.HIGHEST, preferred_element_type=F32,
    )


def whole_spec(shape):
    return pl.BlockSpec(shape, lambda *_: (0,) * len(shape))


def row_spec(rows, columns):
    return pl.BlockSpec((rows, columns), lambda t, *_: (t, 0))


def take_tile(refs, tile_ref, step):
    rows, tile = refs[0].shape[0], tile_ref.shape[0]
    for i, ref in enumerate(refs):

        @pl.when(step == i * rows // tile)
        def _(i=i, ref=ref):
            tile_ref[i * rows % tile : i * rows % tile + rows, :] = ref[...]


def give_tile(value, refs, step):
    rows, (tile, columns) = refs[0].shape[0], value.shape
    for i, ref in enumerate(refs):

        @pl.when(step == i * rows // tile)
        def _(i=i, ref=ref):
            ref[:, :columns] = value[i * rows % tile : i * rows % tile + rows]
            ref[:, columns:] = jnp.zeros((rows, ref.shape[1] - columns), ref.dtype)


def total_of(refs):
    total = refs[0][...].astype(F32)
    for ref in refs[1:]:
        total = total + ref[...].astype(F32)
    return total


def by_piece(ref, row, value):
    local = ref.shape[2]
    for k in range(ref.shape[0]):
        ref[k, row : row + value.shape[0], :] = value[:, k * local : (k + 1) * local].astype(
            ref.dtype
        )


def params(semantics=1):
    return pltpu.CompilerParams(
        dimension_semantics=("arbitrary",) * semantics, vmem_limit_bytes=VMEM_LIMIT
    )


def cost(flops, moved, exps=0):
    return pl.CostEstimate(
        flops=int(flops) or 1000, bytes_accessed=int(moved) or 1000, transcendentals=int(exps)
    )


def sds(shape, dtype):
    return jax.ShapeDtypeStruct(shape, dtype)


def query_kernel(weight, part, count, places_ref, *refs):
    w_refs, refs = refs[: weight.count], refs[weight.count :]
    blocks, (gain_ref, bias_ref, down_ref, cos_ref, left_ref, right_ref), refs = (
        refs[:count],
        refs[count : count + 6],
        refs[count + 6 :],
    )
    q_ref, k_ref, v_ref, low_ref, n_ref, x_ref, w_ref, sems = refs
    step = pl.program_id(0)

    begin, end = weight.at_first(step, w_refs, places_ref, w_ref, sems, *part[:2])
    begin()
    take_tile(blocks, x_ref, step)
    local, width = q_ref.shape[1], x_ref.shape[1]
    normed = layer_norm(x_ref[...].astype(F32), gain_ref[...], bias_ref[...])
    n_ref[...] = normed
    low = dot_nt(normed, down_ref[...]).astype(BF)
    low_ref[...] = low
    end()
    at = slice(part[2], part[2] + 3 * local)
    mixed = dot(normed, w_ref[:width, at]) + dot(low, w_ref[width:, at])
    tables = cos_ref[...], left_ref[...], right_ref[...]
    for at, breadth, turned in turn(mixed[:, :local], *tables):
        q_ref[:, at : at + breadth] = (turned * HEAD_DIM**-0.5).astype(BF)
    for at, breadth, turned in turn(mixed[:, local : 2 * local], *tables):
        k_ref[:, at : at + breadth] = turned.astype(BF)
    v_ref[...] = mixed[:, 2 * local :].astype(BF)


def project_self(blocks, gain, bias, down, weight, tables, rows):
    width = blocks[0].shape[1]
    tokens = len(blocks) * blocks[0].shape[0]
    local = weight.shape[1] // 4
    part = weight.columns(0, 3 * local)
    return weight_call(
        functools.partial(query_kernel, weight, part, len(blocks)),
        weight,
        (tokens // rows,),
        [whole_spec(b.shape) for b in blocks]
        + [whole_spec(gain.shape), whole_spec(bias.shape), whole_spec(down.shape)]
        + [row_spec(rows, t.shape[1]) for t in tables],
        [row_spec(rows, local)] * 3 + [row_spec(rows, down.shape[0]), row_spec(rows, width)],
        [sds((tokens, local), BF)] * 3
        + [sds((tokens, down.shape[0]), BF), sds((tokens, width), BF)],
        [pltpu.VMEM((rows, width), BF), *weight.scratch(part[1])],
        cost(8 * tokens * width * local, 8 * width * local),
        [*blocks, gain, bias, down, *tables],
    )


def attend_kernel(weight, part, places_ref, *refs):
    w_refs, refs = refs[: weight.count], refs[weight.count :]
    q_ref, k_ref, v_ref, o_ref, lse_ref, *y_refs, w_ref, sems = refs
    rows, local = q_ref.shape
    step = pl.program_id(0)

    begin, end = weight.at_first(step, w_refs, places_ref, w_ref, sems, *part[:2])
    begin()
    lanes = lax.broadcasted_iota(jnp.int32, (rows, 128), 1)
    logsums = jnp.zeros((rows, 128), F32)
    for head in range(local // HEAD_DIM):
        at = slice(head * HEAD_DIM, (head + 1) * HEAD_DIM)
        scores = dot_nt(q_ref[:, at], k_ref[:, at])
        top = jnp.max(scores, axis=1, keepdims=True)
        powers = jnp.exp(scores - top)
        total = jnp.sum(powers, axis=1, keepdims=True)
        out = dot(powers.astype(BF), v_ref[:, at]) / total
        o_ref[:, at] = out.astype(BF)
        logsums = jnp.where(lanes == head, top + jnp.log(total), logsums)
    lse_ref[...] = logsums.T[: lse_ref.shape[0]]
    end()
    y = dot_nt(o_ref[...], w_ref[:, part[2] : part[2] + local]).astype(BF)
    give_tile(y, y_refs, step)


def wide_of(weight):
    return weight.shape[-2] // LANES * LANES + LANES


def attend_self(query, keys, values, weight, rows, first, count, block):
    tokens, local = query.shape
    heads = -(-local // HEAD_DIM // 8) * 8
    part = weight.columns(3 * local, local)
    blocks = count * rows // block
    return weight_call(
        functools.partial(attend_kernel, weight, part),
        weight,
        (count,),
        [
            pl.BlockSpec((rows, local), lambda t, *_: (first + t, 0)),
            whole_spec(keys.shape),
            whole_spec(values.shape),
        ],
        [row_spec(rows, local), pl.BlockSpec((heads, rows), lambda t, *_: (0, t))]
        + [whole_spec((block, wide_of(weight)))] * blocks,
        [sds((count * rows, local), BF), sds((heads, count * rows), F32)]
        + [sds((block, wide_of(weight)), BF)] * blocks,
        weight.scratch(part[1]),
        cost(16 * count * rows * tokens * local, 8 * query.size, count * rows * tokens),
        [query, keys, values],
    )


def attend_back_kernel(weight, part, first, last, tiles, number, blocks, places_ref, *refs):
    w_refs, refs = refs[: weight.count], refs[weight.count :]
    grads, refs = refs[:number], refs[number:]
    (
        up_ref, q_ref, k_ref, v_ref, o_ref, lse_ref, cos_ref, left_ref, right_ref, low_ref,
    ), refs = refs[:10], refs[10:]
    *refs, g_ref, w_ref, sems = refs
    begin, end = weight.at_first(pl.program_id(0), w_refs, places_ref, w_ref, sems, *part[:2])
    begin()
    take_tile(grads, g_ref, pl.program_id(0))
    if not first:
        (mq_ref, gk_in, gv_in, down_in), refs = refs[:4], refs[4:]
    if last:
        (n_ref, z_ref, r_ref), refs = refs[:3], refs[3:]
        (down_ref, gup_ref, rows_ref), refs = refs[:3], refs[3:]
        dn_refs, (m_ref, gk_ref, gv_ref) = refs[:blocks], refs[blocks:]
    else:
        m_ref, gk_ref, gv_ref, down_ref = refs
    step, rows = pl.program_id(0), q_ref.shape[0]
    width, local = g_ref.shape[1], q_ref.shape[1]
    at_rows = pl.ds(pl.multiple_of((step + tiles) * rows, rows), rows)
    at_query = at_rows if last else pl.ds(pl.multiple_of(step * rows, rows), rows)

    @pl.when(step == 0)
    def _():
        if first:
            gk_ref[...] = jnp.zeros_like(gk_ref)
            gv_ref[...] = jnp.zeros_like(gv_ref)
            down_ref[...] = jnp.zeros_like(down_ref)
        else:
            gk_ref[...] = gk_in[...]
            gv_ref[...] = gv_in[...]
            down_ref[...] = down_in[...]
            m_ref[: mq_ref.shape[0], :local] = mq_ref[...]

    grad = g_ref[...]
    grad_low = dot_nt(grad, up_ref[...]).astype(BF)
    end()
    at = slice(part[2], part[2] + local)
    grad_out = dot(grad, w_ref[:width, at]) + dot(grad_low, w_ref[width:, at])
    grad_out = grad_out.astype(BF)
    out = o_ref[...]
    down_ref[...] += dot_tn(grad_low, out)
    product = grad_out.astype(F32) * out.astype(F32)
    deltas = head_sums(product)
    parts = []
    for head in range(local // HEAD_DIM):
        at = slice(head * HEAD_DIM, (head + 1) * HEAD_DIM)
        q, k, v, g = q_ref[:, at], k_ref[:, at], v_ref[:, at], grad_out[:, at]
        delta = deltas[head : head + 1]
        probs = jnp.exp(dot_nt(k, q) - lse_ref[head : head + 1, :])
        grad_scores = (probs * (dot_nt(v, g) - delta)).astype(BF)
        gv_ref[:, at] += dot(probs.astype(BF), g)
        gk_ref[:, at] += dot(grad_scores, q)
        parts.append(dot_tn(grad_scores, k) * HEAD_DIM**-0.5)
    tables = cos_ref[at_rows, :], -left_ref[at_rows, :], -right_ref[at_rows, :]
    for at, breadth, turned in turn(jnp.concatenate(parts, axis=1), *tables):
        m_ref[at_query, at : at + breadth] = turned.astype(BF)

    if last:

        @pl.when(step == pl.num_programs(0) - 1)
        def _():
            tables = cos_ref[...], -left_ref[...], -right_ref[...]
            for at, breadth, turned in turn(gk_ref[...], *tables):
                m_ref[:, local + at : local + at + breadth] = turned.astype(BF)
            m_ref[:, 2 * local :] = gv_ref[...].astype(BF)
            gup_ref[...] = dot_tn(low_ref[...], m_ref[...])
            rank, block = up_ref.shape[0], dn_refs[0].shape[0]
            down = 0.0
            for i, ref in enumerate(dn_refs):
                at = slice(i * block, (i + 1) * block)
                value = dot_nt(m_ref[at, :], w_ref[:, : 3 * local]).astype(BF)
                ref[:, : width + rank] = value
                ref[:, width + rank :] = jnp.zeros((block, ref.shape[1] - width - rank), BF)
                down = down + dot_tn(value[:, width:], n_ref[at, :])
            by_piece(rows_ref, 0, down)
            by_piece(rows_ref, rank, dot_tn(z_ref[...], r_ref[...]))


def attend_back(
    grads, up, weight, query, keys, values, out, lse, tables, low, rows, start, before, ends
):
    tokens, local = query.shape
    block, width = grads[0].shape
    rank = up.shape[0]
    count = len(grads) * block // rows
    first, last = before is None, ends is not None
    before = () if first else before
    ends = ends if last else ()
    sums = [sds((tokens, local), F32)] * 2 + [sds((rank, local), F32)]
    blocks = tokens // block if last else 0
    if last:
        members = width // local
        shapes = [sums[2], sds((rank, 3 * local), F32), sds((members, 2 * rank, local), BF)]
        shapes += [sds((block, wide_of(weight)), BF)] * blocks
        scratch = [pltpu.VMEM((tokens, 3 * local), BF)]
        scratch += [pltpu.VMEM((tokens, local), F32)] * 2
        part = 0, 4 * local, 3 * local
    else:
        shapes, scratch = [sds((count * rows, local), BF), *sums], []
        part = weight.columns(3 * local, local)
    scratch.append(pltpu.VMEM((rows, width), BF))

    def tile(columns):
        return pl.BlockSpec((rows, columns), lambda t, *_: (start + t, 0))

    return weight_call(
        functools.partial(attend_back_kernel, weight, part, first, last, start, len(grads), blocks),
        weight,
        (count,),
        [
            *[whole_spec(g.shape) for g in grads],
            whole_spec(up.shape),
            tile(local),
            whole_spec(keys.shape),
            whole_spec(values.shape),
            row_spec(rows, local),
            pl.BlockSpec((lse.shape[0], rows), lambda t, *_: (0, t)),
            *[whole_spec(t.shape) for t in tables],
            whole_spec(low.shape),
            *[whole_spec(b.shape) for b in before],
            *[whole_spec(e.shape) for e in ends],
        ],
        [whole_spec(s.shape) for s in shapes],
        shapes,
        scratch + weight.scratch(part[1]),
        cost(40 * count * rows * tokens * local, 10 * query.size, count * rows * tokens),
        [*grads, up, query, keys, values, out, lse, *tables, low, *before, *ends],
    )


def in_order(swap, first, second):
    keep = swap == 0
    return jnp.where(keep, first, second), jnp.where(keep, second, first)


def cross_kernel(weight, members, local, core_at, places_ref, *refs):
    w_refs, refs = refs[: weight.count], refs[weight.count :]
    *refs, w_ref, sems = refs
    copies = weight.bring(w_refs, places_ref, w_ref, sems)
    (x_ref, up_self_ref, up_cross_ref, down_ref, gain_ref, bias_ref), refs = refs[:6], refs[6:]
    kv_refs, refs = refs[:members], refs[members:]
    y_refs, refs = refs[:-10], refs[-10:]
    branch = total_of(y_refs)
    s1_ref, s2_ref, n2_ref, n3_ref, q_ref, o_ref, lse_ref, z2_ref, u_ref, z4_ref = refs
    rows, width = x_ref.shape
    rank = down_ref.shape[0]
    deep = slice(width, width + rank)
    low = branch[:, deep].astype(BF)
    z2_ref[...] = low
    stream = x_ref[...].astype(F32) + branch[:, :width] + dot(low, up_self_ref[...])
    s1_ref[...] = stream
    normed = layer_norm(stream, gain_ref[1:2, :], bias_ref[1:2, :])
    n2_ref[...] = normed
    low = dot_nt(normed, down_ref[...]).astype(BF)
    u_ref[...] = low
    total = jnp.zeros((rows, width + rank), F32)
    wait_for(copies)
    both = 2 * local
    for n in range(members // 2):
        query = dot(normed, w_ref[n, :width, :both]) + dot(low, w_ref[n, deep, :both])
        query = (query * HEAD_DIM**-0.5).astype(BF)
        q_ref[:, n * both : (n + 1) * both] = query
        found = in_order(places_ref[core_at], kv_refs[2 * n][...], kv_refs[2 * n + 1][...])
        parts, logsums = [], []
        for head in range(both // HEAD_DIM):
            keyval, own = found[head * HEAD_DIM // local], head * HEAD_DIM % local
            keys = keyval[:, own : own + HEAD_DIM]
            values = keyval[:, local + own : local + own + HEAD_DIM]
            scores = dot_nt(keys, query[:, head * HEAD_DIM : (head + 1) * HEAD_DIM])
            top = jnp.max(scores, axis=0, keepdims=True)
            powers = jnp.exp(scores - top)
            sums = jnp.sum(powers, axis=0, keepdims=True)
            parts.append(dot_tn(values, powers.astype(BF)) / sums)
            logsums.append(top + jnp.log(sums))
        out = jnp.concatenate(parts, axis=0).T.astype(BF)
        o_ref[:, n * both : (n + 1) * both] = out
        lse_ref[n] = jnp.concatenate(logsums, axis=0)
        total = total + dot_nt(out, w_ref[n, :, both:])
    low = total[:, deep].astype(BF)
    z4_ref[...] = low
    stream = stream + total[:, :width] + dot(low, up_cross_ref[...])
    s2_ref[...] = stream
    n3_ref[...] = layer_norm(stream, gain_ref[2:3, :], bias_ref[2:3, :])


def cross_forward(x, ys, up_self, up_cross, down, gains, biases, weight, keyvals, core_at):
    rows, width = x.shape
    members, local = len(keyvals), weight.shape[2] // 4
    plain, wide = sds((rows, width), BF), sds((rows, width), F32)
    low = sds((rows, down.shape[0]), BF)
    logsums = sds((members // 2, 2 * local // HEAD_DIM, rows), F32)
    shapes = [wide, wide, plain, plain, plain, plain, logsums, low, low, low]
    arrays = [x, up_self, up_cross, down, gains, biases, *keyvals, *ys]
    return weight_call(
        functools.partial(cross_kernel, weight, members, local, core_at),
        weight,
        (1,),
        [whole_spec(a.shape) for a in arrays],
        [whole_spec(o.shape) for o in shapes],
        shapes,
        weight.scratch(),
        cost(24 * rows * width * width, 8 * width * width),
        arrays,
    )


def cross_back_kernel(weight, members, local, core_at, places_ref, *refs):
    w_refs, refs = refs[: weight.count], refs[weight.count :]
    *refs, w_ref, sems = refs
    copies = weight.bring(w_refs, places_ref, w_ref, sems)
    (
        g_ref, s1_ref, s2_ref, n2_ref, q_ref, o_ref, lse_ref, u_ref, z4_ref,
        up_ref, down5_ref, down2_ref, gain_ref, bias_ref,
    ), refs = refs[:14], refs[14:]
    kv_refs, refs = refs[:members], refs[members:]
    dn_refs, (r1_ref, r1b_ref, fixed_ref, near_ref, *gkv_refs) = (
        refs[: -4 - members],
        refs[-4 - members :],
    )
    summed = total_of(dn_refs)
    width = g_ref.shape[1]
    rank = up_ref.shape[0]
    deep = slice(width, width + rank)
    stream = s2_ref[...]
    low = summed[:, deep].astype(BF)
    grad_normed = summed[:, :width] + dot(low, down5_ref[...])
    normed = layer_norm(stream, gain_ref[2:3, :], bias_ref[2:3, :])
    by_piece(fixed_ref, rank, dot_tn(low, normed))
    grad = g_ref[...].astype(F32) + norm_backward(stream, gain_ref[2:3, :], grad_normed)
    branch = grad.astype(BF)
    low = dot_nt(branch, up_ref[...]).astype(BF)
    by_piece(fixed_ref, 2 * rank, dot_tn(z4_ref[...], branch))
    by_piece(near_ref, 0, dot_tn(low, o_ref[...]))
    total = jnp.zeros((g_ref.shape[0], width + rank), F32)
    wait_for(copies)
    both, swap = 2 * local, places_ref[core_at]
    for n in range(members // 2):
        columns = slice(n * both, (n + 1) * both)
        grad_out = dot(branch, w_ref[n, :width, both:]) + dot(low, w_ref[n, deep, both:])
        grad_out = grad_out.astype(BF)
        query = q_ref[:, columns]
        deltas = head_sums(grad_out.astype(F32) * o_ref[:, columns].astype(F32))
        found = in_order(swap, kv_refs[2 * n][...], kv_refs[2 * n + 1][...])
        queries, keys, values = [], [], []
        for head in range(both // HEAD_DIM):
            keyval, own = found[head * HEAD_DIM // local], head * HEAD_DIM % local
            key = keyval[:, own : own + HEAD_DIM]
            value = keyval[:, local + own : local + own + HEAD_DIM]
            at = slice(head * HEAD_DIM, (head + 1) * HEAD_DIM)
            q, g = query[:, at], grad_out[:, at]
            probs = jnp.exp(dot_nt(key, q) - lse_ref[n, head : head + 1, :])
            grad_scores = (probs * (dot_nt(value, g) - deltas[head : head + 1])).astype(BF)
            queries.append(dot_tn(key, grad_scores))
            keys.append(dot(grad_scores, q))
            values.append(dot(probs.astype(BF), g))
        grad_query = (jnp.concatenate(queries, axis=0).T * HEAD_DIM**-0.5).astype(BF)
        half = len(keys) // 2
        first = jnp.concatenate(keys[:half] + values[:half], axis=1).astype(BF)
        second = jnp.concatenate(keys[half:] + values[half:], axis=1).astype(BF)
        gkv_refs[2 * n][...], gkv_refs[2 * n + 1][...] = in_order(swap, first, second)
        ups = dot_tn(u_ref[...], grad_query).astype(BF)
        near_ref[2 * n, rank:, :] = ups[:, :local]
        near_ref[2 * n + 1, rank:, :] = ups[:, local:]
        total = total + dot_nt(grad_query, w_ref[n, :, :both])
    low = total[:, deep].astype(BF)
    by_piece(fixed_ref, 0, dot_tn(low, n2_ref[...]))
    grad_normed = total[:, :width] + dot(low, down2_ref[...])
    grad = grad + norm_backward(s1_ref[...], gain_ref[1:2, :], grad_normed)
    r1_ref[...] = grad
    r1b_ref[...] = grad.astype(BF)


def cross_back(
    g, dns, s1, s2, n2, q, o, lse, u, z4, up, down5, down2, gains, biases, weight, keyvals, core_at
):
    rows, width = g.shape
    rank = up.shape[0]
    members, local = len(keyvals), weight.shape[2] // 4
    shapes = [sds((rows, width), F32), sds((rows, width), BF)]
    shapes += [sds((members, n * rank, local), BF) for n in (3, 2)]
    shapes += [sds(keyvals[0].shape, BF)] * members
    arrays = [g, s1, s2, n2, q, o, lse, u, z4, up, down5, down2, gains, biases, *keyvals, *dns]
    return weight_call(
        functools.partial(cross_back_kernel, weight, members, local, core_at),
        weight,
        (1,),
        [whole_spec(a.shape) for a in arrays],
        [whole_spec(o.shape) for o in shapes],
        shapes,
        weight.scratch(),
        cost(32 * rows * width * width, 8 * width * width),
        arrays,
    )


def output_kernel(s2_ref, up_ref, g_ref, *refs):
    *y_refs, out_ref, gup_ref = refs
    width, rank = out_ref.shape[1], up_ref.shape[0]
    total = total_of(y_refs)
    low = total[:, width : width + rank].astype(BF)
    out_ref[...] = (s2_ref[...] + total[:, :width] + dot(low, up_ref[...])).astype(BF)
    by_piece(gup_ref, 0, dot_tn(low, g_ref[...]))


def output_end(s2, ys, up, g, members):
    rank, width = up.shape
    return pl.pallas_call(
        output_kernel,
        out_shape=[sds(g.shape, BF), sds((members, rank, width // members), BF)],
        compiler_params=pltpu.CompilerParams(vmem_limit_bytes=VMEM_LIMIT),
        cost_estimate=cost(0, 0),
    )(s2, up, g, *ys)


def input_kernel(x_ref, r_ref, down_ref, gain_ref, *refs):
    *dn_refs, out_ref = refs
    width, rank = out_ref.shape[1], down_ref.shape[0]
    total = total_of(dn_refs)
    low = total[:, width : width + rank].astype(BF)
    grad = total[:, :width] + dot(low, down_ref[...])
    back = norm_backward(x_ref[...].astype(F32), gain_ref[...], grad)
    out_ref[...] = (r_ref[...] + back).astype(BF)


def input_end(x, r1, dns, down, gain):
    return pl.pallas_call(
        input_kernel,
        out_shape=sds(x.shape, BF),
        compiler_params=pltpu.CompilerParams(vmem_limit_bytes=VMEM_LIMIT),
        cost_estimate=cost(0, 0),
    )(x, r1, down, gain, *dns)


def context_kernel(weight, members, at_pieces, places_ref, *refs):
    w_refs, refs = refs[: weight.count], refs[weight.count :]
    blocks, (down_ref, kv_ref, low_ref, w_ref, sems) = refs[:members], refs[members:]
    wait_for(weight.bring(w_refs, places_ref, w_ref, sems))
    rank, local = down_ref.shape[1], blocks[0].shape[1]
    width = members * local
    low, keyval = 0.0, 0.0
    for k in range(members):
        at = pl.ds(pl.multiple_of(places_ref[at_pieces + k], local), local)
        low = low + dot(blocks[k][...], down_ref[at, :])
        keyval = keyval + dot(blocks[k][...], w_ref[at, :])
    low = low.astype(BF)
    low_ref[...] = low
    kv_ref[...] = (keyval + dot(low, w_ref[width : width + rank, :])).astype(BF)


def context_forward(at_pieces, blocks, weight, down):
    count = blocks[0].shape[0]
    arrays = (*blocks, down)
    shapes = [sds((count, weight.shape[1]), BF), sds((count, down.shape[1]), BF)]
    return weight_call(
        functools.partial(context_kernel, weight, len(blocks), at_pieces),
        weight,
        (1,),
        [whole_spec(a.shape) for a in arrays],
        [whole_spec(s.shape) for s in shapes],
        shapes,
        weight.scratch(),
        cost(0, 0),
        arrays,
    )


def context_back_kernel(weight, members, at_pieces, places_ref, *refs):
    w_refs, refs = refs[: weight.count], refs[weight.count :]
    blocks, (down_ref, low_ref, g_ref), refs = (
        refs[:members],
        refs[members : members + 3],
        refs[members + 3 :],
    )
    gup_ref, *refs, w_ref, sems = refs
    wait_for(weight.bring(w_refs, places_ref, w_ref, sems))
    rank, local = down_ref.shape[1], blocks[0].shape[1]
    width = members * local
    grad = g_ref[...]
    low = dot_nt(grad, w_ref[width : width + rank, :]).astype(BF)
    gup_ref[...] = dot_tn(low_ref[...], grad)
    for k in range(members):
        at = pl.ds(pl.multiple_of(places_ref[at_pieces + k], local), local)
        out = dot_nt(grad, w_ref[at, :]) + dot_nt(low, down_ref[at, :])
        refs[k][...] = out.astype(BF)
        refs[members + k][...] = dot_tn(low, blocks[k][...]).astype(BF)


def context_back(at_pieces, blocks, weight, down, low, grad):
    count, local = blocks[0].shape
    rank, members = down.shape[1], len(blocks)
    arrays = (*blocks, down, low, grad)
    shapes = (
        [sds((rank, weight.shape[1]), F32)]
        + [sds((count, local), BF)] * members
        + [sds((rank, local), BF)] * members
    )
    return weight_call(
        functools.partial(context_back_kernel, weight, members, at_pieces),
        weight,
        (1,),
        [whole_spec(a.shape) for a in arrays],
        [whole_spec(s.shape) for s in shapes],
        shapes,
        weight.scratch(),
        cost(10**10, 10**6),
        arrays,
    )


def table_kernel(cos_ref, sin_ref, out_cos_ref, out_left_ref, out_right_ref):
    half, breadth = ROT // 2, 2 * HEAD_DIM
    lane = lax.broadcasted_iota(jnp.int32, (half, breadth), 1)
    row = lax.broadcasted_iota(jnp.int32, (half, breadth), 0)
    within = lane % HEAD_DIM
    first = jnp.where(within == row, 1.0, 0.0)
    second = jnp.where(within == row + half, 1.0, 0.0)

    def spread(ref, pattern):
        return lax.dot_general(
            ref[...], pattern, (((0,), (0,)), ((), ())),
            precision=lax.Precision.HIGHEST, preferred_element_type=F32,
        )

    lanes = lax.broadcasted_iota(jnp.int32, out_cos_ref.shape, 1) % HEAD_DIM
    out_cos_ref[...] = jnp.where(lanes < ROT, spread(cos_ref, first + second), 1.0)
    out_left_ref[...] = -spread(sin_ref, first)
    out_right_ref[...] = spread(sin_ref, second)


def rotary_tables(cosines, sines):
    tokens = cosines.shape[1]
    return pl.pallas_call(
        table_kernel,
        out_shape=[sds((tokens, 2 * HEAD_DIM), F32)] * 3,
        compiler_params=pltpu.CompilerParams(vmem_limit_bytes=VMEM_LIMIT),
        cost_estimate=cost(0, 0),
    )(cosines, sines)


def feed_kernel(weight, first, last, number, places_ref, *refs):
    w_refs, refs = refs[: weight.count], refs[weight.count :]
    n_refs, g_refs, (down_ref, up_ref), refs = (
        refs[:number],
        refs[number : 2 * number],
        refs[2 * number : 2 * number + 2],
        refs[2 * number + 2 :],
    )
    if not first:
        (low_in, glow_in, y_in, dn_in), refs = refs[:4], refs[4:]
    *refs, gdown_ref, ggate_ref, gupper_ref, n_ref, g_ref, w_ref, sems = refs
    step, width = pl.program_id(0), n_ref.shape[1]
    rank, part = gdown_ref.shape
    take_tile(n_refs, n_ref, step)
    take_tile(g_refs, g_ref, step)

    @pl.when(step == 0)
    def _():
        wait_for(weight.bring(w_refs, places_ref, w_ref, sems))
        for ref in (gdown_ref, ggate_ref, gupper_ref):
            ref[...] = jnp.zeros_like(ref)

    normed, grad = n_ref[...], g_ref[...]
    if first:
        low = dot_nt(normed, down_ref[...]).astype(BF)
        grad_low = dot_nt(grad, up_ref[...]).astype(BF)
        refs[2][...] = low
        refs[3][...] = grad_low
    else:
        low, grad_low = low_in[...], glow_in[...]
    deep = slice(width, width + rank)
    both = dot(normed, w_ref[:width, : 2 * part]) + dot(low, w_ref[deep, : 2 * part])
    gate, upper = both[:, :part], both[:, part:]
    grad_unit = dot(grad, w_ref[:width, 2 * part :]) + dot(grad_low, w_ref[deep, 2 * part :])
    sigmoid = 1.0 / (1.0 + jnp.exp(-gate))
    acted = gate * sigmoid
    unit = (acted * upper).astype(BF)
    grad_gate = (grad_unit * upper * (sigmoid + acted * (1.0 - sigmoid))).astype(BF)
    grad_upper = (grad_unit * acted).astype(BF)
    y = dot_nt(unit, w_ref[:, 2 * part :])
    dn = dot_nt(grad_gate, w_ref[:, :part]) + dot_nt(grad_upper, w_ref[:, part : 2 * part])
    if not first:
        y, dn = y + y_in[...].astype(F32), dn + dn_in[...].astype(F32)
    if last:
        give_tile(y.astype(BF), refs[:number], step)
        give_tile(dn.astype(BF), refs[number:], step)
    else:
        refs[0][...] = y.astype(BF)
        refs[1][...] = dn.astype(BF)
    gdown_ref[...] += dot_tn(grad_low, unit)
    ggate_ref[...] += dot_tn(low, grad_gate)
    gupper_ref[...] += dot_tn(low, grad_upper)


def feed(normed, grads, down, up, weight, sums, rows, start, last):
    block, width = normed[0].shape
    rank, number = down.shape[0], len(normed)
    deep, part = weight.shape[0], weight.shape[1] // 3
    narrow = sds((rank, part), F32)
    tokens = number * block
    if last:
        wide = sds((block, deep // LANES * LANES + LANES), BF)
        shapes, specs = [wide] * (2 * number), [whole_spec(wide.shape)] * (2 * number)
    else:
        shapes, specs = [sds((tokens, deep), BF)] * 2, [row_spec(rows, deep)] * 2
    first = not sums
    if first:
        shapes, specs = shapes + [sds((tokens, rank), BF)] * 2, specs + [row_spec(rows, rank)] * 2
    arrays = (*normed, *grads, down, up)
    size = weight.shape[0] * weight.shape[1]
    return weight_call(
        functools.partial(feed_kernel, weight, first, last, number),
        weight,
        (tokens // rows,),
        [whole_spec(a.shape) for a in arrays]
        + [pl.BlockSpec((rows, a.shape[1]), lambda t, *_: (start + t, 0)) for a in sums],
        specs + [whole_spec(narrow.shape)] * 3,
        shapes + [narrow] * 3,
        [pltpu.VMEM((rows, width), BF)] * 2 + weight.scratch(),
        cost(8 * tokens * size, 2 * size),
        [*arrays, *sums],
    )


def settle_first_kernel(fold, labels_ref, in_ref, down_ref, hid_ref, gate_ref):
    slot = pl.program_id(0)
    local = down_ref.shape[-1]
    for ref in (down_ref, hid_ref, gate_ref):
        ref[...] = jnp.zeros_like(ref)
    for s in range(in_ref.shape[0]):

        @pl.when(labels_ref[s] == slot)
        def _(s=s):
            for n, k in enumerate(DOWN_FIRST):
                down_ref[0, k] += in_ref[s, n].astype(F32)
            for k in range(fold):
                at, n = slice(k * local, (k + 1) * local), len(DOWN_FIRST) + k
                hid_ref[0, :, at] += in_ref[s, n].astype(F32)
                gate_ref[0, 0, :, at] += in_ref[s, n + fold].astype(F32)
                gate_ref[0, 1, :, at] += in_ref[s, n + 2 * fold].astype(F32)


def settle_second_kernel(labels_ref, in_ref, down_in, down_ref, up_ref):
    del down_in
    slot = pl.program_id(0)
    downs, ups = down_ref.shape[1], up_ref.shape[1]
    for ref in (down_ref, up_ref):
        ref[...] = jnp.zeros_like(ref)
    for s in range(in_ref.shape[0]):

        @pl.when(labels_ref[s] == slot)
        def _(s=s):
            down_ref[0] += in_ref[s, :downs].astype(F32)
            up_ref[0] += in_ref[s, downs : downs + ups].astype(F32)


DOWN_FIRST = (4, 5)


def slot_spec(shape):
    return pl.BlockSpec((1,) + shape[1:], lambda i, *_, n=len(shape): (i,) + (0,) * (n - 1))


def settle_first(labels, grads, slots, fold):
    rank, local = grads.shape[2:]
    hidden = fold * local
    shapes = [
        (slots, 6, rank, local),
        (slots, rank, hidden),
        (slots, 2, rank, hidden),
    ]
    return pl.pallas_call(
        functools.partial(settle_first_kernel, fold),
        grid_spec=pltpu.PrefetchScalarGridSpec(
            num_scalar_prefetch=1,
            grid=(slots,),
            in_specs=[whole_spec(grads.shape)],
            out_specs=[slot_spec(s) for s in shapes],
        ),
        out_shape=[sds(s, F32) for s in shapes],
        compiler_params=params(),
        cost_estimate=cost(0, 0),
    )(labels, grads)


def settle_second(labels, grads, down):
    downs = DOWN_FIRST[0]
    up = down.shape[:1] + (9,) + down.shape[2:]
    return pl.pallas_call(
        settle_second_kernel,
        grid_spec=pltpu.PrefetchScalarGridSpec(
            num_scalar_prefetch=1,
            grid=(down.shape[0],),
            in_specs=[whole_spec(grads.shape), pl.BlockSpec(memory_space=pl.ANY)],
            out_specs=[slot_spec((1, downs) + down.shape[2:]), slot_spec(up)],
        ),
        out_shape=[sds(down.shape, F32), sds(up, F32)],
        input_output_aliases={2: 0},
        compiler_params=params(),
        cost_estimate=cost(0, 0),
    )(labels, grads, down)


def chunks(hidden):
    return 2 * hidden // 3, hidden // 3


def body(
    inputs,
    context,
    positions,
    adapter_index,
    self_in_weight,
    self_out_weight,
    cross_query_weight,
    cross_keyval_weight,
    cross_out_weight,
    feed_in_weight,
    feed_out_weight,
    norm_gains,
    norm_biases,
    adapter_down,
    adapter_down_hidden,
    adapter_up,
    adapter_up_hidden,
    out_cotangent,
    *,
    pairs,
    chips,
):
    group = Group(pairs, chips)
    members = 2 * pairs
    rows, width = inputs.shape[1], inputs.shape[2]
    block = self_in_weight.shape[0]
    local = self_in_weight.shape[2]
    hidden = feed_in_weight.shape[2]
    slots, rank = adapter_down.shape[0], adapter_down.shape[3]
    deep = width + rank
    parts = chunks(hidden)
    fold = hidden // local
    pieces = group.pieces
    gains, biases = norm_gains, norm_biases
    tile = min(256, members * rows)
    tiles = members * rows // tile
    near_tiles = tiles // pairs

    def packed(*parts):
        return jnp.concatenate(parts, axis=1)

    def stacked(*parts):
        return jnp.concatenate(parts, axis=0)

    def listed(values):
        return list(values) if isinstance(values, (list, tuple)) else [values]

    def piece(array, k, size):
        return lax.dynamic_slice_in_dim(array, pieces[k] * size, size, array.ndim - 1)

    def own(array):
        return piece(array, 0, local)

    near_chips = [1, 2] if chips == 4 else list(range(1, chips))
    chip_rows = [(group.chip ^ k) * 2 * block for k in range(chips)]
    one = [[c + o * block for c in chip_rows] for o in (group.core, 1 - group.core)]
    one += [[c + o * block for c in chip_rows] for o in (group.zhi, 1 - group.zhi)]
    row_places = jnp.stack(
        [r for found in one for r in found] + [jnp.zeros_like(group.core)]
        + [p * local for p in pieces] + [group.core]
    ).astype(jnp.int32)
    mine_at, other_at, first_at, second_at, zero = (n * chips for n in range(5))
    at_pieces = zero + 1
    core_at = at_pieces + members

    def chip_weight(own_entry, near, rest, low, columns, halves):
        weight = Weight((deep, columns), row_places)
        entries = [own_entry, *near]
        for k, (array, row) in zip([0, *near_chips], entries):
            weight.add(
                array,
                *[(row + r, block, c, columns, None, at + k, 0) for r, c, at in halves],
            )
        if rest:
            side_by_side = halves[1][0] == 0
            for n, (array, row) in enumerate(rest):
                size = block // 2 if side_by_side else block
                picked = halves if side_by_side else halves[n : n + 1]
                weight.add(
                    array,
                    *[
                        (row, size, c, columns, None, at + 3, n * size if side_by_side else 0)
                        for _, c, at in picked
                    ],
                )
        weight.add(low, (0, rank, 0, columns, None, zero, width))
        return weight

    stacked_halves = [(0, 0, first_at), (block, 0, second_at)]
    packed_halves = [(0, 0, mine_at), (0, 2 * local, other_at)]

    def spread(got, half_at, half, own_block):
        if got and chips == 4:
            turns = [
                got[1][half_at : half_at + half],
                got[0][half_at + half : half_at + 2 * half],
            ]
            if own_block is not None:
                turns = listed(step.mark(*[stacked(turn, own_block) for turn in turns]))
            return [xor_move(turn, "chip", 4, k) for turn, k in zip(turns, near_chips)]
        if own_block is None:
            return []
        return [xor_move(own_block, "chip", chips, k) for k in near_chips]

    def skip(half):
        return half if chips == 4 else 0

    def flat(*groups):
        return [x for g in groups for x in listed(g)]

    def wait_all(*groups):
        groups = [listed(g) for g in groups]
        values = iter(listed(step.wait(*flat(*groups))))
        return [[next(values) for _ in g] for g in groups]

    def swap_all(blocks):
        if not blocks:
            return []
        blocks = listed(step.wait(*blocks))
        return listed(step.wait(*[core_swap(b) for b in blocks]))

    shard_self = packed(*[self_in_weight[:, i] for i in range(3)], self_out_weight.T)
    step = Order(shard_self[:8, :128])
    self_from = [home_swap(shard_self), turned(shard_self)]
    stream_own, context_own = home_swap(inputs[0]), home_swap(context[0])
    index, positions = step.wait(adapter_index, positions)
    index_other, positions_other = step.wait(core_swap(index), core_swap(positions))
    index = jnp.where(group.home, index, index_other)[0]
    positions = jnp.where(group.home, positions, positions_other)[0]
    down = lax.dynamic_index_in_dim(adapter_down.transpose(0, 1, 3, 2), index, 0, keepdims=False)
    up = lax.dynamic_index_in_dim(adapter_up.transpose(0, 2, 1, 3), index, 0, keepdims=False)
    down, up = step.mark(down, up)
    low_self = packed(*[own(up[i]) for i in range(3)], own(down[1]))
    low_keyval = packed(own(up[5]), own(up[6]))
    low_cross = []
    for k in range(pairs):
        two = [
            (group.p ^ k) * local + core * pairs * local for core in (0, 1)
        ]
        low_cross.append(
            packed(
                *[
                    lax.dynamic_slice_in_dim(table[4], where, local, 1)
                    for table in (up, down)
                    for where in two
                ]
            )
        )
    low_cross = stacked(*low_cross)
    low_self, low_keyval, low_cross = step.mark(low_self, low_keyval, low_cross)
    keyval_parts = step.wait(cross_keyval_weight)
    keyval_parts = step.mark(keyval_parts[:, 0], keyval_parts[:, 1])
    shard_cross = step.mark(packed(cross_query_weight, cross_out_weight.T, *keyval_parts))
    far_cross = group.cross(shard_cross)
    blocks_at = [
        lax.dynamic_slice_in_dim(positions, pieces[k] * rows, rows, 0) for k in range(members)
    ]
    half = ROT // 2
    inverse = 10000.0 ** (-jnp.arange(half, dtype=F32) / half)
    angles = inverse[:, None] * step.wait(jnp.concatenate(blocks_at)).astype(F32)[None]
    tables = step.mark(*rotary_tables(*step.mark(jnp.cos(angles), jnp.sin(angles))))
    feed_in, feed_out = step.wait(feed_in_weight, feed_out_weight)
    gate_rows, upper_rows = step.mark(feed_in[:, 0], feed_in[:, 1])
    at = [sum(parts[:i]) for i in range(len(parts))]

    def feed_shard(i):
        to = slice(at[i], at[i] + parts[i])
        gate, upper, out = step.wait(gate_rows, upper_rows, feed_out)
        return step.mark(packed(gate[:, to], upper[:, to], out.T[:, to]))

    shard_feed = [feed_shard(i) for i in range(len(parts))]

    self_from = step.wait(*self_from)
    ready_self = step.mark(stacked(*self_from))
    near_self = spread([], 0, 0, ready_self)
    stream_own, context_own = step.wait(stream_own, context_own)
    stream_far, context_far = group.far_p(stream_own), group.far_p(context_own)
    (near_self,) = wait_all(near_self)
    rest_self = spread(near_self, 0, block, None)
    rest_self, stream_far, context_far, (far_cross,) = wait_all(
        rest_self, stream_far, context_far, [far_cross]
    )
    stream_other, *stream_far_other = swap_all([stream_own, *stream_far])
    stream = [stream_own, stream_other]
    for far, far_other in zip(stream_far, stream_far_other):
        stream += [far, far_other]
    self_weight = chip_weight(
        (ready_self, 0), [(g, 0) for g in near_self], [(g, 0) for g in rest_self], low_self,
        4 * local, stacked_halves,
    )

    mine = jnp.where(group.home, shard_cross, far_cross)
    given = jnp.where(group.home, far_cross, shard_cross)
    keyval_mine, keyval_give = mine[:, 2 * local :], given[:, 2 * local :]
    low_zhi = jnp.where(group.zhi == 0, shard_cross, far_cross)
    high_zhi = jnp.where(group.zhi == 0, far_cross, shard_cross)
    pair = packed(
        *[two[:, n * local : (n + 1) * local] for n in (0, 1) for two in (low_zhi, high_zhi)]
    )
    keyval_mine, keyval_give, pair = step.mark(keyval_mine, keyval_give, pair)
    (keyval_other,) = swap_all([keyval_give])
    ready_keyval = step.mark(stacked(packed(keyval_mine, keyval_other), pair))

    got_one = spread([], 0, 0, ready_keyval)
    pair_far = group.far_p(pair)
    half_columns = shard_feed[0].shape[1] // 2
    halves = step.wait(shard_feed[0][:, :half_columns], shard_feed[0][:, half_columns:])
    feed_one = [home_swap(halves[0]), turned(halves[0])]
    query, keys, values, low_one, normed_one = project_self(
        listed(step.wait(*stream)), gains[0:1], biases[0:1], down[0], self_weight, tables, tile
    )
    query, keys, values = step.mark(query, keys, values)
    heads_far, logsum_far, *y_far = attend_self(
        query, keys, values, self_weight, tile, near_tiles, tiles - near_tiles, rows
    )
    y_far = listed(step.mark(*y_far))

    def far_sums(*groups):
        others = iter(swap_all([g[2 * k + 1] for g in groups for k in range(pairs - 1)]))
        sums = [
            [group.near_sums(g[2 * k], next(others)).astype(BF) for k in range(pairs - 1)]
            for g in groups
        ]
        values = iter(listed(step.mark(*flat(*sums))))
        return [[next(values) for _ in s] for s in sums]

    def move_p(sums):
        return [xor_move(s, "p", pairs, k + 1) for k, s in enumerate(sums)]

    def sum_up(blocks, other, far):
        total = group.near_sums(blocks[0], other)
        for f in far:
            total = total + f.astype(F32)
        return step.mark(total)

    got_one, pair_far, feed_one = wait_all(got_one, pair_far, feed_one)
    (y_sums,) = far_sums(y_far)

    far = move_p(y_sums)
    quarter = block // 2
    if chips == 4:
        turns = [
            stacked(got[start : start + quarter], got[start + block : start + block + quarter], pair_far[0])
            for got, start in ((got_one[1], 0), (got_one[0], quarter))
        ]
        turns = step.mark(*turns)
        got_two = [xor_move(turn, "chip", 4, k) for turn, k in zip(turns, near_chips)]
    else:
        got_two = flat(*[spread([], 0, 0, p) for p in pair_far])
    feed_two = [home_swap(halves[1]), turned(halves[1])]
    heads_near, logsum_near, *y_rows = attend_self(
        step.wait(query), keys, values, self_weight, tile, 0, near_tiles, rows
    )
    y_rows = listed(step.mark(*y_rows))
    far, got_two, feed_two = wait_all(far, got_two, feed_two)
    y_other, context_other, *swapped = swap_all([y_rows[1], context_own, *context_far])
    branch = [y_rows[0], y_other, *far]
    context_blocks = [context_own, context_other]
    for far, far_other in zip(context_far, swapped):
        context_blocks += [far, far_other]
    keyval_weight = chip_weight(
        (ready_keyval, 0), [(g, 0) for g in got_one],
        [(g, 0) for g in got_two] if chips == 4 else [], low_keyval, 2 * local, packed_halves,
    )
    down_context = step.mark(down[3].T)
    keyval, low_context = context_forward(at_pieces, context_blocks, keyval_weight, down_context)
    keyval = step.mark(keyval)

    keyval_far = group.far_p(keyval)
    ready_feed = [step.mark(stacked(*[packed(*two) for two in zip(feed_one, feed_two)]))]
    found = [(ready_keyval, block, block, 0, 0, 0)]
    found += [(g, block, block, k, 0, 0) for g, k in zip(got_one, near_chips)]
    if chips == 4:
        turns = [got_two[1][block : block + quarter], got_two[0][block + quarter :]]
        got_three = [xor_move(turn, "chip", 4, k) for turn, k in zip(turns, near_chips)]
        keyval_far, got_three = wait_all(keyval_far, got_three)
        found += [(g, 0, quarter, 3, n * quarter, 1) for n, g in enumerate(got_three)]
        found.append((pair_far[0], 0, block, 0, 0, 1))
        for n, (g, k) in enumerate(zip(got_two, near_chips)):
            found += [(g, block, block, k, 0, 1), (g, quarter, quarter, 3, n * quarter, 0)]
    else:
        (keyval_far,) = wait_all(keyval_far)
        count = len(near_chips)
        for n, p in enumerate(pair_far):
            found.append((p, 0, block, 0, 0, n + 1))
            found += [
                (g, 0, block, k, 0, n + 1)
                for g, k in zip(got_two[n * count : (n + 1) * count], near_chips)
            ]
    arrays = []
    for entry in found:
        if not any(entry[0] is a for a in arrays):
            arrays.append(entry[0])
    swapped = swap_all([keyval, *keyval_far, *arrays])
    keyvals = [keyval, swapped[0]]
    for far, far_other in zip(keyval_far, swapped[1:]):
        keyvals += [far, far_other]
    others = swapped[1 + len(keyval_far) :]
    cross_weight = Weight((pairs, deep, 4 * local), row_places)
    for array, other in zip(arrays, others):
        entries = [e[1:] for e in found if e[0] is array]
        for source, places in ((array, mine_at), (other, other_at)):
            cross_weight.add(
                source,
                *[
                    (row, size, 0, 4 * local, n, places + k, offset)
                    for row, size, k, offset, n in entries
                ],
            )
    cross_weight.add(
        low_cross, *[(n * rank, rank, 0, 4 * local, n, zero, width) for n in range(pairs)]
    )

    near_feed = [spread([], 0, 0, ready_feed[0])]
    feed_from = [home_swap(step.wait(shard_feed[1])), turned(step.wait(shard_feed[1]))]
    stream_own, *branch = step.wait(stream_own, *branch)

    (
        stream_one, stream_two, normed_two, normed_three, query_cross, heads_cross, logsum_cross,
        low_two, low_three, low_four,
    ) = cross_forward(
        stream_own, branch, up[3], up[7], down[2], gains, biases, cross_weight, keyvals, core_at,
    )
    normed_own = step.mark(normed_three)
    (feed_from,) = wait_all(feed_from)
    ready_feed.append(step.mark(stacked(*feed_from)))

    normed_far = group.far_p(normed_own)
    cotangent_own = home_swap(step.wait(out_cotangent[0]))
    (normed_other,) = swap_all([normed_own])
    down_hidden = lax.dynamic_index_in_dim(
        adapter_down_hidden.transpose(0, 2, 1), index, 0, keepdims=False
    )
    up_hidden = lax.dynamic_index_in_dim(
        adapter_up_hidden.transpose(0, 2, 1, 3), index, 0, keepdims=False
    )
    feed_down, feed_up = piece(down_hidden, 0, hidden), piece(up_hidden, 0, hidden)
    feed_down, feed_gate, feed_upper = step.mark(feed_down, feed_up[0], feed_up[1])
    low_feed = [
        packed(feed_gate[:, to], feed_upper[:, to], feed_down[:, to])
        for to in [slice(a, a + p) for a, p in zip(at, parts)]
    ]
    low_feed = step.mark(*low_feed)
    (near_feed[0],) = wait_all(near_feed[0])
    rest_feed = spread(near_feed[0], 0, block, None)
    normed_far, (cotangent_own,) = wait_all(normed_far, [cotangent_own])
    cotangent_other, *normed_swapped = swap_all([cotangent_own, *normed_far])

    def feed_weight(i, rest):
        return chip_weight(
            (ready_feed[i], 0), [(g, 0) for g in near_feed[i]], [(g, 0) for g in rest],
            low_feed[i], 3 * parts[i], stacked_halves,
        )

    normed_blocks = [[normed_own, normed_other], []]
    cotangent_blocks = [[cotangent_own, cotangent_other], []]

    def feed_pass(weight, half, state, last):
        normed, cotangent = wait_all(normed_blocks[half], cotangent_blocks[half])
        found = feed(normed, cotangent, down[5], up[8], weight, state, tile, 0, last)
        *values, gdown, ggate, gupper = found
        return listed(step.mark(*values)), [gdown, ggate, gupper]

    def added(one, two):
        return [a + b for a, b in zip(one, two)]

    (rest_feed,) = wait_all(rest_feed) if rest_feed else ([],)
    weight = feed_weight(0, rest_feed)
    near_feed.append(spread([], 0, 0, ready_feed[1]))
    cotangent_far = group.far_p(cotangent_own)
    (y, dn, *lows), grads = feed_pass(weight, 0, (), False)
    states = [(*lows, y, dn)]
    near_feed[1], cotangent_far = wait_all(near_feed[1], cotangent_far)
    swapped = normed_swapped + swap_all(cotangent_far)
    for blocks, fars, others in (
        (normed_blocks[1], normed_far, swapped[: pairs - 1]),
        (cotangent_blocks[1], cotangent_far, swapped[pairs - 1 :]),
    ):
        for far, far_other in zip(fars, others):
            blocks += [far, far_other]
    rest_feed = spread(near_feed[1], 0, block, None)
    (y, dn, *lows), more = feed_pass(weight, 1, (), False)
    states.append((*lows, y, dn))
    feed_grads = [added(grads, more)]
    (rest_feed,) = wait_all(rest_feed) if rest_feed else ([],)

    weight = feed_weight(1, rest_feed)
    found, grads = feed_pass(weight, 1, states[1], True)
    y_far, dn_far = found[: len(found) // 2], found[len(found) // 2 :]

    dn_sums, y_sums = far_sums(dn_far, y_far)
    far = move_p(dn_sums)
    found, more = feed_pass(weight, 0, states[0], True)
    y_rows, dn_rows = found[:2], found[2:]
    feed_grads.append(added(grads, more))
    (far,) = wait_all(far)
    dn_other, y_other = swap_all([dn_rows[1], y_rows[1]])
    grad_normed = [dn_rows[0], dn_other, *far]

    far = move_p(step.mark(*y_sums) if len(y_sums) > 1 else [step.mark(*y_sums)])
    grad_stream, branch_grad, fixed_rows, near_rows, *keyval_rows = cross_back(
        cotangent_own, listed(step.wait(*grad_normed)), stream_one, stream_two, normed_two,
        query_cross, heads_cross, logsum_cross, low_three, low_four, up[7], down[5], down[2],
        gains, biases, cross_weight, keyvals, core_at,
    )
    branch_grad, *keyval_rows = step.mark(branch_grad, *keyval_rows)
    (far,) = wait_all(far)

    branch_far = group.far_p(branch_grad)
    (branch_other,) = swap_all([branch_grad])

    def back(grad, heads, logsum, first, before, ends):
        return attend_back(
            grad, up[3], self_weight, query, keys, values, heads, logsum, tables, low_one, tile,
            first, before, ends,
        )

    def taken(by_piece, k):
        return lax.dynamic_index_in_dim(by_piece, pieces[k], 0, keepdims=False)

    def taken_near(by_member, k):
        member = k // 2 * 2 + (group.core ^ (k % 2))
        return lax.dynamic_index_in_dim(by_member, member, 0, keepdims=False)

    first_rows = listed(
        step.mark(
            *[
                stacked(taken_near(near_rows, k)[:rank], taken(fixed_rows, k)[rank : 2 * rank])
                for k in range(members)
            ]
        )
    )
    others = swap_all([*keyval_rows[1::2], *first_rows[1::2]])
    keyval_sums, first_sums = (
        [group.near_sums(a, b) for a, b in zip(own[::2], others[n * pairs : (n + 1) * pairs])]
        for n, own in enumerate((keyval_rows, first_rows))
    )
    moving = listed(step.mark(*[x.astype(BF) for x in keyval_sums[1:] + first_sums[1:]]))
    keyval_far, first_far = move_p(moving[: pairs - 1]), move_p(moving[pairs - 1 :])
    grads = listed(step.wait(branch_grad, branch_other))
    near_back = step.mark(*back(grads, heads_near, logsum_near, 0, None, None))
    branch_far, keyval_far, first_far = wait_all(branch_far, keyval_far, first_far)

    output, grad_up_eight = step.mark(
        *output_end(
            stream_two, [step.wait(y_rows[0]), y_other, *far], up[8], cotangent_own, members
        )
    )
    swapped = swap_all(branch_far)
    branch_blocks = []
    for f, o in zip(branch_far, swapped):
        branch_blocks += [f, o]

    def columns(array):
        return array.reshape(rank, -1, local).transpose(1, 0, 2)

    def sent(parts):
        parts.append(jnp.full((1, rank, local), index, F32))
        grads = step.mark(jnp.concatenate(parts, axis=0).astype(BF))
        return [home_swap(grads), turned_back(grads)]

    def to_chips(blocks):
        both = step.mark(stacked(*blocks))
        return [both] + [xor_move(both, "chip", chips, k) for k in range(1, chips)]

    def every(blocks):
        grads = stacked(*blocks)
        grads = grads.reshape(-1, grads.shape[0] // (2 * chips), rank, local)
        return grads, grads[:, -1, 0, 0].astype(jnp.int32)

    def total(own, far):
        for f in far:
            own = own + f.astype(F32)
        return own

    grad_keyval = step.mark(total(keyval_sums[0], keyval_far).astype(BF))
    grad_up_keyval, *found = step.mark(
        *context_back(
            at_pieces, context_blocks, keyval_weight, down_context, low_context, grad_keyval
        )
    )
    context_rows, grad_down_three = found[:members], found[members:]
    summed = total(first_sums[0], first_far).reshape(-1, rank, local)
    first = sent([summed, *[columns(jnp.concatenate(g, axis=1)) for g in zip(*feed_grads)]])
    block_output = home_swap(step.wait(output))
    branch_blocks = listed(step.wait(*branch_blocks))
    found = back(
        branch_blocks, heads_far, logsum_far, near_tiles, near_back,
        (normed_one, low_two, branch_grad),
    )
    first, (block_output,), found = wait_all(first, [block_output], found)
    grad_down_one, grad_up_self, own_rows, *dn_blocks = found

    second_rows = listed(
        step.mark(
            *[
                stacked(
                    taken(own_rows, k), taken(fixed_rows, k)[:rank],
                    taken(fixed_rows, k)[2 * rank :], taken(grad_up_eight, k), grad_down_three[k],
                    taken_near(near_rows, k)[rank:],
                )
                for k in range(members)
            ]
        )
    )
    swapped = swap_all([*dn_blocks[1::2], *second_rows[1::2], *context_rows[1::2]])
    dn_sums, second_sums, context_sums = (
        [group.near_sums(a, b) for a, b in zip(own[::2], swapped[n * pairs : (n + 1) * pairs])]
        for n, own in enumerate((dn_blocks, second_rows, context_rows))
    )
    moving = [x.astype(BF) for x in dn_sums[1:] + second_sums[1:] + context_sums[1:]]
    moving = listed(step.mark(*moving))
    count = pairs - 1
    far = move_p(moving[:count])
    second_far = move_p(listed(step.wait(*moving[count : 2 * count])))
    context_far = move_p(listed(step.wait(*moving[2 * count :])))
    first = to_chips(first)
    far, second_far, context_far, first = wait_all(far, second_far, context_far, first)

    grad_inputs = step.mark(
        input_end(
            stream_own, grad_stream, [dn_blocks[0], swapped[0], *far], down[0], gains[0:1]
        )
    )
    summed = total(second_sums[0], second_far).reshape(-1, rank, local)
    second = sent(
        [
            summed[0:1],
            grad_down_one[None],
            summed[2:3],
            summed[5:6],
            columns(grad_up_self),
            summed[1:2],
            summed[6:7],
            columns(grad_up_keyval),
            summed[3:5],
        ]
    )
    grad_inputs = home_swap(step.wait(grad_inputs))
    grad_context = home_swap(step.mark(total(context_sums[0], context_far).astype(BF)))
    first, labels = every(first)
    grad_down, grad_hidden, grad_gate = settle_first(labels, first, slots, fold)
    grad_down = step.mark(grad_down)
    (second,) = wait_all(second)
    (second,) = wait_all(to_chips(second))
    second, labels = every(second)
    labels = labels + (step.token[0, 0].astype(F32) * 0.0).astype(jnp.int32)
    grad_down, grad_up = settle_second(labels, second, grad_down)
    return (
        block_output[None],
        grad_inputs.astype(F32)[None],
        grad_context.astype(F32)[None],
        grad_down.transpose(0, 1, 3, 2),
        grad_hidden.transpose(0, 2, 1),
        grad_up.transpose(0, 2, 1, 3),
        grad_gate.transpose(0, 2, 1, 3),
    )


def solution(mesh):
    members = mesh.shape["tensor"]
    chips = mesh.shape["dp"] // 2
    mesh = Mesh(
        mesh.devices.reshape(chips, 2, 2, members // 2), ("chip", "core", "zhi", "p")
    )
    dp, tensor = ("chip", "core"), ("zhi", "p")
    in_specs = (
        P(dp, tensor, None),
        P(dp, None, tensor),
        P(dp, None),
        P(dp),
        P(dp, None, tensor),
        P(tensor, dp),
        P(dp, tensor),
        P(dp, None, tensor),
        P(tensor, dp),
        P(dp, None, tensor),
        P(tensor, dp),
        P(),
        P(),
        P(),
        P(),
        P(),
        P(),
        P(dp, tensor, None),
    )
    out_specs = (
        P(dp, tensor, None),
        P(dp, tensor, None),
        P(dp, None, tensor),
        P(None, None, tensor, None),
        P(None, tensor, None),
        P(None, None, None, tensor),
        P(None, None, None, tensor),
    )

    def run(*args):
        return body(*args, pairs=members // 2, chips=chips)

    return jax.shard_map(run, mesh=mesh, in_specs=in_specs, out_specs=out_specs, check_vma=False)
```

```python
import functools

import jax
import jax.numpy as jnp
from jax import lax
from jax.experimental import pallas as pl
from jax.experimental.pallas import tpu as pltpu
from jax.sharding import Mesh, PartitionSpec as P

HEAD_DIM = 64
ROT = 32
EPSILON = 1e-05
F32 = jnp.float32
BF = jnp.bfloat16
SWAP = ((0, 1), (1, 0))
LANES = 128
VMEM_LIMIT = 56 * 1024 * 1024


def dot(left, right):
    return jnp.dot(left, right, preferred_element_type=F32)


def dot_nt(left, right):
    return lax.dot_general(left, right, (((1,), (1,)), ((), ())), preferred_element_type=F32)


def dot_tn(left, right):
    return lax.dot_general(left, right, (((0,), (0,)), ((), ())), preferred_element_type=F32)


class Order:
    def __init__(self, first):
        self.token = first

    def wait(self, *values):
        *values, self.token = lax.optimization_barrier((*values, self.token))
        return values[0] if len(values) == 1 else values

    mark = wait


def core_swap(x):
    return lax.ppermute(x, "core", SWAP)


def xor_move(x, axis, size, k):
    return lax.ppermute(x, axis, [(i, i ^ k) for i in range(size)])


def home_swap(x):
    return lax.ppermute(x, ("core", "zhi"), [(0, 0), (1, 2), (2, 1), (3, 3)])


def turned(x):
    return lax.ppermute(x, ("core", "zhi"), [(0, 1), (1, 3), (2, 0), (3, 2)])


def turned_back(x):
    return lax.ppermute(x, ("core", "zhi"), [(0, 2), (1, 0), (2, 3), (3, 1)])


class Group:
    def __init__(self, pairs, chips):
        self.pairs, self.chips = pairs, chips
        self.core, self.zhi, self.p = (lax.axis_index(n) for n in ("core", "zhi", "p"))
        self.chip = lax.axis_index("chip")
        self.home = self.core == self.zhi
        self.pieces = [
            (self.core ^ kc) * pairs + (self.p ^ kp) for kp in range(pairs) for kc in (0, 1)
        ]

    def far_p(self, own):
        return [xor_move(own, "p", self.pairs, k) for k in range(1, self.pairs)]

    def near_sums(self, own, other):
        return own.astype(F32) + other.astype(F32)

    def cross(self, shard):
        return xor_move(shard, "zhi", 2, 1)

    def spread_one(self, block):
        if self.chips == 4:
            return [xor_move(block, "chip", 4, k) for k in (1, 2)]
        return [xor_move(block, "chip", self.chips, k) for k in range(1, self.chips)]

    def spread_two(self, got):
        if self.chips != 4:
            return []
        half = got[0].shape[0] // 2
        return [xor_move(got[1][:half], "chip", 4, 1), xor_move(got[0][half:], "chip", 4, 2)]

    def places(self, rows):
        if self.chips == 4:
            diagonal = (self.chip ^ 3) * rows
            return [(self.chip ^ 1) * rows, (self.chip ^ 2) * rows, diagonal, diagonal + rows // 2]
        return [(self.chip ^ k) * rows for k in range(1, self.chips)]


class Weight:
    def __init__(self, shape, places):
        self.shape, self.places, self.arrays, self.moves = shape, places, [], []

    def add(self, array, *parts):
        self.moves += [(len(self.arrays), *part) for part in parts]
        self.arrays.append(array)

    @property
    def count(self):
        return len(self.arrays)

    def specs(self):
        return [pl.BlockSpec(memory_space=pl.ANY)] * self.count

    def columns(self, start, size):
        if size % 128 or start % 128:
            return 0, self.shape[-1], start
        return start, size, 0

    def scratch(self, size=None):
        shape = self.shape if size is None else self.shape[:-1] + (size,)
        return [pltpu.VMEM(shape, BF), pltpu.SemaphoreType.DMA((len(self.moves),))]

    def at_first(self, step, refs, places_ref, target, sems, start=0, size=None):
        def begin():
            @pl.when(step == 0)
            def _():
                self.bring(refs, places_ref, target, sems, start, size)

        def end():
            @pl.when(step == 0)
            def _():
                wait_for(self.bring(refs, places_ref, target, sems, start, size, go=False))

        return begin, end

    def bring(self, refs, places_ref, target, sems, start=0, size=None, go=True):
        copies = []
        for number, (source, row, rows, column, columns, lead, place, offset) in enumerate(self.moves):
            at = pl.ds(pl.multiple_of(places_ref[place] + offset, 16), rows)
            to = target.at[at] if lead is None else target.at[lead, at]
            if size is not None:
                column, columns = column + start, size
            found = refs[source].at[pl.ds(row, rows), pl.ds(column, columns)]
            copies.append(pltpu.make_async_copy(found, to, sems.at[number]))
        if go:
            for copy in copies:
                copy.start()
        return copies


def wait_for(copies):
    for copy in copies:
        copy.wait()


def weight_call(kernel, weight, grid, in_specs, out_specs, out_shape, scratch, estimate, arrays):
    return pl.pallas_call(
        kernel,
        grid_spec=pltpu.PrefetchScalarGridSpec(
            num_scalar_prefetch=1,
            grid=grid,
            in_specs=weight.specs() + in_specs,
            out_specs=out_specs,
            scratch_shapes=scratch,
        ),
        out_shape=out_shape,
        compiler_params=params(),
        cost_estimate=estimate,
    )(weight.places, *weight.arrays, *arrays)


def stats(stream):
    average = jnp.mean(stream, axis=-1, keepdims=True)
    centred = stream - average
    variance = jnp.mean(centred * centred, axis=-1, keepdims=True)
    scale = lax.rsqrt(variance + EPSILON)
    return centred * scale, scale


def layer_norm(stream, gain, bias):
    return (stats(stream)[0] * gain + bias).astype(BF)


def norm_backward(stream, gain, grad):
    unit, scale = stats(stream)
    grad = grad * gain
    return scale * (
        grad
        - jnp.mean(grad, axis=-1, keepdims=True)
        - unit * jnp.mean(grad * unit, axis=-1, keepdims=True)
    )


def turn(x, cosines, left_sines, right_sines):
    breadth = 2 * HEAD_DIM if x.shape[1] % (2 * HEAD_DIM) == 0 else HEAD_DIM
    half = ROT // 2
    for at in range(0, x.shape[1], breadth):
        group = x[:, at : at + breadth]
        if breadth % 128 == 0:
            left, right = pltpu.roll(group, breadth - half, 1), pltpu.roll(group, half, 1)
        else:
            left = jnp.concatenate([group[:, half:], group[:, :half]], axis=1)
            right = jnp.concatenate([group[:, -half:], group[:, :-half]], axis=1)
        yield (
            at,
            breadth,
            group * cosines[:, :breadth]
            + left * left_sines[:, :breadth]
            + right * right_sines[:, :breadth],
        )


def head_sums(product):
    columns = product.shape[1]
    rows = -(-columns // HEAD_DIM // 8) * 8
    head = lax.broadcasted_iota(jnp.int32, (rows, columns), 0)
    lane = lax.broadcasted_iota(jnp.int32, (rows, columns), 1)
    picked = jnp.where(lane // HEAD_DIM == head, 1.0, 0.0).astype(F32)
    return lax.dot_general(
        picked, product, (((1,), (1,)), ((), ())),
        precision=lax.Precision.HIGHEST, preferred_element_type=F32,
    )


def whole_spec(shape):
    return pl.BlockSpec(shape, lambda *_: (0,) * len(shape))


def row_spec(rows, columns):
    return pl.BlockSpec((rows, columns), lambda t, *_: (t, 0))


def take_tile(refs, tile_ref, step):
    rows, tile = refs[0].shape[0], tile_ref.shape[0]
    for i, ref in enumerate(refs):

        @pl.when(step == i * rows // tile)
        def _(i=i, ref=ref):
            tile_ref[i * rows % tile : i * rows % tile + rows, :] = ref[...]


def give_tile(value, refs, step):
    rows, (tile, columns) = refs[0].shape[0], value.shape
    for i, ref in enumerate(refs):

        @pl.when(step == i * rows // tile)
        def _(i=i, ref=ref):
            ref[:, :columns] = value[i * rows % tile : i * rows % tile + rows]
            ref[:, columns:] = jnp.zeros((rows, ref.shape[1] - columns), ref.dtype)


def total_of(refs):
    total = refs[0][...].astype(F32)
    for ref in refs[1:]:
        total = total + ref[...].astype(F32)
    return total


def by_piece(ref, row, value):
    local = ref.shape[2]
    for k in range(ref.shape[0]):
        ref[k, row : row + value.shape[0], :] = value[:, k * local : (k + 1) * local].astype(
            ref.dtype
        )


def params(semantics=1):
    return pltpu.CompilerParams(
        dimension_semantics=("arbitrary",) * semantics, vmem_limit_bytes=VMEM_LIMIT
    )


def cost(flops, moved, exps=0):
    return pl.CostEstimate(
        flops=int(flops) or 1000, bytes_accessed=int(moved) or 1000, transcendentals=int(exps)
    )


def sds(shape, dtype):
    return jax.ShapeDtypeStruct(shape, dtype)


def query_kernel(weight, part, count, places_ref, *refs):
    w_refs, refs = refs[: weight.count], refs[weight.count :]
    blocks, (gain_ref, bias_ref, down_ref, cos_ref, left_ref, right_ref), refs = (
        refs[:count],
        refs[count : count + 6],
        refs[count + 6 :],
    )
    q_ref, k_ref, v_ref, low_ref, n_ref, x_ref, w_ref, sems = refs
    step = pl.program_id(0)

    begin, end = weight.at_first(step, w_refs, places_ref, w_ref, sems, *part[:2])
    begin()
    take_tile(blocks, x_ref, step)
    local, width = q_ref.shape[1], x_ref.shape[1]
    normed = layer_norm(x_ref[...].astype(F32), gain_ref[...], bias_ref[...])
    n_ref[...] = normed
    low = dot_nt(normed, down_ref[...]).astype(BF)
    low_ref[...] = low
    end()
    at = slice(part[2], part[2] + 3 * local)
    mixed = dot(normed, w_ref[:width, at]) + dot(low, w_ref[width:, at])
    tables = cos_ref[...], left_ref[...], right_ref[...]
    for at, breadth, turned in turn(mixed[:, :local], *tables):
        q_ref[:, at : at + breadth] = (turned * HEAD_DIM**-0.5).astype(BF)
    for at, breadth, turned in turn(mixed[:, local : 2 * local], *tables):
        k_ref[:, at : at + breadth] = turned.astype(BF)
    v_ref[...] = mixed[:, 2 * local :].astype(BF)


def project_self(blocks, gain, bias, down, weight, tables, rows):
    width = blocks[0].shape[1]
    tokens = len(blocks) * blocks[0].shape[0]
    local = weight.shape[1] // 4
    part = weight.columns(0, 3 * local)
    return weight_call(
        functools.partial(query_kernel, weight, part, len(blocks)),
        weight,
        (tokens // rows,),
        [whole_spec(b.shape) for b in blocks]
        + [whole_spec(gain.shape), whole_spec(bias.shape), whole_spec(down.shape)]
        + [row_spec(rows, t.shape[1]) for t in tables],
        [row_spec(rows, local)] * 3 + [row_spec(rows, down.shape[0]), row_spec(rows, width)],
        [sds((tokens, local), BF)] * 3
        + [sds((tokens, down.shape[0]), BF), sds((tokens, width), BF)],
        [pltpu.VMEM((rows, width), BF), *weight.scratch(part[1])],
        cost(8 * tokens * width * local, 8 * width * local),
        [*blocks, gain, bias, down, *tables],
    )


def attend_kernel(weight, part, places_ref, *refs):
    w_refs, refs = refs[: weight.count], refs[weight.count :]
    q_ref, k_ref, v_ref, o_ref, lse_ref, *y_refs, w_ref, sems = refs
    rows, local = q_ref.shape
    step = pl.program_id(0)

    begin, end = weight.at_first(step, w_refs, places_ref, w_ref, sems, *part[:2])
    begin()
    lanes = lax.broadcasted_iota(jnp.int32, (rows, 128), 1)
    logsums = jnp.zeros((rows, 128), F32)
    for head in range(local // HEAD_DIM):
        at = slice(head * HEAD_DIM, (head + 1) * HEAD_DIM)
        scores = dot_nt(q_ref[:, at], k_ref[:, at])
        top = jnp.max(scores, axis=1, keepdims=True)
        powers = jnp.exp(scores - top)
        total = jnp.sum(powers, axis=1, keepdims=True)
        out = dot(powers.astype(BF), v_ref[:, at]) / total
        o_ref[:, at] = out.astype(BF)
        logsums = jnp.where(lanes == head, top + jnp.log(total), logsums)
    lse_ref[...] = logsums.T[: lse_ref.shape[0]]
    end()
    y = dot_nt(o_ref[...], w_ref[:, part[2] : part[2] + local]).astype(BF)
    give_tile(y, y_refs, step)


def wide_of(weight):
    return weight.shape[-2] // LANES * LANES + LANES


def attend_self(query, keys, values, weight, rows, first, count, block):
    tokens, local = query.shape
    heads = -(-local // HEAD_DIM // 8) * 8
    part = weight.columns(3 * local, local)
    blocks = count * rows // block
    return weight_call(
        functools.partial(attend_kernel, weight, part),
        weight,
        (count,),
        [
            pl.BlockSpec((rows, local), lambda t, *_: (first + t, 0)),
            whole_spec(keys.shape),
            whole_spec(values.shape),
        ],
        [row_spec(rows, local), pl.BlockSpec((heads, rows), lambda t, *_: (0, t))]
        + [whole_spec((block, wide_of(weight)))] * blocks,
        [sds((count * rows, local), BF), sds((heads, count * rows), F32)]
        + [sds((block, wide_of(weight)), BF)] * blocks,
        weight.scratch(part[1]),
        cost(16 * count * rows * tokens * local, 8 * query.size, count * rows * tokens),
        [query, keys, values],
    )


def attend_back_kernel(weight, part, first, last, tiles, number, blocks, places_ref, *refs):
    w_refs, refs = refs[: weight.count], refs[weight.count :]
    grads, refs = refs[:number], refs[number:]
    (
        up_ref, q_ref, k_ref, v_ref, o_ref, lse_ref, cos_ref, left_ref, right_ref, low_ref,
    ), refs = refs[:10], refs[10:]
    *refs, g_ref, w_ref, sems = refs
    begin, end = weight.at_first(pl.program_id(0), w_refs, places_ref, w_ref, sems, *part[:2])
    begin()
    take_tile(grads, g_ref, pl.program_id(0))
    if not first:
        (mq_ref, gk_in, gv_in, down_in), refs = refs[:4], refs[4:]
    if last:
        (n_ref, z_ref, r_ref), refs = refs[:3], refs[3:]
        (down_ref, gup_ref, rows_ref), refs = refs[:3], refs[3:]
        dn_refs, (m_ref, gk_ref, gv_ref) = refs[:blocks], refs[blocks:]
    else:
        m_ref, gk_ref, gv_ref, down_ref = refs
    step, rows = pl.program_id(0), q_ref.shape[0]
    width, local = g_ref.shape[1], q_ref.shape[1]
    at_rows = pl.ds(pl.multiple_of((step + tiles) * rows, rows), rows)
    at_query = at_rows if last else pl.ds(pl.multiple_of(step * rows, rows), rows)

    @pl.when(step == 0)
    def _():
        if first:
            gk_ref[...] = jnp.zeros_like(gk_ref)
            gv_ref[...] = jnp.zeros_like(gv_ref)
            down_ref[...] = jnp.zeros_like(down_ref)
        else:
            gk_ref[...] = gk_in[...]
            gv_ref[...] = gv_in[...]
            down_ref[...] = down_in[...]
            m_ref[: mq_ref.shape[0], :local] = mq_ref[...]

    grad = g_ref[...]
    grad_low = dot_nt(grad, up_ref[...]).astype(BF)
    end()
    at = slice(part[2], part[2] + local)
    grad_out = dot(grad, w_ref[:width, at]) + dot(grad_low, w_ref[width:, at])
    grad_out = grad_out.astype(BF)
    out = o_ref[...]
    down_ref[...] += dot_tn(grad_low, out)
    product = grad_out.astype(F32) * out.astype(F32)
    deltas = head_sums(product)
    parts = []
    for head in range(local // HEAD_DIM):
        at = slice(head * HEAD_DIM, (head + 1) * HEAD_DIM)
        q, k, v, g = q_ref[:, at], k_ref[:, at], v_ref[:, at], grad_out[:, at]
        delta = deltas[head : head + 1]
        probs = jnp.exp(dot_nt(k, q) - lse_ref[head : head + 1, :])
        grad_scores = (probs * (dot_nt(v, g) - delta)).astype(BF)
        gv_ref[:, at] += dot(probs.astype(BF), g)
        gk_ref[:, at] += dot(grad_scores, q)
        parts.append(dot_tn(grad_scores, k) * HEAD_DIM**-0.5)
    tables = cos_ref[at_rows, :], -left_ref[at_rows, :], -right_ref[at_rows, :]
    for at, breadth, turned in turn(jnp.concatenate(parts, axis=1), *tables):
        m_ref[at_query, at : at + breadth] = turned.astype(BF)

    if last:

        @pl.when(step == pl.num_programs(0) - 1)
        def _():
            tables = cos_ref[...], -left_ref[...], -right_ref[...]
            for at, breadth, turned in turn(gk_ref[...], *tables):
                m_ref[:, local + at : local + at + breadth] = turned.astype(BF)
            m_ref[:, 2 * local :] = gv_ref[...].astype(BF)
            gup_ref[...] = dot_tn(low_ref[...], m_ref[...])
            rank, block = up_ref.shape[0], dn_refs[0].shape[0]
            down = 0.0
            for i, ref in enumerate(dn_refs):
                at = slice(i * block, (i + 1) * block)
                value = dot_nt(m_ref[at, :], w_ref[:, : 3 * local]).astype(BF)
                ref[:, : width + rank] = value
                ref[:, width + rank :] = jnp.zeros((block, ref.shape[1] - width - rank), BF)
                down = down + dot_tn(value[:, width:], n_ref[at, :])
            by_piece(rows_ref, 0, down)
            by_piece(rows_ref, rank, dot_tn(z_ref[...], r_ref[...]))


def attend_back(
    grads, up, weight, query, keys, values, out, lse, tables, low, rows, start, before, ends
):
    tokens, local = query.shape
    block, width = grads[0].shape
    rank = up.shape[0]
    count = len(grads) * block // rows
    first, last = before is None, ends is not None
    before = () if first else before
    ends = ends if last else ()
    sums = [sds((tokens, local), F32)] * 2 + [sds((rank, local), F32)]
    blocks = tokens // block if last else 0
    if last:
        members = width // local
        shapes = [sums[2], sds((rank, 3 * local), F32), sds((members, 2 * rank, local), BF)]
        shapes += [sds((block, wide_of(weight)), BF)] * blocks
        scratch = [pltpu.VMEM((tokens, 3 * local), BF)]
        scratch += [pltpu.VMEM((tokens, local), F32)] * 2
        part = 0, 4 * local, 3 * local
    else:
        shapes, scratch = [sds((count * rows, local), BF), *sums], []
        part = weight.columns(3 * local, local)
    scratch.append(pltpu.VMEM((rows, width), BF))

    def tile(columns):
        return pl.BlockSpec((rows, columns), lambda t, *_: (start + t, 0))

    return weight_call(
        functools.partial(attend_back_kernel, weight, part, first, last, start, len(grads), blocks),
        weight,
        (count,),
        [
            *[whole_spec(g.shape) for g in grads],
            whole_spec(up.shape),
            tile(local),
            whole_spec(keys.shape),
            whole_spec(values.shape),
            row_spec(rows, local),
            pl.BlockSpec((lse.shape[0], rows), lambda t, *_: (0, t)),
            *[whole_spec(t.shape) for t in tables],
            whole_spec(low.shape),
            *[whole_spec(b.shape) for b in before],
            *[whole_spec(e.shape) for e in ends],
        ],
        [whole_spec(s.shape) for s in shapes],
        shapes,
        scratch + weight.scratch(part[1]),
        cost(40 * count * rows * tokens * local, 10 * query.size, count * rows * tokens),
        [*grads, up, query, keys, values, out, lse, *tables, low, *before, *ends],
    )


def in_order(swap, first, second):
    keep = swap == 0
    return jnp.where(keep, first, second), jnp.where(keep, second, first)


def cross_kernel(weight, members, local, core_at, places_ref, *refs):
    w_refs, refs = refs[: weight.count], refs[weight.count :]
    *refs, w_ref, sems = refs
    copies = weight.bring(w_refs, places_ref, w_ref, sems)
    (x_ref, up_self_ref, up_cross_ref, down_ref, gain_ref, bias_ref), refs = refs[:6], refs[6:]
    kv_refs, refs = refs[:members], refs[members:]
    y_refs, refs = refs[:-10], refs[-10:]
    branch = total_of(y_refs)
    s1_ref, s2_ref, n2_ref, n3_ref, q_ref, o_ref, lse_ref, z2_ref, u_ref, z4_ref = refs
    rows, width = x_ref.shape
    rank = down_ref.shape[0]
    deep = slice(width, width + rank)
    low = branch[:, deep].astype(BF)
    z2_ref[...] = low
    stream = x_ref[...].astype(F32) + branch[:, :width] + dot(low, up_self_ref[...])
    s1_ref[...] = stream
    normed = layer_norm(stream, gain_ref[1:2, :], bias_ref[1:2, :])
    n2_ref[...] = normed
    low = dot_nt(normed, down_ref[...]).astype(BF)
    u_ref[...] = low
    total = jnp.zeros((rows, width + rank), F32)
    wait_for(copies)
    both = 2 * local
    for n in range(members // 2):
        query = dot(normed, w_ref[n, :width, :both]) + dot(low, w_ref[n, deep, :both])
        query = (query * HEAD_DIM**-0.5).astype(BF)
        q_ref[:, n * both : (n + 1) * both] = query
        found = in_order(places_ref[core_at], kv_refs[2 * n][...], kv_refs[2 * n + 1][...])
        parts, logsums = [], []
        for head in range(both // HEAD_DIM):
            keyval, own = found[head * HEAD_DIM // local], head * HEAD_DIM % local
            keys = keyval[:, own : own + HEAD_DIM]
            values = keyval[:, local + own : local + own + HEAD_DIM]
            scores = dot_nt(keys, query[:, head * HEAD_DIM : (head + 1) * HEAD_DIM])
            top = jnp.max(scores, axis=0, keepdims=True)
            powers = jnp.exp(scores - top)
            sums = jnp.sum(powers, axis=0, keepdims=True)
            parts.append(dot_tn(values, powers.astype(BF)) / sums)
            logsums.append(top + jnp.log(sums))
        out = jnp.concatenate(parts, axis=0).T.astype(BF)
        o_ref[:, n * both : (n + 1) * both] = out
        lse_ref[n] = jnp.concatenate(logsums, axis=0)
        total = total + dot_nt(out, w_ref[n, :, both:])
    low = total[:, deep].astype(BF)
    z4_ref[...] = low
    stream = stream + total[:, :width] + dot(low, up_cross_ref[...])
    s2_ref[...] = stream
    n3_ref[...] = layer_norm(stream, gain_ref[2:3, :], bias_ref[2:3, :])


def cross_forward(x, ys, up_self, up_cross, down, gains, biases, weight, keyvals, core_at):
    rows, width = x.shape
    members, local = len(keyvals), weight.shape[2] // 4
    plain, wide = sds((rows, width), BF), sds((rows, width), F32)
    low = sds((rows, down.shape[0]), BF)
    logsums = sds((members // 2, 2 * local // HEAD_DIM, rows), F32)
    shapes = [wide, wide, plain, plain, plain, plain, logsums, low, low, low]
    arrays = [x, up_self, up_cross, down, gains, biases, *keyvals, *ys]
    return weight_call(
        functools.partial(cross_kernel, weight, members, local, core_at),
        weight,
        (1,),
        [whole_spec(a.shape) for a in arrays],
        [whole_spec(o.shape) for o in shapes],
        shapes,
        weight.scratch(),
        cost(24 * rows * width * width, 8 * width * width),
        arrays,
    )


def cross_back_kernel(weight, members, local, core_at, places_ref, *refs):
    w_refs, refs = refs[: weight.count], refs[weight.count :]
    *refs, w_ref, sems = refs
    copies = weight.bring(w_refs, places_ref, w_ref, sems)
    (
        g_ref, s1_ref, s2_ref, n2_ref, q_ref, o_ref, lse_ref, u_ref, z4_ref,
        up_ref, down5_ref, down2_ref, gain_ref, bias_ref,
    ), refs = refs[:14], refs[14:]
    kv_refs, refs = refs[:members], refs[members:]
    dn_refs, (r1_ref, r1b_ref, fixed_ref, near_ref, *gkv_refs) = (
        refs[: -4 - members],
        refs[-4 - members :],
    )
    summed = total_of(dn_refs)
    width = g_ref.shape[1]
    rank = up_ref.shape[0]
    deep = slice(width, width + rank)
    stream = s2_ref[...]
    low = summed[:, deep].astype(BF)
    grad_normed = summed[:, :width] + dot(low, down5_ref[...])
    normed = layer_norm(stream, gain_ref[2:3, :], bias_ref[2:3, :])
    by_piece(fixed_ref, rank, dot_tn(low, normed))
    grad = g_ref[...].astype(F32) + norm_backward(stream, gain_ref[2:3, :], grad_normed)
    branch = grad.astype(BF)
    low = dot_nt(branch, up_ref[...]).astype(BF)
    by_piece(fixed_ref, 2 * rank, dot_tn(z4_ref[...], branch))
    by_piece(near_ref, 0, dot_tn(low, o_ref[...]))
    total = jnp.zeros((g_ref.shape[0], width + rank), F32)
    wait_for(copies)
    both, swap = 2 * local, places_ref[core_at]
    for n in range(members // 2):
        columns = slice(n * both, (n + 1) * both)
        grad_out = dot(branch, w_ref[n, :width, both:]) + dot(low, w_ref[n, deep, both:])
        grad_out = grad_out.astype(BF)
        query = q_ref[:, columns]
        deltas = head_sums(grad_out.astype(F32) * o_ref[:, columns].astype(F32))
        found = in_order(swap, kv_refs[2 * n][...], kv_refs[2 * n + 1][...])
        queries, keys, values = [], [], []
        for head in range(both // HEAD_DIM):
            keyval, own = found[head * HEAD_DIM // local], head * HEAD_DIM % local
            key = keyval[:, own : own + HEAD_DIM]
            value = keyval[:, local + own : local + own + HEAD_DIM]
            at = slice(head * HEAD_DIM, (head + 1) * HEAD_DIM)
            q, g = query[:, at], grad_out[:, at]
            probs = jnp.exp(dot_nt(key, q) - lse_ref[n, head : head + 1, :])
            grad_scores = (probs * (dot_nt(value, g) - deltas[head : head + 1])).astype(BF)
            queries.append(dot_tn(key, grad_scores))
            keys.append(dot(grad_scores, q))
            values.append(dot(probs.astype(BF), g))
        grad_query = (jnp.concatenate(queries, axis=0).T * HEAD_DIM**-0.5).astype(BF)
        half = len(keys) // 2
        first = jnp.concatenate(keys[:half] + values[:half], axis=1).astype(BF)
        second = jnp.concatenate(keys[half:] + values[half:], axis=1).astype(BF)
        gkv_refs[2 * n][...], gkv_refs[2 * n + 1][...] = in_order(swap, first, second)
        ups = dot_tn(u_ref[...], grad_query).astype(BF)
        near_ref[2 * n, rank:, :] = ups[:, :local]
        near_ref[2 * n + 1, rank:, :] = ups[:, local:]
        total = total + dot_nt(grad_query, w_ref[n, :, :both])
    low = total[:, deep].astype(BF)
    by_piece(fixed_ref, 0, dot_tn(low, n2_ref[...]))
    grad_normed = total[:, :width] + dot(low, down2_ref[...])
    grad = grad + norm_backward(s1_ref[...], gain_ref[1:2, :], grad_normed)
    r1_ref[...] = grad
    r1b_ref[...] = grad.astype(BF)


def cross_back(
    g, dns, s1, s2, n2, q, o, lse, u, z4, up, down5, down2, gains, biases, weight, keyvals, core_at
):
    rows, width = g.shape
    rank = up.shape[0]
    members, local = len(keyvals), weight.shape[2] // 4
    shapes = [sds((rows, width), F32), sds((rows, width), BF)]
    shapes += [sds((members, n * rank, local), BF) for n in (3, 2)]
    shapes += [sds(keyvals[0].shape, BF)] * members
    arrays = [g, s1, s2, n2, q, o, lse, u, z4, up, down5, down2, gains, biases, *keyvals, *dns]
    return weight_call(
        functools.partial(cross_back_kernel, weight, members, local, core_at),
        weight,
        (1,),
        [whole_spec(a.shape) for a in arrays],
        [whole_spec(o.shape) for o in shapes],
        shapes,
        weight.scratch(),
        cost(32 * rows * width * width, 8 * width * width),
        arrays,
    )


def output_kernel(s2_ref, up_ref, g_ref, *refs):
    *y_refs, out_ref, gup_ref = refs
    width, rank = out_ref.shape[1], up_ref.shape[0]
    total = total_of(y_refs)
    low = total[:, width : width + rank].astype(BF)
    out_ref[...] = (s2_ref[...] + total[:, :width] + dot(low, up_ref[...])).astype(BF)
    by_piece(gup_ref, 0, dot_tn(low, g_ref[...]))


def output_end(s2, ys, up, g, members):
    rank, width = up.shape
    return pl.pallas_call(
        output_kernel,
        out_shape=[sds(g.shape, BF), sds((members, rank, width // members), BF)],
        compiler_params=pltpu.CompilerParams(vmem_limit_bytes=VMEM_LIMIT),
        cost_estimate=cost(0, 0),
    )(s2, up, g, *ys)


def input_kernel(x_ref, r_ref, down_ref, gain_ref, *refs):
    *dn_refs, out_ref = refs
    width, rank = out_ref.shape[1], down_ref.shape[0]
    total = total_of(dn_refs)
    low = total[:, width : width + rank].astype(BF)
    grad = total[:, :width] + dot(low, down_ref[...])
    back = norm_backward(x_ref[...].astype(F32), gain_ref[...], grad)
    out_ref[...] = (r_ref[...] + back).astype(BF)


def input_end(x, r1, dns, down, gain):
    return pl.pallas_call(
        input_kernel,
        out_shape=sds(x.shape, BF),
        compiler_params=pltpu.CompilerParams(vmem_limit_bytes=VMEM_LIMIT),
        cost_estimate=cost(0, 0),
    )(x, r1, down, gain, *dns)


def context_kernel(weight, members, at_pieces, places_ref, *refs):
    w_refs, refs = refs[: weight.count], refs[weight.count :]
    blocks, (down_ref, kv_ref, low_ref, w_ref, sems) = refs[:members], refs[members:]
    wait_for(weight.bring(w_refs, places_ref, w_ref, sems))
    rank, local = down_ref.shape[1], blocks[0].shape[1]
    width = members * local
    low, keyval = 0.0, 0.0
    for k in range(members):
        at = pl.ds(pl.multiple_of(places_ref[at_pieces + k], local), local)
        low = low + dot(blocks[k][...], down_ref[at, :])
        keyval = keyval + dot(blocks[k][...], w_ref[at, :])
    low = low.astype(BF)
    low_ref[...] = low
    kv_ref[...] = (keyval + dot(low, w_ref[width : width + rank, :])).astype(BF)


def context_forward(at_pieces, blocks, weight, down):
    count = blocks[0].shape[0]
    arrays = (*blocks, down)
    shapes = [sds((count, weight.shape[1]), BF), sds((count, down.shape[1]), BF)]
    return weight_call(
        functools.partial(context_kernel, weight, len(blocks), at_pieces),
        weight,
        (1,),
        [whole_spec(a.shape) for a in arrays],
        [whole_spec(s.shape) for s in shapes],
        shapes,
        weight.scratch(),
        cost(0, 0),
        arrays,
    )


def context_back_kernel(weight, members, at_pieces, places_ref, *refs):
    w_refs, refs = refs[: weight.count], refs[weight.count :]
    blocks, (down_ref, low_ref, g_ref), refs = (
        refs[:members],
        refs[members : members + 3],
        refs[members + 3 :],
    )
    gup_ref, *refs, w_ref, sems = refs
    wait_for(weight.bring(w_refs, places_ref, w_ref, sems))
    rank, local = down_ref.shape[1], blocks[0].shape[1]
    width = members * local
    grad = g_ref[...]
    low = dot_nt(grad, w_ref[width : width + rank, :]).astype(BF)
    gup_ref[...] = dot_tn(low_ref[...], grad)
    for k in range(members):
        at = pl.ds(pl.multiple_of(places_ref[at_pieces + k], local), local)
        out = dot_nt(grad, w_ref[at, :]) + dot_nt(low, down_ref[at, :])
        refs[k][...] = out.astype(BF)
        refs[members + k][...] = dot_tn(low, blocks[k][...]).astype(BF)


def context_back(at_pieces, blocks, weight, down, low, grad):
    count, local = blocks[0].shape
    rank, members = down.shape[1], len(blocks)
    arrays = (*blocks, down, low, grad)
    shapes = (
        [sds((rank, weight.shape[1]), F32)]
        + [sds((count, local), BF)] * members
        + [sds((rank, local), BF)] * members
    )
    return weight_call(
        functools.partial(context_back_kernel, weight, members, at_pieces),
        weight,
        (1,),
        [whole_spec(a.shape) for a in arrays],
        [whole_spec(s.shape) for s in shapes],
        shapes,
        weight.scratch(),
        cost(10**10, 10**6),
        arrays,
    )


def table_kernel(cos_ref, sin_ref, out_cos_ref, out_left_ref, out_right_ref):
    half, breadth = ROT // 2, 2 * HEAD_DIM
    lane = lax.broadcasted_iota(jnp.int32, (half, breadth), 1)
    row = lax.broadcasted_iota(jnp.int32, (half, breadth), 0)
    within = lane % HEAD_DIM
    first = jnp.where(within == row, 1.0, 0.0)
    second = jnp.where(within == row + half, 1.0, 0.0)

    def spread(ref, pattern):
        return lax.dot_general(
            ref[...], pattern, (((0,), (0,)), ((), ())),
            precision=lax.Precision.HIGHEST, preferred_element_type=F32,
        )

    lanes = lax.broadcasted_iota(jnp.int32, out_cos_ref.shape, 1) % HEAD_DIM
    out_cos_ref[...] = jnp.where(lanes < ROT, spread(cos_ref, first + second), 1.0)
    out_left_ref[...] = -spread(sin_ref, first)
    out_right_ref[...] = spread(sin_ref, second)


def rotary_tables(cosines, sines):
    tokens = cosines.shape[1]
    return pl.pallas_call(
        table_kernel,
        out_shape=[sds((tokens, 2 * HEAD_DIM), F32)] * 3,
        compiler_params=pltpu.CompilerParams(vmem_limit_bytes=VMEM_LIMIT),
        cost_estimate=cost(0, 0),
    )(cosines, sines)


def feed_kernel(weight, first, last, number, places_ref, *refs):
    w_refs, refs = refs[: weight.count], refs[weight.count :]
    n_refs, g_refs, (down_ref, up_ref), refs = (
        refs[:number],
        refs[number : 2 * number],
        refs[2 * number : 2 * number + 2],
        refs[2 * number + 2 :],
    )
    if not first:
        (low_in, glow_in, y_in, dn_in), refs = refs[:4], refs[4:]
    *refs, gdown_ref, ggate_ref, gupper_ref, n_ref, g_ref, w_ref, sems = refs
    step, width = pl.program_id(0), n_ref.shape[1]
    rank, part = gdown_ref.shape
    take_tile(n_refs, n_ref, step)
    take_tile(g_refs, g_ref, step)

    @pl.when(step == 0)
    def _():
        wait_for(weight.bring(w_refs, places_ref, w_ref, sems))
        for ref in (gdown_ref, ggate_ref, gupper_ref):
            ref[...] = jnp.zeros_like(ref)

    normed, grad = n_ref[...], g_ref[...]
    if first:
        low = dot_nt(normed, down_ref[...]).astype(BF)
        grad_low = dot_nt(grad, up_ref[...]).astype(BF)
        refs[2][...] = low
        refs[3][...] = grad_low
    else:
        low, grad_low = low_in[...], glow_in[...]
    deep = slice(width, width + rank)
    both = dot(normed, w_ref[:width, : 2 * part]) + dot(low, w_ref[deep, : 2 * part])
    gate, upper = both[:, :part], both[:, part:]
    grad_unit = dot(grad, w_ref[:width, 2 * part :]) + dot(grad_low, w_ref[deep, 2 * part :])
    sigmoid = 1.0 / (1.0 + jnp.exp(-gate))
    acted = gate * sigmoid
    unit = (acted * upper).astype(BF)
    grad_gate = (grad_unit * upper * (sigmoid + acted * (1.0 - sigmoid))).astype(BF)
    grad_upper = (grad_unit * acted).astype(BF)
    y = dot_nt(unit, w_ref[:, 2 * part :])
    dn = dot_nt(grad_gate, w_ref[:, :part]) + dot_nt(grad_upper, w_ref[:, part : 2 * part])
    if not first:
        y, dn = y + y_in[...].astype(F32), dn + dn_in[...].astype(F32)
    if last:
        give_tile(y.astype(BF), refs[:number], step)
        give_tile(dn.astype(BF), refs[number:], step)
    else:
        refs[0][...] = y.astype(BF)
        refs[1][...] = dn.astype(BF)
    gdown_ref[...] += dot_tn(grad_low, unit)
    ggate_ref[...] += dot_tn(low, grad_gate)
    gupper_ref[...] += dot_tn(low, grad_upper)


def feed(normed, grads, down, up, weight, sums, rows, start, last):
    block, width = normed[0].shape
    rank, number = down.shape[0], len(normed)
    deep, part = weight.shape[0], weight.shape[1] // 3
    narrow = sds((rank, part), F32)
    tokens = number * block
    if last:
        wide = sds((block, deep // LANES * LANES + LANES), BF)
        shapes, specs = [wide] * (2 * number), [whole_spec(wide.shape)] * (2 * number)
    else:
        shapes, specs = [sds((tokens, deep), BF)] * 2, [row_spec(rows, deep)] * 2
    first = not sums
    if first:
        shapes, specs = shapes + [sds((tokens, rank), BF)] * 2, specs + [row_spec(rows, rank)] * 2
    arrays = (*normed, *grads, down, up)
    size = weight.shape[0] * weight.shape[1]
    return weight_call(
        functools.partial(feed_kernel, weight, first, last, number),
        weight,
        (tokens // rows,),
        [whole_spec(a.shape) for a in arrays]
        + [pl.BlockSpec((rows, a.shape[1]), lambda t, *_: (start + t, 0)) for a in sums],
        specs + [whole_spec(narrow.shape)] * 3,
        shapes + [narrow] * 3,
        [pltpu.VMEM((rows, width), BF)] * 2 + weight.scratch(),
        cost(8 * tokens * size, 2 * size),
        [*arrays, *sums],
    )


def settle_first_kernel(fold, labels_ref, in_ref, down_ref, hid_ref, gate_ref):
    slot = pl.program_id(0)
    local = down_ref.shape[-1]
    for ref in (down_ref, hid_ref, gate_ref):
        ref[...] = jnp.zeros_like(ref)
    for s in range(in_ref.shape[0]):

        @pl.when(labels_ref[s] == slot)
        def _(s=s):
            for n, k in enumerate(DOWN_FIRST):
                down_ref[0, k] += in_ref[s, n].astype(F32)
            for k in range(fold):
                at, n = slice(k * local, (k + 1) * local), len(DOWN_FIRST) + k
                hid_ref[0, :, at] += in_ref[s, n].astype(F32)
                gate_ref[0, 0, :, at] += in_ref[s, n + fold].astype(F32)
                gate_ref[0, 1, :, at] += in_ref[s, n + 2 * fold].astype(F32)


def settle_second_kernel(labels_ref, in_ref, down_in, down_ref, up_ref):
    del down_in
    slot = pl.program_id(0)
    downs, ups = down_ref.shape[1], up_ref.shape[1]
    for ref in (down_ref, up_ref):
        ref[...] = jnp.zeros_like(ref)
    for s in range(in_ref.shape[0]):

        @pl.when(labels_ref[s] == slot)
        def _(s=s):
            down_ref[0] += in_ref[s, :downs].astype(F32)
            up_ref[0] += in_ref[s, downs : downs + ups].astype(F32)


DOWN_FIRST = (4, 5)


def slot_spec(shape):
    return pl.BlockSpec((1,) + shape[1:], lambda i, *_, n=len(shape): (i,) + (0,) * (n - 1))


def settle_first(labels, grads, slots, fold):
    rank, local = grads.shape[2:]
    hidden = fold * local
    shapes = [
        (slots, 6, rank, local),
        (slots, rank, hidden),
        (slots, 2, rank, hidden),
    ]
    return pl.pallas_call(
        functools.partial(settle_first_kernel, fold),
        grid_spec=pltpu.PrefetchScalarGridSpec(
            num_scalar_prefetch=1,
            grid=(slots,),
            in_specs=[whole_spec(grads.shape)],
            out_specs=[slot_spec(s) for s in shapes],
        ),
        out_shape=[sds(s, F32) for s in shapes],
        compiler_params=params(),
        cost_estimate=cost(0, 0),
    )(labels, grads)


def settle_second(labels, grads, down):
    downs = DOWN_FIRST[0]
    up = down.shape[:1] + (9,) + down.shape[2:]
    return pl.pallas_call(
        settle_second_kernel,
        grid_spec=pltpu.PrefetchScalarGridSpec(
            num_scalar_prefetch=1,
            grid=(down.shape[0],),
            in_specs=[whole_spec(grads.shape), pl.BlockSpec(memory_space=pl.ANY)],
            out_specs=[slot_spec((1, downs) + down.shape[2:]), slot_spec(up)],
        ),
        out_shape=[sds(down.shape, F32), sds(up, F32)],
        input_output_aliases={2: 0},
        compiler_params=params(),
        cost_estimate=cost(0, 0),
    )(labels, grads, down)


def chunks(hidden):
    return 2 * hidden // 3, hidden // 3


def body(
    inputs,
    context,
    positions,
    adapter_index,
    self_in_weight,
    self_out_weight,
    cross_query_weight,
    cross_keyval_weight,
    cross_out_weight,
    feed_in_weight,
    feed_out_weight,
    norm_gains,
    norm_biases,
    adapter_down,
    adapter_down_hidden,
    adapter_up,
    adapter_up_hidden,
    out_cotangent,
    *,
    pairs,
    chips,
):
    group = Group(pairs, chips)
    members = 2 * pairs
    rows, width = inputs.shape[1], inputs.shape[2]
    block = self_in_weight.shape[0]
    local = self_in_weight.shape[2]
    hidden = feed_in_weight.shape[2]
    slots, rank = adapter_down.shape[0], adapter_down.shape[3]
    deep = width + rank
    parts = chunks(hidden)
    fold = hidden // local
    pieces = group.pieces
    gains, biases = norm_gains, norm_biases
    tile = min(256, members * rows)
    tiles = members * rows // tile
    near_tiles = tiles // pairs

    def packed(*parts):
        return jnp.concatenate(parts, axis=1)

    def stacked(*parts):
        return jnp.concatenate(parts, axis=0)

    def listed(values):
        return list(values) if isinstance(values, (list, tuple)) else [values]

    def piece(array, k, size):
        return lax.dynamic_slice_in_dim(array, pieces[k] * size, size, array.ndim - 1)

    def own(array):
        return piece(array, 0, local)

    near_chips = [1, 2] if chips == 4 else list(range(1, chips))
    chip_rows = [(group.chip ^ k) * 2 * block for k in range(chips)]
    one = [[c + o * block for c in chip_rows] for o in (group.core, 1 - group.core)]
    one += [[c + o * block for c in chip_rows] for o in (group.zhi, 1 - group.zhi)]
    row_places = jnp.stack(
        [r for found in one for r in found] + [jnp.zeros_like(group.core)]
        + [p * local for p in pieces] + [group.core]
    ).astype(jnp.int32)
    mine_at, other_at, first_at, second_at, zero = (n * chips for n in range(5))
    at_pieces = zero + 1
    core_at = at_pieces + members

    def chip_weight(own_entry, near, rest, low, columns, halves):
        weight = Weight((deep, columns), row_places)
        entries = [own_entry, *near]
        for k, (array, row) in zip([0, *near_chips], entries):
            weight.add(
                array,
                *[(row + r, block, c, columns, None, at + k, 0) for r, c, at in halves],
            )
        if rest:
            side_by_side = halves[1][0] == 0
            for n, (array, row) in enumerate(rest):
                size = block // 2 if side_by_side else block
                picked = halves if side_by_side else halves[n : n + 1]
                weight.add(
                    array,
                    *[
                        (row, size, c, columns, None, at + 3, n * size if side_by_side else 0)
                        for _, c, at in picked
                    ],
                )
        weight.add(low, (0, rank, 0, columns, None, zero, width))
        return weight

    stacked_halves = [(0, 0, first_at), (block, 0, second_at)]
    packed_halves = [(0, 0, mine_at), (0, 2 * local, other_at)]

    def spread(got, half_at, half, own_block):
        if got and chips == 4:
            turns = [
                got[1][half_at : half_at + half],
                got[0][half_at + half : half_at + 2 * half],
            ]
            if own_block is not None:
                turns = listed(step.mark(*[stacked(turn, own_block) for turn in turns]))
            return [xor_move(turn, "chip", 4, k) for turn, k in zip(turns, near_chips)]
        if own_block is None:
            return []
        return [xor_move(own_block, "chip", chips, k) for k in near_chips]

    def skip(half):
        return half if chips == 4 else 0

    def flat(*groups):
        return [x for g in groups for x in listed(g)]

    def wait_all(*groups):
        groups = [listed(g) for g in groups]
        values = iter(listed(step.wait(*flat(*groups))))
        return [[next(values) for _ in g] for g in groups]

    def swap_all(blocks):
        if not blocks:
            return []
        blocks = listed(step.wait(*blocks))
        return listed(step.wait(*[core_swap(b) for b in blocks]))

    shard_self = packed(*[self_in_weight[:, i] for i in range(3)], self_out_weight.T)
    step = Order(shard_self[:8, :128])
    self_from = [home_swap(shard_self), turned(shard_self)]
    stream_own, context_own = home_swap(inputs[0]), home_swap(context[0])
    index, positions = step.wait(adapter_index, positions)
    index_other, positions_other = step.wait(core_swap(index), core_swap(positions))
    index = jnp.where(group.home, index, index_other)[0]
    positions = jnp.where(group.home, positions, positions_other)[0]
    down = lax.dynamic_index_in_dim(adapter_down.transpose(0, 1, 3, 2), index, 0, keepdims=False)
    up = lax.dynamic_index_in_dim(adapter_up.transpose(0, 2, 1, 3), index, 0, keepdims=False)
    down, up = step.mark(down, up)
    low_self = packed(*[own(up[i]) for i in range(3)], own(down[1]))
    low_keyval = packed(own(up[5]), own(up[6]))
    low_cross = []
    for k in range(pairs):
        two = [
            (group.p ^ k) * local + core * pairs * local for core in (0, 1)
        ]
        low_cross.append(
            packed(
                *[
                    lax.dynamic_slice_in_dim(table[4], where, local, 1)
                    for table in (up, down)
                    for where in two
                ]
            )
        )
    low_cross = stacked(*low_cross)
    low_self, low_keyval, low_cross = step.mark(low_self, low_keyval, low_cross)
    keyval_parts = step.wait(cross_keyval_weight)
    keyval_parts = step.mark(keyval_parts[:, 0], keyval_parts[:, 1])
    shard_cross = step.mark(packed(cross_query_weight, cross_out_weight.T, *keyval_parts))
    far_cross = group.cross(shard_cross)
    blocks_at = [
        lax.dynamic_slice_in_dim(positions, pieces[k] * rows, rows, 0) for k in range(members)
    ]
    half = ROT // 2
    inverse = 10000.0 ** (-jnp.arange(half, dtype=F32) / half)
    angles = inverse[:, None] * step.wait(jnp.concatenate(blocks_at)).astype(F32)[None]
    tables = step.mark(*rotary_tables(*step.mark(jnp.cos(angles), jnp.sin(angles))))
    feed_in, feed_out = step.wait(feed_in_weight, feed_out_weight)
    gate_rows, upper_rows = step.mark(feed_in[:, 0], feed_in[:, 1])
    at = [sum(parts[:i]) for i in range(len(parts))]

    def feed_shard(i):
        to = slice(at[i], at[i] + parts[i])
        gate, upper, out = step.wait(gate_rows, upper_rows, feed_out)
        return step.mark(packed(gate[:, to], upper[:, to], out.T[:, to]))

    shard_feed = [feed_shard(i) for i in range(len(parts))]

    self_from = step.wait(*self_from)
    ready_self = step.mark(stacked(*self_from))
    near_self = spread([], 0, 0, ready_self)
    stream_own, context_own = step.wait(stream_own, context_own)
    stream_far, context_far = group.far_p(stream_own), group.far_p(context_own)
    (near_self,) = wait_all(near_self)
    rest_self = spread(near_self, 0, block, None)
    rest_self, stream_far, context_far, (far_cross,) = wait_all(
        rest_self, stream_far, context_far, [far_cross]
    )
    stream_other, *stream_far_other = swap_all([stream_own, *stream_far])
    stream = [stream_own, stream_other]
    for far, far_other in zip(stream_far, stream_far_other):
        stream += [far, far_other]
    self_weight = chip_weight(
        (ready_self, 0), [(g, 0) for g in near_self], [(g, 0) for g in rest_self], low_self,
        4 * local, stacked_halves,
    )

    mine = jnp.where(group.home, shard_cross, far_cross)
    given = jnp.where(group.home, far_cross, shard_cross)
    keyval_mine, keyval_give = mine[:, 2 * local :], given[:, 2 * local :]
    low_zhi = jnp.where(group.zhi == 0, shard_cross, far_cross)
    high_zhi = jnp.where(group.zhi == 0, far_cross, shard_cross)
    pair = packed(
        *[two[:, n * local : (n + 1) * local] for n in (0, 1) for two in (low_zhi, high_zhi)]
    )
    keyval_mine, keyval_give, pair = step.mark(keyval_mine, keyval_give, pair)
    (keyval_other,) = swap_all([keyval_give])
    ready_keyval = step.mark(stacked(packed(keyval_mine, keyval_other), pair))

    got_one = spread([], 0, 0, ready_keyval)
    pair_far = group.far_p(pair)
    half_columns = shard_feed[0].shape[1] // 2
    halves = step.wait(shard_feed[0][:, :half_columns], shard_feed[0][:, half_columns:])
    feed_one = [home_swap(halves[0]), turned(halves[0])]
    query, keys, values, low_one, normed_one = project_self(
        listed(step.wait(*stream)), gains[0:1], biases[0:1], down[0], self_weight, tables, tile
    )
    query, keys, values = step.mark(query, keys, values)
    heads_far, logsum_far, *y_far = attend_self(
        query, keys, values, self_weight, tile, near_tiles, tiles - near_tiles, rows
    )
    y_far = listed(step.mark(*y_far))

    def far_sums(*groups):
        others = iter(swap_all([g[2 * k + 1] for g in groups for k in range(pairs - 1)]))
        sums = [
            [group.near_sums(g[2 * k], next(others)).astype(BF) for k in range(pairs - 1)]
            for g in groups
        ]
        values = iter(listed(step.mark(*flat(*sums))))
        return [[next(values) for _ in s] for s in sums]

    def move_p(sums):
        return [xor_move(s, "p", pairs, k + 1) for k, s in enumerate(sums)]

    def sum_up(blocks, other, far):
        total = group.near_sums(blocks[0], other)
        for f in far:
            total = total + f.astype(F32)
        return step.mark(total)

    got_one, pair_far, feed_one = wait_all(got_one, pair_far, feed_one)
    (y_sums,) = far_sums(y_far)

    far = move_p(y_sums)
    quarter = block // 2
    if chips == 4:
        turns = [
            stacked(got[start : start + quarter], got[start + block : start + block + quarter], pair_far[0])
            for got, start in ((got_one[1], 0), (got_one[0], quarter))
        ]
        turns = step.mark(*turns)
        got_two = [xor_move(turn, "chip", 4, k) for turn, k in zip(turns, near_chips)]
    else:
        got_two = flat(*[spread([], 0, 0, p) for p in pair_far])
    feed_two = [home_swap(halves[1]), turned(halves[1])]
    heads_near, logsum_near, *y_rows = attend_self(
        step.wait(query), keys, values, self_weight, tile, 0, near_tiles, rows
    )
    y_rows = listed(step.mark(*y_rows))
    far, got_two, feed_two = wait_all(far, got_two, feed_two)
    y_other, context_other, *swapped = swap_all([y_rows[1], context_own, *context_far])
    branch = [y_rows[0], y_other, *far]
    context_blocks = [context_own, context_other]
    for far, far_other in zip(context_far, swapped):
        context_blocks += [far, far_other]
    keyval_weight = chip_weight(
        (ready_keyval, 0), [(g, 0) for g in got_one],
        [(g, 0) for g in got_two] if chips == 4 else [], low_keyval, 2 * local, packed_halves,
    )
    down_context = step.mark(down[3].T)
    keyval, low_context = context_forward(at_pieces, context_blocks, keyval_weight, down_context)
    keyval = step.mark(keyval)

    keyval_far = group.far_p(keyval)
    ready_feed = [step.mark(stacked(*[packed(*two) for two in zip(feed_one, feed_two)]))]
    found = [(ready_keyval, block, block, 0, 0, 0)]
    found += [(g, block, block, k, 0, 0) for g, k in zip(got_one, near_chips)]
    if chips == 4:
        turns = [got_two[1][block : block + quarter], got_two[0][block + quarter :]]
        got_three = [xor_move(turn, "chip", 4, k) for turn, k in zip(turns, near_chips)]
        keyval_far, got_three = wait_all(keyval_far, got_three)
        found += [(g, 0, quarter, 3, n * quarter, 1) for n, g in enumerate(got_three)]
        found.append((pair_far[0], 0, block, 0, 0, 1))
        for n, (g, k) in enumerate(zip(got_two, near_chips)):
            found += [(g, block, block, k, 0, 1), (g, quarter, quarter, 3, n * quarter, 0)]
    else:
        (keyval_far,) = wait_all(keyval_far)
        count = len(near_chips)
        for n, p in enumerate(pair_far):
            found.append((p, 0, block, 0, 0, n + 1))
            found += [
                (g, 0, block, k, 0, n + 1)
                for g, k in zip(got_two[n * count : (n + 1) * count], near_chips)
            ]
    arrays = []
    for entry in found:
        if not any(entry[0] is a for a in arrays):
            arrays.append(entry[0])
    swapped = swap_all([keyval, *keyval_far, *arrays])
    keyvals = [keyval, swapped[0]]
    for far, far_other in zip(keyval_far, swapped[1:]):
        keyvals += [far, far_other]
    others = swapped[1 + len(keyval_far) :]
    cross_weight = Weight((pairs, deep, 4 * local), row_places)
    for array, other in zip(arrays, others):
        entries = [e[1:] for e in found if e[0] is array]
        for source, places in ((array, mine_at), (other, other_at)):
            cross_weight.add(
                source,
                *[
                    (row, size, 0, 4 * local, n, places + k, offset)
                    for row, size, k, offset, n in entries
                ],
            )
    cross_weight.add(
        low_cross, *[(n * rank, rank, 0, 4 * local, n, zero, width) for n in range(pairs)]
    )

    near_feed = [spread([], 0, 0, ready_feed[0])]
    feed_from = [home_swap(step.wait(shard_feed[1])), turned(step.wait(shard_feed[1]))]
    stream_own, *branch = step.wait(stream_own, *branch)

    (
        stream_one, stream_two, normed_two, normed_three, query_cross, heads_cross, logsum_cross,
        low_two, low_three, low_four,
    ) = cross_forward(
        stream_own, branch, up[3], up[7], down[2], gains, biases, cross_weight, keyvals, core_at,
    )
    normed_own = step.mark(normed_three)
    (feed_from,) = wait_all(feed_from)
    ready_feed.append(step.mark(stacked(*feed_from)))

    normed_far = group.far_p(normed_own)
    cotangent_own = home_swap(step.wait(out_cotangent[0]))
    (normed_other,) = swap_all([normed_own])
    down_hidden = lax.dynamic_index_in_dim(
        adapter_down_hidden.transpose(0, 2, 1), index, 0, keepdims=False
    )
    up_hidden = lax.dynamic_index_in_dim(
        adapter_up_hidden.transpose(0, 2, 1, 3), index, 0, keepdims=False
    )
    feed_down, feed_up = piece(down_hidden, 0, hidden), piece(up_hidden, 0, hidden)
    feed_down, feed_gate, feed_upper = step.mark(feed_down, feed_up[0], feed_up[1])
    low_feed = [
        packed(feed_gate[:, to], feed_upper[:, to], feed_down[:, to])
        for to in [slice(a, a + p) for a, p in zip(at, parts)]
    ]
    low_feed = step.mark(*low_feed)
    (near_feed[0],) = wait_all(near_feed[0])
    rest_feed = spread(near_feed[0], 0, block, None)
    normed_far, (cotangent_own,) = wait_all(normed_far, [cotangent_own])
    cotangent_other, *normed_swapped = swap_all([cotangent_own, *normed_far])

    def feed_weight(i, rest):
        return chip_weight(
            (ready_feed[i], 0), [(g, 0) for g in near_feed[i]], [(g, 0) for g in rest],
            low_feed[i], 3 * parts[i], stacked_halves,
        )

    normed_blocks = [[normed_own, normed_other], []]
    cotangent_blocks = [[cotangent_own, cotangent_other], []]

    def feed_pass(weight, half, state, last):
        normed, cotangent = wait_all(normed_blocks[half], cotangent_blocks[half])
        found = feed(normed, cotangent, down[5], up[8], weight, state, tile, 0, last)
        *values, gdown, ggate, gupper = found
        return listed(step.mark(*values)), [gdown, ggate, gupper]

    def added(one, two):
        return [a + b for a, b in zip(one, two)]

    (rest_feed,) = wait_all(rest_feed) if rest_feed else ([],)
    weight = feed_weight(0, rest_feed)
    near_feed.append(spread([], 0, 0, ready_feed[1]))
    cotangent_far = group.far_p(cotangent_own)
    (y, dn, *lows), grads = feed_pass(weight, 0, (), False)
    states = [(*lows, y, dn)]
    near_feed[1], cotangent_far = wait_all(near_feed[1], cotangent_far)
    swapped = normed_swapped + swap_all(cotangent_far)
    for blocks, fars, others in (
        (normed_blocks[1], normed_far, swapped[: pairs - 1]),
        (cotangent_blocks[1], cotangent_far, swapped[pairs - 1 :]),
    ):
        for far, far_other in zip(fars, others):
            blocks += [far, far_other]
    rest_feed = spread(near_feed[1], 0, block, None)
    (y, dn, *lows), more = feed_pass(weight, 1, (), False)
    states.append((*lows, y, dn))
    feed_grads = [added(grads, more)]
    (rest_feed,) = wait_all(rest_feed) if rest_feed else ([],)

    weight = feed_weight(1, rest_feed)
    found, grads = feed_pass(weight, 1, states[1], True)
    y_far, dn_far = found[: len(found) // 2], found[len(found) // 2 :]

    dn_sums, y_sums = far_sums(dn_far, y_far)
    far = move_p(dn_sums)
    found, more = feed_pass(weight, 0, states[0], True)
    y_rows, dn_rows = found[:2], found[2:]
    feed_grads.append(added(grads, more))
    (far,) = wait_all(far)
    dn_other, y_other = swap_all([dn_rows[1], y_rows[1]])
    grad_normed = [dn_rows[0], dn_other, *far]

    far = move_p(step.mark(*y_sums) if len(y_sums) > 1 else [step.mark(*y_sums)])
    grad_stream, branch_grad, fixed_rows, near_rows, *keyval_rows = cross_back(
        cotangent_own, listed(step.wait(*grad_normed)), stream_one, stream_two, normed_two,
        query_cross, heads_cross, logsum_cross, low_three, low_four, up[7], down[5], down[2],
        gains, biases, cross_weight, keyvals, core_at,
    )
    branch_grad, *keyval_rows = step.mark(branch_grad, *keyval_rows)
    (far,) = wait_all(far)

    branch_far = group.far_p(branch_grad)
    (branch_other,) = swap_all([branch_grad])

    def back(grad, heads, logsum, first, before, ends):
        return attend_back(
            grad, up[3], self_weight, query, keys, values, heads, logsum, tables, low_one, tile,
            first, before, ends,
        )

    def taken(by_piece, k):
        return lax.dynamic_index_in_dim(by_piece, pieces[k], 0, keepdims=False)

    def taken_near(by_member, k):
        member = k // 2 * 2 + (group.core ^ (k % 2))
        return lax.dynamic_index_in_dim(by_member, member, 0, keepdims=False)

    first_rows = listed(
        step.mark(
            *[
                stacked(taken_near(near_rows, k)[:rank], taken(fixed_rows, k)[rank : 2 * rank])
                for k in range(members)
            ]
        )
    )
    others = swap_all([*keyval_rows[1::2], *first_rows[1::2]])
    keyval_sums, first_sums = (
        [group.near_sums(a, b) for a, b in zip(own[::2], others[n * pairs : (n + 1) * pairs])]
        for n, own in enumerate((keyval_rows, first_rows))
    )
    moving = listed(step.mark(*[x.astype(BF) for x in keyval_sums[1:] + first_sums[1:]]))
    keyval_far, first_far = move_p(moving[: pairs - 1]), move_p(moving[pairs - 1 :])
    grads = listed(step.wait(branch_grad, branch_other))
    near_back = step.mark(*back(grads, heads_near, logsum_near, 0, None, None))
    branch_far, keyval_far, first_far = wait_all(branch_far, keyval_far, first_far)

    output, grad_up_eight = step.mark(
        *output_end(
            stream_two, [step.wait(y_rows[0]), y_other, *far], up[8], cotangent_own, members
        )
    )
    swapped = swap_all(branch_far)
    branch_blocks = []
    for f, o in zip(branch_far, swapped):
        branch_blocks += [f, o]

    def columns(array):
        return array.reshape(rank, -1, local).transpose(1, 0, 2)

    def sent(parts):
        parts.append(jnp.full((1, rank, local), index, F32))
        grads = step.mark(jnp.concatenate(parts, axis=0).astype(BF))
        return [home_swap(grads), turned_back(grads)]

    def to_chips(blocks):
        both = step.mark(stacked(*blocks))
        return [both] + [xor_move(both, "chip", chips, k) for k in range(1, chips)]

    def every(blocks):
        grads = stacked(*blocks)
        grads = grads.reshape(-1, grads.shape[0] // (2 * chips), rank, local)
        return grads, grads[:, -1, 0, 0].astype(jnp.int32)

    def total(own, far):
        for f in far:
            own = own + f.astype(F32)
        return own

    summed = total(first_sums[0], first_far).reshape(-1, rank, local)
    first = sent([summed, *[columns(jnp.concatenate(g, axis=1)) for g in zip(*feed_grads)]])
    block_output = home_swap(step.wait(output))
    branch_blocks = listed(step.wait(*branch_blocks))
    found = back(
        branch_blocks, heads_far, logsum_far, near_tiles, near_back,
        (normed_one, low_two, branch_grad),
    )
    first, (block_output,), found = wait_all(first, [block_output], found)
    grad_down_one, grad_up_self, own_rows, *dn_blocks = found

    count = pairs - 1
    dn_others = swap_all(dn_blocks[1::2])
    dn_sums = [group.near_sums(a, b) for a, b in zip(dn_blocks[::2], dn_others)]
    far = move_p(listed(step.mark(*[x.astype(BF) for x in dn_sums[1:]])))
    first = to_chips(first)
    grad_keyval = step.mark(total(keyval_sums[0], keyval_far).astype(BF))
    grad_up_keyval, *found = step.mark(
        *context_back(
            at_pieces, context_blocks, keyval_weight, down_context, low_context, grad_keyval
        )
    )
    context_rows, grad_down_three = found[:members], found[members:]
    far, first = wait_all(far, first)

    second_rows = listed(
        step.mark(
            *[
                stacked(
                    taken(own_rows, k), taken(fixed_rows, k)[:rank],
                    taken(fixed_rows, k)[2 * rank :], taken(grad_up_eight, k), grad_down_three[k],
                    taken_near(near_rows, k)[rank:],
                )
                for k in range(members)
            ]
        )
    )
    swapped = swap_all([*second_rows[1::2], *context_rows[1::2]])
    second_sums, context_sums = (
        [group.near_sums(a, b) for a, b in zip(own[::2], swapped[n * pairs : (n + 1) * pairs])]
        for n, own in enumerate((second_rows, context_rows))
    )
    moving = [x.astype(BF) for x in second_sums[1:] + context_sums[1:]]
    moving = listed(step.mark(*moving))
    second_far, context_far = move_p(moving[:count]), move_p(moving[count:])
    grad_inputs = step.mark(
        input_end(
            stream_own, grad_stream, [dn_blocks[0], dn_others[0], *far], down[0], gains[0:1]
        )
    )
    second_far, context_far = wait_all(second_far, context_far)
    summed = total(second_sums[0], second_far).reshape(-1, rank, local)
    second = sent(
        [
            summed[0:1],
            grad_down_one[None],
            summed[2:3],
            summed[5:6],
            columns(grad_up_self),
            summed[1:2],
            summed[6:7],
            columns(grad_up_keyval),
            summed[3:5],
        ]
    )
    grad_context = home_swap(step.mark(total(context_sums[0], context_far).astype(BF)))
    (second,) = wait_all(second)
    second = to_chips(second)
    grad_inputs = home_swap(step.wait(grad_inputs))
    first, labels = every(listed(step.wait(*first)))
    grad_down, grad_hidden, grad_gate = settle_first(labels, first, slots, fold)
    grad_down = step.mark(grad_down)
    (second,) = wait_all(second)
    second, labels = every(second)
    labels = labels + (step.token[0, 0].astype(F32) * 0.0).astype(jnp.int32)
    grad_down, grad_up = settle_second(labels, second, grad_down)
    return (
        block_output[None],
        grad_inputs.astype(F32)[None],
        grad_context.astype(F32)[None],
        grad_down.transpose(0, 1, 3, 2),
        grad_hidden.transpose(0, 2, 1),
        grad_up.transpose(0, 2, 1, 3),
        grad_gate.transpose(0, 2, 1, 3),
    )


def solution(mesh):
    members = mesh.shape["tensor"]
    chips = mesh.shape["dp"] // 2
    mesh = Mesh(
        mesh.devices.reshape(chips, 2, 2, members // 2), ("chip", "core", "zhi", "p")
    )
    dp, tensor = ("chip", "core"), ("zhi", "p")
    in_specs = (
        P(dp, tensor, None),
        P(dp, None, tensor),
        P(dp, None),
        P(dp),
        P(dp, None, tensor),
        P(tensor, dp),
        P(dp, tensor),
        P(dp, None, tensor),
        P(tensor, dp),
        P(dp, None, tensor),
        P(tensor, dp),
        P(),
        P(),
        P(),
        P(),
        P(),
        P(),
        P(dp, tensor, None),
    )
    out_specs = (
        P(dp, tensor, None),
        P(dp, tensor, None),
        P(dp, None, tensor),
        P(None, None, tensor, None),
        P(None, tensor, None),
        P(None, None, None, tensor),
        P(None, None, None, tensor),
    )

    def run(*args):
        return body(*args, pairs=members // 2, chips=chips)

    return jax.shard_map(run, mesh=mesh, in_specs=in_specs, out_specs=out_specs, check_vma=False)
```

```python
import functools

import jax
import jax.numpy as jnp
from jax import lax
from jax.experimental import pallas as pl
from jax.experimental.pallas import tpu as pltpu
from jax.sharding import Mesh, PartitionSpec as P

HEAD_DIM = 64
ROT = 32
EPSILON = 1e-05
F32 = jnp.float32
BF = jnp.bfloat16
SWAP = ((0, 1), (1, 0))
LANES = 128
VMEM_LIMIT = 56 * 1024 * 1024


def dot(left, right):
    return jnp.dot(left, right, preferred_element_type=F32)


def dot_nt(left, right):
    return lax.dot_general(left, right, (((1,), (1,)), ((), ())), preferred_element_type=F32)


def dot_tn(left, right):
    return lax.dot_general(left, right, (((0,), (0,)), ((), ())), preferred_element_type=F32)


class Order:
    def __init__(self, first):
        self.token = first

    def wait(self, *values):
        *values, self.token = lax.optimization_barrier((*values, self.token))
        return values[0] if len(values) == 1 else values

    mark = wait


def core_swap(x):
    return lax.ppermute(x, "core", SWAP)


def xor_move(x, axis, size, k):
    return lax.ppermute(x, axis, [(i, i ^ k) for i in range(size)])


def home_swap(x):
    return lax.ppermute(x, ("core", "zhi"), [(0, 0), (1, 2), (2, 1), (3, 3)])


def turned(x):
    return lax.ppermute(x, ("core", "zhi"), [(0, 1), (1, 3), (2, 0), (3, 2)])


def turned_back(x):
    return lax.ppermute(x, ("core", "zhi"), [(0, 2), (1, 0), (2, 3), (3, 1)])


class Group:
    def __init__(self, pairs, chips):
        self.pairs, self.chips = pairs, chips
        self.core, self.zhi, self.p = (lax.axis_index(n) for n in ("core", "zhi", "p"))
        self.chip = lax.axis_index("chip")
        self.home = self.core == self.zhi
        self.pieces = [
            (self.core ^ kc) * pairs + (self.p ^ kp) for kp in range(pairs) for kc in (0, 1)
        ]

    def far_p(self, own):
        return [xor_move(own, "p", self.pairs, k) for k in range(1, self.pairs)]

    def near_sums(self, own, other):
        return own.astype(F32) + other.astype(F32)

    def cross(self, shard):
        return xor_move(shard, "zhi", 2, 1)

    def spread_one(self, block):
        if self.chips == 4:
            return [xor_move(block, "chip", 4, k) for k in (1, 2)]
        return [xor_move(block, "chip", self.chips, k) for k in range(1, self.chips)]

    def spread_two(self, got):
        if self.chips != 4:
            return []
        half = got[0].shape[0] // 2
        return [xor_move(got[1][:half], "chip", 4, 1), xor_move(got[0][half:], "chip", 4, 2)]

    def places(self, rows):
        if self.chips == 4:
            diagonal = (self.chip ^ 3) * rows
            return [(self.chip ^ 1) * rows, (self.chip ^ 2) * rows, diagonal, diagonal + rows // 2]
        return [(self.chip ^ k) * rows for k in range(1, self.chips)]


class Weight:
    def __init__(self, shape, places):
        self.shape, self.places, self.arrays, self.moves = shape, places, [], []

    def add(self, array, *parts):
        self.moves += [(len(self.arrays), *part) for part in parts]
        self.arrays.append(array)

    @property
    def count(self):
        return len(self.arrays)

    def specs(self):
        return [pl.BlockSpec(memory_space=pl.ANY)] * self.count

    def columns(self, start, size):
        if size % 128 or start % 128:
            return 0, self.shape[-1], start
        return start, size, 0

    def scratch(self, size=None):
        shape = self.shape if size is None else self.shape[:-1] + (size,)
        return [pltpu.VMEM(shape, BF), pltpu.SemaphoreType.DMA((len(self.moves),))]

    def at_first(self, step, refs, places_ref, target, sems, start=0, size=None):
        def begin():
            @pl.when(step == 0)
            def _():
                self.bring(refs, places_ref, target, sems, start, size)

        def end():
            @pl.when(step == 0)
            def _():
                wait_for(self.bring(refs, places_ref, target, sems, start, size, go=False))

        return begin, end

    def bring(self, refs, places_ref, target, sems, start=0, size=None, go=True):
        copies = []
        for number, (source, row, rows, column, columns, lead, place, offset) in enumerate(self.moves):
            at = pl.ds(pl.multiple_of(places_ref[place] + offset, 16), rows)
            to = target.at[at] if lead is None else target.at[lead, at]
            if size is not None:
                column, columns = column + start, size
            found = refs[source].at[pl.ds(row, rows), pl.ds(column, columns)]
            copies.append(pltpu.make_async_copy(found, to, sems.at[number]))
        if go:
            for copy in copies:
                copy.start()
        return copies


def wait_for(copies):
    for copy in copies:
        copy.wait()


def weight_call(kernel, weight, grid, in_specs, out_specs, out_shape, scratch, estimate, arrays):
    return pl.pallas_call(
        kernel,
        grid_spec=pltpu.PrefetchScalarGridSpec(
            num_scalar_prefetch=1,
            grid=grid,
            in_specs=weight.specs() + in_specs,
            out_specs=out_specs,
            scratch_shapes=scratch,
        ),
        out_shape=out_shape,
        compiler_params=params(),
        cost_estimate=estimate,
    )(weight.places, *weight.arrays, *arrays)


def stats(stream):
    average = jnp.mean(stream, axis=-1, keepdims=True)
    centred = stream - average
    variance = jnp.mean(centred * centred, axis=-1, keepdims=True)
    scale = lax.rsqrt(variance + EPSILON)
    return centred * scale, scale


def layer_norm(stream, gain, bias):
    return (stats(stream)[0] * gain + bias).astype(BF)


def norm_backward(stream, gain, grad):
    unit, scale = stats(stream)
    grad = grad * gain
    return scale * (
        grad
        - jnp.mean(grad, axis=-1, keepdims=True)
        - unit * jnp.mean(grad * unit, axis=-1, keepdims=True)
    )


def turn(x, cosines, left_sines, right_sines):
    breadth = 2 * HEAD_DIM if x.shape[1] % (2 * HEAD_DIM) == 0 else HEAD_DIM
    half = ROT // 2
    for at in range(0, x.shape[1], breadth):
        group = x[:, at : at + breadth]
        if breadth % 128 == 0:
            left, right = pltpu.roll(group, breadth - half, 1), pltpu.roll(group, half, 1)
        else:
            left = jnp.concatenate([group[:, half:], group[:, :half]], axis=1)
            right = jnp.concatenate([group[:, -half:], group[:, :-half]], axis=1)
        yield (
            at,
            breadth,
            group * cosines[:, :breadth]
            + left * left_sines[:, :breadth]
            + right * right_sines[:, :breadth],
        )


def head_sums(product):
    columns = product.shape[1]
    rows = -(-columns // HEAD_DIM // 8) * 8
    head = lax.broadcasted_iota(jnp.int32, (rows, columns), 0)
    lane = lax.broadcasted_iota(jnp.int32, (rows, columns), 1)
    picked = jnp.where(lane // HEAD_DIM == head, 1.0, 0.0).astype(F32)
    return lax.dot_general(
        picked, product, (((1,), (1,)), ((), ())),
        precision=lax.Precision.HIGHEST, preferred_element_type=F32,
    )


def whole_spec(shape):
    return pl.BlockSpec(shape, lambda *_: (0,) * len(shape))


def row_spec(rows, columns):
    return pl.BlockSpec((rows, columns), lambda t, *_: (t, 0))


def take_tile(refs, tile_ref, step):
    rows, tile = refs[0].shape[0], tile_ref.shape[0]
    for i, ref in enumerate(refs):

        @pl.when(step == i * rows // tile)
        def _(i=i, ref=ref):
            tile_ref[i * rows % tile : i * rows % tile + rows, :] = ref[...]


def give_tile(value, refs, step):
    rows, (tile, columns) = refs[0].shape[0], value.shape
    for i, ref in enumerate(refs):

        @pl.when(step == i * rows // tile)
        def _(i=i, ref=ref):
            ref[:, :columns] = value[i * rows % tile : i * rows % tile + rows]
            ref[:, columns:] = jnp.zeros((rows, ref.shape[1] - columns), ref.dtype)


def total_of(refs):
    total = refs[0][...].astype(F32)
    for ref in refs[1:]:
        total = total + ref[...].astype(F32)
    return total


def by_piece(ref, row, value):
    local = ref.shape[2]
    for k in range(ref.shape[0]):
        ref[k, row : row + value.shape[0], :] = value[:, k * local : (k + 1) * local].astype(
            ref.dtype
        )


def params(semantics=1):
    return pltpu.CompilerParams(
        dimension_semantics=("arbitrary",) * semantics, vmem_limit_bytes=VMEM_LIMIT
    )


def cost(flops, moved, exps=0):
    return pl.CostEstimate(
        flops=int(flops) or 1000, bytes_accessed=int(moved) or 1000, transcendentals=int(exps)
    )


def sds(shape, dtype):
    return jax.ShapeDtypeStruct(shape, dtype)


def query_kernel(weight, part, count, places_ref, *refs):
    w_refs, refs = refs[: weight.count], refs[weight.count :]
    blocks, (gain_ref, bias_ref, down_ref, cos_ref, left_ref, right_ref), refs = (
        refs[:count],
        refs[count : count + 6],
        refs[count + 6 :],
    )
    q_ref, k_ref, v_ref, low_ref, n_ref, x_ref, w_ref, sems = refs
    step = pl.program_id(0)

    begin, end = weight.at_first(step, w_refs, places_ref, w_ref, sems, *part[:2])
    begin()
    take_tile(blocks, x_ref, step)
    local, width = q_ref.shape[1], x_ref.shape[1]
    normed = layer_norm(x_ref[...].astype(F32), gain_ref[...], bias_ref[...])
    n_ref[...] = normed
    low = dot_nt(normed, down_ref[...]).astype(BF)
    low_ref[...] = low
    end()
    at = slice(part[2], part[2] + 3 * local)
    mixed = dot(normed, w_ref[:width, at]) + dot(low, w_ref[width:, at])
    tables = cos_ref[...], left_ref[...], right_ref[...]
    for at, breadth, turned in turn(mixed[:, :local], *tables):
        q_ref[:, at : at + breadth] = (turned * HEAD_DIM**-0.5).astype(BF)
    for at, breadth, turned in turn(mixed[:, local : 2 * local], *tables):
        k_ref[:, at : at + breadth] = turned.astype(BF)
    v_ref[...] = mixed[:, 2 * local :].astype(BF)


def project_self(blocks, gain, bias, down, weight, tables, rows):
    width = blocks[0].shape[1]
    tokens = len(blocks) * blocks[0].shape[0]
    local = weight.shape[1] // 4
    part = weight.columns(0, 3 * local)
    return weight_call(
        functools.partial(query_kernel, weight, part, len(blocks)),
        weight,
        (tokens // rows,),
        [whole_spec(b.shape) for b in blocks]
        + [whole_spec(gain.shape), whole_spec(bias.shape), whole_spec(down.shape)]
        + [row_spec(rows, t.shape[1]) for t in tables],
        [row_spec(rows, local)] * 3 + [row_spec(rows, down.shape[0]), row_spec(rows, width)],
        [sds((tokens, local), BF)] * 3
        + [sds((tokens, down.shape[0]), BF), sds((tokens, width), BF)],
        [pltpu.VMEM((rows, width), BF), *weight.scratch(part[1])],
        cost(8 * tokens * width * local, 8 * width * local),
        [*blocks, gain, bias, down, *tables],
    )


def attend_kernel(weight, part, places_ref, *refs):
    w_refs, refs = refs[: weight.count], refs[weight.count :]
    q_ref, k_ref, v_ref, o_ref, lse_ref, *y_refs, w_ref, sems = refs
    rows, local = q_ref.shape
    step = pl.program_id(0)

    begin, end = weight.at_first(step, w_refs, places_ref, w_ref, sems, *part[:2])
    begin()
    lanes = lax.broadcasted_iota(jnp.int32, (rows, 128), 1)
    logsums = jnp.zeros((rows, 128), F32)
    for head in range(local // HEAD_DIM):
        at = slice(head * HEAD_DIM, (head + 1) * HEAD_DIM)
        scores = dot_nt(q_ref[:, at], k_ref[:, at])
        top = jnp.max(scores, axis=1, keepdims=True)
        powers = jnp.exp(scores - top)
        total = jnp.sum(powers, axis=1, keepdims=True)
        out = dot(powers.astype(BF), v_ref[:, at]) / total
        o_ref[:, at] = out.astype(BF)
        logsums = jnp.where(lanes == head, top + jnp.log(total), logsums)
    lse_ref[...] = logsums.T[: lse_ref.shape[0]]
    end()
    y = dot_nt(o_ref[...], w_ref[:, part[2] : part[2] + local]).astype(BF)
    give_tile(y, y_refs, step)


def wide_of(weight):
    return weight.shape[-2] // LANES * LANES + LANES


def attend_self(query, keys, values, weight, rows, first, count, block):
    tokens, local = query.shape
    heads = -(-local // HEAD_DIM // 8) * 8
    part = weight.columns(3 * local, local)
    blocks = count * rows // block
    return weight_call(
        functools.partial(attend_kernel, weight, part),
        weight,
        (count,),
        [
            pl.BlockSpec((rows, local), lambda t, *_: (first + t, 0)),
            whole_spec(keys.shape),
            whole_spec(values.shape),
        ],
        [row_spec(rows, local), pl.BlockSpec((heads, rows), lambda t, *_: (0, t))]
        + [whole_spec((block, wide_of(weight)))] * blocks,
        [sds((count * rows, local), BF), sds((heads, count * rows), F32)]
        + [sds((block, wide_of(weight)), BF)] * blocks,
        weight.scratch(part[1]),
        cost(16 * count * rows * tokens * local, 8 * query.size, count * rows * tokens),
        [query, keys, values],
    )


def attend_back_kernel(weight, part, first, last, tiles, number, blocks, places_ref, *refs):
    w_refs, refs = refs[: weight.count], refs[weight.count :]
    grads, refs = refs[:number], refs[number:]
    (
        up_ref, q_ref, k_ref, v_ref, o_ref, lse_ref, cos_ref, left_ref, right_ref, low_ref,
    ), refs = refs[:10], refs[10:]
    *refs, g_ref, w_ref, sems = refs
    begin, end = weight.at_first(pl.program_id(0), w_refs, places_ref, w_ref, sems, *part[:2])
    begin()
    take_tile(grads, g_ref, pl.program_id(0))
    if not first:
        (mq_ref, gk_in, gv_in, down_in), refs = refs[:4], refs[4:]
    if last:
        (n_ref, z_ref, r_ref), refs = refs[:3], refs[3:]
        (down_ref, gup_ref, rows_ref), refs = refs[:3], refs[3:]
        dn_refs, (m_ref, gk_ref, gv_ref) = refs[:blocks], refs[blocks:]
    else:
        m_ref, gk_ref, gv_ref, down_ref = refs
    step, rows = pl.program_id(0), q_ref.shape[0]
    width, local = g_ref.shape[1], q_ref.shape[1]
    at_rows = pl.ds(pl.multiple_of((step + tiles) * rows, rows), rows)
    at_query = at_rows if last else pl.ds(pl.multiple_of(step * rows, rows), rows)

    @pl.when(step == 0)
    def _():
        if first:
            gk_ref[...] = jnp.zeros_like(gk_ref)
            gv_ref[...] = jnp.zeros_like(gv_ref)
            down_ref[...] = jnp.zeros_like(down_ref)
        else:
            gk_ref[...] = gk_in[...]
            gv_ref[...] = gv_in[...]
            down_ref[...] = down_in[...]
            m_ref[: mq_ref.shape[0], :local] = mq_ref[...]

    grad = g_ref[...]
    grad_low = dot_nt(grad, up_ref[...]).astype(BF)
    end()
    at = slice(part[2], part[2] + local)
    grad_out = dot(grad, w_ref[:width, at]) + dot(grad_low, w_ref[width:, at])
    grad_out = grad_out.astype(BF)
    out = o_ref[...]
    down_ref[...] += dot_tn(grad_low, out)
    product = grad_out.astype(F32) * out.astype(F32)
    deltas = head_sums(product)
    parts = []
    for head in range(local // HEAD_DIM):
        at = slice(head * HEAD_DIM, (head + 1) * HEAD_DIM)
        q, k, v, g = q_ref[:, at], k_ref[:, at], v_ref[:, at], grad_out[:, at]
        delta = deltas[head : head + 1]
        probs = jnp.exp(dot_nt(k, q) - lse_ref[head : head + 1, :])
        grad_scores = (probs * (dot_nt(v, g) - delta)).astype(BF)
        gv_ref[:, at] += dot(probs.astype(BF), g)
        gk_ref[:, at] += dot(grad_scores, q)
        parts.append(dot_tn(grad_scores, k) * HEAD_DIM**-0.5)
    tables = cos_ref[at_rows, :], -left_ref[at_rows, :], -right_ref[at_rows, :]
    for at, breadth, turned in turn(jnp.concatenate(parts, axis=1), *tables):
        m_ref[at_query, at : at + breadth] = turned.astype(BF)

    if last:

        @pl.when(step == pl.num_programs(0) - 1)
        def _():
            tables = cos_ref[...], -left_ref[...], -right_ref[...]
            for at, breadth, turned in turn(gk_ref[...], *tables):
                m_ref[:, local + at : local + at + breadth] = turned.astype(BF)
            m_ref[:, 2 * local :] = gv_ref[...].astype(BF)
            gup_ref[...] = dot_tn(low_ref[...], m_ref[...])
            rank, block = up_ref.shape[0], dn_refs[0].shape[0]
            down = 0.0
            for i, ref in enumerate(dn_refs):
                at = slice(i * block, (i + 1) * block)
                value = dot_nt(m_ref[at, :], w_ref[:, : 3 * local]).astype(BF)
                ref[:, : width + rank] = value
                ref[:, width + rank :] = jnp.zeros((block, ref.shape[1] - width - rank), BF)
                down = down + dot_tn(value[:, width:], n_ref[at, :])
            by_piece(rows_ref, 0, down)
            by_piece(rows_ref, rank, dot_tn(z_ref[...], r_ref[...]))


def attend_back(
    grads, up, weight, query, keys, values, out, lse, tables, low, rows, start, before, ends
):
    tokens, local = query.shape
    block, width = grads[0].shape
    rank = up.shape[0]
    count = len(grads) * block // rows
    first, last = before is None, ends is not None
    before = () if first else before
    ends = ends if last else ()
    sums = [sds((tokens, local), F32)] * 2 + [sds((rank, local), F32)]
    blocks = tokens // block if last else 0
    if last:
        members = width // local
        shapes = [sums[2], sds((rank, 3 * local), F32), sds((members, 2 * rank, local), BF)]
        shapes += [sds((block, wide_of(weight)), BF)] * blocks
        scratch = [pltpu.VMEM((tokens, 3 * local), BF)]
        scratch += [pltpu.VMEM((tokens, local), F32)] * 2
        part = 0, 4 * local, 3 * local
    else:
        shapes, scratch = [sds((count * rows, local), BF), *sums], []
        part = weight.columns(3 * local, local)
    scratch.append(pltpu.VMEM((rows, width), BF))

    def tile(columns):
        return pl.BlockSpec((rows, columns), lambda t, *_: (start + t, 0))

    return weight_call(
        functools.partial(attend_back_kernel, weight, part, first, last, start, len(grads), blocks),
        weight,
        (count,),
        [
            *[whole_spec(g.shape) for g in grads],
            whole_spec(up.shape),
            tile(local),
            whole_spec(keys.shape),
            whole_spec(values.shape),
            row_spec(rows, local),
            pl.BlockSpec((lse.shape[0], rows), lambda t, *_: (0, t)),
            *[whole_spec(t.shape) for t in tables],
            whole_spec(low.shape),
            *[whole_spec(b.shape) for b in before],
            *[whole_spec(e.shape) for e in ends],
        ],
        [whole_spec(s.shape) for s in shapes],
        shapes,
        scratch + weight.scratch(part[1]),
        cost(40 * count * rows * tokens * local, 10 * query.size, count * rows * tokens),
        [*grads, up, query, keys, values, out, lse, *tables, low, *before, *ends],
    )


def in_order(swap, first, second):
    keep = swap == 0
    return jnp.where(keep, first, second), jnp.where(keep, second, first)


def cross_kernel(weight, members, local, core_at, places_ref, *refs):
    w_refs, refs = refs[: weight.count], refs[weight.count :]
    *refs, w_ref, sems = refs
    copies = weight.bring(w_refs, places_ref, w_ref, sems)
    (x_ref, up_self_ref, up_cross_ref, down_ref, gain_ref, bias_ref), refs = refs[:6], refs[6:]
    kv_refs, refs = refs[:members], refs[members:]
    y_refs, refs = refs[:-10], refs[-10:]
    branch = total_of(y_refs)
    s1_ref, s2_ref, n2_ref, n3_ref, q_ref, o_ref, lse_ref, z2_ref, u_ref, z4_ref = refs
    rows, width = x_ref.shape
    rank = down_ref.shape[0]
    deep = slice(width, width + rank)
    low = branch[:, deep].astype(BF)
    z2_ref[...] = low
    stream = x_ref[...].astype(F32) + branch[:, :width] + dot(low, up_self_ref[...])
    s1_ref[...] = stream
    normed = layer_norm(stream, gain_ref[1:2, :], bias_ref[1:2, :])
    n2_ref[...] = normed
    low = dot_nt(normed, down_ref[...]).astype(BF)
    u_ref[...] = low
    total = jnp.zeros((rows, width + rank), F32)
    wait_for(copies)
    both = 2 * local
    for n in range(members // 2):
        query = dot(normed, w_ref[n, :width, :both]) + dot(low, w_ref[n, deep, :both])
        query = (query * HEAD_DIM**-0.5).astype(BF)
        q_ref[:, n * both : (n + 1) * both] = query
        found = in_order(places_ref[core_at], kv_refs[2 * n][...], kv_refs[2 * n + 1][...])
        parts, logsums = [], []
        for head in range(both // HEAD_DIM):
            keyval, own = found[head * HEAD_DIM // local], head * HEAD_DIM % local
            keys = keyval[:, own : own + HEAD_DIM]
            values = keyval[:, local + own : local + own + HEAD_DIM]
            scores = dot_nt(keys, query[:, head * HEAD_DIM : (head + 1) * HEAD_DIM])
            top = jnp.max(scores, axis=0, keepdims=True)
            powers = jnp.exp(scores - top)
            sums = jnp.sum(powers, axis=0, keepdims=True)
            parts.append(dot_tn(values, powers.astype(BF)) / sums)
            logsums.append(top + jnp.log(sums))
        out = jnp.concatenate(parts, axis=0).T.astype(BF)
        o_ref[:, n * both : (n + 1) * both] = out
        lse_ref[n] = jnp.concatenate(logsums, axis=0)
        total = total + dot_nt(out, w_ref[n, :, both:])
    low = total[:, deep].astype(BF)
    z4_ref[...] = low
    stream = stream + total[:, :width] + dot(low, up_cross_ref[...])
    s2_ref[...] = stream
    n3_ref[...] = layer_norm(stream, gain_ref[2:3, :], bias_ref[2:3, :])


def cross_forward(x, ys, up_self, up_cross, down, gains, biases, weight, keyvals, core_at):
    rows, width = x.shape
    members, local = len(keyvals), weight.shape[2] // 4
    plain, wide = sds((rows, width), BF), sds((rows, width), F32)
    low = sds((rows, down.shape[0]), BF)
    logsums = sds((members // 2, 2 * local // HEAD_DIM, rows), F32)
    shapes = [wide, wide, plain, plain, plain, plain, logsums, low, low, low]
    arrays = [x, up_self, up_cross, down, gains, biases, *keyvals, *ys]
    return weight_call(
        functools.partial(cross_kernel, weight, members, local, core_at),
        weight,
        (1,),
        [whole_spec(a.shape) for a in arrays],
        [whole_spec(o.shape) for o in shapes],
        shapes,
        weight.scratch(),
        cost(24 * rows * width * width, 8 * width * width),
        arrays,
    )


def cross_back_kernel(weight, members, local, core_at, places_ref, *refs):
    w_refs, refs = refs[: weight.count], refs[weight.count :]
    *refs, w_ref, sems = refs
    copies = weight.bring(w_refs, places_ref, w_ref, sems)
    (
        g_ref, s1_ref, s2_ref, n2_ref, q_ref, o_ref, lse_ref, u_ref, z4_ref,
        up_ref, down5_ref, down2_ref, gain_ref, bias_ref,
    ), refs = refs[:14], refs[14:]
    kv_refs, refs = refs[:members], refs[members:]
    dn_refs, (r1_ref, r1b_ref, fixed_ref, near_ref, *gkv_refs) = (
        refs[: -4 - members],
        refs[-4 - members :],
    )
    summed = total_of(dn_refs)
    width = g_ref.shape[1]
    rank = up_ref.shape[0]
    deep = slice(width, width + rank)
    stream = s2_ref[...]
    low = summed[:, deep].astype(BF)
    grad_normed = summed[:, :width] + dot(low, down5_ref[...])
    normed = layer_norm(stream, gain_ref[2:3, :], bias_ref[2:3, :])
    by_piece(fixed_ref, rank, dot_tn(low, normed))
    grad = g_ref[...].astype(F32) + norm_backward(stream, gain_ref[2:3, :], grad_normed)
    branch = grad.astype(BF)
    low = dot_nt(branch, up_ref[...]).astype(BF)
    by_piece(fixed_ref, 2 * rank, dot_tn(z4_ref[...], branch))
    by_piece(near_ref, 0, dot_tn(low, o_ref[...]))
    total = jnp.zeros((g_ref.shape[0], width + rank), F32)
    wait_for(copies)
    both, swap = 2 * local, places_ref[core_at]
    for n in range(members // 2):
        columns = slice(n * both, (n + 1) * both)
        grad_out = dot(branch, w_ref[n, :width, both:]) + dot(low, w_ref[n, deep, both:])
        grad_out = grad_out.astype(BF)
        query = q_ref[:, columns]
        deltas = head_sums(grad_out.astype(F32) * o_ref[:, columns].astype(F32))
        found = in_order(swap, kv_refs[2 * n][...], kv_refs[2 * n + 1][...])
        queries, keys, values = [], [], []
        for head in range(both // HEAD_DIM):
            keyval, own = found[head * HEAD_DIM // local], head * HEAD_DIM % local
            key = keyval[:, own : own + HEAD_DIM]
            value = keyval[:, local + own : local + own + HEAD_DIM]
            at = slice(head * HEAD_DIM, (head + 1) * HEAD_DIM)
            q, g = query[:, at], grad_out[:, at]
            probs = jnp.exp(dot_nt(key, q) - lse_ref[n, head : head + 1, :])
            grad_scores = (probs * (dot_nt(value, g) - deltas[head : head + 1])).astype(BF)
            queries.append(dot_tn(key, grad_scores))
            keys.append(dot(grad_scores, q))
            values.append(dot(probs.astype(BF), g))
        grad_query = (jnp.concatenate(queries, axis=0).T * HEAD_DIM**-0.5).astype(BF)
        half = len(keys) // 2
        first = jnp.concatenate(keys[:half] + values[:half], axis=1).astype(BF)
        second = jnp.concatenate(keys[half:] + values[half:], axis=1).astype(BF)
        gkv_refs[2 * n][...], gkv_refs[2 * n + 1][...] = in_order(swap, first, second)
        ups = dot_tn(u_ref[...], grad_query).astype(BF)
        near_ref[2 * n, rank:, :] = ups[:, :local]
        near_ref[2 * n + 1, rank:, :] = ups[:, local:]
        total = total + dot_nt(grad_query, w_ref[n, :, :both])
    low = total[:, deep].astype(BF)
    by_piece(fixed_ref, 0, dot_tn(low, n2_ref[...]))
    grad_normed = total[:, :width] + dot(low, down2_ref[...])
    grad = grad + norm_backward(s1_ref[...], gain_ref[1:2, :], grad_normed)
    r1_ref[...] = grad
    r1b_ref[...] = grad.astype(BF)


def cross_back(
    g, dns, s1, s2, n2, q, o, lse, u, z4, up, down5, down2, gains, biases, weight, keyvals, core_at
):
    rows, width = g.shape
    rank = up.shape[0]
    members, local = len(keyvals), weight.shape[2] // 4
    shapes = [sds((rows, width), F32), sds((rows, width), BF)]
    shapes += [sds((members, n * rank, local), BF) for n in (3, 2)]
    shapes += [sds(keyvals[0].shape, BF)] * members
    arrays = [g, s1, s2, n2, q, o, lse, u, z4, up, down5, down2, gains, biases, *keyvals, *dns]
    return weight_call(
        functools.partial(cross_back_kernel, weight, members, local, core_at),
        weight,
        (1,),
        [whole_spec(a.shape) for a in arrays],
        [whole_spec(o.shape) for o in shapes],
        shapes,
        weight.scratch(),
        cost(32 * rows * width * width, 8 * width * width),
        arrays,
    )


def output_kernel(s2_ref, up_ref, g_ref, *refs):
    *y_refs, out_ref, gup_ref = refs
    width, rank = out_ref.shape[1], up_ref.shape[0]
    total = total_of(y_refs)
    low = total[:, width : width + rank].astype(BF)
    out_ref[...] = (s2_ref[...] + total[:, :width] + dot(low, up_ref[...])).astype(BF)
    by_piece(gup_ref, 0, dot_tn(low, g_ref[...]))


def output_end(s2, ys, up, g, members):
    rank, width = up.shape
    return pl.pallas_call(
        output_kernel,
        out_shape=[sds(g.shape, BF), sds((members, rank, width // members), BF)],
        compiler_params=pltpu.CompilerParams(vmem_limit_bytes=VMEM_LIMIT),
        cost_estimate=cost(0, 0),
    )(s2, up, g, *ys)


def input_kernel(x_ref, r_ref, down_ref, gain_ref, *refs):
    *dn_refs, out_ref = refs
    width, rank = out_ref.shape[1], down_ref.shape[0]
    total = total_of(dn_refs)
    low = total[:, width : width + rank].astype(BF)
    grad = total[:, :width] + dot(low, down_ref[...])
    back = norm_backward(x_ref[...].astype(F32), gain_ref[...], grad)
    out_ref[...] = (r_ref[...] + back).astype(BF)


def input_end(x, r1, dns, down, gain):
    return pl.pallas_call(
        input_kernel,
        out_shape=sds(x.shape, BF),
        compiler_params=pltpu.CompilerParams(vmem_limit_bytes=VMEM_LIMIT),
        cost_estimate=cost(0, 0),
    )(x, r1, down, gain, *dns)


def context_kernel(weight, members, at_pieces, places_ref, *refs):
    w_refs, refs = refs[: weight.count], refs[weight.count :]
    blocks, (down_ref, kv_ref, low_ref, w_ref, sems) = refs[:members], refs[members:]
    wait_for(weight.bring(w_refs, places_ref, w_ref, sems))
    rank, local = down_ref.shape[1], blocks[0].shape[1]
    width = members * local
    low, keyval = 0.0, 0.0
    for k in range(members):
        at = pl.ds(pl.multiple_of(places_ref[at_pieces + k], local), local)
        low = low + dot(blocks[k][...], down_ref[at, :])
        keyval = keyval + dot(blocks[k][...], w_ref[at, :])
    low = low.astype(BF)
    low_ref[...] = low
    kv_ref[...] = (keyval + dot(low, w_ref[width : width + rank, :])).astype(BF)


def context_forward(at_pieces, blocks, weight, down):
    count = blocks[0].shape[0]
    arrays = (*blocks, down)
    shapes = [sds((count, weight.shape[1]), BF), sds((count, down.shape[1]), BF)]
    return weight_call(
        functools.partial(context_kernel, weight, len(blocks), at_pieces),
        weight,
        (1,),
        [whole_spec(a.shape) for a in arrays],
        [whole_spec(s.shape) for s in shapes],
        shapes,
        weight.scratch(),
        cost(0, 0),
        arrays,
    )


def context_back_kernel(weight, members, at_pieces, places_ref, *refs):
    w_refs, refs = refs[: weight.count], refs[weight.count :]
    blocks, (down_ref, low_ref, g_ref), refs = (
        refs[:members],
        refs[members : members + 3],
        refs[members + 3 :],
    )
    gup_ref, *refs, w_ref, sems = refs
    wait_for(weight.bring(w_refs, places_ref, w_ref, sems))
    rank, local = down_ref.shape[1], blocks[0].shape[1]
    width = members * local
    grad = g_ref[...]
    low = dot_nt(grad, w_ref[width : width + rank, :]).astype(BF)
    gup_ref[...] = dot_tn(low_ref[...], grad)
    for k in range(members):
        at = pl.ds(pl.multiple_of(places_ref[at_pieces + k], local), local)
        out = dot_nt(grad, w_ref[at, :]) + dot_nt(low, down_ref[at, :])
        refs[k][...] = out.astype(BF)
        refs[members + k][...] = dot_tn(low, blocks[k][...]).astype(BF)


def context_back(at_pieces, blocks, weight, down, low, grad):
    count, local = blocks[0].shape
    rank, members = down.shape[1], len(blocks)
    arrays = (*blocks, down, low, grad)
    shapes = (
        [sds((rank, weight.shape[1]), F32)]
        + [sds((count, local), BF)] * members
        + [sds((rank, local), BF)] * members
    )
    return weight_call(
        functools.partial(context_back_kernel, weight, members, at_pieces),
        weight,
        (1,),
        [whole_spec(a.shape) for a in arrays],
        [whole_spec(s.shape) for s in shapes],
        shapes,
        weight.scratch(),
        cost(10**10, 10**6),
        arrays,
    )


def table_kernel(cos_ref, sin_ref, out_cos_ref, out_left_ref, out_right_ref):
    half, breadth = ROT // 2, 2 * HEAD_DIM
    lane = lax.broadcasted_iota(jnp.int32, (half, breadth), 1)
    row = lax.broadcasted_iota(jnp.int32, (half, breadth), 0)
    within = lane % HEAD_DIM
    first = jnp.where(within == row, 1.0, 0.0)
    second = jnp.where(within == row + half, 1.0, 0.0)

    def spread(ref, pattern):
        return lax.dot_general(
            ref[...], pattern, (((0,), (0,)), ((), ())),
            precision=lax.Precision.HIGHEST, preferred_element_type=F32,
        )

    lanes = lax.broadcasted_iota(jnp.int32, out_cos_ref.shape, 1) % HEAD_DIM
    out_cos_ref[...] = jnp.where(lanes < ROT, spread(cos_ref, first + second), 1.0)
    out_left_ref[...] = -spread(sin_ref, first)
    out_right_ref[...] = spread(sin_ref, second)


def rotary_tables(cosines, sines):
    tokens = cosines.shape[1]
    return pl.pallas_call(
        table_kernel,
        out_shape=[sds((tokens, 2 * HEAD_DIM), F32)] * 3,
        compiler_params=pltpu.CompilerParams(vmem_limit_bytes=VMEM_LIMIT),
        cost_estimate=cost(0, 0),
    )(cosines, sines)


def feed_kernel(weight, first, last, number, places_ref, *refs):
    w_refs, refs = refs[: weight.count], refs[weight.count :]
    n_refs, g_refs, (down_ref, up_ref), refs = (
        refs[:number],
        refs[number : 2 * number],
        refs[2 * number : 2 * number + 2],
        refs[2 * number + 2 :],
    )
    if not first:
        (low_in, glow_in, y_in, dn_in), refs = refs[:4], refs[4:]
    *refs, gdown_ref, ggate_ref, gupper_ref, n_ref, g_ref, w_ref, sems = refs
    step, width = pl.program_id(0), n_ref.shape[1]
    rank, part = gdown_ref.shape
    take_tile(n_refs, n_ref, step)
    take_tile(g_refs, g_ref, step)

    @pl.when(step == 0)
    def _():
        wait_for(weight.bring(w_refs, places_ref, w_ref, sems))
        for ref in (gdown_ref, ggate_ref, gupper_ref):
            ref[...] = jnp.zeros_like(ref)

    normed, grad = n_ref[...], g_ref[...]
    if first:
        low = dot_nt(normed, down_ref[...]).astype(BF)
        grad_low = dot_nt(grad, up_ref[...]).astype(BF)
        refs[2][...] = low
        refs[3][...] = grad_low
    else:
        low, grad_low = low_in[...], glow_in[...]
    deep = slice(width, width + rank)
    both = dot(normed, w_ref[:width, : 2 * part]) + dot(low, w_ref[deep, : 2 * part])
    gate, upper = both[:, :part], both[:, part:]
    grad_unit = dot(grad, w_ref[:width, 2 * part :]) + dot(grad_low, w_ref[deep, 2 * part :])
    sigmoid = 1.0 / (1.0 + jnp.exp(-gate))
    acted = gate * sigmoid
    unit = (acted * upper).astype(BF)
    grad_gate = (grad_unit * upper * (sigmoid + acted * (1.0 - sigmoid))).astype(BF)
    grad_upper = (grad_unit * acted).astype(BF)
    y = dot_nt(unit, w_ref[:, 2 * part :])
    dn = dot_nt(grad_gate, w_ref[:, :part]) + dot_nt(grad_upper, w_ref[:, part : 2 * part])
    if not first:
        y, dn = y + y_in[...].astype(F32), dn + dn_in[...].astype(F32)
    if last:
        give_tile(y.astype(BF), refs[:number], step)
        give_tile(dn.astype(BF), refs[number:], step)
    else:
        refs[0][...] = y.astype(BF)
        refs[1][...] = dn.astype(BF)
    gdown_ref[...] += dot_tn(grad_low, unit)
    ggate_ref[...] += dot_tn(low, grad_gate)
    gupper_ref[...] += dot_tn(low, grad_upper)


def feed(normed, grads, down, up, weight, sums, rows, start, last):
    block, width = normed[0].shape
    rank, number = down.shape[0], len(normed)
    deep, part = weight.shape[0], weight.shape[1] // 3
    narrow = sds((rank, part), F32)
    tokens = number * block
    if last:
        wide = sds((block, deep // LANES * LANES + LANES), BF)
        shapes, specs = [wide] * (2 * number), [whole_spec(wide.shape)] * (2 * number)
    else:
        shapes, specs = [sds((tokens, deep), BF)] * 2, [row_spec(rows, deep)] * 2
    first = not sums
    if first:
        shapes, specs = shapes + [sds((tokens, rank), BF)] * 2, specs + [row_spec(rows, rank)] * 2
    arrays = (*normed, *grads, down, up)
    size = weight.shape[0] * weight.shape[1]
    return weight_call(
        functools.partial(feed_kernel, weight, first, last, number),
        weight,
        (tokens // rows,),
        [whole_spec(a.shape) for a in arrays]
        + [pl.BlockSpec((rows, a.shape[1]), lambda t, *_: (start + t, 0)) for a in sums],
        specs + [whole_spec(narrow.shape)] * 3,
        shapes + [narrow] * 3,
        [pltpu.VMEM((rows, width), BF)] * 2 + weight.scratch(),
        cost(8 * tokens * size, 2 * size),
        [*arrays, *sums],
    )


def settle_first_kernel(fold, labels_ref, in_ref, down_ref, hid_ref, gate_ref):
    slot = pl.program_id(0)
    local = down_ref.shape[-1]
    for ref in (down_ref, hid_ref, gate_ref):
        ref[...] = jnp.zeros_like(ref)
    for s in range(in_ref.shape[0]):

        @pl.when(labels_ref[s] == slot)
        def _(s=s):
            for n, k in enumerate(DOWN_FIRST):
                down_ref[0, k] += in_ref[s, n].astype(F32)
            for k in range(fold):
                at, n = slice(k * local, (k + 1) * local), len(DOWN_FIRST) + k
                hid_ref[0, :, at] += in_ref[s, n].astype(F32)
                gate_ref[0, 0, :, at] += in_ref[s, n + fold].astype(F32)
                gate_ref[0, 1, :, at] += in_ref[s, n + 2 * fold].astype(F32)


def settle_second_kernel(labels_ref, in_ref, down_in, down_ref, up_ref):
    del down_in
    slot = pl.program_id(0)
    downs, ups = down_ref.shape[1], up_ref.shape[1]
    for ref in (down_ref, up_ref):
        ref[...] = jnp.zeros_like(ref)
    for s in range(in_ref.shape[0]):

        @pl.when(labels_ref[s] == slot)
        def _(s=s):
            down_ref[0] += in_ref[s, :downs].astype(F32)
            up_ref[0] += in_ref[s, downs : downs + ups].astype(F32)


DOWN_FIRST = (4, 5)


def slot_spec(shape):
    return pl.BlockSpec((1,) + shape[1:], lambda i, *_, n=len(shape): (i,) + (0,) * (n - 1))


def settle_first(labels, grads, slots, fold):
    rank, local = grads.shape[2:]
    hidden = fold * local
    shapes = [
        (slots, 6, rank, local),
        (slots, rank, hidden),
        (slots, 2, rank, hidden),
    ]
    return pl.pallas_call(
        functools.partial(settle_first_kernel, fold),
        grid_spec=pltpu.PrefetchScalarGridSpec(
            num_scalar_prefetch=1,
            grid=(slots,),
            in_specs=[whole_spec(grads.shape)],
            out_specs=[slot_spec(s) for s in shapes],
        ),
        out_shape=[sds(s, F32) for s in shapes],
        compiler_params=params(),
        cost_estimate=cost(0, 0),
    )(labels, grads)


def settle_second(labels, grads, down):
    downs = DOWN_FIRST[0]
    up = down.shape[:1] + (9,) + down.shape[2:]
    return pl.pallas_call(
        settle_second_kernel,
        grid_spec=pltpu.PrefetchScalarGridSpec(
            num_scalar_prefetch=1,
            grid=(down.shape[0],),
            in_specs=[whole_spec(grads.shape), pl.BlockSpec(memory_space=pl.ANY)],
            out_specs=[slot_spec((1, downs) + down.shape[2:]), slot_spec(up)],
        ),
        out_shape=[sds(down.shape, F32), sds(up, F32)],
        input_output_aliases={2: 0},
        compiler_params=params(),
        cost_estimate=cost(0, 0),
    )(labels, grads, down)


def chunks(hidden):
    return 2 * hidden // 3, hidden // 3


def body(
    inputs,
    context,
    positions,
    adapter_index,
    self_in_weight,
    self_out_weight,
    cross_query_weight,
    cross_keyval_weight,
    cross_out_weight,
    feed_in_weight,
    feed_out_weight,
    norm_gains,
    norm_biases,
    adapter_down,
    adapter_down_hidden,
    adapter_up,
    adapter_up_hidden,
    out_cotangent,
    *,
    pairs,
    chips,
):
    group = Group(pairs, chips)
    members = 2 * pairs
    rows, width = inputs.shape[1], inputs.shape[2]
    block = self_in_weight.shape[0]
    local = self_in_weight.shape[2]
    hidden = feed_in_weight.shape[2]
    slots, rank = adapter_down.shape[0], adapter_down.shape[3]
    deep = width + rank
    parts = chunks(hidden)
    fold = hidden // local
    pieces = group.pieces
    gains, biases = norm_gains, norm_biases
    tile = min(256, members * rows)
    tiles = members * rows // tile
    near_tiles = tiles // pairs

    def packed(*parts):
        return jnp.concatenate(parts, axis=1)

    def stacked(*parts):
        return jnp.concatenate(parts, axis=0)

    def listed(values):
        return list(values) if isinstance(values, (list, tuple)) else [values]

    def piece(array, k, size):
        return lax.dynamic_slice_in_dim(array, pieces[k] * size, size, array.ndim - 1)

    def own(array):
        return piece(array, 0, local)

    near_chips = [1, 2] if chips == 4 else list(range(1, chips))
    chip_rows = [(group.chip ^ k) * 2 * block for k in range(chips)]
    one = [[c + o * block for c in chip_rows] for o in (group.core, 1 - group.core)]
    one += [[c + o * block for c in chip_rows] for o in (group.zhi, 1 - group.zhi)]
    row_places = jnp.stack(
        [r for found in one for r in found] + [jnp.zeros_like(group.core)]
        + [p * local for p in pieces] + [group.core]
    ).astype(jnp.int32)
    mine_at, other_at, first_at, second_at, zero = (n * chips for n in range(5))
    at_pieces = zero + 1
    core_at = at_pieces + members

    def chip_weight(own_entry, near, rest, low, columns, halves):
        weight = Weight((deep, columns), row_places)
        entries = [own_entry, *near]
        for k, (array, row) in zip([0, *near_chips], entries):
            weight.add(
                array,
                *[(row + r, block, c, columns, None, at + k, 0) for r, c, at in halves],
            )
        if rest:
            side_by_side = halves[1][0] == 0
            for n, (array, row) in enumerate(rest):
                size = block // 2 if side_by_side else block
                picked = halves if side_by_side else halves[n : n + 1]
                weight.add(
                    array,
                    *[
                        (row, size, c, columns, None, at + 3, n * size if side_by_side else 0)
                        for _, c, at in picked
                    ],
                )
        weight.add(low, (0, rank, 0, columns, None, zero, width))
        return weight

    stacked_halves = [(0, 0, first_at), (block, 0, second_at)]
    packed_halves = [(0, 0, mine_at), (0, 2 * local, other_at)]

    def spread(got, half_at, half, own_block):
        if got and chips == 4:
            turns = [
                got[1][half_at : half_at + half],
                got[0][half_at + half : half_at + 2 * half],
            ]
            if own_block is not None:
                turns = listed(step.mark(*[stacked(turn, own_block) for turn in turns]))
            return [xor_move(turn, "chip", 4, k) for turn, k in zip(turns, near_chips)]
        if own_block is None:
            return []
        return [xor_move(own_block, "chip", chips, k) for k in near_chips]

    def skip(half):
        return half if chips == 4 else 0

    def flat(*groups):
        return [x for g in groups for x in listed(g)]

    def wait_all(*groups):
        groups = [listed(g) for g in groups]
        values = iter(listed(step.wait(*flat(*groups))))
        return [[next(values) for _ in g] for g in groups]

    def swap_all(blocks):
        if not blocks:
            return []
        blocks = listed(step.wait(*blocks))
        return listed(step.wait(*[core_swap(b) for b in blocks]))

    shard_self = packed(*[self_in_weight[:, i] for i in range(3)], self_out_weight.T)
    step = Order(shard_self[:8, :128])
    self_from = [home_swap(shard_self), turned(shard_self)]
    stream_own, context_own = home_swap(inputs[0]), home_swap(context[0])
    index, positions = step.wait(adapter_index, positions)
    index_other, positions_other = step.wait(core_swap(index), core_swap(positions))
    index = jnp.where(group.home, index, index_other)[0]
    positions = jnp.where(group.home, positions, positions_other)[0]
    down = lax.dynamic_index_in_dim(adapter_down.transpose(0, 1, 3, 2), index, 0, keepdims=False)
    up = lax.dynamic_index_in_dim(adapter_up.transpose(0, 2, 1, 3), index, 0, keepdims=False)
    down, up = step.mark(down, up)
    low_self = packed(*[own(up[i]) for i in range(3)], own(down[1]))
    low_keyval = packed(own(up[5]), own(up[6]))
    low_cross = []
    for k in range(pairs):
        two = [
            (group.p ^ k) * local + core * pairs * local for core in (0, 1)
        ]
        low_cross.append(
            packed(
                *[
                    lax.dynamic_slice_in_dim(table[4], where, local, 1)
                    for table in (up, down)
                    for where in two
                ]
            )
        )
    low_cross = stacked(*low_cross)
    low_self, low_keyval, low_cross = step.mark(low_self, low_keyval, low_cross)
    keyval_parts = step.wait(cross_keyval_weight)
    keyval_parts = step.mark(keyval_parts[:, 0], keyval_parts[:, 1])
    shard_cross = step.mark(packed(cross_query_weight, cross_out_weight.T, *keyval_parts))
    far_cross = group.cross(shard_cross)
    blocks_at = [
        lax.dynamic_slice_in_dim(positions, pieces[k] * rows, rows, 0) for k in range(members)
    ]
    half = ROT // 2
    inverse = 10000.0 ** (-jnp.arange(half, dtype=F32) / half)
    angles = inverse[:, None] * step.wait(jnp.concatenate(blocks_at)).astype(F32)[None]
    tables = step.mark(*rotary_tables(*step.mark(jnp.cos(angles), jnp.sin(angles))))
    feed_in, feed_out = step.wait(feed_in_weight, feed_out_weight)
    gate_rows, upper_rows = step.mark(feed_in[:, 0], feed_in[:, 1])
    at = [sum(parts[:i]) for i in range(len(parts))]

    def feed_shard(i):
        to = slice(at[i], at[i] + parts[i])
        gate, upper, out = step.wait(gate_rows, upper_rows, feed_out)
        return step.mark(packed(gate[:, to], upper[:, to], out.T[:, to]))

    shard_feed = [feed_shard(i) for i in range(len(parts))]

    self_from = step.wait(*self_from)
    ready_self = step.mark(stacked(*self_from))
    near_self = spread([], 0, 0, ready_self)
    stream_own, context_own = step.wait(stream_own, context_own)
    stream_far, context_far = group.far_p(stream_own), group.far_p(context_own)
    (near_self,) = wait_all(near_self)
    rest_self = spread(near_self, 0, block, None)
    rest_self, stream_far, context_far, (far_cross,) = wait_all(
        rest_self, stream_far, context_far, [far_cross]
    )
    stream_other, context_other, *found = swap_all(
        [stream_own, context_own, *stream_far, *context_far]
    )
    stream_far_other, swapped = found[: pairs - 1], found[pairs - 1 :]
    context_blocks = [context_own, context_other]
    for far, far_other in zip(context_far, swapped):
        context_blocks += [far, far_other]
    stream = [stream_own, stream_other]
    for far, far_other in zip(stream_far, stream_far_other):
        stream += [far, far_other]
    self_weight = chip_weight(
        (ready_self, 0), [(g, 0) for g in near_self], [(g, 0) for g in rest_self], low_self,
        4 * local, stacked_halves,
    )

    mine = jnp.where(group.home, shard_cross, far_cross)
    given = jnp.where(group.home, far_cross, shard_cross)
    keyval_mine, keyval_give = mine[:, 2 * local :], given[:, 2 * local :]
    low_zhi = jnp.where(group.zhi == 0, shard_cross, far_cross)
    high_zhi = jnp.where(group.zhi == 0, far_cross, shard_cross)
    pair = packed(
        *[two[:, n * local : (n + 1) * local] for n in (0, 1) for two in (low_zhi, high_zhi)]
    )
    keyval_mine, keyval_give, pair = step.mark(keyval_mine, keyval_give, pair)
    (keyval_other,) = swap_all([keyval_give])
    ready_keyval = step.mark(stacked(packed(keyval_mine, keyval_other), pair))

    got_one = spread([], 0, 0, ready_keyval)
    pair_far = group.far_p(pair)
    half_columns = shard_feed[0].shape[1] // 2
    halves = step.wait(shard_feed[0][:, :half_columns], shard_feed[0][:, half_columns:])
    feed_one = [home_swap(halves[0]), turned(halves[0])]
    query, keys, values, low_one, normed_one = project_self(
        listed(step.wait(*stream)), gains[0:1], biases[0:1], down[0], self_weight, tables, tile
    )
    query, keys, values = step.mark(query, keys, values)
    heads_far, logsum_far, *y_far = attend_self(
        query, keys, values, self_weight, tile, near_tiles, tiles - near_tiles, rows
    )
    y_far = listed(step.mark(*y_far))

    def far_sums(*groups):
        others = iter(swap_all([g[2 * k + 1] for g in groups for k in range(pairs - 1)]))
        sums = [
            [group.near_sums(g[2 * k], next(others)).astype(BF) for k in range(pairs - 1)]
            for g in groups
        ]
        values = iter(listed(step.mark(*flat(*sums))))
        return [[next(values) for _ in s] for s in sums]

    def move_p(sums):
        return [xor_move(s, "p", pairs, k + 1) for k, s in enumerate(sums)]

    def sum_up(blocks, other, far):
        total = group.near_sums(blocks[0], other)
        for f in far:
            total = total + f.astype(F32)
        return step.mark(total)

    got_one, pair_far, feed_one = wait_all(got_one, pair_far, feed_one)
    (y_sums,) = far_sums(y_far)

    far = move_p(y_sums)
    quarter = block // 2
    if chips == 4:
        turns = [
            stacked(got[start : start + quarter], got[start + block : start + block + quarter], pair_far[0])
            for got, start in ((got_one[1], 0), (got_one[0], quarter))
        ]
        turns = step.mark(*turns)
        got_two = [xor_move(turn, "chip", 4, k) for turn, k in zip(turns, near_chips)]
    else:
        got_two = flat(*[spread([], 0, 0, p) for p in pair_far])
    feed_two = [home_swap(halves[1]), turned(halves[1])]
    heads_near, logsum_near, *y_rows = attend_self(
        step.wait(query), keys, values, self_weight, tile, 0, near_tiles, rows
    )
    y_rows = listed(step.mark(*y_rows))
    (got_two,) = wait_all(got_two)
    keyval_weight = chip_weight(
        (ready_keyval, 0), [(g, 0) for g in got_one],
        [(g, 0) for g in got_two] if chips == 4 else [], low_keyval, 2 * local, packed_halves,
    )
    down_context = step.mark(down[3].T)
    keyval, low_context = context_forward(at_pieces, context_blocks, keyval_weight, down_context)
    keyval = step.mark(keyval)

    far, feed_two = wait_all(far, feed_two)
    (y_other,) = swap_all([y_rows[1]])
    branch = [y_rows[0], y_other, *far]
    keyval_far = group.far_p(keyval)
    ready_feed = [step.mark(stacked(*[packed(*two) for two in zip(feed_one, feed_two)]))]
    found = [(ready_keyval, block, block, 0, 0, 0)]
    found += [(g, block, block, k, 0, 0) for g, k in zip(got_one, near_chips)]
    if chips == 4:
        turns = [got_two[1][block : block + quarter], got_two[0][block + quarter :]]
        got_three = [xor_move(turn, "chip", 4, k) for turn, k in zip(turns, near_chips)]
        keyval_far, got_three = wait_all(keyval_far, got_three)
        found += [(g, 0, quarter, 3, n * quarter, 1) for n, g in enumerate(got_three)]
        found.append((pair_far[0], 0, block, 0, 0, 1))
        for n, (g, k) in enumerate(zip(got_two, near_chips)):
            found += [(g, block, block, k, 0, 1), (g, quarter, quarter, 3, n * quarter, 0)]
    else:
        (keyval_far,) = wait_all(keyval_far)
        count = len(near_chips)
        for n, p in enumerate(pair_far):
            found.append((p, 0, block, 0, 0, n + 1))
            found += [
                (g, 0, block, k, 0, n + 1)
                for g, k in zip(got_two[n * count : (n + 1) * count], near_chips)
            ]
    arrays = []
    for entry in found:
        if not any(entry[0] is a for a in arrays):
            arrays.append(entry[0])
    swapped = swap_all([keyval, *keyval_far, *arrays])
    keyvals = [keyval, swapped[0]]
    for far, far_other in zip(keyval_far, swapped[1:]):
        keyvals += [far, far_other]
    others = swapped[1 + len(keyval_far) :]
    cross_weight = Weight((pairs, deep, 4 * local), row_places)
    for array, other in zip(arrays, others):
        entries = [e[1:] for e in found if e[0] is array]
        for source, places in ((array, mine_at), (other, other_at)):
            cross_weight.add(
                source,
                *[
                    (row, size, 0, 4 * local, n, places + k, offset)
                    for row, size, k, offset, n in entries
                ],
            )
    cross_weight.add(
        low_cross, *[(n * rank, rank, 0, 4 * local, n, zero, width) for n in range(pairs)]
    )

    near_feed = [spread([], 0, 0, ready_feed[0])]
    feed_from = [home_swap(step.wait(shard_feed[1])), turned(step.wait(shard_feed[1]))]
    stream_own, *branch = step.wait(stream_own, *branch)

    (
        stream_one, stream_two, normed_two, normed_three, query_cross, heads_cross, logsum_cross,
        low_two, low_three, low_four,
    ) = cross_forward(
        stream_own, branch, up[3], up[7], down[2], gains, biases, cross_weight, keyvals, core_at,
    )
    normed_own = step.mark(normed_three)
    (feed_from,) = wait_all(feed_from)
    ready_feed.append(step.mark(stacked(*feed_from)))

    normed_far = group.far_p(normed_own)
    cotangent_own = home_swap(step.wait(out_cotangent[0]))
    (normed_other,) = swap_all([normed_own])
    down_hidden = lax.dynamic_index_in_dim(
        adapter_down_hidden.transpose(0, 2, 1), index, 0, keepdims=False
    )
    up_hidden = lax.dynamic_index_in_dim(
        adapter_up_hidden.transpose(0, 2, 1, 3), index, 0, keepdims=False
    )
    feed_down, feed_up = piece(down_hidden, 0, hidden), piece(up_hidden, 0, hidden)
    feed_down, feed_gate, feed_upper = step.mark(feed_down, feed_up[0], feed_up[1])
    low_feed = [
        packed(feed_gate[:, to], feed_upper[:, to], feed_down[:, to])
        for to in [slice(a, a + p) for a, p in zip(at, parts)]
    ]
    low_feed = step.mark(*low_feed)
    (near_feed[0],) = wait_all(near_feed[0])
    rest_feed = spread(near_feed[0], 0, block, None)
    normed_far, (cotangent_own,) = wait_all(normed_far, [cotangent_own])
    cotangent_other, *normed_swapped = swap_all([cotangent_own, *normed_far])

    def feed_weight(i, rest):
        return chip_weight(
            (ready_feed[i], 0), [(g, 0) for g in near_feed[i]], [(g, 0) for g in rest],
            low_feed[i], 3 * parts[i], stacked_halves,
        )

    normed_blocks = [[normed_own, normed_other], []]
    cotangent_blocks = [[cotangent_own, cotangent_other], []]

    def feed_pass(weight, half, state, last):
        normed, cotangent = wait_all(normed_blocks[half], cotangent_blocks[half])
        found = feed(normed, cotangent, down[5], up[8], weight, state, tile, 0, last)
        *values, gdown, ggate, gupper = found
        return listed(step.mark(*values)), [gdown, ggate, gupper]

    def added(one, two):
        return [a + b for a, b in zip(one, two)]

    (rest_feed,) = wait_all(rest_feed) if rest_feed else ([],)
    weight = feed_weight(0, rest_feed)
    near_feed.append(spread([], 0, 0, ready_feed[1]))
    cotangent_far = group.far_p(cotangent_own)
    (y, dn, *lows), grads = feed_pass(weight, 0, (), False)
    states = [(*lows, y, dn)]
    near_feed[1], cotangent_far = wait_all(near_feed[1], cotangent_far)
    swapped = normed_swapped + swap_all(cotangent_far)
    for blocks, fars, others in (
        (normed_blocks[1], normed_far, swapped[: pairs - 1]),
        (cotangent_blocks[1], cotangent_far, swapped[pairs - 1 :]),
    ):
        for far, far_other in zip(fars, others):
            blocks += [far, far_other]
    rest_feed = spread(near_feed[1], 0, block, None)
    (y, dn, *lows), more = feed_pass(weight, 1, (), False)
    states.append((*lows, y, dn))
    feed_grads = [added(grads, more)]
    (rest_feed,) = wait_all(rest_feed) if rest_feed else ([],)

    weight = feed_weight(1, rest_feed)
    found, grads = feed_pass(weight, 1, states[1], True)
    y_far, dn_far = found[: len(found) // 2], found[len(found) // 2 :]

    dn_sums, y_sums = far_sums(dn_far, y_far)
    far = move_p(dn_sums)
    found, more = feed_pass(weight, 0, states[0], True)
    y_rows, dn_rows = found[:2], found[2:]
    feed_grads.append(added(grads, more))
    (far,) = wait_all(far)
    dn_other, y_other = swap_all([dn_rows[1], y_rows[1]])
    grad_normed = [dn_rows[0], dn_other, *far]

    far = move_p(step.mark(*y_sums) if len(y_sums) > 1 else [step.mark(*y_sums)])
    grad_stream, branch_grad, fixed_rows, near_rows, *keyval_rows = cross_back(
        cotangent_own, listed(step.wait(*grad_normed)), stream_one, stream_two, normed_two,
        query_cross, heads_cross, logsum_cross, low_three, low_four, up[7], down[5], down[2],
        gains, biases, cross_weight, keyvals, core_at,
    )
    branch_grad, *keyval_rows = step.mark(branch_grad, *keyval_rows)
    (far,) = wait_all(far)

    branch_far = group.far_p(branch_grad)
    (branch_other,) = swap_all([branch_grad])

    def back(grad, heads, logsum, first, before, ends):
        return attend_back(
            grad, up[3], self_weight, query, keys, values, heads, logsum, tables, low_one, tile,
            first, before, ends,
        )

    def taken(by_piece, k):
        return lax.dynamic_index_in_dim(by_piece, pieces[k], 0, keepdims=False)

    def taken_near(by_member, k):
        member = k // 2 * 2 + (group.core ^ (k % 2))
        return lax.dynamic_index_in_dim(by_member, member, 0, keepdims=False)

    first_rows = listed(
        step.mark(
            *[
                stacked(taken_near(near_rows, k)[:rank], taken(fixed_rows, k)[rank : 2 * rank])
                for k in range(members)
            ]
        )
    )
    others = swap_all([*keyval_rows[1::2], *first_rows[1::2]])
    keyval_sums, first_sums = (
        [group.near_sums(a, b) for a, b in zip(own[::2], others[n * pairs : (n + 1) * pairs])]
        for n, own in enumerate((keyval_rows, first_rows))
    )
    moving = listed(step.mark(*[x.astype(BF) for x in keyval_sums[1:] + first_sums[1:]]))
    keyval_far, first_far = move_p(moving[: pairs - 1]), move_p(moving[pairs - 1 :])
    grads = listed(step.wait(branch_grad, branch_other))
    near_back = step.mark(*back(grads, heads_near, logsum_near, 0, None, None))
    branch_far, keyval_far, first_far = wait_all(branch_far, keyval_far, first_far)

    output, grad_up_eight = step.mark(
        *output_end(
            stream_two, [step.wait(y_rows[0]), y_other, *far], up[8], cotangent_own, members
        )
    )
    swapped = swap_all(branch_far)
    branch_blocks = []
    for f, o in zip(branch_far, swapped):
        branch_blocks += [f, o]

    def columns(array):
        return array.reshape(rank, -1, local).transpose(1, 0, 2)

    def sent(parts):
        parts.append(jnp.full((1, rank, local), index, F32))
        grads = step.mark(jnp.concatenate(parts, axis=0).astype(BF))
        return [home_swap(grads), turned_back(grads)]

    def to_chips(blocks):
        both = step.mark(stacked(*blocks))
        return [both] + [xor_move(both, "chip", chips, k) for k in range(1, chips)]

    def every(blocks):
        grads = stacked(*blocks)
        grads = grads.reshape(-1, grads.shape[0] // (2 * chips), rank, local)
        return grads, grads[:, -1, 0, 0].astype(jnp.int32)

    def total(own, far):
        for f in far:
            own = own + f.astype(F32)
        return own

    summed = total(first_sums[0], first_far).reshape(-1, rank, local)
    first = sent([summed, *[columns(jnp.concatenate(g, axis=1)) for g in zip(*feed_grads)]])
    block_output = home_swap(step.wait(output))
    branch_blocks = listed(step.wait(*branch_blocks))
    found = back(
        branch_blocks, heads_far, logsum_far, near_tiles, near_back,
        (normed_one, low_two, branch_grad),
    )
    first, (block_output,), found = wait_all(first, [block_output], found)
    grad_down_one, grad_up_self, own_rows, *dn_blocks = found

    count = pairs - 1
    dn_others = swap_all(dn_blocks[1::2])
    dn_sums = [group.near_sums(a, b) for a, b in zip(dn_blocks[::2], dn_others)]
    far = move_p(listed(step.mark(*[x.astype(BF) for x in dn_sums[1:]])))
    first = to_chips(first)
    grad_keyval = step.mark(total(keyval_sums[0], keyval_far).astype(BF))
    grad_up_keyval, *found = step.mark(
        *context_back(
            at_pieces, context_blocks, keyval_weight, down_context, low_context, grad_keyval
        )
    )
    context_rows, grad_down_three = found[:members], found[members:]
    far, first = wait_all(far, first)

    second_rows = listed(
        step.mark(
            *[
                stacked(
                    taken(own_rows, k), taken(fixed_rows, k)[:rank],
                    taken(fixed_rows, k)[2 * rank :], taken(grad_up_eight, k), grad_down_three[k],
                    taken_near(near_rows, k)[rank:],
                )
                for k in range(members)
            ]
        )
    )
    swapped = swap_all([*second_rows[1::2], *context_rows[1::2]])
    second_sums, context_sums = (
        [group.near_sums(a, b) for a, b in zip(own[::2], swapped[n * pairs : (n + 1) * pairs])]
        for n, own in enumerate((second_rows, context_rows))
    )
    moving = [x.astype(BF) for x in second_sums[1:] + context_sums[1:]]
    moving = listed(step.mark(*moving))
    second_far, context_far = move_p(moving[:count]), move_p(moving[count:])
    grad_inputs = step.mark(
        input_end(
            stream_own, grad_stream, [dn_blocks[0], dn_others[0], *far], down[0], gains[0:1]
        )
    )
    second_far, context_far = wait_all(second_far, context_far)
    summed = total(second_sums[0], second_far).reshape(-1, rank, local)
    second = sent(
        [
            summed[0:1],
            grad_down_one[None],
            summed[2:3],
            summed[5:6],
            columns(grad_up_self),
            summed[1:2],
            summed[6:7],
            columns(grad_up_keyval),
            summed[3:5],
        ]
    )
    grad_context = home_swap(step.mark(total(context_sums[0], context_far).astype(BF)))
    (second,) = wait_all(second)
    second = to_chips(second)
    grad_inputs = home_swap(step.wait(grad_inputs))
    first, labels = every(listed(step.wait(*first)))
    grad_down, grad_hidden, grad_gate = settle_first(labels, first, slots, fold)
    grad_down = step.mark(grad_down)
    (second,) = wait_all(second)
    second, labels = every(second)
    labels = labels + (step.token[0, 0].astype(F32) * 0.0).astype(jnp.int32)
    grad_down, grad_up = settle_second(labels, second, grad_down)
    return (
        block_output[None],
        grad_inputs.astype(F32)[None],
        grad_context.astype(F32)[None],
        grad_down.transpose(0, 1, 3, 2),
        grad_hidden.transpose(0, 2, 1),
        grad_up.transpose(0, 2, 1, 3),
        grad_gate.transpose(0, 2, 1, 3),
    )


def solution(mesh):
    members = mesh.shape["tensor"]
    chips = mesh.shape["dp"] // 2
    mesh = Mesh(
        mesh.devices.reshape(chips, 2, 2, members // 2), ("chip", "core", "zhi", "p")
    )
    dp, tensor = ("chip", "core"), ("zhi", "p")
    in_specs = (
        P(dp, tensor, None),
        P(dp, None, tensor),
        P(dp, None),
        P(dp),
        P(dp, None, tensor),
        P(tensor, dp),
        P(dp, tensor),
        P(dp, None, tensor),
        P(tensor, dp),
        P(dp, None, tensor),
        P(tensor, dp),
        P(),
        P(),
        P(),
        P(),
        P(),
        P(),
        P(dp, tensor, None),
    )
    out_specs = (
        P(dp, tensor, None),
        P(dp, tensor, None),
        P(dp, None, tensor),
        P(None, None, tensor, None),
        P(None, tensor, None),
        P(None, None, None, tensor),
        P(None, None, None, tensor),
    )

    def run(*args):
        return body(*args, pairs=members // 2, chips=chips)

    return jax.shard_map(run, mesh=mesh, in_specs=in_specs, out_specs=out_specs, check_vma=False)
```

```python
import functools

import jax
import jax.numpy as jnp
from jax import lax
from jax.experimental import pallas as pl
from jax.experimental.pallas import tpu as pltpu
from jax.sharding import Mesh, PartitionSpec as P

HEAD_DIM = 64
ROT = 32
EPSILON = 1e-05
F32 = jnp.float32
BF = jnp.bfloat16
SWAP = ((0, 1), (1, 0))
LANES = 128
VMEM_LIMIT = 56 * 1024 * 1024


def dot(left, right):
    return jnp.dot(left, right, preferred_element_type=F32)


def dot_nt(left, right):
    return lax.dot_general(left, right, (((1,), (1,)), ((), ())), preferred_element_type=F32)


def dot_tn(left, right):
    return lax.dot_general(left, right, (((0,), (0,)), ((), ())), preferred_element_type=F32)


class Order:
    def __init__(self, first):
        self.token = first

    def wait(self, *values):
        *values, self.token = lax.optimization_barrier((*values, self.token))
        return values[0] if len(values) == 1 else values

    mark = wait


def core_swap(x):
    return lax.ppermute(x, "core", SWAP)


def xor_move(x, axis, size, k):
    return lax.ppermute(x, axis, [(i, i ^ k) for i in range(size)])


def home_swap(x):
    return lax.ppermute(x, ("core", "zhi"), [(0, 0), (1, 2), (2, 1), (3, 3)])


def turned(x):
    return lax.ppermute(x, ("core", "zhi"), [(0, 1), (1, 3), (2, 0), (3, 2)])


def turned_back(x):
    return lax.ppermute(x, ("core", "zhi"), [(0, 2), (1, 0), (2, 3), (3, 1)])


class Group:
    def __init__(self, pairs, chips):
        self.pairs, self.chips = pairs, chips
        self.core, self.zhi, self.p = (lax.axis_index(n) for n in ("core", "zhi", "p"))
        self.chip = lax.axis_index("chip")
        self.home = self.core == self.zhi
        self.pieces = [
            (self.core ^ kc) * pairs + (self.p ^ kp) for kp in range(pairs) for kc in (0, 1)
        ]

    def far_p(self, own):
        return [xor_move(own, "p", self.pairs, k) for k in range(1, self.pairs)]

    def near_sums(self, own, other):
        return own.astype(F32) + other.astype(F32)

    def cross(self, shard):
        return xor_move(shard, "zhi", 2, 1)

    def spread_one(self, block):
        if self.chips == 4:
            return [xor_move(block, "chip", 4, k) for k in (1, 2)]
        return [xor_move(block, "chip", self.chips, k) for k in range(1, self.chips)]

    def spread_two(self, got):
        if self.chips != 4:
            return []
        half = got[0].shape[0] // 2
        return [xor_move(got[1][:half], "chip", 4, 1), xor_move(got[0][half:], "chip", 4, 2)]

    def places(self, rows):
        if self.chips == 4:
            diagonal = (self.chip ^ 3) * rows
            return [(self.chip ^ 1) * rows, (self.chip ^ 2) * rows, diagonal, diagonal + rows // 2]
        return [(self.chip ^ k) * rows for k in range(1, self.chips)]


class Weight:
    def __init__(self, shape, places):
        self.shape, self.places, self.arrays, self.moves = shape, places, [], []

    def add(self, array, *parts):
        self.moves += [(len(self.arrays), *part) for part in parts]
        self.arrays.append(array)

    @property
    def count(self):
        return len(self.arrays)

    def specs(self):
        return [pl.BlockSpec(memory_space=pl.ANY)] * self.count

    def columns(self, start, size):
        if size % 128 or start % 128:
            return 0, self.shape[-1], start
        return start, size, 0

    def scratch(self, size=None):
        shape = self.shape if size is None else self.shape[:-1] + (size,)
        return [pltpu.VMEM(shape, BF), pltpu.SemaphoreType.DMA((len(self.moves),))]

    def at_first(self, step, refs, places_ref, target, sems, start=0, size=None):
        def begin():
            @pl.when(step == 0)
            def _():
                self.bring(refs, places_ref, target, sems, start, size)

        def end():
            @pl.when(step == 0)
            def _():
                wait_for(self.bring(refs, places_ref, target, sems, start, size, go=False))

        return begin, end

    def bring(self, refs, places_ref, target, sems, start=0, size=None, go=True):
        copies = []
        for number, (source, row, rows, column, columns, lead, place, offset) in enumerate(self.moves):
            at = pl.ds(pl.multiple_of(places_ref[place] + offset, 16), rows)
            to = target.at[at] if lead is None else target.at[lead, at]
            if size is not None:
                column, columns = column + start, size
            found = refs[source].at[pl.ds(row, rows), pl.ds(column, columns)]
            copies.append(pltpu.make_async_copy(found, to, sems.at[number]))
        if go:
            for copy in copies:
                copy.start()
        return copies


def wait_for(copies):
    for copy in copies:
        copy.wait()


def weight_call(kernel, weight, grid, in_specs, out_specs, out_shape, scratch, estimate, arrays):
    return pl.pallas_call(
        kernel,
        grid_spec=pltpu.PrefetchScalarGridSpec(
            num_scalar_prefetch=1,
            grid=grid,
            in_specs=weight.specs() + in_specs,
            out_specs=out_specs,
            scratch_shapes=scratch,
        ),
        out_shape=out_shape,
        compiler_params=params(),
        cost_estimate=estimate,
    )(weight.places, *weight.arrays, *arrays)


def stats(stream):
    average = jnp.mean(stream, axis=-1, keepdims=True)
    centred = stream - average
    variance = jnp.mean(centred * centred, axis=-1, keepdims=True)
    scale = lax.rsqrt(variance + EPSILON)
    return centred * scale, scale


def layer_norm(stream, gain, bias):
    return (stats(stream)[0] * gain + bias).astype(BF)


def norm_backward(stream, gain, grad):
    unit, scale = stats(stream)
    grad = grad * gain
    return scale * (
        grad
        - jnp.mean(grad, axis=-1, keepdims=True)
        - unit * jnp.mean(grad * unit, axis=-1, keepdims=True)
    )


def turn(x, cosines, left_sines, right_sines):
    breadth = 2 * HEAD_DIM if x.shape[1] % (2 * HEAD_DIM) == 0 else HEAD_DIM
    half = ROT // 2
    for at in range(0, x.shape[1], breadth):
        group = x[:, at : at + breadth]
        if breadth % 128 == 0:
            left, right = pltpu.roll(group, breadth - half, 1), pltpu.roll(group, half, 1)
        else:
            left = jnp.concatenate([group[:, half:], group[:, :half]], axis=1)
            right = jnp.concatenate([group[:, -half:], group[:, :-half]], axis=1)
        yield (
            at,
            breadth,
            group * cosines[:, :breadth]
            + left * left_sines[:, :breadth]
            + right * right_sines[:, :breadth],
        )


def head_sums(product):
    columns = product.shape[1]
    rows = -(-columns // HEAD_DIM // 8) * 8
    head = lax.broadcasted_iota(jnp.int32, (rows, columns), 0)
    lane = lax.broadcasted_iota(jnp.int32, (rows, columns), 1)
    picked = jnp.where(lane // HEAD_DIM == head, 1.0, 0.0).astype(F32)
    return lax.dot_general(
        picked, product, (((1,), (1,)), ((), ())),
        precision=lax.Precision.HIGHEST, preferred_element_type=F32,
    )


def whole_spec(shape):
    return pl.BlockSpec(shape, lambda *_: (0,) * len(shape))


def row_spec(rows, columns):
    return pl.BlockSpec((rows, columns), lambda t, *_: (t, 0))


def take_tile(refs, tile_ref, step):
    rows, tile = refs[0].shape[0], tile_ref.shape[0]
    for i, ref in enumerate(refs):

        @pl.when(step == i * rows // tile)
        def _(i=i, ref=ref):
            tile_ref[i * rows % tile : i * rows % tile + rows, :] = ref[...]


def give_tile(value, refs, step):
    rows, (tile, columns) = refs[0].shape[0], value.shape
    for i, ref in enumerate(refs):

        @pl.when(step == i * rows // tile)
        def _(i=i, ref=ref):
            ref[:, :columns] = value[i * rows % tile : i * rows % tile + rows]
            ref[:, columns:] = jnp.zeros((rows, ref.shape[1] - columns), ref.dtype)


def total_of(refs):
    total = refs[0][...].astype(F32)
    for ref in refs[1:]:
        total = total + ref[...].astype(F32)
    return total


def by_piece(ref, row, value):
    local = ref.shape[2]
    for k in range(ref.shape[0]):
        ref[k, row : row + value.shape[0], :] = value[:, k * local : (k + 1) * local].astype(
            ref.dtype
        )


def params(semantics=1):
    return pltpu.CompilerParams(
        dimension_semantics=("arbitrary",) * semantics, vmem_limit_bytes=VMEM_LIMIT
    )


def cost(flops, moved, exps=0):
    return pl.CostEstimate(
        flops=int(flops) or 1000, bytes_accessed=int(moved) or 1000, transcendentals=int(exps)
    )


def sds(shape, dtype):
    return jax.ShapeDtypeStruct(shape, dtype)


def query_kernel(weight, part, count, places_ref, *refs):
    w_refs, refs = refs[: weight.count], refs[weight.count :]
    blocks, (gain_ref, bias_ref, down_ref, cos_ref, left_ref, right_ref), refs = (
        refs[:count],
        refs[count : count + 6],
        refs[count + 6 :],
    )
    q_ref, k_ref, v_ref, low_ref, n_ref, x_ref, w_ref, sems = refs
    step = pl.program_id(0)

    begin, end = weight.at_first(step, w_refs, places_ref, w_ref, sems, *part[:2])
    begin()
    take_tile(blocks, x_ref, step)
    local, width = q_ref.shape[1], x_ref.shape[1]
    normed = layer_norm(x_ref[...].astype(F32), gain_ref[...], bias_ref[...])
    n_ref[...] = normed
    low = dot_nt(normed, down_ref[...]).astype(BF)
    low_ref[...] = low
    end()
    at = slice(part[2], part[2] + 3 * local)
    mixed = dot(normed, w_ref[:width, at]) + dot(low, w_ref[width:, at])
    tables = cos_ref[...], left_ref[...], right_ref[...]
    for at, breadth, turned in turn(mixed[:, :local], *tables):
        q_ref[:, at : at + breadth] = (turned * HEAD_DIM**-0.5).astype(BF)
    for at, breadth, turned in turn(mixed[:, local : 2 * local], *tables):
        k_ref[:, at : at + breadth] = turned.astype(BF)
    v_ref[...] = mixed[:, 2 * local :].astype(BF)


def project_self(blocks, gain, bias, down, weight, tables, rows):
    width = blocks[0].shape[1]
    tokens = len(blocks) * blocks[0].shape[0]
    local = weight.shape[1] // 4
    part = weight.columns(0, 3 * local)
    return weight_call(
        functools.partial(query_kernel, weight, part, len(blocks)),
        weight,
        (tokens // rows,),
        [whole_spec(b.shape) for b in blocks]
        + [whole_spec(gain.shape), whole_spec(bias.shape), whole_spec(down.shape)]
        + [row_spec(rows, t.shape[1]) for t in tables],
        [row_spec(rows, local)] * 3 + [row_spec(rows, down.shape[0]), row_spec(rows, width)],
        [sds((tokens, local), BF)] * 3
        + [sds((tokens, down.shape[0]), BF), sds((tokens, width), BF)],
        [pltpu.VMEM((rows, width), BF), *weight.scratch(part[1])],
        cost(8 * tokens * width * local, 8 * width * local),
        [*blocks, gain, bias, down, *tables],
    )


def attend_kernel(weight, part, places_ref, *refs):
    w_refs, refs = refs[: weight.count], refs[weight.count :]
    q_ref, k_ref, v_ref, o_ref, lse_ref, *y_refs, w_ref, sems = refs
    rows, local = q_ref.shape
    step = pl.program_id(0)

    begin, end = weight.at_first(step, w_refs, places_ref, w_ref, sems, *part[:2])
    begin()
    lanes = lax.broadcasted_iota(jnp.int32, (rows, 128), 1)
    logsums = jnp.zeros((rows, 128), F32)
    for head in range(local // HEAD_DIM):
        at = slice(head * HEAD_DIM, (head + 1) * HEAD_DIM)
        scores = dot_nt(q_ref[:, at], k_ref[:, at])
        top = jnp.max(scores, axis=1, keepdims=True)
        powers = jnp.exp(scores - top)
        total = jnp.sum(powers, axis=1, keepdims=True)
        out = dot(powers.astype(BF), v_ref[:, at]) / total
        o_ref[:, at] = out.astype(BF)
        logsums = jnp.where(lanes == head, top + jnp.log(total), logsums)
    lse_ref[...] = logsums.T[: lse_ref.shape[0]]
    end()
    y = dot_nt(o_ref[...], w_ref[:, part[2] : part[2] + local]).astype(BF)
    give_tile(y, y_refs, step)


def wide_of(weight):
    return weight.shape[-2] // LANES * LANES + LANES


def attend_self(query, keys, values, weight, rows, first, count, block):
    tokens, local = query.shape
    heads = -(-local // HEAD_DIM // 8) * 8
    part = weight.columns(3 * local, local)
    blocks = count * rows // block
    return weight_call(
        functools.partial(attend_kernel, weight, part),
        weight,
        (count,),
        [
            pl.BlockSpec((rows, local), lambda t, *_: (first + t, 0)),
            whole_spec(keys.shape),
            whole_spec(values.shape),
        ],
        [row_spec(rows, local), pl.BlockSpec((heads, rows), lambda t, *_: (0, t))]
        + [whole_spec((block, wide_of(weight)))] * blocks,
        [sds((count * rows, local), BF), sds((heads, count * rows), F32)]
        + [sds((block, wide_of(weight)), BF)] * blocks,
        weight.scratch(part[1]),
        cost(16 * count * rows * tokens * local, 8 * query.size, count * rows * tokens),
        [query, keys, values],
    )


def attend_back_kernel(weight, part, first, last, tiles, number, blocks, places_ref, *refs):
    w_refs, refs = refs[: weight.count], refs[weight.count :]
    grads, refs = refs[:number], refs[number:]
    (
        up_ref, q_ref, k_ref, v_ref, o_ref, lse_ref, cos_ref, left_ref, right_ref, low_ref,
    ), refs = refs[:10], refs[10:]
    *refs, g_ref, w_ref, sems = refs
    begin, end = weight.at_first(pl.program_id(0), w_refs, places_ref, w_ref, sems, *part[:2])
    begin()
    take_tile(grads, g_ref, pl.program_id(0))
    if not first:
        (mq_ref, gk_in, gv_in, down_in), refs = refs[:4], refs[4:]
    if last:
        (n_ref, z_ref, r_ref), refs = refs[:3], refs[3:]
        (down_ref, gup_ref, rows_ref), refs = refs[:3], refs[3:]
        dn_refs, (m_ref, gk_ref, gv_ref) = refs[:blocks], refs[blocks:]
    else:
        m_ref, gk_ref, gv_ref, down_ref = refs
    step, rows = pl.program_id(0), q_ref.shape[0]
    width, local = g_ref.shape[1], q_ref.shape[1]
    at_rows = pl.ds(pl.multiple_of((step + tiles) * rows, rows), rows)
    at_query = at_rows if last else pl.ds(pl.multiple_of(step * rows, rows), rows)

    @pl.when(step == 0)
    def _():
        if first:
            gk_ref[...] = jnp.zeros_like(gk_ref)
            gv_ref[...] = jnp.zeros_like(gv_ref)
            down_ref[...] = jnp.zeros_like(down_ref)
        else:
            gk_ref[...] = gk_in[...]
            gv_ref[...] = gv_in[...]
            down_ref[...] = down_in[...]
            m_ref[: mq_ref.shape[0], :local] = mq_ref[...]

    grad = g_ref[...]
    grad_low = dot_nt(grad, up_ref[...]).astype(BF)
    end()
    at = slice(part[2], part[2] + local)
    grad_out = dot(grad, w_ref[:width, at]) + dot(grad_low, w_ref[width:, at])
    grad_out = grad_out.astype(BF)
    out = o_ref[...]
    down_ref[...] += dot_tn(grad_low, out)
    product = grad_out.astype(F32) * out.astype(F32)
    deltas = head_sums(product)
    parts = []
    for head in range(local // HEAD_DIM):
        at = slice(head * HEAD_DIM, (head + 1) * HEAD_DIM)
        q, k, v, g = q_ref[:, at], k_ref[:, at], v_ref[:, at], grad_out[:, at]
        delta = deltas[head : head + 1]
        probs = jnp.exp(dot_nt(k, q) - lse_ref[head : head + 1, :])
        grad_scores = (probs * (dot_nt(v, g) - delta)).astype(BF)
        gv_ref[:, at] += dot(probs.astype(BF), g)
        gk_ref[:, at] += dot(grad_scores, q)
        parts.append(dot_tn(grad_scores, k) * HEAD_DIM**-0.5)
    tables = cos_ref[at_rows, :], -left_ref[at_rows, :], -right_ref[at_rows, :]
    for at, breadth, turned in turn(jnp.concatenate(parts, axis=1), *tables):
        m_ref[at_query, at : at + breadth] = turned.astype(BF)

    if last:

        @pl.when(step == pl.num_programs(0) - 1)
        def _():
            tables = cos_ref[...], -left_ref[...], -right_ref[...]
            for at, breadth, turned in turn(gk_ref[...], *tables):
                m_ref[:, local + at : local + at + breadth] = turned.astype(BF)
            m_ref[:, 2 * local :] = gv_ref[...].astype(BF)
            gup_ref[...] = dot_tn(low_ref[...], m_ref[...])
            rank, block = up_ref.shape[0], dn_refs[0].shape[0]
            down = 0.0
            for i, ref in enumerate(dn_refs):
                at = slice(i * block, (i + 1) * block)
                value = dot_nt(m_ref[at, :], w_ref[:, : 3 * local]).astype(BF)
                ref[:, : width + rank] = value
                ref[:, width + rank :] = jnp.zeros((block, ref.shape[1] - width - rank), BF)
                down = down + dot_tn(value[:, width:], n_ref[at, :])
            by_piece(rows_ref, 0, down)
            by_piece(rows_ref, rank, dot_tn(z_ref[...], r_ref[...]))


def attend_back(
    grads, up, weight, query, keys, values, out, lse, tables, low, rows, start, before, ends
):
    tokens, local = query.shape
    block, width = grads[0].shape
    rank = up.shape[0]
    count = len(grads) * block // rows
    first, last = before is None, ends is not None
    before = () if first else before
    ends = ends if last else ()
    sums = [sds((tokens, local), F32)] * 2 + [sds((rank, local), F32)]
    blocks = tokens // block if last else 0
    if last:
        members = width // local
        shapes = [sums[2], sds((rank, 3 * local), F32), sds((members, 2 * rank, local), BF)]
        shapes += [sds((block, wide_of(weight)), BF)] * blocks
        scratch = [pltpu.VMEM((tokens, 3 * local), BF)]
        scratch += [pltpu.VMEM((tokens, local), F32)] * 2
        part = 0, 4 * local, 3 * local
    else:
        shapes, scratch = [sds((count * rows, local), BF), *sums], []
        part = weight.columns(3 * local, local)
    scratch.append(pltpu.VMEM((rows, width), BF))

    def tile(columns):
        return pl.BlockSpec((rows, columns), lambda t, *_: (start + t, 0))

    return weight_call(
        functools.partial(attend_back_kernel, weight, part, first, last, start, len(grads), blocks),
        weight,
        (count,),
        [
            *[whole_spec(g.shape) for g in grads],
            whole_spec(up.shape),
            tile(local),
            whole_spec(keys.shape),
            whole_spec(values.shape),
            row_spec(rows, local),
            pl.BlockSpec((lse.shape[0], rows), lambda t, *_: (0, t)),
            *[whole_spec(t.shape) for t in tables],
            whole_spec(low.shape),
            *[whole_spec(b.shape) for b in before],
            *[whole_spec(e.shape) for e in ends],
        ],
        [whole_spec(s.shape) for s in shapes],
        shapes,
        scratch + weight.scratch(part[1]),
        cost(40 * count * rows * tokens * local, 10 * query.size, count * rows * tokens),
        [*grads, up, query, keys, values, out, lse, *tables, low, *before, *ends],
    )


def in_order(swap, first, second):
    keep = swap == 0
    return jnp.where(keep, first, second), jnp.where(keep, second, first)


def cross_kernel(weight, members, local, core_at, places_ref, *refs):
    w_refs, refs = refs[: weight.count], refs[weight.count :]
    *refs, w_ref, sems = refs
    copies = weight.bring(w_refs, places_ref, w_ref, sems)
    (x_ref, up_self_ref, up_cross_ref, down_ref, gain_ref, bias_ref), refs = refs[:6], refs[6:]
    kv_refs, refs = refs[:members], refs[members:]
    y_refs, refs = refs[:-10], refs[-10:]
    branch = total_of(y_refs)
    s1_ref, s2_ref, n2_ref, n3_ref, q_ref, o_ref, lse_ref, z2_ref, u_ref, z4_ref = refs
    rows, width = x_ref.shape
    rank = down_ref.shape[0]
    deep = slice(width, width + rank)
    low = branch[:, deep].astype(BF)
    z2_ref[...] = low
    stream = x_ref[...].astype(F32) + branch[:, :width] + dot(low, up_self_ref[...])
    s1_ref[...] = stream
    normed = layer_norm(stream, gain_ref[1:2, :], bias_ref[1:2, :])
    n2_ref[...] = normed
    low = dot_nt(normed, down_ref[...]).astype(BF)
    u_ref[...] = low
    total = jnp.zeros((rows, width + rank), F32)
    wait_for(copies)
    both = 2 * local
    for n in range(members // 2):
        query = dot(normed, w_ref[n, :width, :both]) + dot(low, w_ref[n, deep, :both])
        query = (query * HEAD_DIM**-0.5).astype(BF)
        q_ref[:, n * both : (n + 1) * both] = query
        found = in_order(places_ref[core_at], kv_refs[2 * n][...], kv_refs[2 * n + 1][...])
        parts, logsums = [], []
        for head in range(both // HEAD_DIM):
            keyval, own = found[head * HEAD_DIM // local], head * HEAD_DIM % local
            keys = keyval[:, own : own + HEAD_DIM]
            values = keyval[:, local + own : local + own + HEAD_DIM]
            scores = dot_nt(keys, query[:, head * HEAD_DIM : (head + 1) * HEAD_DIM])
            top = jnp.max(scores, axis=0, keepdims=True)
            powers = jnp.exp(scores - top)
            sums = jnp.sum(powers, axis=0, keepdims=True)
            parts.append(dot_tn(values, powers.astype(BF)) / sums)
            logsums.append(top + jnp.log(sums))
        out = jnp.concatenate(parts, axis=0).T.astype(BF)
        o_ref[:, n * both : (n + 1) * both] = out
        lse_ref[n] = jnp.concatenate(logsums, axis=0)
        total = total + dot_nt(out, w_ref[n, :, both:])
    low = total[:, deep].astype(BF)
    z4_ref[...] = low
    stream = stream + total[:, :width] + dot(low, up_cross_ref[...])
    s2_ref[...] = stream
    n3_ref[...] = layer_norm(stream, gain_ref[2:3, :], bias_ref[2:3, :])


def cross_forward(x, ys, up_self, up_cross, down, gains, biases, weight, keyvals, core_at):
    rows, width = x.shape
    members, local = len(keyvals), weight.shape[2] // 4
    plain, wide = sds((rows, width), BF), sds((rows, width), F32)
    low = sds((rows, down.shape[0]), BF)
    logsums = sds((members // 2, 2 * local // HEAD_DIM, rows), F32)
    shapes = [wide, wide, plain, plain, plain, plain, logsums, low, low, low]
    arrays = [x, up_self, up_cross, down, gains, biases, *keyvals, *ys]
    return weight_call(
        functools.partial(cross_kernel, weight, members, local, core_at),
        weight,
        (1,),
        [whole_spec(a.shape) for a in arrays],
        [whole_spec(o.shape) for o in shapes],
        shapes,
        weight.scratch(),
        cost(24 * rows * width * width, 8 * width * width),
        arrays,
    )


def cross_back_kernel(weight, members, local, core_at, places_ref, *refs):
    w_refs, refs = refs[: weight.count], refs[weight.count :]
    *refs, w_ref, sems = refs
    copies = weight.bring(w_refs, places_ref, w_ref, sems)
    (
        g_ref, s1_ref, s2_ref, n2_ref, q_ref, o_ref, lse_ref, u_ref, z4_ref,
        up_ref, down5_ref, down2_ref, gain_ref, bias_ref,
    ), refs = refs[:14], refs[14:]
    kv_refs, refs = refs[:members], refs[members:]
    dn_refs, (r1_ref, r1b_ref, fixed_ref, near_ref, *gkv_refs) = (
        refs[: -4 - members],
        refs[-4 - members :],
    )
    summed = total_of(dn_refs)
    width = g_ref.shape[1]
    rank = up_ref.shape[0]
    deep = slice(width, width + rank)
    stream = s2_ref[...]
    low = summed[:, deep].astype(BF)
    grad_normed = summed[:, :width] + dot(low, down5_ref[...])
    normed = layer_norm(stream, gain_ref[2:3, :], bias_ref[2:3, :])
    by_piece(fixed_ref, rank, dot_tn(low, normed))
    grad = g_ref[...].astype(F32) + norm_backward(stream, gain_ref[2:3, :], grad_normed)
    branch = grad.astype(BF)
    low = dot_nt(branch, up_ref[...]).astype(BF)
    by_piece(fixed_ref, 2 * rank, dot_tn(z4_ref[...], branch))
    by_piece(near_ref, 0, dot_tn(low, o_ref[...]))
    total = jnp.zeros((g_ref.shape[0], width + rank), F32)
    wait_for(copies)
    both, swap = 2 * local, places_ref[core_at]
    for n in range(members // 2):
        columns = slice(n * both, (n + 1) * both)
        grad_out = dot(branch, w_ref[n, :width, both:]) + dot(low, w_ref[n, deep, both:])
        grad_out = grad_out.astype(BF)
        query = q_ref[:, columns]
        deltas = head_sums(grad_out.astype(F32) * o_ref[:, columns].astype(F32))
        found = in_order(swap, kv_refs[2 * n][...], kv_refs[2 * n + 1][...])
        queries, keys, values = [], [], []
        for head in range(both // HEAD_DIM):
            keyval, own = found[head * HEAD_DIM // local], head * HEAD_DIM % local
            key = keyval[:, own : own + HEAD_DIM]
            value = keyval[:, local + own : local + own + HEAD_DIM]
            at = slice(head * HEAD_DIM, (head + 1) * HEAD_DIM)
            q, g = query[:, at], grad_out[:, at]
            probs = jnp.exp(dot_nt(key, q) - lse_ref[n, head : head + 1, :])
            grad_scores = (probs * (dot_nt(value, g) - deltas[head : head + 1])).astype(BF)
            queries.append(dot_tn(key, grad_scores))
            keys.append(dot(grad_scores, q))
            values.append(dot(probs.astype(BF), g))
        grad_query = (jnp.concatenate(queries, axis=0).T * HEAD_DIM**-0.5).astype(BF)
        half = len(keys) // 2
        first = jnp.concatenate(keys[:half] + values[:half], axis=1).astype(BF)
        second = jnp.concatenate(keys[half:] + values[half:], axis=1).astype(BF)
        gkv_refs[2 * n][...], gkv_refs[2 * n + 1][...] = in_order(swap, first, second)
        ups = dot_tn(u_ref[...], grad_query).astype(BF)
        near_ref[2 * n, rank:, :] = ups[:, :local]
        near_ref[2 * n + 1, rank:, :] = ups[:, local:]
        total = total + dot_nt(grad_query, w_ref[n, :, :both])
    low = total[:, deep].astype(BF)
    by_piece(fixed_ref, 0, dot_tn(low, n2_ref[...]))
    grad_normed = total[:, :width] + dot(low, down2_ref[...])
    grad = grad + norm_backward(s1_ref[...], gain_ref[1:2, :], grad_normed)
    r1_ref[...] = grad
    r1b_ref[...] = grad.astype(BF)


def cross_back(
    g, dns, s1, s2, n2, q, o, lse, u, z4, up, down5, down2, gains, biases, weight, keyvals, core_at
):
    rows, width = g.shape
    rank = up.shape[0]
    members, local = len(keyvals), weight.shape[2] // 4
    shapes = [sds((rows, width), F32), sds((rows, width), BF)]
    shapes += [sds((members, n * rank, local), BF) for n in (3, 2)]
    shapes += [sds(keyvals[0].shape, BF)] * members
    arrays = [g, s1, s2, n2, q, o, lse, u, z4, up, down5, down2, gains, biases, *keyvals, *dns]
    return weight_call(
        functools.partial(cross_back_kernel, weight, members, local, core_at),
        weight,
        (1,),
        [whole_spec(a.shape) for a in arrays],
        [whole_spec(o.shape) for o in shapes],
        shapes,
        weight.scratch(),
        cost(32 * rows * width * width, 8 * width * width),
        arrays,
    )


def output_kernel(s2_ref, up_ref, g_ref, *refs):
    *y_refs, out_ref, gup_ref = refs
    width, rank = out_ref.shape[1], up_ref.shape[0]
    total = total_of(y_refs)
    low = total[:, width : width + rank].astype(BF)
    out_ref[...] = (s2_ref[...] + total[:, :width] + dot(low, up_ref[...])).astype(BF)
    by_piece(gup_ref, 0, dot_tn(low, g_ref[...]))


def output_end(s2, ys, up, g, members):
    rank, width = up.shape
    return pl.pallas_call(
        output_kernel,
        out_shape=[sds(g.shape, BF), sds((members, rank, width // members), BF)],
        compiler_params=pltpu.CompilerParams(vmem_limit_bytes=VMEM_LIMIT),
        cost_estimate=cost(0, 0),
    )(s2, up, g, *ys)


def input_kernel(x_ref, r_ref, down_ref, gain_ref, *refs):
    *dn_refs, out_ref = refs
    width, rank = out_ref.shape[1], down_ref.shape[0]
    total = total_of(dn_refs)
    low = total[:, width : width + rank].astype(BF)
    grad = total[:, :width] + dot(low, down_ref[...])
    back = norm_backward(x_ref[...].astype(F32), gain_ref[...], grad)
    out_ref[...] = (r_ref[...] + back).astype(BF)


def input_end(x, r1, dns, down, gain):
    return pl.pallas_call(
        input_kernel,
        out_shape=sds(x.shape, BF),
        compiler_params=pltpu.CompilerParams(vmem_limit_bytes=VMEM_LIMIT),
        cost_estimate=cost(0, 0),
    )(x, r1, down, gain, *dns)


def context_kernel(weight, members, at_pieces, places_ref, *refs):
    w_refs, refs = refs[: weight.count], refs[weight.count :]
    blocks, (down_ref, kv_ref, low_ref, w_ref, sems) = refs[:members], refs[members:]
    wait_for(weight.bring(w_refs, places_ref, w_ref, sems))
    rank, local = down_ref.shape[1], blocks[0].shape[1]
    width = members * local
    low, keyval = 0.0, 0.0
    for k in range(members):
        at = pl.ds(pl.multiple_of(places_ref[at_pieces + k], local), local)
        low = low + dot(blocks[k][...], down_ref[at, :])
        keyval = keyval + dot(blocks[k][...], w_ref[at, :])
    low = low.astype(BF)
    low_ref[...] = low
    kv_ref[...] = (keyval + dot(low, w_ref[width : width + rank, :])).astype(BF)


def context_forward(at_pieces, blocks, weight, down):
    count = blocks[0].shape[0]
    arrays = (*blocks, down)
    shapes = [sds((count, weight.shape[1]), BF), sds((count, down.shape[1]), BF)]
    return weight_call(
        functools.partial(context_kernel, weight, len(blocks), at_pieces),
        weight,
        (1,),
        [whole_spec(a.shape) for a in arrays],
        [whole_spec(s.shape) for s in shapes],
        shapes,
        weight.scratch(),
        cost(0, 0),
        arrays,
    )


def context_back_kernel(weight, members, at_pieces, places_ref, *refs):
    w_refs, refs = refs[: weight.count], refs[weight.count :]
    blocks, (down_ref, low_ref, g_ref), refs = (
        refs[:members],
        refs[members : members + 3],
        refs[members + 3 :],
    )
    gup_ref, *refs, w_ref, sems = refs
    wait_for(weight.bring(w_refs, places_ref, w_ref, sems))
    rank, local = down_ref.shape[1], blocks[0].shape[1]
    width = members * local
    grad = g_ref[...]
    low = dot_nt(grad, w_ref[width : width + rank, :]).astype(BF)
    gup_ref[...] = dot_tn(low_ref[...], grad)
    for k in range(members):
        at = pl.ds(pl.multiple_of(places_ref[at_pieces + k], local), local)
        out = dot_nt(grad, w_ref[at, :]) + dot_nt(low, down_ref[at, :])
        refs[k][...] = out.astype(BF)
        refs[members + k][...] = dot_tn(low, blocks[k][...]).astype(BF)


def context_back(at_pieces, blocks, weight, down, low, grad):
    count, local = blocks[0].shape
    rank, members = down.shape[1], len(blocks)
    arrays = (*blocks, down, low, grad)
    shapes = (
        [sds((rank, weight.shape[1]), F32)]
        + [sds((count, local), BF)] * members
        + [sds((rank, local), BF)] * members
    )
    return weight_call(
        functools.partial(context_back_kernel, weight, members, at_pieces),
        weight,
        (1,),
        [whole_spec(a.shape) for a in arrays],
        [whole_spec(s.shape) for s in shapes],
        shapes,
        weight.scratch(),
        cost(10**10, 10**6),
        arrays,
    )


def table_kernel(cos_ref, sin_ref, out_cos_ref, out_left_ref, out_right_ref):
    half, breadth = ROT // 2, 2 * HEAD_DIM
    lane = lax.broadcasted_iota(jnp.int32, (half, breadth), 1)
    row = lax.broadcasted_iota(jnp.int32, (half, breadth), 0)
    within = lane % HEAD_DIM
    first = jnp.where(within == row, 1.0, 0.0)
    second = jnp.where(within == row + half, 1.0, 0.0)

    def spread(ref, pattern):
        return lax.dot_general(
            ref[...], pattern, (((0,), (0,)), ((), ())),
            precision=lax.Precision.HIGHEST, preferred_element_type=F32,
        )

    lanes = lax.broadcasted_iota(jnp.int32, out_cos_ref.shape, 1) % HEAD_DIM
    out_cos_ref[...] = jnp.where(lanes < ROT, spread(cos_ref, first + second), 1.0)
    out_left_ref[...] = -spread(sin_ref, first)
    out_right_ref[...] = spread(sin_ref, second)


def rotary_tables(cosines, sines):
    tokens = cosines.shape[1]
    return pl.pallas_call(
        table_kernel,
        out_shape=[sds((tokens, 2 * HEAD_DIM), F32)] * 3,
        compiler_params=pltpu.CompilerParams(vmem_limit_bytes=VMEM_LIMIT),
        cost_estimate=cost(0, 0),
    )(cosines, sines)


def feed_kernel(weight, first, last, number, places_ref, *refs):
    w_refs, refs = refs[: weight.count], refs[weight.count :]
    n_refs, g_refs, (down_ref, up_ref), refs = (
        refs[:number],
        refs[number : 2 * number],
        refs[2 * number : 2 * number + 2],
        refs[2 * number + 2 :],
    )
    if not first:
        (low_in, glow_in, y_in, dn_in), refs = refs[:4], refs[4:]
    *refs, gdown_ref, ggate_ref, gupper_ref, n_ref, g_ref, w_ref, sems = refs
    step, width = pl.program_id(0), n_ref.shape[1]
    rank, part = gdown_ref.shape
    take_tile(n_refs, n_ref, step)
    take_tile(g_refs, g_ref, step)

    @pl.when(step == 0)
    def _():
        wait_for(weight.bring(w_refs, places_ref, w_ref, sems))
        for ref in (gdown_ref, ggate_ref, gupper_ref):
            ref[...] = jnp.zeros_like(ref)

    normed, grad = n_ref[...], g_ref[...]
    if first:
        low = dot_nt(normed, down_ref[...]).astype(BF)
        grad_low = dot_nt(grad, up_ref[...]).astype(BF)
        refs[2][...] = low
        refs[3][...] = grad_low
    else:
        low, grad_low = low_in[...], glow_in[...]
    deep = slice(width, width + rank)
    both = dot(normed, w_ref[:width, : 2 * part]) + dot(low, w_ref[deep, : 2 * part])
    gate, upper = both[:, :part], both[:, part:]
    grad_unit = dot(grad, w_ref[:width, 2 * part :]) + dot(grad_low, w_ref[deep, 2 * part :])
    sigmoid = 1.0 / (1.0 + jnp.exp(-gate))
    acted = gate * sigmoid
    unit = (acted * upper).astype(BF)
    grad_gate = (grad_unit * upper * (sigmoid + acted * (1.0 - sigmoid))).astype(BF)
    grad_upper = (grad_unit * acted).astype(BF)
    y = dot_nt(unit, w_ref[:, 2 * part :])
    dn = dot_nt(grad_gate, w_ref[:, :part]) + dot_nt(grad_upper, w_ref[:, part : 2 * part])
    if not first:
        y, dn = y + y_in[...].astype(F32), dn + dn_in[...].astype(F32)
    if last:
        give_tile(y.astype(BF), refs[:number], step)
        give_tile(dn.astype(BF), refs[number:], step)
    else:
        refs[0][...] = y.astype(BF)
        refs[1][...] = dn.astype(BF)
    gdown_ref[...] += dot_tn(grad_low, unit)
    ggate_ref[...] += dot_tn(low, grad_gate)
    gupper_ref[...] += dot_tn(low, grad_upper)


def feed(normed, grads, down, up, weight, sums, rows, start, last):
    block, width = normed[0].shape
    rank, number = down.shape[0], len(normed)
    deep, part = weight.shape[0], weight.shape[1] // 3
    narrow = sds((rank, part), F32)
    tokens = number * block
    if last:
        wide = sds((block, deep // LANES * LANES + LANES), BF)
        shapes, specs = [wide] * (2 * number), [whole_spec(wide.shape)] * (2 * number)
    else:
        shapes, specs = [sds((tokens, deep), BF)] * 2, [row_spec(rows, deep)] * 2
    first = not sums
    if first:
        shapes, specs = shapes + [sds((tokens, rank), BF)] * 2, specs + [row_spec(rows, rank)] * 2
    arrays = (*normed, *grads, down, up)
    size = weight.shape[0] * weight.shape[1]
    return weight_call(
        functools.partial(feed_kernel, weight, first, last, number),
        weight,
        (tokens // rows,),
        [whole_spec(a.shape) for a in arrays]
        + [pl.BlockSpec((rows, a.shape[1]), lambda t, *_: (start + t, 0)) for a in sums],
        specs + [whole_spec(narrow.shape)] * 3,
        shapes + [narrow] * 3,
        [pltpu.VMEM((rows, width), BF)] * 2 + weight.scratch(),
        cost(8 * tokens * size, 2 * size),
        [*arrays, *sums],
    )


STEP_SLOTS = 4


def each_slot(labels_ref, in_refs):
    for j in range(STEP_SLOTS):
        slot = pl.program_id(0) * STEP_SLOTS + j
        for n, ref in enumerate(in_refs):
            for s in range(ref.shape[0]):
                yield j, labels_ref[n * ref.shape[0] + s] == slot, ref.at[s]


def settle_first_kernel(fold, labels_ref, *refs):
    *in_refs, down_ref, hid_ref, gate_ref = refs
    local = down_ref.shape[-1]
    for ref in (down_ref, hid_ref, gate_ref):
        ref[...] = jnp.zeros_like(ref)
    for j, here, found in each_slot(labels_ref, in_refs):

        @pl.when(here)
        def _(j=j, found=found):
            for n, k in enumerate(DOWN_FIRST):
                down_ref[j, k] += found[n].astype(F32)
            for k in range(fold):
                at, n = slice(k * local, (k + 1) * local), len(DOWN_FIRST) + k
                hid_ref[j, :, at] += found[n].astype(F32)
                gate_ref[j, 0, :, at] += found[n + fold].astype(F32)
                gate_ref[j, 1, :, at] += found[n + 2 * fold].astype(F32)


def settle_second_kernel(labels_ref, *refs):
    *in_refs, _, down_ref, up_ref = refs
    downs, ups = down_ref.shape[1], up_ref.shape[1]
    for ref in (down_ref, up_ref):
        ref[...] = jnp.zeros_like(ref)
    for j, here, found in each_slot(labels_ref, in_refs):

        @pl.when(here)
        def _(j=j, found=found):
            down_ref[j] += found[:downs].astype(F32)
            up_ref[j] += found[downs : downs + ups].astype(F32)


DOWN_FIRST = (4, 5)


def slot_spec(shape):
    block = (STEP_SLOTS,) + shape[1:]
    return pl.BlockSpec(block, lambda i, *_, n=len(shape): (i,) + (0,) * (n - 1))


def settle_call(kernel, labels, grads, before, shapes, blocks, aliases):
    slots = shapes[0][0]
    return pl.pallas_call(
        kernel,
        grid_spec=pltpu.PrefetchScalarGridSpec(
            num_scalar_prefetch=1,
            grid=(slots // STEP_SLOTS,),
            in_specs=[whole_spec(g.shape) for g in grads]
            + [pl.BlockSpec(memory_space=pl.ANY) for _ in before],
            out_specs=[slot_spec(b) for b in blocks],
        ),
        out_shape=[sds(s, F32) for s in shapes],
        input_output_aliases=aliases,
        compiler_params=params(),
        cost_estimate=cost(0, 0),
    )(labels, *grads, *before)


def settle_first(labels, grads, slots, fold):
    rank, local = grads[0].shape[2:]
    hidden = fold * local
    shapes = [(slots, 6, rank, local), (slots, rank, hidden), (slots, 2, rank, hidden)]
    kernel = functools.partial(settle_first_kernel, fold)
    return settle_call(kernel, labels, grads, [], shapes, shapes, {})


def settle_second(labels, grads, down):
    up = down.shape[:1] + (9,) + down.shape[2:]
    part = (down.shape[0], DOWN_FIRST[0]) + down.shape[2:]
    aliases = {1 + len(grads): 0}
    return settle_call(
        settle_second_kernel, labels, grads, [down], [down.shape, up], [part, up], aliases
    )


def chunks(hidden):
    return 2 * hidden // 3, hidden // 3


def body(
    inputs,
    context,
    positions,
    adapter_index,
    self_in_weight,
    self_out_weight,
    cross_query_weight,
    cross_keyval_weight,
    cross_out_weight,
    feed_in_weight,
    feed_out_weight,
    norm_gains,
    norm_biases,
    adapter_down,
    adapter_down_hidden,
    adapter_up,
    adapter_up_hidden,
    out_cotangent,
    *,
    pairs,
    chips,
):
    group = Group(pairs, chips)
    members = 2 * pairs
    rows, width = inputs.shape[1], inputs.shape[2]
    block = self_in_weight.shape[0]
    local = self_in_weight.shape[2]
    hidden = feed_in_weight.shape[2]
    slots, rank = adapter_down.shape[0], adapter_down.shape[3]
    deep = width + rank
    parts = chunks(hidden)
    fold = hidden // local
    pieces = group.pieces
    gains, biases = norm_gains, norm_biases
    tile = min(256, members * rows)
    tiles = members * rows // tile
    near_tiles = tiles // pairs

    def packed(*parts):
        return jnp.concatenate(parts, axis=1)

    def stacked(*parts):
        return jnp.concatenate(parts, axis=0)

    def listed(values):
        return list(values) if isinstance(values, (list, tuple)) else [values]

    def piece(array, k, size):
        return lax.dynamic_slice_in_dim(array, pieces[k] * size, size, array.ndim - 1)

    def own(array):
        return piece(array, 0, local)

    near_chips = [1, 2] if chips == 4 else list(range(1, chips))
    chip_rows = [(group.chip ^ k) * 2 * block for k in range(chips)]
    one = [[c + o * block for c in chip_rows] for o in (group.core, 1 - group.core)]
    one += [[c + o * block for c in chip_rows] for o in (group.zhi, 1 - group.zhi)]
    row_places = jnp.stack(
        [r for found in one for r in found] + [jnp.zeros_like(group.core)]
        + [p * local for p in pieces] + [group.core]
    ).astype(jnp.int32)
    mine_at, other_at, first_at, second_at, zero = (n * chips for n in range(5))
    at_pieces = zero + 1
    core_at = at_pieces + members

    def chip_weight(own_entry, near, rest, low, columns, halves):
        weight = Weight((deep, columns), row_places)
        entries = [own_entry, *near]
        for k, (array, row) in zip([0, *near_chips], entries):
            weight.add(
                array,
                *[(row + r, block, c, columns, None, at + k, 0) for r, c, at in halves],
            )
        if rest:
            side_by_side = halves[1][0] == 0
            for n, (array, row) in enumerate(rest):
                size = block // 2 if side_by_side else block
                picked = halves if side_by_side else halves[n : n + 1]
                weight.add(
                    array,
                    *[
                        (row, size, c, columns, None, at + 3, n * size if side_by_side else 0)
                        for _, c, at in picked
                    ],
                )
        weight.add(low, (0, rank, 0, columns, None, zero, width))
        return weight

    stacked_halves = [(0, 0, first_at), (block, 0, second_at)]
    packed_halves = [(0, 0, mine_at), (0, 2 * local, other_at)]

    def spread(got, half_at, half, own_block):
        if got and chips == 4:
            turns = [
                got[1][half_at : half_at + half],
                got[0][half_at + half : half_at + 2 * half],
            ]
            if own_block is not None:
                turns = listed(step.mark(*[stacked(turn, own_block) for turn in turns]))
            return [xor_move(turn, "chip", 4, k) for turn, k in zip(turns, near_chips)]
        if own_block is None:
            return []
        return [xor_move(own_block, "chip", chips, k) for k in near_chips]

    def skip(half):
        return half if chips == 4 else 0

    def flat(*groups):
        return [x for g in groups for x in listed(g)]

    def wait_all(*groups):
        groups = [listed(g) for g in groups]
        values = iter(listed(step.wait(*flat(*groups))))
        return [[next(values) for _ in g] for g in groups]

    def swap_all(blocks):
        if not blocks:
            return []
        blocks = listed(step.wait(*blocks))
        return listed(step.wait(*[core_swap(b) for b in blocks]))

    shard_self = packed(*[self_in_weight[:, i] for i in range(3)], self_out_weight.T)
    step = Order(shard_self[:8, :128])
    self_from = [home_swap(shard_self), turned(shard_self)]
    stream_own, context_own = home_swap(inputs[0]), home_swap(context[0])
    index, positions = step.wait(adapter_index, positions)
    index_other, positions_other = step.wait(core_swap(index), core_swap(positions))
    index = jnp.where(group.home, index, index_other)[0]
    positions = jnp.where(group.home, positions, positions_other)[0]
    down = lax.dynamic_index_in_dim(adapter_down.transpose(0, 1, 3, 2), index, 0, keepdims=False)
    up = lax.dynamic_index_in_dim(adapter_up.transpose(0, 2, 1, 3), index, 0, keepdims=False)
    down, up = step.mark(down, up)
    low_self = packed(*[own(up[i]) for i in range(3)], own(down[1]))
    low_keyval = packed(own(up[5]), own(up[6]))
    low_cross = []
    for k in range(pairs):
        two = [
            (group.p ^ k) * local + core * pairs * local for core in (0, 1)
        ]
        low_cross.append(
            packed(
                *[
                    lax.dynamic_slice_in_dim(table[4], where, local, 1)
                    for table in (up, down)
                    for where in two
                ]
            )
        )
    low_cross = stacked(*low_cross)
    low_self, low_keyval, low_cross = step.mark(low_self, low_keyval, low_cross)
    keyval_parts = step.wait(cross_keyval_weight)
    keyval_parts = step.mark(keyval_parts[:, 0], keyval_parts[:, 1])
    shard_cross = step.mark(packed(cross_query_weight, cross_out_weight.T, *keyval_parts))
    far_cross = group.cross(shard_cross)
    blocks_at = [
        lax.dynamic_slice_in_dim(positions, pieces[k] * rows, rows, 0) for k in range(members)
    ]
    half = ROT // 2
    inverse = 10000.0 ** (-jnp.arange(half, dtype=F32) / half)
    angles = inverse[:, None] * step.wait(jnp.concatenate(blocks_at)).astype(F32)[None]
    tables = step.mark(*rotary_tables(*step.mark(jnp.cos(angles), jnp.sin(angles))))
    feed_in, feed_out = step.wait(feed_in_weight, feed_out_weight)
    gate_rows, upper_rows = step.mark(feed_in[:, 0], feed_in[:, 1])
    at = [sum(parts[:i]) for i in range(len(parts))]

    def feed_shard(i):
        to = slice(at[i], at[i] + parts[i])
        gate, upper, out = step.wait(gate_rows, upper_rows, feed_out)
        return step.mark(packed(gate[:, to], upper[:, to], out.T[:, to]))

    shard_feed = [feed_shard(i) for i in range(len(parts))]

    self_from = step.wait(*self_from)
    ready_self = step.mark(stacked(*self_from))
    near_self = spread([], 0, 0, ready_self)
    stream_own, context_own = step.wait(stream_own, context_own)
    stream_far, context_far = group.far_p(stream_own), group.far_p(context_own)
    (near_self,) = wait_all(near_self)
    rest_self = spread(near_self, 0, block, None)
    rest_self, stream_far, context_far, (far_cross,) = wait_all(
        rest_self, stream_far, context_far, [far_cross]
    )
    stream_other, context_other, *found = swap_all(
        [stream_own, context_own, *stream_far, *context_far]
    )
    stream_far_other, swapped = found[: pairs - 1], found[pairs - 1 :]
    context_blocks = [context_own, context_other]
    for far, far_other in zip(context_far, swapped):
        context_blocks += [far, far_other]
    stream = [stream_own, stream_other]
    for far, far_other in zip(stream_far, stream_far_other):
        stream += [far, far_other]
    self_weight = chip_weight(
        (ready_self, 0), [(g, 0) for g in near_self], [(g, 0) for g in rest_self], low_self,
        4 * local, stacked_halves,
    )

    mine = jnp.where(group.home, shard_cross, far_cross)
    given = jnp.where(group.home, far_cross, shard_cross)
    keyval_mine, keyval_give = mine[:, 2 * local :], given[:, 2 * local :]
    low_zhi = jnp.where(group.zhi == 0, shard_cross, far_cross)
    high_zhi = jnp.where(group.zhi == 0, far_cross, shard_cross)
    pair = packed(
        *[two[:, n * local : (n + 1) * local] for n in (0, 1) for two in (low_zhi, high_zhi)]
    )
    keyval_mine, keyval_give, pair = step.mark(keyval_mine, keyval_give, pair)
    (keyval_other,) = swap_all([keyval_give])
    ready_keyval = step.mark(stacked(packed(keyval_mine, keyval_other), pair))

    got_one = spread([], 0, 0, ready_keyval)
    pair_far = group.far_p(pair)
    half_columns = shard_feed[0].shape[1] // 2
    halves = step.wait(shard_feed[0][:, :half_columns], shard_feed[0][:, half_columns:])
    feed_one = [home_swap(halves[0]), turned(halves[0])]
    query, keys, values, low_one, normed_one = project_self(
        listed(step.wait(*stream)), gains[0:1], biases[0:1], down[0], self_weight, tables, tile
    )
    query, keys, values = step.mark(query, keys, values)
    heads_far, logsum_far, *y_far = attend_self(
        query, keys, values, self_weight, tile, near_tiles, tiles - near_tiles, rows
    )
    y_far = listed(step.mark(*y_far))

    def far_sums(*groups):
        others = iter(swap_all([g[2 * k + 1] for g in groups for k in range(pairs - 1)]))
        sums = [
            [group.near_sums(g[2 * k], next(others)).astype(BF) for k in range(pairs - 1)]
            for g in groups
        ]
        values = iter(listed(step.mark(*flat(*sums))))
        return [[next(values) for _ in s] for s in sums]

    def move_p(sums):
        return [xor_move(s, "p", pairs, k + 1) for k, s in enumerate(sums)]

    def sum_up(blocks, other, far):
        total = group.near_sums(blocks[0], other)
        for f in far:
            total = total + f.astype(F32)
        return step.mark(total)

    got_one, pair_far, feed_one = wait_all(got_one, pair_far, feed_one)
    (y_sums,) = far_sums(y_far)

    far = move_p(y_sums)
    quarter = block // 2
    if chips == 4:
        turns = [
            stacked(got[start : start + quarter], got[start + block : start + block + quarter], pair_far[0])
            for got, start in ((got_one[1], 0), (got_one[0], quarter))
        ]
        turns = step.mark(*turns)
        got_two = [xor_move(turn, "chip", 4, k) for turn, k in zip(turns, near_chips)]
    else:
        got_two = flat(*[spread([], 0, 0, p) for p in pair_far])
    feed_two = [home_swap(halves[1]), turned(halves[1])]
    heads_near, logsum_near, *y_rows = attend_self(
        step.wait(query), keys, values, self_weight, tile, 0, near_tiles, rows
    )
    y_rows = listed(step.mark(*y_rows))
    (got_two,) = wait_all(got_two)
    keyval_weight = chip_weight(
        (ready_keyval, 0), [(g, 0) for g in got_one],
        [(g, 0) for g in got_two] if chips == 4 else [], low_keyval, 2 * local, packed_halves,
    )
    down_context = step.mark(down[3].T)
    keyval, low_context = context_forward(at_pieces, context_blocks, keyval_weight, down_context)
    keyval = step.mark(keyval)

    far, feed_two = wait_all(far, feed_two)
    (y_other,) = swap_all([y_rows[1]])
    branch = [y_rows[0], y_other, *far]
    keyval_far = group.far_p(keyval)
    ready_feed = [step.mark(stacked(*[packed(*two) for two in zip(feed_one, feed_two)]))]
    found = [(ready_keyval, block, block, 0, 0, 0)]
    found += [(g, block, block, k, 0, 0) for g, k in zip(got_one, near_chips)]
    if chips == 4:
        turns = [got_two[1][block : block + quarter], got_two[0][block + quarter :]]
        got_three = [xor_move(turn, "chip", 4, k) for turn, k in zip(turns, near_chips)]
        keyval_far, got_three = wait_all(keyval_far, got_three)
        found += [(g, 0, quarter, 3, n * quarter, 1) for n, g in enumerate(got_three)]
        found.append((pair_far[0], 0, block, 0, 0, 1))
        for n, (g, k) in enumerate(zip(got_two, near_chips)):
            found += [(g, block, block, k, 0, 1), (g, quarter, quarter, 3, n * quarter, 0)]
    else:
        (keyval_far,) = wait_all(keyval_far)
        count = len(near_chips)
        for n, p in enumerate(pair_far):
            found.append((p, 0, block, 0, 0, n + 1))
            found += [
                (g, 0, block, k, 0, n + 1)
                for g, k in zip(got_two[n * count : (n + 1) * count], near_chips)
            ]
    arrays = []
    for entry in found:
        if not any(entry[0] is a for a in arrays):
            arrays.append(entry[0])
    swapped = swap_all([keyval, *keyval_far, *arrays])
    keyvals = [keyval, swapped[0]]
    for far, far_other in zip(keyval_far, swapped[1:]):
        keyvals += [far, far_other]
    others = swapped[1 + len(keyval_far) :]
    cross_weight = Weight((pairs, deep, 4 * local), row_places)
    for array, other in zip(arrays, others):
        entries = [e[1:] for e in found if e[0] is array]
        for source, places in ((array, mine_at), (other, other_at)):
            cross_weight.add(
                source,
                *[
                    (row, size, 0, 4 * local, n, places + k, offset)
                    for row, size, k, offset, n in entries
                ],
            )
    cross_weight.add(
        low_cross, *[(n * rank, rank, 0, 4 * local, n, zero, width) for n in range(pairs)]
    )

    near_feed = [spread([], 0, 0, ready_feed[0])]
    feed_from = [home_swap(step.wait(shard_feed[1])), turned(step.wait(shard_feed[1]))]
    stream_own, *branch = step.wait(stream_own, *branch)

    (
        stream_one, stream_two, normed_two, normed_three, query_cross, heads_cross, logsum_cross,
        low_two, low_three, low_four,
    ) = cross_forward(
        stream_own, branch, up[3], up[7], down[2], gains, biases, cross_weight, keyvals, core_at,
    )
    normed_own = step.mark(normed_three)
    (feed_from,) = wait_all(feed_from)
    ready_feed.append(step.mark(stacked(*feed_from)))

    normed_far = group.far_p(normed_own)
    cotangent_own = home_swap(step.wait(out_cotangent[0]))
    (normed_other,) = swap_all([normed_own])
    down_hidden = lax.dynamic_index_in_dim(
        adapter_down_hidden.transpose(0, 2, 1), index, 0, keepdims=False
    )
    up_hidden = lax.dynamic_index_in_dim(
        adapter_up_hidden.transpose(0, 2, 1, 3), index, 0, keepdims=False
    )
    feed_down, feed_up = piece(down_hidden, 0, hidden), piece(up_hidden, 0, hidden)
    feed_down, feed_gate, feed_upper = step.mark(feed_down, feed_up[0], feed_up[1])
    low_feed = [
        packed(feed_gate[:, to], feed_upper[:, to], feed_down[:, to])
        for to in [slice(a, a + p) for a, p in zip(at, parts)]
    ]
    low_feed = step.mark(*low_feed)
    (near_feed[0],) = wait_all(near_feed[0])
    rest_feed = spread(near_feed[0], 0, block, None)
    normed_far, (cotangent_own,) = wait_all(normed_far, [cotangent_own])
    cotangent_other, *normed_swapped = swap_all([cotangent_own, *normed_far])

    def feed_weight(i, rest):
        return chip_weight(
            (ready_feed[i], 0), [(g, 0) for g in near_feed[i]], [(g, 0) for g in rest],
            low_feed[i], 3 * parts[i], stacked_halves,
        )

    normed_blocks = [[normed_own, normed_other], []]
    cotangent_blocks = [[cotangent_own, cotangent_other], []]

    def feed_pass(weight, half, state, last):
        normed, cotangent = wait_all(normed_blocks[half], cotangent_blocks[half])
        found = feed(normed, cotangent, down[5], up[8], weight, state, tile, 0, last)
        *values, gdown, ggate, gupper = found
        return listed(step.mark(*values)), [gdown, ggate, gupper]

    def added(one, two):
        return [a + b for a, b in zip(one, two)]

    (rest_feed,) = wait_all(rest_feed) if rest_feed else ([],)
    weight = feed_weight(0, rest_feed)
    near_feed.append(spread([], 0, 0, ready_feed[1]))
    cotangent_far = group.far_p(cotangent_own)
    (y, dn, *lows), grads = feed_pass(weight, 0, (), False)
    states = [(*lows, y, dn)]
    near_feed[1], cotangent_far = wait_all(near_feed[1], cotangent_far)
    swapped = normed_swapped + swap_all(cotangent_far)
    for blocks, fars, others in (
        (normed_blocks[1], normed_far, swapped[: pairs - 1]),
        (cotangent_blocks[1], cotangent_far, swapped[pairs - 1 :]),
    ):
        for far, far_other in zip(fars, others):
            blocks += [far, far_other]
    rest_feed = spread(near_feed[1], 0, block, None)
    (y, dn, *lows), more = feed_pass(weight, 1, (), False)
    states.append((*lows, y, dn))
    feed_grads = [added(grads, more)]
    (rest_feed,) = wait_all(rest_feed) if rest_feed else ([],)

    weight = feed_weight(1, rest_feed)
    found, grads = feed_pass(weight, 1, states[1], True)
    y_far, dn_far = found[: len(found) // 2], found[len(found) // 2 :]

    dn_sums, y_sums = far_sums(dn_far, y_far)
    far = move_p(dn_sums)
    found, more = feed_pass(weight, 0, states[0], True)
    y_rows, dn_rows = found[:2], found[2:]
    feed_grads.append(added(grads, more))
    (far,) = wait_all(far)
    dn_other, y_other = swap_all([dn_rows[1], y_rows[1]])
    grad_normed = [dn_rows[0], dn_other, *far]

    far = move_p(step.mark(*y_sums) if len(y_sums) > 1 else [step.mark(*y_sums)])
    grad_stream, branch_grad, fixed_rows, near_rows, *keyval_rows = cross_back(
        cotangent_own, listed(step.wait(*grad_normed)), stream_one, stream_two, normed_two,
        query_cross, heads_cross, logsum_cross, low_three, low_four, up[7], down[5], down[2],
        gains, biases, cross_weight, keyvals, core_at,
    )
    branch_grad, *keyval_rows = step.mark(branch_grad, *keyval_rows)
    (far,) = wait_all(far)

    branch_far = group.far_p(branch_grad)
    (branch_other,) = swap_all([branch_grad])

    def back(grad, heads, logsum, first, before, ends):
        return attend_back(
            grad, up[3], self_weight, query, keys, values, heads, logsum, tables, low_one, tile,
            first, before, ends,
        )

    def taken(by_piece, k):
        return lax.dynamic_index_in_dim(by_piece, pieces[k], 0, keepdims=False)

    def taken_near(by_member, k):
        member = k // 2 * 2 + (group.core ^ (k % 2))
        return lax.dynamic_index_in_dim(by_member, member, 0, keepdims=False)

    first_rows = listed(
        step.mark(
            *[
                stacked(taken_near(near_rows, k)[:rank], taken(fixed_rows, k)[rank : 2 * rank])
                for k in range(members)
            ]
        )
    )
    others = swap_all([*keyval_rows[1::2], *first_rows[1::2]])
    keyval_sums, first_sums = (
        [group.near_sums(a, b) for a, b in zip(own[::2], others[n * pairs : (n + 1) * pairs])]
        for n, own in enumerate((keyval_rows, first_rows))
    )
    moving = listed(step.mark(*[x.astype(BF) for x in keyval_sums[1:] + first_sums[1:]]))
    keyval_far, first_far = move_p(moving[: pairs - 1]), move_p(moving[pairs - 1 :])
    grads = listed(step.wait(branch_grad, branch_other))
    near_back = step.mark(*back(grads, heads_near, logsum_near, 0, None, None))
    branch_far, keyval_far, first_far = wait_all(branch_far, keyval_far, first_far)

    output, grad_up_eight = step.mark(
        *output_end(
            stream_two, [step.wait(y_rows[0]), y_other, *far], up[8], cotangent_own, members
        )
    )
    swapped = swap_all(branch_far)
    branch_blocks = []
    for f, o in zip(branch_far, swapped):
        branch_blocks += [f, o]

    def columns(array):
        return array.reshape(rank, -1, local).transpose(1, 0, 2)

    def sent(parts):
        parts.append(jnp.full((1, rank, local), index, F32))
        grads = jnp.concatenate(parts, axis=0).astype(BF).reshape(-1, local)
        grads = step.mark(grads)
        return [home_swap(grads), turned_back(grads)]

    def to_chips(blocks):
        both = step.mark(stacked(*blocks))
        return [both] + [xor_move(both, "chip", chips, k) for k in range(1, chips)]

    def every(blocks):
        blocks = [b.reshape(2, -1, rank, local) for b in blocks]
        labels = jnp.concatenate([b[:, -1, 0, 0] for b in blocks])
        return blocks, labels.astype(jnp.int32)

    def total(own, far):
        for f in far:
            own = own + f.astype(F32)
        return own

    summed = total(first_sums[0], first_far).reshape(-1, rank, local)
    first = sent([summed, *[columns(jnp.concatenate(g, axis=1)) for g in zip(*feed_grads)]])
    block_output = home_swap(step.wait(output))
    branch_blocks = listed(step.wait(*branch_blocks))
    found = back(
        branch_blocks, heads_far, logsum_far, near_tiles, near_back,
        (normed_one, low_two, branch_grad),
    )
    first, (block_output,), found = wait_all(first, [block_output], found)
    grad_down_one, grad_up_self, own_rows, *dn_blocks = found

    count = pairs - 1
    dn_others = swap_all(dn_blocks[1::2])
    dn_sums = [group.near_sums(a, b) for a, b in zip(dn_blocks[::2], dn_others)]
    far = move_p(listed(step.mark(*[x.astype(BF) for x in dn_sums[1:]])))
    first = to_chips(first)
    grad_keyval = step.mark(total(keyval_sums[0], keyval_far).astype(BF))
    grad_up_keyval, *found = step.mark(
        *context_back(
            at_pieces, context_blocks, keyval_weight, down_context, low_context, grad_keyval
        )
    )
    context_rows, grad_down_three = found[:members], found[members:]
    far, first = wait_all(far, first)

    second_rows = listed(
        step.mark(
            *[
                stacked(
                    taken(own_rows, k), taken(fixed_rows, k)[:rank],
                    taken(fixed_rows, k)[2 * rank :], taken(grad_up_eight, k), grad_down_three[k],
                    taken_near(near_rows, k)[rank:],
                )
                for k in range(members)
            ]
        )
    )
    swapped = swap_all([*second_rows[1::2], *context_rows[1::2]])
    second_sums, context_sums = (
        [group.near_sums(a, b) for a, b in zip(own[::2], swapped[n * pairs : (n + 1) * pairs])]
        for n, own in enumerate((second_rows, context_rows))
    )
    moving = [x.astype(BF) for x in second_sums[1:] + context_sums[1:]]
    moving = listed(step.mark(*moving))
    second_far, context_far = move_p(moving[:count]), move_p(moving[count:])
    grad_inputs = step.mark(
        input_end(
            stream_own, grad_stream, [dn_blocks[0], dn_others[0], *far], down[0], gains[0:1]
        )
    )
    second_far, context_far = wait_all(second_far, context_far)
    summed = total(second_sums[0], second_far).reshape(-1, rank, local)
    second = sent(
        [
            summed[0:1],
            grad_down_one[None],
            summed[2:3],
            summed[5:6],
            columns(grad_up_self),
            summed[1:2],
            summed[6:7],
            columns(grad_up_keyval),
            summed[3:5],
        ]
    )
    grad_context = home_swap(step.mark(total(context_sums[0], context_far).astype(BF)))
    (second,) = wait_all(second)
    second = to_chips(second)
    grad_inputs = home_swap(step.wait(grad_inputs))
    first, labels = every(listed(step.wait(*first)))
    grad_down, grad_hidden, grad_gate = settle_first(labels, first, slots, fold)
    grad_down = step.mark(grad_down)
    (second,) = wait_all(second)
    second, labels = every(second)
    labels = labels + (step.token[0, 0].astype(F32) * 0.0).astype(jnp.int32)
    grad_down, grad_up = settle_second(labels, second, grad_down)
    return (
        block_output[None],
        grad_inputs.astype(F32)[None],
        grad_context.astype(F32)[None],
        grad_down.transpose(0, 1, 3, 2),
        grad_hidden.transpose(0, 2, 1),
        grad_up.transpose(0, 2, 1, 3),
        grad_gate.transpose(0, 2, 1, 3),
    )


def solution(mesh):
    members = mesh.shape["tensor"]
    chips = mesh.shape["dp"] // 2
    mesh = Mesh(
        mesh.devices.reshape(chips, 2, 2, members // 2), ("chip", "core", "zhi", "p")
    )
    dp, tensor = ("chip", "core"), ("zhi", "p")
    in_specs = (
        P(dp, tensor, None),
        P(dp, None, tensor),
        P(dp, None),
        P(dp),
        P(dp, None, tensor),
        P(tensor, dp),
        P(dp, tensor),
        P(dp, None, tensor),
        P(tensor, dp),
        P(dp, None, tensor),
        P(tensor, dp),
        P(),
        P(),
        P(),
        P(),
        P(),
        P(),
        P(dp, tensor, None),
    )
    out_specs = (
        P(dp, tensor, None),
        P(dp, tensor, None),
        P(dp, None, tensor),
        P(None, None, tensor, None),
        P(None, tensor, None),
        P(None, None, None, tensor),
        P(None, None, None, tensor),
    )

    def run(*args):
        return body(*args, pairs=members // 2, chips=chips)

    return jax.shard_map(run, mesh=mesh, in_specs=in_specs, out_specs=out_specs, check_vma=False)
```

```python
import functools

import jax
import jax.numpy as jnp
from jax import lax
from jax.experimental import pallas as pl
from jax.experimental.pallas import tpu as pltpu
from jax.sharding import Mesh, PartitionSpec as P

HEAD_DIM = 64
ROT = 32
EPSILON = 1e-05
F32 = jnp.float32
BF = jnp.bfloat16
SWAP = ((0, 1), (1, 0))
LANES = 128
VMEM_LIMIT = 56 * 1024 * 1024


def dot(left, right):
    return jnp.dot(left, right, preferred_element_type=F32)


def dot_nt(left, right):
    return lax.dot_general(left, right, (((1,), (1,)), ((), ())), preferred_element_type=F32)


def dot_tn(left, right):
    return lax.dot_general(left, right, (((0,), (0,)), ((), ())), preferred_element_type=F32)


class Order:
    def __init__(self, first):
        self.token = first

    def wait(self, *values):
        *values, self.token = lax.optimization_barrier((*values, self.token))
        return values[0] if len(values) == 1 else values

    mark = wait


def core_swap(x):
    return lax.ppermute(x, "core", SWAP)


def xor_move(x, axis, size, k):
    return lax.ppermute(x, axis, [(i, i ^ k) for i in range(size)])


def home_swap(x):
    return lax.ppermute(x, ("core", "zhi"), [(0, 0), (1, 2), (2, 1), (3, 3)])


def turned(x):
    return lax.ppermute(x, ("core", "zhi"), [(0, 1), (1, 3), (2, 0), (3, 2)])


def turned_back(x):
    return lax.ppermute(x, ("core", "zhi"), [(0, 2), (1, 0), (2, 3), (3, 1)])


class Group:
    def __init__(self, pairs, chips):
        self.pairs, self.chips = pairs, chips
        self.core, self.zhi, self.p = (lax.axis_index(n) for n in ("core", "zhi", "p"))
        self.chip = lax.axis_index("chip")
        self.home = self.core == self.zhi
        self.pieces = [
            (self.core ^ kc) * pairs + (self.p ^ kp) for kp in range(pairs) for kc in (0, 1)
        ]

    def far_p(self, own):
        return [xor_move(own, "p", self.pairs, k) for k in range(1, self.pairs)]

    def near_sums(self, own, other):
        return own.astype(F32) + other.astype(F32)

    def cross(self, shard):
        return xor_move(shard, "zhi", 2, 1)

    def spread_one(self, block):
        if self.chips == 4:
            return [xor_move(block, "chip", 4, k) for k in (1, 2)]
        return [xor_move(block, "chip", self.chips, k) for k in range(1, self.chips)]

    def spread_two(self, got):
        if self.chips != 4:
            return []
        half = got[0].shape[0] // 2
        return [xor_move(got[1][:half], "chip", 4, 1), xor_move(got[0][half:], "chip", 4, 2)]

    def places(self, rows):
        if self.chips == 4:
            diagonal = (self.chip ^ 3) * rows
            return [(self.chip ^ 1) * rows, (self.chip ^ 2) * rows, diagonal, diagonal + rows // 2]
        return [(self.chip ^ k) * rows for k in range(1, self.chips)]


class Weight:
    def __init__(self, shape, places):
        self.shape, self.places, self.arrays, self.moves = shape, places, [], []

    def add(self, array, *parts):
        self.moves += [(len(self.arrays), *part) for part in parts]
        self.arrays.append(array)

    @property
    def count(self):
        return len(self.arrays)

    def specs(self):
        return [pl.BlockSpec(memory_space=pl.ANY)] * self.count

    def columns(self, start, size):
        if size % 128 or start % 128:
            return 0, self.shape[-1], start
        return start, size, 0

    def scratch(self, size=None):
        shape = self.shape if size is None else self.shape[:-1] + (size,)
        return [pltpu.VMEM(shape, BF), pltpu.SemaphoreType.DMA((len(self.moves),))]

    def at_first(self, step, refs, places_ref, target, sems, start=0, size=None):
        def begin():
            @pl.when(step == 0)
            def _():
                self.bring(refs, places_ref, target, sems, start, size)

        def end():
            @pl.when(step == 0)
            def _():
                wait_for(self.bring(refs, places_ref, target, sems, start, size, go=False))

        return begin, end

    def bring(self, refs, places_ref, target, sems, start=0, size=None, go=True):
        copies = []
        for number, (source, row, rows, column, columns, lead, place, offset) in enumerate(self.moves):
            at = pl.ds(pl.multiple_of(places_ref[place] + offset, 16), rows)
            to = target.at[at] if lead is None else target.at[lead, at]
            if size is not None:
                column, columns = column + start, size
            found = refs[source].at[pl.ds(row, rows), pl.ds(column, columns)]
            copies.append(pltpu.make_async_copy(found, to, sems.at[number]))
        if go:
            for copy in copies:
                copy.start()
        return copies


def wait_for(copies):
    for copy in copies:
        copy.wait()


def weight_call(kernel, weight, grid, in_specs, out_specs, out_shape, scratch, estimate, arrays):
    return pl.pallas_call(
        kernel,
        grid_spec=pltpu.PrefetchScalarGridSpec(
            num_scalar_prefetch=1,
            grid=grid,
            in_specs=weight.specs() + in_specs,
            out_specs=out_specs,
            scratch_shapes=scratch,
        ),
        out_shape=out_shape,
        compiler_params=params(),
        cost_estimate=estimate,
    )(weight.places, *weight.arrays, *arrays)


def stats(stream):
    average = jnp.mean(stream, axis=-1, keepdims=True)
    centred = stream - average
    variance = jnp.mean(centred * centred, axis=-1, keepdims=True)
    scale = lax.rsqrt(variance + EPSILON)
    return centred * scale, scale


def layer_norm(stream, gain, bias):
    return (stats(stream)[0] * gain + bias).astype(BF)


def norm_backward(stream, gain, grad):
    unit, scale = stats(stream)
    grad = grad * gain
    return scale * (
        grad
        - jnp.mean(grad, axis=-1, keepdims=True)
        - unit * jnp.mean(grad * unit, axis=-1, keepdims=True)
    )


def turn(x, cosines, left_sines, right_sines):
    breadth = 2 * HEAD_DIM if x.shape[1] % (2 * HEAD_DIM) == 0 else HEAD_DIM
    half = ROT // 2
    for at in range(0, x.shape[1], breadth):
        group = x[:, at : at + breadth]
        if breadth % 128 == 0:
            left, right = pltpu.roll(group, breadth - half, 1), pltpu.roll(group, half, 1)
        else:
            left = jnp.concatenate([group[:, half:], group[:, :half]], axis=1)
            right = jnp.concatenate([group[:, -half:], group[:, :-half]], axis=1)
        yield (
            at,
            breadth,
            group * cosines[:, :breadth]
            + left * left_sines[:, :breadth]
            + right * right_sines[:, :breadth],
        )


def head_sums(product):
    columns = product.shape[1]
    rows = -(-columns // HEAD_DIM // 8) * 8
    head = lax.broadcasted_iota(jnp.int32, (rows, columns), 0)
    lane = lax.broadcasted_iota(jnp.int32, (rows, columns), 1)
    picked = jnp.where(lane // HEAD_DIM == head, 1.0, 0.0).astype(F32)
    return lax.dot_general(
        picked, product, (((1,), (1,)), ((), ())),
        precision=lax.Precision.HIGHEST, preferred_element_type=F32,
    )


def whole_spec(shape):
    return pl.BlockSpec(shape, lambda *_: (0,) * len(shape))


def row_spec(rows, columns):
    return pl.BlockSpec((rows, columns), lambda t, *_: (t, 0))


def take_tile(refs, tile_ref, step):
    rows, tile = refs[0].shape[0], tile_ref.shape[0]
    for i, ref in enumerate(refs):

        @pl.when(step == i * rows // tile)
        def _(i=i, ref=ref):
            tile_ref[i * rows % tile : i * rows % tile + rows, :] = ref[...]


def give_tile(value, refs, step):
    rows, (tile, columns) = refs[0].shape[0], value.shape
    for i, ref in enumerate(refs):

        @pl.when(step == i * rows // tile)
        def _(i=i, ref=ref):
            ref[:, :columns] = value[i * rows % tile : i * rows % tile + rows]
            ref[:, columns:] = jnp.zeros((rows, ref.shape[1] - columns), ref.dtype)


def total_of(refs):
    total = refs[0][...].astype(F32)
    for ref in refs[1:]:
        total = total + ref[...].astype(F32)
    return total


def by_piece(ref, row, value):
    local = ref.shape[2]
    for k in range(ref.shape[0]):
        ref[k, row : row + value.shape[0], :] = value[:, k * local : (k + 1) * local].astype(
            ref.dtype
        )


def params(semantics=1):
    return pltpu.CompilerParams(
        dimension_semantics=("arbitrary",) * semantics, vmem_limit_bytes=VMEM_LIMIT
    )


def cost(flops, moved, exps=0):
    return pl.CostEstimate(
        flops=int(flops) or 1000, bytes_accessed=int(moved) or 1000, transcendentals=int(exps)
    )


def sds(shape, dtype):
    return jax.ShapeDtypeStruct(shape, dtype)


def query_kernel(weight, part, count, places_ref, *refs):
    w_refs, refs = refs[: weight.count], refs[weight.count :]
    blocks, (gain_ref, bias_ref, down_ref, cos_ref, left_ref, right_ref), refs = (
        refs[:count],
        refs[count : count + 6],
        refs[count + 6 :],
    )
    q_ref, k_ref, v_ref, low_ref, n_ref, x_ref, w_ref, sems = refs
    step = pl.program_id(0)

    begin, end = weight.at_first(step, w_refs, places_ref, w_ref, sems, *part[:2])
    begin()
    take_tile(blocks, x_ref, step)
    local, width = q_ref.shape[1], x_ref.shape[1]
    normed = layer_norm(x_ref[...].astype(F32), gain_ref[...], bias_ref[...])
    n_ref[...] = normed
    low = dot_nt(normed, down_ref[...]).astype(BF)
    low_ref[...] = low
    end()
    at = slice(part[2], part[2] + 3 * local)
    mixed = dot(normed, w_ref[:width, at]) + dot(low, w_ref[width:, at])
    tables = cos_ref[...], left_ref[...], right_ref[...]
    for at, breadth, turned in turn(mixed[:, :local], *tables):
        q_ref[:, at : at + breadth] = (turned * HEAD_DIM**-0.5).astype(BF)
    for at, breadth, turned in turn(mixed[:, local : 2 * local], *tables):
        k_ref[:, at : at + breadth] = turned.astype(BF)
    v_ref[...] = mixed[:, 2 * local :].astype(BF)


def project_self(blocks, gain, bias, down, weight, tables, rows):
    width = blocks[0].shape[1]
    tokens = len(blocks) * blocks[0].shape[0]
    local = weight.shape[1] // 4
    part = weight.columns(0, 3 * local)
    return weight_call(
        functools.partial(query_kernel, weight, part, len(blocks)),
        weight,
        (tokens // rows,),
        [whole_spec(b.shape) for b in blocks]
        + [whole_spec(gain.shape), whole_spec(bias.shape), whole_spec(down.shape)]
        + [row_spec(rows, t.shape[1]) for t in tables],
        [row_spec(rows, local)] * 3 + [row_spec(rows, down.shape[0]), row_spec(rows, width)],
        [sds((tokens, local), BF)] * 3
        + [sds((tokens, down.shape[0]), BF), sds((tokens, width), BF)],
        [pltpu.VMEM((rows, width), BF), *weight.scratch(part[1])],
        cost(8 * tokens * width * local, 8 * width * local),
        [*blocks, gain, bias, down, *tables],
    )


def attend_kernel(weight, part, places_ref, *refs):
    w_refs, refs = refs[: weight.count], refs[weight.count :]
    q_ref, k_ref, v_ref, o_ref, lse_ref, *y_refs, w_ref, sems = refs
    rows, local = q_ref.shape
    step = pl.program_id(0)

    begin, end = weight.at_first(step, w_refs, places_ref, w_ref, sems, *part[:2])
    begin()
    lanes = lax.broadcasted_iota(jnp.int32, (rows, 128), 1)
    logsums = jnp.zeros((rows, 128), F32)
    for head in range(local // HEAD_DIM):
        at = slice(head * HEAD_DIM, (head + 1) * HEAD_DIM)
        scores = dot_nt(q_ref[:, at], k_ref[:, at])
        top = jnp.max(scores, axis=1, keepdims=True)
        powers = jnp.exp(scores - top)
        total = jnp.sum(powers, axis=1, keepdims=True)
        out = dot(powers.astype(BF), v_ref[:, at]) / total
        o_ref[:, at] = out.astype(BF)
        logsums = jnp.where(lanes == head, top + jnp.log(total), logsums)
    lse_ref[...] = logsums.T[: lse_ref.shape[0]]
    end()
    y = dot_nt(o_ref[...], w_ref[:, part[2] : part[2] + local]).astype(BF)
    give_tile(y, y_refs, step)


def wide_of(weight):
    return weight.shape[-2] // LANES * LANES + LANES


def attend_self(query, keys, values, weight, rows, first, count, block):
    tokens, local = query.shape
    heads = -(-local // HEAD_DIM // 8) * 8
    part = weight.columns(3 * local, local)
    blocks = count * rows // block
    return weight_call(
        functools.partial(attend_kernel, weight, part),
        weight,
        (count,),
        [
            pl.BlockSpec((rows, local), lambda t, *_: (first + t, 0)),
            whole_spec(keys.shape),
            whole_spec(values.shape),
        ],
        [row_spec(rows, local), pl.BlockSpec((heads, rows), lambda t, *_: (0, t))]
        + [whole_spec((block, wide_of(weight)))] * blocks,
        [sds((count * rows, local), BF), sds((heads, count * rows), F32)]
        + [sds((block, wide_of(weight)), BF)] * blocks,
        weight.scratch(part[1]),
        cost(16 * count * rows * tokens * local, 8 * query.size, count * rows * tokens),
        [query, keys, values],
    )


def attend_back_kernel(weight, part, first, last, tiles, number, blocks, places_ref, *refs):
    w_refs, refs = refs[: weight.count], refs[weight.count :]
    grads, refs = refs[:number], refs[number:]
    (
        up_ref, q_ref, k_ref, v_ref, o_ref, lse_ref, cos_ref, left_ref, right_ref, low_ref,
    ), refs = refs[:10], refs[10:]
    *refs, g_ref, w_ref, sems = refs
    begin, end = weight.at_first(pl.program_id(0), w_refs, places_ref, w_ref, sems, *part[:2])
    begin()
    take_tile(grads, g_ref, pl.program_id(0))
    if not first:
        (mq_ref, gk_in, gv_in, down_in), refs = refs[:4], refs[4:]
    if last:
        (n_ref, z_ref, r_ref), refs = refs[:3], refs[3:]
        (down_ref, gup_ref, rows_ref), refs = refs[:3], refs[3:]
        dn_refs, (m_ref, gk_ref, gv_ref) = refs[:blocks], refs[blocks:]
    else:
        m_ref, gk_ref, gv_ref, down_ref = refs
    step, rows = pl.program_id(0), q_ref.shape[0]
    width, local = g_ref.shape[1], q_ref.shape[1]
    at_rows = pl.ds(pl.multiple_of((step + tiles) * rows, rows), rows)
    at_query = at_rows if last else pl.ds(pl.multiple_of(step * rows, rows), rows)

    @pl.when(step == 0)
    def _():
        if first:
            gk_ref[...] = jnp.zeros_like(gk_ref)
            gv_ref[...] = jnp.zeros_like(gv_ref)
            down_ref[...] = jnp.zeros_like(down_ref)
        else:
            gk_ref[...] = gk_in[...]
            gv_ref[...] = gv_in[...]
            down_ref[...] = down_in[...]
            m_ref[: mq_ref.shape[0], :local] = mq_ref[...]

    grad = g_ref[...]
    grad_low = dot_nt(grad, up_ref[...]).astype(BF)
    end()
    at = slice(part[2], part[2] + local)
    grad_out = dot(grad, w_ref[:width, at]) + dot(grad_low, w_ref[width:, at])
    grad_out = grad_out.astype(BF)
    out = o_ref[...]
    down_ref[...] += dot_tn(grad_low, out)
    product = grad_out.astype(F32) * out.astype(F32)
    deltas = head_sums(product)
    parts = []
    for head in range(local // HEAD_DIM):
        at = slice(head * HEAD_DIM, (head + 1) * HEAD_DIM)
        q, k, v, g = q_ref[:, at], k_ref[:, at], v_ref[:, at], grad_out[:, at]
        delta = deltas[head : head + 1]
        probs = jnp.exp(dot_nt(k, q) - lse_ref[head : head + 1, :])
        grad_scores = (probs * (dot_nt(v, g) - delta)).astype(BF)
        gv_ref[:, at] += dot(probs.astype(BF), g)
        gk_ref[:, at] += dot(grad_scores, q)
        parts.append(dot_tn(grad_scores, k) * HEAD_DIM**-0.5)
    tables = cos_ref[at_rows, :], -left_ref[at_rows, :], -right_ref[at_rows, :]
    for at, breadth, turned in turn(jnp.concatenate(parts, axis=1), *tables):
        m_ref[at_query, at : at + breadth] = turned.astype(BF)

    if last:

        @pl.when(step == pl.num_programs(0) - 1)
        def _():
            tables = cos_ref[...], -left_ref[...], -right_ref[...]
            for at, breadth, turned in turn(gk_ref[...], *tables):
                m_ref[:, local + at : local + at + breadth] = turned.astype(BF)
            m_ref[:, 2 * local :] = gv_ref[...].astype(BF)
            gup_ref[...] = dot_tn(low_ref[...], m_ref[...])
            rank, block = up_ref.shape[0], dn_refs[0].shape[0]
            down = 0.0
            for i, ref in enumerate(dn_refs):
                at = slice(i * block, (i + 1) * block)
                value = dot_nt(m_ref[at, :], w_ref[:, : 3 * local]).astype(BF)
                ref[:, : width + rank] = value
                ref[:, width + rank :] = jnp.zeros((block, ref.shape[1] - width - rank), BF)
                down = down + dot_tn(value[:, width:], n_ref[at, :])
            by_piece(rows_ref, 0, down)
            by_piece(rows_ref, rank, dot_tn(z_ref[...], r_ref[...]))


def attend_back(
    grads, up, weight, query, keys, values, out, lse, tables, low, rows, start, before, ends
):
    tokens, local = query.shape
    block, width = grads[0].shape
    rank = up.shape[0]
    count = len(grads) * block // rows
    first, last = before is None, ends is not None
    before = () if first else before
    ends = ends if last else ()
    sums = [sds((tokens, local), F32)] * 2 + [sds((rank, local), F32)]
    blocks = tokens // block if last else 0
    if last:
        members = width // local
        shapes = [sums[2], sds((rank, 3 * local), F32), sds((members, 2 * rank, local), BF)]
        shapes += [sds((block, wide_of(weight)), BF)] * blocks
        scratch = [pltpu.VMEM((tokens, 3 * local), BF)]
        scratch += [pltpu.VMEM((tokens, local), F32)] * 2
        part = 0, 4 * local, 3 * local
    else:
        shapes, scratch = [sds((count * rows, local), BF), *sums], []
        part = weight.columns(3 * local, local)
    scratch.append(pltpu.VMEM((rows, width), BF))

    def tile(columns):
        return pl.BlockSpec((rows, columns), lambda t, *_: (start + t, 0))

    return weight_call(
        functools.partial(attend_back_kernel, weight, part, first, last, start, len(grads), blocks),
        weight,
        (count,),
        [
            *[whole_spec(g.shape) for g in grads],
            whole_spec(up.shape),
            tile(local),
            whole_spec(keys.shape),
            whole_spec(values.shape),
            row_spec(rows, local),
            pl.BlockSpec((lse.shape[0], rows), lambda t, *_: (0, t)),
            *[whole_spec(t.shape) for t in tables],
            whole_spec(low.shape),
            *[whole_spec(b.shape) for b in before],
            *[whole_spec(e.shape) for e in ends],
        ],
        [whole_spec(s.shape) for s in shapes],
        shapes,
        scratch + weight.scratch(part[1]),
        cost(40 * count * rows * tokens * local, 10 * query.size, count * rows * tokens),
        [*grads, up, query, keys, values, out, lse, *tables, low, *before, *ends],
    )


def in_order(swap, first, second):
    keep = swap == 0
    return jnp.where(keep, first, second), jnp.where(keep, second, first)


def cross_kernel(weight, members, local, core_at, places_ref, *refs):
    w_refs, refs = refs[: weight.count], refs[weight.count :]
    *refs, w_ref, sems = refs
    copies = weight.bring(w_refs, places_ref, w_ref, sems)
    (x_ref, up_self_ref, up_cross_ref, down_ref, gain_ref, bias_ref), refs = refs[:6], refs[6:]
    kv_refs, refs = refs[:members], refs[members:]
    y_refs, refs = refs[:-10], refs[-10:]
    branch = total_of(y_refs)
    s1_ref, s2_ref, n2_ref, n3_ref, q_ref, o_ref, lse_ref, z2_ref, u_ref, z4_ref = refs
    rows, width = x_ref.shape
    rank = down_ref.shape[0]
    deep = slice(width, width + rank)
    low = branch[:, deep].astype(BF)
    z2_ref[...] = low
    stream = x_ref[...].astype(F32) + branch[:, :width] + dot(low, up_self_ref[...])
    s1_ref[...] = stream
    normed = layer_norm(stream, gain_ref[1:2, :], bias_ref[1:2, :])
    n2_ref[...] = normed
    low = dot_nt(normed, down_ref[...]).astype(BF)
    u_ref[...] = low
    total = jnp.zeros((rows, width + rank), F32)
    wait_for(copies)
    both = 2 * local
    for n in range(members // 2):
        query = dot(normed, w_ref[n, :width, :both]) + dot(low, w_ref[n, deep, :both])
        query = (query * HEAD_DIM**-0.5).astype(BF)
        q_ref[:, n * both : (n + 1) * both] = query
        found = in_order(places_ref[core_at], kv_refs[2 * n][...], kv_refs[2 * n + 1][...])
        parts, logsums = [], []
        for head in range(both // HEAD_DIM):
            keyval, own = found[head * HEAD_DIM // local], head * HEAD_DIM % local
            keys = keyval[:, own : own + HEAD_DIM]
            values = keyval[:, local + own : local + own + HEAD_DIM]
            scores = dot_nt(keys, query[:, head * HEAD_DIM : (head + 1) * HEAD_DIM])
            top = jnp.max(scores, axis=0, keepdims=True)
            powers = jnp.exp(scores - top)
            sums = jnp.sum(powers, axis=0, keepdims=True)
            parts.append(dot_tn(values, powers.astype(BF)) / sums)
            logsums.append(top + jnp.log(sums))
        out = jnp.concatenate(parts, axis=0).T.astype(BF)
        o_ref[:, n * both : (n + 1) * both] = out
        lse_ref[n] = jnp.concatenate(logsums, axis=0)
        total = total + dot_nt(out, w_ref[n, :, both:])
    low = total[:, deep].astype(BF)
    z4_ref[...] = low
    stream = stream + total[:, :width] + dot(low, up_cross_ref[...])
    s2_ref[...] = stream
    n3_ref[...] = layer_norm(stream, gain_ref[2:3, :], bias_ref[2:3, :])


def cross_forward(x, ys, up_self, up_cross, down, gains, biases, weight, keyvals, core_at):
    rows, width = x.shape
    members, local = len(keyvals), weight.shape[2] // 4
    plain, wide = sds((rows, width), BF), sds((rows, width), F32)
    low = sds((rows, down.shape[0]), BF)
    logsums = sds((members // 2, 2 * local // HEAD_DIM, rows), F32)
    shapes = [wide, wide, plain, plain, plain, plain, logsums, low, low, low]
    arrays = [x, up_self, up_cross, down, gains, biases, *keyvals, *ys]
    return weight_call(
        functools.partial(cross_kernel, weight, members, local, core_at),
        weight,
        (1,),
        [whole_spec(a.shape) for a in arrays],
        [whole_spec(o.shape) for o in shapes],
        shapes,
        weight.scratch(),
        cost(24 * rows * width * width, 8 * width * width),
        arrays,
    )


def cross_back_kernel(weight, members, local, core_at, places_ref, *refs):
    w_refs, refs = refs[: weight.count], refs[weight.count :]
    *refs, w_ref, sems = refs
    copies = weight.bring(w_refs, places_ref, w_ref, sems)
    (
        g_ref, s1_ref, s2_ref, n2_ref, q_ref, o_ref, lse_ref, u_ref, z4_ref,
        up_ref, down5_ref, down2_ref, gain_ref, bias_ref,
    ), refs = refs[:14], refs[14:]
    kv_refs, refs = refs[:members], refs[members:]
    dn_refs, (r1_ref, r1b_ref, fixed_ref, near_ref, *gkv_refs) = (
        refs[: -4 - members],
        refs[-4 - members :],
    )
    summed = total_of(dn_refs)
    width = g_ref.shape[1]
    rank = up_ref.shape[0]
    deep = slice(width, width + rank)
    stream = s2_ref[...]
    low = summed[:, deep].astype(BF)
    grad_normed = summed[:, :width] + dot(low, down5_ref[...])
    normed = layer_norm(stream, gain_ref[2:3, :], bias_ref[2:3, :])
    by_piece(fixed_ref, rank, dot_tn(low, normed))
    grad = g_ref[...].astype(F32) + norm_backward(stream, gain_ref[2:3, :], grad_normed)
    branch = grad.astype(BF)
    low = dot_nt(branch, up_ref[...]).astype(BF)
    by_piece(fixed_ref, 2 * rank, dot_tn(z4_ref[...], branch))
    by_piece(near_ref, 0, dot_tn(low, o_ref[...]))
    total = jnp.zeros((g_ref.shape[0], width + rank), F32)
    wait_for(copies)
    both, swap = 2 * local, places_ref[core_at]
    for n in range(members // 2):
        columns = slice(n * both, (n + 1) * both)
        grad_out = dot(branch, w_ref[n, :width, both:]) + dot(low, w_ref[n, deep, both:])
        grad_out = grad_out.astype(BF)
        query = q_ref[:, columns]
        deltas = head_sums(grad_out.astype(F32) * o_ref[:, columns].astype(F32))
        found = in_order(swap, kv_refs[2 * n][...], kv_refs[2 * n + 1][...])
        queries, keys, values = [], [], []
        for head in range(both // HEAD_DIM):
            keyval, own = found[head * HEAD_DIM // local], head * HEAD_DIM % local
            key = keyval[:, own : own + HEAD_DIM]
            value = keyval[:, local + own : local + own + HEAD_DIM]
            at = slice(head * HEAD_DIM, (head + 1) * HEAD_DIM)
            q, g = query[:, at], grad_out[:, at]
            probs = jnp.exp(dot_nt(key, q) - lse_ref[n, head : head + 1, :])
            grad_scores = (probs * (dot_nt(value, g) - deltas[head : head + 1])).astype(BF)
            queries.append(dot_tn(key, grad_scores))
            keys.append(dot(grad_scores, q))
            values.append(dot(probs.astype(BF), g))
        grad_query = (jnp.concatenate(queries, axis=0).T * HEAD_DIM**-0.5).astype(BF)
        half = len(keys) // 2
        first = jnp.concatenate(keys[:half] + values[:half], axis=1).astype(BF)
        second = jnp.concatenate(keys[half:] + values[half:], axis=1).astype(BF)
        gkv_refs[2 * n][...], gkv_refs[2 * n + 1][...] = in_order(swap, first, second)
        ups = dot_tn(u_ref[...], grad_query).astype(BF)
        near_ref[2 * n, rank:, :] = ups[:, :local]
        near_ref[2 * n + 1, rank:, :] = ups[:, local:]
        total = total + dot_nt(grad_query, w_ref[n, :, :both])
    low = total[:, deep].astype(BF)
    by_piece(fixed_ref, 0, dot_tn(low, n2_ref[...]))
    grad_normed = total[:, :width] + dot(low, down2_ref[...])
    grad = grad + norm_backward(s1_ref[...], gain_ref[1:2, :], grad_normed)
    r1_ref[...] = grad
    r1b_ref[...] = grad.astype(BF)


def cross_back(
    g, dns, s1, s2, n2, q, o, lse, u, z4, up, down5, down2, gains, biases, weight, keyvals, core_at
):
    rows, width = g.shape
    rank = up.shape[0]
    members, local = len(keyvals), weight.shape[2] // 4
    shapes = [sds((rows, width), F32), sds((rows, width), BF)]
    shapes += [sds((members, n * rank, local), BF) for n in (3, 2)]
    shapes += [sds(keyvals[0].shape, BF)] * members
    arrays = [g, s1, s2, n2, q, o, lse, u, z4, up, down5, down2, gains, biases, *keyvals, *dns]
    return weight_call(
        functools.partial(cross_back_kernel, weight, members, local, core_at),
        weight,
        (1,),
        [whole_spec(a.shape) for a in arrays],
        [whole_spec(o.shape) for o in shapes],
        shapes,
        weight.scratch(),
        cost(32 * rows * width * width, 8 * width * width),
        arrays,
    )


def output_kernel(s2_ref, up_ref, g_ref, *refs):
    *y_refs, out_ref, gup_ref = refs
    width, rank = out_ref.shape[1], up_ref.shape[0]
    total = total_of(y_refs)
    low = total[:, width : width + rank].astype(BF)
    out_ref[...] = (s2_ref[...] + total[:, :width] + dot(low, up_ref[...])).astype(BF)
    by_piece(gup_ref, 0, dot_tn(low, g_ref[...]))


def output_end(s2, ys, up, g, members):
    rank, width = up.shape
    return pl.pallas_call(
        output_kernel,
        out_shape=[sds(g.shape, BF), sds((members, rank, width // members), BF)],
        compiler_params=pltpu.CompilerParams(vmem_limit_bytes=VMEM_LIMIT),
        cost_estimate=cost(0, 0),
    )(s2, up, g, *ys)


def input_kernel(x_ref, r_ref, down_ref, gain_ref, *refs):
    *dn_refs, out_ref = refs
    width, rank = out_ref.shape[1], down_ref.shape[0]
    total = total_of(dn_refs)
    low = total[:, width : width + rank].astype(BF)
    grad = total[:, :width] + dot(low, down_ref[...])
    back = norm_backward(x_ref[...].astype(F32), gain_ref[...], grad)
    out_ref[...] = (r_ref[...] + back).astype(BF)


def input_end(x, r1, dns, down, gain):
    return pl.pallas_call(
        input_kernel,
        out_shape=sds(x.shape, BF),
        compiler_params=pltpu.CompilerParams(vmem_limit_bytes=VMEM_LIMIT),
        cost_estimate=cost(0, 0),
    )(x, r1, down, gain, *dns)


def context_kernel(weight, members, at_pieces, places_ref, *refs):
    w_refs, refs = refs[: weight.count], refs[weight.count :]
    blocks, (down_ref, kv_ref, low_ref, w_ref, sems) = refs[:members], refs[members:]
    wait_for(weight.bring(w_refs, places_ref, w_ref, sems))
    rank, local = down_ref.shape[1], blocks[0].shape[1]
    width = members * local
    low, keyval = 0.0, 0.0
    for k in range(members):
        at = pl.ds(pl.multiple_of(places_ref[at_pieces + k], local), local)
        low = low + dot(blocks[k][...], down_ref[at, :])
        keyval = keyval + dot(blocks[k][...], w_ref[at, :])
    low = low.astype(BF)
    low_ref[...] = low
    kv_ref[...] = (keyval + dot(low, w_ref[width : width + rank, :])).astype(BF)


def context_forward(at_pieces, blocks, weight, down):
    count = blocks[0].shape[0]
    arrays = (*blocks, down)
    shapes = [sds((count, weight.shape[1]), BF), sds((count, down.shape[1]), BF)]
    return weight_call(
        functools.partial(context_kernel, weight, len(blocks), at_pieces),
        weight,
        (1,),
        [whole_spec(a.shape) for a in arrays],
        [whole_spec(s.shape) for s in shapes],
        shapes,
        weight.scratch(),
        cost(0, 0),
        arrays,
    )


def context_back_kernel(weight, members, at_pieces, places_ref, *refs):
    w_refs, refs = refs[: weight.count], refs[weight.count :]
    blocks, (down_ref, low_ref, g_ref), refs = (
        refs[:members],
        refs[members : members + 3],
        refs[members + 3 :],
    )
    gup_ref, *refs, w_ref, sems = refs
    wait_for(weight.bring(w_refs, places_ref, w_ref, sems))
    rank, local = down_ref.shape[1], blocks[0].shape[1]
    width = members * local
    grad = g_ref[...]
    low = dot_nt(grad, w_ref[width : width + rank, :]).astype(BF)
    gup_ref[...] = dot_tn(low_ref[...], grad)
    for k in range(members):
        at = pl.ds(pl.multiple_of(places_ref[at_pieces + k], local), local)
        out = dot_nt(grad, w_ref[at, :]) + dot_nt(low, down_ref[at, :])
        refs[k][...] = out.astype(BF)
        refs[members + k][...] = dot_tn(low, blocks[k][...]).astype(BF)


def context_back(at_pieces, blocks, weight, down, low, grad):
    count, local = blocks[0].shape
    rank, members = down.shape[1], len(blocks)
    arrays = (*blocks, down, low, grad)
    shapes = (
        [sds((rank, weight.shape[1]), F32)]
        + [sds((count, local), BF)] * members
        + [sds((rank, local), BF)] * members
    )
    return weight_call(
        functools.partial(context_back_kernel, weight, members, at_pieces),
        weight,
        (1,),
        [whole_spec(a.shape) for a in arrays],
        [whole_spec(s.shape) for s in shapes],
        shapes,
        weight.scratch(),
        cost(10**10, 10**6),
        arrays,
    )


def table_kernel(cos_ref, sin_ref, out_cos_ref, out_left_ref, out_right_ref):
    half, breadth = ROT // 2, 2 * HEAD_DIM
    lane = lax.broadcasted_iota(jnp.int32, (half, breadth), 1)
    row = lax.broadcasted_iota(jnp.int32, (half, breadth), 0)
    within = lane % HEAD_DIM
    first = jnp.where(within == row, 1.0, 0.0)
    second = jnp.where(within == row + half, 1.0, 0.0)

    def spread(ref, pattern):
        return lax.dot_general(
            ref[...], pattern, (((0,), (0,)), ((), ())),
            precision=lax.Precision.HIGHEST, preferred_element_type=F32,
        )

    lanes = lax.broadcasted_iota(jnp.int32, out_cos_ref.shape, 1) % HEAD_DIM
    out_cos_ref[...] = jnp.where(lanes < ROT, spread(cos_ref, first + second), 1.0)
    out_left_ref[...] = -spread(sin_ref, first)
    out_right_ref[...] = spread(sin_ref, second)


def rotary_tables(cosines, sines):
    tokens = cosines.shape[1]
    return pl.pallas_call(
        table_kernel,
        out_shape=[sds((tokens, 2 * HEAD_DIM), F32)] * 3,
        compiler_params=pltpu.CompilerParams(vmem_limit_bytes=VMEM_LIMIT),
        cost_estimate=cost(0, 0),
    )(cosines, sines)


def feed_kernel(weight, first, last, number, tile, places_ref, *refs):
    w_refs, refs = refs[: weight.count], refs[weight.count :]
    n_refs, g_refs, (down_ref, up_ref), refs = (
        refs[:number],
        refs[number : 2 * number],
        refs[2 * number : 2 * number + 2],
        refs[2 * number + 2 :],
    )
    if not first:
        (low_in, glow_in, y_in, dn_in), refs = refs[:4], refs[4:]
    *refs, gdown_ref, ggate_ref, gupper_ref, n_ref, g_ref, block_sems, w_ref, sems = refs
    step, width = pl.program_id(0), n_ref.shape[1]
    rank, part = gdown_ref.shape
    block = n_refs[0].shape[0]

    @pl.when(step == 0)
    def _():
        copies = weight.bring(w_refs, places_ref, w_ref, sems)
        for i, ref in enumerate([*n_refs, *g_refs]):
            to = (n_ref, g_ref)[i // number].at[pl.ds(i % number * block, block)]
            copies.append(pltpu.make_async_copy(ref, to, block_sems.at[i]))
            copies[-1].start()
        wait_for(copies)
        for ref in (gdown_ref, ggate_ref, gupper_ref):
            ref[...] = jnp.zeros_like(ref)

    at_tile = pl.ds(pl.multiple_of(step * tile, tile), tile)
    normed, grad = n_ref[at_tile, :], g_ref[at_tile, :]
    if first:
        low = dot_nt(normed, down_ref[...]).astype(BF)
        grad_low = dot_nt(grad, up_ref[...]).astype(BF)
        refs[2][...] = low
        refs[3][...] = grad_low
    else:
        low, grad_low = low_in[...], glow_in[...]
    deep = slice(width, width + rank)
    both = dot(normed, w_ref[:width, : 2 * part]) + dot(low, w_ref[deep, : 2 * part])
    gate, upper = both[:, :part], both[:, part:]
    grad_unit = dot(grad, w_ref[:width, 2 * part :]) + dot(grad_low, w_ref[deep, 2 * part :])
    sigmoid = 1.0 / (1.0 + jnp.exp(-gate))
    acted = gate * sigmoid
    unit = (acted * upper).astype(BF)
    grad_gate = (grad_unit * upper * (sigmoid + acted * (1.0 - sigmoid))).astype(BF)
    grad_upper = (grad_unit * acted).astype(BF)
    y = dot_nt(unit, w_ref[:, 2 * part :])
    dn = dot_nt(grad_gate, w_ref[:, :part]) + dot_nt(grad_upper, w_ref[:, part : 2 * part])
    if not first:
        y, dn = y + y_in[...].astype(F32), dn + dn_in[...].astype(F32)
    if last:
        give_tile(y.astype(BF), refs[:number], step)
        give_tile(dn.astype(BF), refs[number:], step)
    else:
        refs[0][...] = y.astype(BF)
        refs[1][...] = dn.astype(BF)
    gdown_ref[...] += dot_tn(grad_low, unit)
    ggate_ref[...] += dot_tn(low, grad_gate)
    gupper_ref[...] += dot_tn(low, grad_upper)


def feed(normed, grads, down, up, weight, sums, rows, start, last):
    block, width = normed[0].shape
    rank, number = down.shape[0], len(normed)
    deep, part = weight.shape[0], weight.shape[1] // 3
    narrow = sds((rank, part), F32)
    tokens = number * block
    if last:
        wide = sds((block, deep // LANES * LANES + LANES), BF)
        shapes, specs = [wide] * (2 * number), [whole_spec(wide.shape)] * (2 * number)
    else:
        shapes, specs = [sds((tokens, deep), BF)] * 2, [row_spec(rows, deep)] * 2
    first = not sums
    if first:
        shapes, specs = shapes + [sds((tokens, rank), BF)] * 2, specs + [row_spec(rows, rank)] * 2
    arrays = (*normed, *grads, down, up)
    size = weight.shape[0] * weight.shape[1]
    return weight_call(
        functools.partial(feed_kernel, weight, first, last, number, rows),
        weight,
        (tokens // rows,),
        [pl.BlockSpec(memory_space=pl.ANY)] * (2 * number)
        + [whole_spec(down.shape), whole_spec(up.shape)]
        + [pl.BlockSpec((rows, a.shape[1]), lambda t, *_: (start + t, 0)) for a in sums],
        specs + [whole_spec(narrow.shape)] * 3,
        shapes + [narrow] * 3,
        [pltpu.VMEM((tokens, width), BF)] * 2
        + [pltpu.SemaphoreType.DMA((2 * number,))]
        + weight.scratch(),
        cost(8 * tokens * size, 2 * size),
        [*arrays, *sums],
    )


STEP_SLOTS = 4


def each_slot(labels_ref, in_refs):
    for j in range(STEP_SLOTS):
        slot = pl.program_id(0) * STEP_SLOTS + j
        for n, ref in enumerate(in_refs):
            for s in range(ref.shape[0]):
                yield j, labels_ref[n * ref.shape[0] + s] == slot, ref.at[s]


def settle_first_kernel(fold, labels_ref, *refs):
    *in_refs, down_ref, hid_ref, gate_ref = refs
    local = down_ref.shape[-1]
    for ref in (down_ref, hid_ref, gate_ref):
        ref[...] = jnp.zeros_like(ref)
    for j, here, found in each_slot(labels_ref, in_refs):

        @pl.when(here)
        def _(j=j, found=found):
            for n, k in enumerate(DOWN_FIRST):
                down_ref[j, k] += found[n].astype(F32)
            for k in range(fold):
                at, n = slice(k * local, (k + 1) * local), len(DOWN_FIRST) + k
                hid_ref[j, :, at] += found[n].astype(F32)
                gate_ref[j, 0, :, at] += found[n + fold].astype(F32)
                gate_ref[j, 1, :, at] += found[n + 2 * fold].astype(F32)


def settle_second_kernel(labels_ref, *refs):
    *in_refs, _, down_ref, up_ref = refs
    downs, ups = down_ref.shape[1], up_ref.shape[1]
    for ref in (down_ref, up_ref):
        ref[...] = jnp.zeros_like(ref)
    for j, here, found in each_slot(labels_ref, in_refs):

        @pl.when(here)
        def _(j=j, found=found):
            down_ref[j] += found[:downs].astype(F32)
            up_ref[j] += found[downs : downs + ups].astype(F32)


DOWN_FIRST = (4, 5)


def slot_spec(shape):
    block = (STEP_SLOTS,) + shape[1:]
    return pl.BlockSpec(block, lambda i, *_, n=len(shape): (i,) + (0,) * (n - 1))


def settle_call(kernel, labels, grads, before, shapes, blocks, aliases):
    slots = shapes[0][0]
    return pl.pallas_call(
        kernel,
        grid_spec=pltpu.PrefetchScalarGridSpec(
            num_scalar_prefetch=1,
            grid=(slots // STEP_SLOTS,),
            in_specs=[whole_spec(g.shape) for g in grads]
            + [pl.BlockSpec(memory_space=pl.ANY) for _ in before],
            out_specs=[slot_spec(b) for b in blocks],
        ),
        out_shape=[sds(s, F32) for s in shapes],
        input_output_aliases=aliases,
        compiler_params=params(),
        cost_estimate=cost(0, 0),
    )(labels, *grads, *before)


def settle_first(labels, grads, slots, fold):
    rank, local = grads[0].shape[2:]
    hidden = fold * local
    shapes = [(slots, 6, rank, local), (slots, rank, hidden), (slots, 2, rank, hidden)]
    kernel = functools.partial(settle_first_kernel, fold)
    return settle_call(kernel, labels, grads, [], shapes, shapes, {})


def settle_second(labels, grads, down):
    up = down.shape[:1] + (9,) + down.shape[2:]
    part = (down.shape[0], DOWN_FIRST[0]) + down.shape[2:]
    aliases = {1 + len(grads): 0}
    return settle_call(
        settle_second_kernel, labels, grads, [down], [down.shape, up], [part, up], aliases
    )


def chunks(hidden):
    return 2 * hidden // 3, hidden // 3


def body(
    inputs,
    context,
    positions,
    adapter_index,
    self_in_weight,
    self_out_weight,
    cross_query_weight,
    cross_keyval_weight,
    cross_out_weight,
    feed_in_weight,
    feed_out_weight,
    norm_gains,
    norm_biases,
    adapter_down,
    adapter_down_hidden,
    adapter_up,
    adapter_up_hidden,
    out_cotangent,
    *,
    pairs,
    chips,
):
    group = Group(pairs, chips)
    members = 2 * pairs
    rows, width = inputs.shape[1], inputs.shape[2]
    block = self_in_weight.shape[0]
    local = self_in_weight.shape[2]
    hidden = feed_in_weight.shape[2]
    slots, rank = adapter_down.shape[0], adapter_down.shape[3]
    deep = width + rank
    parts = chunks(hidden)
    fold = hidden // local
    pieces = group.pieces
    gains, biases = norm_gains, norm_biases
    tile = min(256, members * rows)
    tiles = members * rows // tile
    near_tiles = tiles // pairs

    def packed(*parts):
        return jnp.concatenate(parts, axis=1)

    def stacked(*parts):
        return jnp.concatenate(parts, axis=0)

    def listed(values):
        return list(values) if isinstance(values, (list, tuple)) else [values]

    def piece(array, k, size):
        return lax.dynamic_slice_in_dim(array, pieces[k] * size, size, array.ndim - 1)

    def own(array):
        return piece(array, 0, local)

    near_chips = [1, 2] if chips == 4 else list(range(1, chips))
    chip_rows = [(group.chip ^ k) * 2 * block for k in range(chips)]
    one = [[c + o * block for c in chip_rows] for o in (group.core, 1 - group.core)]
    one += [[c + o * block for c in chip_rows] for o in (group.zhi, 1 - group.zhi)]
    row_places = jnp.stack(
        [r for found in one for r in found] + [jnp.zeros_like(group.core)]
        + [p * local for p in pieces] + [group.core]
    ).astype(jnp.int32)
    mine_at, other_at, first_at, second_at, zero = (n * chips for n in range(5))
    at_pieces = zero + 1
    core_at = at_pieces + members

    def chip_weight(own_entry, near, rest, low, columns, halves):
        weight = Weight((deep, columns), row_places)
        entries = [own_entry, *near]
        for k, (array, row) in zip([0, *near_chips], entries):
            weight.add(
                array,
                *[(row + r, block, c, columns, None, at + k, 0) for r, c, at in halves],
            )
        if rest:
            side_by_side = halves[1][0] == 0
            for n, (array, row) in enumerate(rest):
                size = block // 2 if side_by_side else block
                picked = halves if side_by_side else halves[n : n + 1]
                weight.add(
                    array,
                    *[
                        (row, size, c, columns, None, at + 3, n * size if side_by_side else 0)
                        for _, c, at in picked
                    ],
                )
        weight.add(low, (0, rank, 0, columns, None, zero, width))
        return weight

    stacked_halves = [(0, 0, first_at), (block, 0, second_at)]
    packed_halves = [(0, 0, mine_at), (0, 2 * local, other_at)]

    def spread(got, half_at, half, own_block):
        if got and chips == 4:
            turns = [
                got[1][half_at : half_at + half],
                got[0][half_at + half : half_at + 2 * half],
            ]
            if own_block is not None:
                turns = listed(step.mark(*[stacked(turn, own_block) for turn in turns]))
            return [xor_move(turn, "chip", 4, k) for turn, k in zip(turns, near_chips)]
        if own_block is None:
            return []
        return [xor_move(own_block, "chip", chips, k) for k in near_chips]

    def skip(half):
        return half if chips == 4 else 0

    def flat(*groups):
        return [x for g in groups for x in listed(g)]

    def wait_all(*groups):
        groups = [listed(g) for g in groups]
        values = iter(listed(step.wait(*flat(*groups))))
        return [[next(values) for _ in g] for g in groups]

    def swap_all(blocks):
        if not blocks:
            return []
        blocks = listed(step.wait(*blocks))
        return listed(step.wait(*[core_swap(b) for b in blocks]))

    shard_self = packed(*[self_in_weight[:, i] for i in range(3)], self_out_weight.T)
    step = Order(shard_self[:8, :128])
    self_from = [home_swap(shard_self), turned(shard_self)]
    stream_own, context_own = home_swap(inputs[0]), home_swap(context[0])
    index, positions = step.wait(adapter_index, positions)
    index_other, positions_other = step.wait(core_swap(index), core_swap(positions))
    index = jnp.where(group.home, index, index_other)[0]
    positions = jnp.where(group.home, positions, positions_other)[0]
    down = lax.dynamic_index_in_dim(adapter_down.transpose(0, 1, 3, 2), index, 0, keepdims=False)
    up = lax.dynamic_index_in_dim(adapter_up.transpose(0, 2, 1, 3), index, 0, keepdims=False)
    down, up = step.mark(down, up)
    low_self = packed(*[own(up[i]) for i in range(3)], own(down[1]))
    low_keyval = packed(own(up[5]), own(up[6]))
    low_cross = []
    for k in range(pairs):
        two = [
            (group.p ^ k) * local + core * pairs * local for core in (0, 1)
        ]
        low_cross.append(
            packed(
                *[
                    lax.dynamic_slice_in_dim(table[4], where, local, 1)
                    for table in (up, down)
                    for where in two
                ]
            )
        )
    low_cross = stacked(*low_cross)
    low_self, low_keyval, low_cross = step.mark(low_self, low_keyval, low_cross)
    keyval_parts = step.wait(cross_keyval_weight)
    keyval_parts = step.mark(keyval_parts[:, 0], keyval_parts[:, 1])
    shard_cross = step.mark(packed(cross_query_weight, cross_out_weight.T, *keyval_parts))
    far_cross = group.cross(shard_cross)
    blocks_at = [
        lax.dynamic_slice_in_dim(positions, pieces[k] * rows, rows, 0) for k in range(members)
    ]
    half = ROT // 2
    inverse = 10000.0 ** (-jnp.arange(half, dtype=F32) / half)
    angles = inverse[:, None] * step.wait(jnp.concatenate(blocks_at)).astype(F32)[None]
    tables = step.mark(*rotary_tables(*step.mark(jnp.cos(angles), jnp.sin(angles))))
    feed_in, feed_out = step.wait(feed_in_weight, feed_out_weight)
    gate_rows, upper_rows = step.mark(feed_in[:, 0], feed_in[:, 1])
    at = [sum(parts[:i]) for i in range(len(parts))]

    def feed_shard(i):
        to = slice(at[i], at[i] + parts[i])
        gate, upper, out = step.wait(gate_rows, upper_rows, feed_out)
        return step.mark(packed(gate[:, to], upper[:, to], out.T[:, to]))

    shard_feed = [feed_shard(i) for i in range(len(parts))]

    self_from = step.wait(*self_from)
    ready_self = step.mark(stacked(*self_from))
    near_self = spread([], 0, 0, ready_self)
    stream_own, context_own = step.wait(stream_own, context_own)
    stream_far, context_far = group.far_p(stream_own), group.far_p(context_own)
    (near_self,) = wait_all(near_self)
    rest_self = spread(near_self, 0, block, None)
    rest_self, stream_far, context_far, (far_cross,) = wait_all(
        rest_self, stream_far, context_far, [far_cross]
    )
    stream_other, context_other, *found = swap_all(
        [stream_own, context_own, *stream_far, *context_far]
    )
    stream_far_other, swapped = found[: pairs - 1], found[pairs - 1 :]
    context_blocks = [context_own, context_other]
    for far, far_other in zip(context_far, swapped):
        context_blocks += [far, far_other]
    stream = [stream_own, stream_other]
    for far, far_other in zip(stream_far, stream_far_other):
        stream += [far, far_other]
    self_weight = chip_weight(
        (ready_self, 0), [(g, 0) for g in near_self], [(g, 0) for g in rest_self], low_self,
        4 * local, stacked_halves,
    )

    mine = jnp.where(group.home, shard_cross, far_cross)
    given = jnp.where(group.home, far_cross, shard_cross)
    keyval_mine, keyval_give = mine[:, 2 * local :], given[:, 2 * local :]
    low_zhi = jnp.where(group.zhi == 0, shard_cross, far_cross)
    high_zhi = jnp.where(group.zhi == 0, far_cross, shard_cross)
    pair = packed(
        *[two[:, n * local : (n + 1) * local] for n in (0, 1) for two in (low_zhi, high_zhi)]
    )
    keyval_mine, keyval_give, pair = step.mark(keyval_mine, keyval_give, pair)
    (keyval_other,) = swap_all([keyval_give])
    ready_keyval = step.mark(stacked(packed(keyval_mine, keyval_other), pair))

    got_one = spread([], 0, 0, ready_keyval)
    pair_far = group.far_p(pair)
    half_columns = shard_feed[0].shape[1] // 2
    halves = step.wait(shard_feed[0][:, :half_columns], shard_feed[0][:, half_columns:])
    feed_one = [home_swap(halves[0]), turned(halves[0])]
    query, keys, values, low_one, normed_one = project_self(
        listed(step.wait(*stream)), gains[0:1], biases[0:1], down[0], self_weight, tables, tile
    )
    query, keys, values = step.mark(query, keys, values)
    heads_far, logsum_far, *y_far = attend_self(
        query, keys, values, self_weight, tile, near_tiles, tiles - near_tiles, rows
    )
    y_far = listed(step.mark(*y_far))

    def far_sums(*groups):
        others = iter(swap_all([g[2 * k + 1] for g in groups for k in range(pairs - 1)]))
        sums = [
            [group.near_sums(g[2 * k], next(others)).astype(BF) for k in range(pairs - 1)]
            for g in groups
        ]
        values = iter(listed(step.mark(*flat(*sums))))
        return [[next(values) for _ in s] for s in sums]

    def move_p(sums):
        return [xor_move(s, "p", pairs, k + 1) for k, s in enumerate(sums)]

    def sum_up(blocks, other, far):
        total = group.near_sums(blocks[0], other)
        for f in far:
            total = total + f.astype(F32)
        return step.mark(total)

    got_one, pair_far, feed_one = wait_all(got_one, pair_far, feed_one)
    (y_sums,) = far_sums(y_far)

    far = move_p(y_sums)
    quarter = block // 2
    if chips == 4:
        turns = [
            stacked(got[start : start + quarter], got[start + block : start + block + quarter], pair_far[0])
            for got, start in ((got_one[1], 0), (got_one[0], quarter))
        ]
        turns = step.mark(*turns)
        got_two = [xor_move(turn, "chip", 4, k) for turn, k in zip(turns, near_chips)]
    else:
        got_two = flat(*[spread([], 0, 0, p) for p in pair_far])
    feed_two = [home_swap(halves[1]), turned(halves[1])]
    heads_near, logsum_near, *y_rows = attend_self(
        step.wait(query), keys, values, self_weight, tile, 0, near_tiles, rows
    )
    y_rows = listed(step.mark(*y_rows))
    (got_two,) = wait_all(got_two)
    keyval_weight = chip_weight(
        (ready_keyval, 0), [(g, 0) for g in got_one],
        [(g, 0) for g in got_two] if chips == 4 else [], low_keyval, 2 * local, packed_halves,
    )
    down_context = step.mark(down[3].T)
    keyval, low_context = context_forward(at_pieces, context_blocks, keyval_weight, down_context)
    keyval = step.mark(keyval)

    far, feed_two = wait_all(far, feed_two)
    (y_other,) = swap_all([y_rows[1]])
    branch = [y_rows[0], y_other, *far]
    keyval_far = group.far_p(keyval)
    ready_feed = [step.mark(stacked(*[packed(*two) for two in zip(feed_one, feed_two)]))]
    found = [(ready_keyval, block, block, 0, 0, 0)]
    found += [(g, block, block, k, 0, 0) for g, k in zip(got_one, near_chips)]
    if chips == 4:
        turns = [got_two[1][block : block + quarter], got_two[0][block + quarter :]]
        got_three = [xor_move(turn, "chip", 4, k) for turn, k in zip(turns, near_chips)]
        keyval_far, got_three = wait_all(keyval_far, got_three)
        found += [(g, 0, quarter, 3, n * quarter, 1) for n, g in enumerate(got_three)]
        found.append((pair_far[0], 0, block, 0, 0, 1))
        for n, (g, k) in enumerate(zip(got_two, near_chips)):
            found += [(g, block, block, k, 0, 1), (g, quarter, quarter, 3, n * quarter, 0)]
    else:
        (keyval_far,) = wait_all(keyval_far)
        count = len(near_chips)
        for n, p in enumerate(pair_far):
            found.append((p, 0, block, 0, 0, n + 1))
            found += [
                (g, 0, block, k, 0, n + 1)
                for g, k in zip(got_two[n * count : (n + 1) * count], near_chips)
            ]
    arrays = []
    for entry in found:
        if not any(entry[0] is a for a in arrays):
            arrays.append(entry[0])
    swapped = swap_all([keyval, *keyval_far, *arrays])
    keyvals = [keyval, swapped[0]]
    for far, far_other in zip(keyval_far, swapped[1:]):
        keyvals += [far, far_other]
    others = swapped[1 + len(keyval_far) :]
    cross_weight = Weight((pairs, deep, 4 * local), row_places)
    for array, other in zip(arrays, others):
        entries = [e[1:] for e in found if e[0] is array]
        for source, places in ((array, mine_at), (other, other_at)):
            cross_weight.add(
                source,
                *[
                    (row, size, 0, 4 * local, n, places + k, offset)
                    for row, size, k, offset, n in entries
                ],
            )
    cross_weight.add(
        low_cross, *[(n * rank, rank, 0, 4 * local, n, zero, width) for n in range(pairs)]
    )

    near_feed = [spread([], 0, 0, ready_feed[0])]
    feed_from = [home_swap(step.wait(shard_feed[1])), turned(step.wait(shard_feed[1]))]
    stream_own, *branch = step.wait(stream_own, *branch)

    (
        stream_one, stream_two, normed_two, normed_three, query_cross, heads_cross, logsum_cross,
        low_two, low_three, low_four,
    ) = cross_forward(
        stream_own, branch, up[3], up[7], down[2], gains, biases, cross_weight, keyvals, core_at,
    )
    normed_own = step.mark(normed_three)
    (feed_from,) = wait_all(feed_from)
    ready_feed.append(step.mark(stacked(*feed_from)))

    normed_far = group.far_p(normed_own)
    cotangent_own = home_swap(step.wait(out_cotangent[0]))
    (normed_other,) = swap_all([normed_own])
    down_hidden = lax.dynamic_index_in_dim(
        adapter_down_hidden.transpose(0, 2, 1), index, 0, keepdims=False
    )
    up_hidden = lax.dynamic_index_in_dim(
        adapter_up_hidden.transpose(0, 2, 1, 3), index, 0, keepdims=False
    )
    feed_down, feed_up = piece(down_hidden, 0, hidden), piece(up_hidden, 0, hidden)
    feed_down, feed_gate, feed_upper = step.mark(feed_down, feed_up[0], feed_up[1])
    low_feed = [
        packed(feed_gate[:, to], feed_upper[:, to], feed_down[:, to])
        for to in [slice(a, a + p) for a, p in zip(at, parts)]
    ]
    low_feed = step.mark(*low_feed)
    (near_feed[0],) = wait_all(near_feed[0])
    rest_feed = spread(near_feed[0], 0, block, None)
    normed_far, (cotangent_own,) = wait_all(normed_far, [cotangent_own])
    cotangent_other, *normed_swapped = swap_all([cotangent_own, *normed_far])

    def feed_weight(i, rest):
        return chip_weight(
            (ready_feed[i], 0), [(g, 0) for g in near_feed[i]], [(g, 0) for g in rest],
            low_feed[i], 3 * parts[i], stacked_halves,
        )

    normed_blocks = [[normed_own, normed_other], []]
    cotangent_blocks = [[cotangent_own, cotangent_other], []]

    def feed_pass(weight, half, state, last):
        normed, cotangent = wait_all(normed_blocks[half], cotangent_blocks[half])
        found = feed(normed, cotangent, down[5], up[8], weight, state, tile, 0, last)
        *values, gdown, ggate, gupper = found
        return listed(step.mark(*values)), [gdown, ggate, gupper]

    def added(one, two):
        return [a + b for a, b in zip(one, two)]

    (rest_feed,) = wait_all(rest_feed) if rest_feed else ([],)
    weight = feed_weight(0, rest_feed)
    near_feed.append(spread([], 0, 0, ready_feed[1]))
    cotangent_far = group.far_p(cotangent_own)
    (y, dn, *lows), grads = feed_pass(weight, 0, (), False)
    states = [(*lows, y, dn)]
    near_feed[1], cotangent_far = wait_all(near_feed[1], cotangent_far)
    swapped = normed_swapped + swap_all(cotangent_far)
    for blocks, fars, others in (
        (normed_blocks[1], normed_far, swapped[: pairs - 1]),
        (cotangent_blocks[1], cotangent_far, swapped[pairs - 1 :]),
    ):
        for far, far_other in zip(fars, others):
            blocks += [far, far_other]
    rest_feed = spread(near_feed[1], 0, block, None)
    (y, dn, *lows), more = feed_pass(weight, 1, (), False)
    states.append((*lows, y, dn))
    feed_grads = [added(grads, more)]
    (rest_feed,) = wait_all(rest_feed) if rest_feed else ([],)

    weight = feed_weight(1, rest_feed)
    found, grads = feed_pass(weight, 1, states[1], True)
    y_far, dn_far = found[: len(found) // 2], found[len(found) // 2 :]

    (dn_sums,) = far_sums(dn_far)
    far = move_p(dn_sums)
    found, more = feed_pass(weight, 0, states[0], True)
    y_rows, dn_rows = found[:2], found[2:]
    feed_grads.append(added(grads, more))
    (far,) = wait_all(far)
    dn_other, y_other, *y_others = swap_all([dn_rows[1], y_rows[1], *y_far[1::2]])
    y_sums = listed(
        step.mark(*[group.near_sums(a, b).astype(BF) for a, b in zip(y_far[::2], y_others)])
    )
    grad_normed = [dn_rows[0], dn_other, *far]

    far = move_p(y_sums)
    grad_stream, branch_grad, fixed_rows, near_rows, *keyval_rows = cross_back(
        cotangent_own, listed(step.wait(*grad_normed)), stream_one, stream_two, normed_two,
        query_cross, heads_cross, logsum_cross, low_three, low_four, up[7], down[5], down[2],
        gains, biases, cross_weight, keyvals, core_at,
    )
    branch_grad, *keyval_rows = step.mark(branch_grad, *keyval_rows)
    (far,) = wait_all(far)

    branch_far = group.far_p(branch_grad)
    (branch_other,) = swap_all([branch_grad])

    def back(grad, heads, logsum, first, before, ends):
        return attend_back(
            grad, up[3], self_weight, query, keys, values, heads, logsum, tables, low_one, tile,
            first, before, ends,
        )

    def taken(by_piece, k):
        return lax.dynamic_index_in_dim(by_piece, pieces[k], 0, keepdims=False)

    def taken_near(by_member, k):
        member = k // 2 * 2 + (group.core ^ (k % 2))
        return lax.dynamic_index_in_dim(by_member, member, 0, keepdims=False)

    first_rows = listed(
        step.mark(
            *[
                stacked(taken_near(near_rows, k)[:rank], taken(fixed_rows, k)[rank : 2 * rank])
                for k in range(members)
            ]
        )
    )
    others = swap_all([*keyval_rows[1::2], *first_rows[1::2]])
    keyval_sums, first_sums = (
        [group.near_sums(a, b) for a, b in zip(own[::2], others[n * pairs : (n + 1) * pairs])]
        for n, own in enumerate((keyval_rows, first_rows))
    )
    moving = listed(step.mark(*[x.astype(BF) for x in keyval_sums[1:] + first_sums[1:]]))
    keyval_far, first_far = move_p(moving[: pairs - 1]), move_p(moving[pairs - 1 :])
    grads = listed(step.wait(branch_grad, branch_other))
    near_back = step.mark(*back(grads, heads_near, logsum_near, 0, None, None))
    branch_far, keyval_far, first_far = wait_all(branch_far, keyval_far, first_far)

    output, grad_up_eight = step.mark(
        *output_end(
            stream_two, [step.wait(y_rows[0]), y_other, *far], up[8], cotangent_own, members
        )
    )
    swapped = swap_all(branch_far)
    branch_blocks = []
    for f, o in zip(branch_far, swapped):
        branch_blocks += [f, o]

    def columns(array):
        return array.reshape(rank, -1, local).transpose(1, 0, 2)

    def sent(parts):
        parts.append(jnp.full((1, rank, local), index, F32))
        grads = jnp.concatenate(parts, axis=0).astype(BF).reshape(-1, local)
        grads = step.mark(grads)
        return [home_swap(grads), turned_back(grads)]

    def to_chips(blocks):
        both = step.mark(stacked(*blocks))
        return [both] + [xor_move(both, "chip", chips, k) for k in range(1, chips)]

    def every(blocks):
        blocks = [b.reshape(2, -1, rank, local) for b in blocks]
        labels = jnp.concatenate([b[:, -1, 0, 0] for b in blocks])
        return blocks, labels.astype(jnp.int32)

    def total(own, far):
        for f in far:
            own = own + f.astype(F32)
        return own

    summed = total(first_sums[0], first_far).reshape(-1, rank, local)
    first = sent([summed, *[columns(jnp.concatenate(g, axis=1)) for g in zip(*feed_grads)]])
    block_output = home_swap(step.wait(output))
    branch_blocks = listed(step.wait(*branch_blocks))
    found = back(
        branch_blocks, heads_far, logsum_far, near_tiles, near_back,
        (normed_one, low_two, branch_grad),
    )
    first, (block_output,), found = wait_all(first, [block_output], found)
    grad_down_one, grad_up_self, own_rows, *dn_blocks = found

    count = pairs - 1
    dn_others = swap_all(dn_blocks[1::2])
    dn_sums = [group.near_sums(a, b) for a, b in zip(dn_blocks[::2], dn_others)]
    far = move_p(listed(step.mark(*[x.astype(BF) for x in dn_sums[1:]])))
    first = to_chips(first)
    grad_keyval = step.mark(total(keyval_sums[0], keyval_far).astype(BF))
    grad_up_keyval, *found = step.mark(
        *context_back(
            at_pieces, context_blocks, keyval_weight, down_context, low_context, grad_keyval
        )
    )
    context_rows, grad_down_three = found[:members], found[members:]
    far, first = wait_all(far, first)

    second_rows = listed(
        step.mark(
            *[
                stacked(
                    taken(own_rows, k), taken(fixed_rows, k)[:rank],
                    taken(fixed_rows, k)[2 * rank :], taken(grad_up_eight, k), grad_down_three[k],
                    taken_near(near_rows, k)[rank:],
                )
                for k in range(members)
            ]
        )
    )
    swapped = swap_all([*second_rows[1::2], *context_rows[1::2]])
    second_sums, context_sums = (
        [group.near_sums(a, b) for a, b in zip(own[::2], swapped[n * pairs : (n + 1) * pairs])]
        for n, own in enumerate((second_rows, context_rows))
    )
    moving = [x.astype(BF) for x in second_sums[1:] + context_sums[1:]]
    moving = listed(step.mark(*moving))
    second_far, context_far = move_p(moving[:count]), move_p(moving[count:])
    grad_inputs = step.mark(
        input_end(
            stream_own, grad_stream, [dn_blocks[0], dn_others[0], *far], down[0], gains[0:1]
        )
    )
    second_far, context_far = wait_all(second_far, context_far)
    summed = total(second_sums[0], second_far).reshape(-1, rank, local)
    second = sent(
        [
            summed[0:1],
            grad_down_one[None],
            summed[2:3],
            summed[5:6],
            columns(grad_up_self),
            summed[1:2],
            summed[6:7],
            columns(grad_up_keyval),
            summed[3:5],
        ]
    )
    grad_context = home_swap(step.mark(total(context_sums[0], context_far).astype(BF)))
    (second,) = wait_all(second)
    second = to_chips(second)
    grad_inputs = home_swap(step.wait(grad_inputs))
    first, labels = every(listed(step.wait(*first)))
    grad_down, grad_hidden, grad_gate = settle_first(labels, first, slots, fold)
    grad_down = step.mark(grad_down)
    (second,) = wait_all(second)
    second, labels = every(second)
    labels = labels + (step.token[0, 0].astype(F32) * 0.0).astype(jnp.int32)
    grad_down, grad_up = settle_second(labels, second, grad_down)
    return (
        block_output[None],
        grad_inputs.astype(F32)[None],
        grad_context.astype(F32)[None],
        grad_down.transpose(0, 1, 3, 2),
        grad_hidden.transpose(0, 2, 1),
        grad_up.transpose(0, 2, 1, 3),
        grad_gate.transpose(0, 2, 1, 3),
    )


def solution(mesh):
    members = mesh.shape["tensor"]
    chips = mesh.shape["dp"] // 2
    mesh = Mesh(
        mesh.devices.reshape(chips, 2, 2, members // 2), ("chip", "core", "zhi", "p")
    )
    dp, tensor = ("chip", "core"), ("zhi", "p")
    in_specs = (
        P(dp, tensor, None),
        P(dp, None, tensor),
        P(dp, None),
        P(dp),
        P(dp, None, tensor),
        P(tensor, dp),
        P(dp, tensor),
        P(dp, None, tensor),
        P(tensor, dp),
        P(dp, None, tensor),
        P(tensor, dp),
        P(),
        P(),
        P(),
        P(),
        P(),
        P(),
        P(dp, tensor, None),
    )
    out_specs = (
        P(dp, tensor, None),
        P(dp, tensor, None),
        P(dp, None, tensor),
        P(None, None, tensor, None),
        P(None, tensor, None),
        P(None, None, None, tensor),
        P(None, None, None, tensor),
    )

    def run(*args):
        return body(*args, pairs=members // 2, chips=chips)

    return jax.shard_map(run, mesh=mesh, in_specs=in_specs, out_specs=out_specs, check_vma=False)
```
